32 devices in a mesh: groups: 2 (over y), gx: 4 (over z), gy: 2 (over x), gz: 2 (over core).
Axes of the slice: x: 2, y: 2, z: 4, core: 2. Of those that a mesh axis runs over, the one named last changes fastest.
Arguments:
- log_perm: float32 [32, 32, 1024], P(('groups', 'gx'), 'gy', 'gz'), parts along dimension 0, may hold values from -4 to 4
- source: float32 [32, 32, 1024], P(('groups', 'gx'), 'gy', 'gz'), parts along dimension 0, may hold values from -24 to 24
- low_bound: float32 [1], replicated, may hold values from 0.05 to 0.4
- high_bound: float32 [1], replicated, may hold values from 1.8 to 2.4
Outputs:
- fine_pressure: float32 [32, 32, 1024], P(('groups', 'gx'), 'gy', 'gz'), parts along dimension 0
- difference: float32 [32, 32, 1024], P(('groups', 'gx'), 'gy', 'gz'), parts along dimension 0
The draws below stay inside these ranges and needn't reach their ends.
There are 2 independent parts, one for each index of `groups`. The reference program is written for one: setup_inputs(seed, part) draws one part's arguments, and reference() takes and returns one part's arrays. A program takes and returns all parts, laid end to end along the dimension named above; an argument that names none is the same for every part. Nothing has to cross between parts.
All inputs are finite; a program needn't handle non-finite values.
Results may differ from the reference program's by a relative error of at most 0.00002.
Values sent between devices are 32-bit elements; how exact they have to be, the bound alone decides.
No kernel may reach another device: no remote copies, remote signals or barrier semaphores. Data moves between devices by JAX's collectives and lax.ppermute only.
A program may use at most 64 MiB of HBM per device.

```python
import jax
import jax.numpy as jnp

DEGREE = 3
NX = 16
NY = 32
NZ = 1024


def steps_of(own_key, dims, split, low, largest):
    factor_of, own = 1.0, jax.random.fold_in(own_key, 6)
    for position, shards_of in split:
        heights = jnp.exp(jax.random.uniform(jax.random.fold_in(own, position), (shards_of,), jnp.float32, low / len(split), largest / len(split)))
        factor_of = factor_of * jnp.repeat(heights, dims[position] // shards_of).reshape([-1 if axis == position else 1 for axis in range(len(dims))])
    return factor_of


def bell_draw(rng, extent, scale, most, split=(), kind=jnp.bfloat16):
    drawn = jax.random.normal(rng, extent, jnp.float32) * scale
    if len(split) > 0:
        drawn = steps_of(rng, extent, split, -0.22, 0.18) * drawn
    return jnp.clip(drawn, min=-most, max=most).astype(kind)


def setup_inputs(seed: int = 0, part: int = 0) -> dict:
    key_list = jax.random.split(jax.random.key(seed), 5)
    own_keys = jax.random.split(jax.random.fold_in(key_list[4], part), 5)
    return {
        "log_perm": bell_draw(own_keys[0], (NX, NY, NZ), 1.0, 4.0, ((0, 4), (1, 2), (2, 2)), jnp.float32),
        "source": bell_draw(own_keys[1], (NX, NY, NZ), 4.0, 24.0, ((0, 4), (1, 2), (2, 2)), jnp.float32),
        "low_bound": jnp.clip(jax.random.uniform(key_list[2], (1,), jnp.float32, 0.05, 0.4), 0.05, 0.4),
        "high_bound": jnp.clip(jax.random.uniform(key_list[3], (1,), jnp.float32, 1.8, 2.4), 1.8, 2.4),
    }


storage_rate = 0.1


def harmonic(first_perm, second_perm, face_scale):
    return face_scale * 2.0 * first_perm * second_perm / (first_perm + second_perm)


def coefficients(padded, face_scale, storage):
    centre = padded[1:-1, 1:-1, 1:-1]
    east_face = harmonic(centre, padded[2:, 1:-1, 1:-1], face_scale)
    west_face = harmonic(centre, padded[:-2, 1:-1, 1:-1], face_scale)
    north_face = harmonic(centre, padded[1:-1, 2:, 1:-1], face_scale)
    south_face = harmonic(centre, padded[1:-1, :-2, 1:-1], face_scale)
    upper_face = harmonic(centre, padded[1:-1, 1:-1, 2:], face_scale)
    lower_face = harmonic(centre, padded[1:-1, 1:-1, :-2], face_scale)
    diagonal = storage + east_face + west_face + north_face + south_face + upper_face + lower_face
    return (east_face, west_face, north_face, south_face, upper_face, lower_face, diagonal)


def operate(padded, face_terms):
    east_face, west_face, north_face, south_face, upper_face, lower_face, diagonal = face_terms
    centre = padded[1:-1, 1:-1, 1:-1]
    beside = east_face * padded[2:, 1:-1, 1:-1] + west_face * padded[:-2, 1:-1, 1:-1]
    beside = beside + north_face * padded[1:-1, 2:, 1:-1] + south_face * padded[1:-1, :-2, 1:-1]
    beside = beside + upper_face * padded[1:-1, 1:-1, 2:] + lower_face * padded[1:-1, 1:-1, :-2]
    return diagonal * centre - beside


def solve_level(log_field, source_field, lower_edge, upper_edge, face_scale, storage):
    face_terms = coefficients(jnp.pad(jnp.exp(log_field), 1), face_scale, storage)
    diagonal = face_terms[6]
    centre_value = (upper_edge + lower_edge) * 0.5
    half_width = (upper_edge - lower_edge) * 0.5
    ratio_sigma = centre_value / half_width
    rho_now = 1.0 / ratio_sigma
    direction = source_field / (centre_value * diagonal)
    solution = direction
    residual = source_field
    for iteration in range(DEGREE):
        residual = residual - operate(jnp.pad(direction, 1), face_terms)
        rho_next = 1.0 / (2.0 * ratio_sigma - rho_now)
        direction = rho_next * rho_now * direction + (2.0 * rho_next / half_width) * residual / diagonal
        solution = solution + direction
        rho_now = rho_next
    return solution


def reference(log_perm, source, low_bound, high_bound):
    lower_edge = low_bound[0]
    upper_edge = high_bound[0]
    fine = solve_level(log_perm, source, lower_edge, upper_edge, 1.0, storage_rate)
    blocks = (NX // 2, 2, NY // 2, 2, NZ // 2, 2)
    coarse_log = log_perm.reshape(blocks).mean(axis=(1, 3, 5))
    coarse_source = source.reshape(blocks).sum(axis=(1, 3, 5))
    coarse = solve_level(coarse_log, coarse_source, lower_edge, upper_edge, 2.0, 8.0 * storage_rate)
    spread = jnp.broadcast_to(coarse[:, None, :, None, :, None], blocks).reshape(NX, NY, NZ)
    return fine, fine - spread
```

```python
import functools

import jax
import jax.numpy as jnp
from jax import lax
from jax.experimental import pallas as pl
from jax.experimental.pallas import tpu as pltpu
from jax.sharding import PartitionSpec as P

DEGREE = 3
REACH = DEGREE + 1
LANES = 128
storage_rate = 0.1
AXES = ("gx", "gy", "gz")
VMEM = pl.BlockSpec(memory_space=pltpu.VMEM)
SMEM = pl.BlockSpec(memory_space=pltpu.SMEM)


def up_pairs(peers):
    return [(i, i + 1) for i in range(peers - 1)]


def down_pairs(peers):
    return [(i + 1, i) for i in range(peers - 1)]


def iota(shape, dim):
    return lax.broadcasted_iota(jnp.int32, shape, dim)


def turned(value, shift, axis):
    size = value.shape[axis]
    return pltpu.roll(value, shift % size, axis)


def numerators(shape, dim, own, index, peers, face_scale):
    place = iota(shape, dim)
    right = jnp.where(index < peers - 1, 2.0 * face_scale, 0.0)
    left = jnp.where(index > 0, 2.0 * face_scale, 0.0)
    return jnp.where(
        place == own - 1, right, jnp.where(place == shape[dim] - 1, left, 2.0 * face_scale)
    )


def iterate(count, log_at, source_at, x_faces, y_top, z_top, low, high, storage, refs):
    tx_ref, ty_ref, tz_ref, w_ref, d_ref, r_ref, p_ref = refs
    theta, delta = (high + low) * 0.5, (high - low) * 0.5
    sigma = theta / delta
    rho = 1.0 / sigma
    over_theta = 1.0 / theta
    after = jnp.exp(-log_at(0))
    tx_before = None
    for k in range(count):
        here = after
        if k + 1 < count:
            after = jnp.exp(-log_at(k + 1))
            tx = x_faces[k] / (here + after)
            tx_ref[k] = tx
        if 1 <= k <= count - 2:
            ty = y_top / (here + turned(here, -1, 0))
            tz = z_top / (here + turned(here, -1, 1))
            diagonal = storage + (tx_before + tx) + (ty + turned(ty, 1, 0)) + (tz + turned(tz, 1, 1))
            w = 1.0 / diagonal
            source = source_at(k)
            d_ref[k] = source * (over_theta * w)
            if 2 <= k <= count - 3:
                ty_ref[k] = ty
                tz_ref[k] = tz
                w_ref[k] = w
                r_ref[k] = source
        tx_before = tx
    for step in range(DEGREE):
        first, last = 2 + step, count - 2 - step
        rho_next = 1.0 / (2.0 * sigma - rho)
        keep, gain = rho_next * rho, 2.0 * rho_next / delta
        rho = rho_next
        here = d_ref[first]
        fx_before = tx_ref[first - 1] * (d_ref[first - 1] - here)
        for k in range(first, last):
            after = d_ref[k + 1]
            fx = tx_ref[k] * (here - after)
            fy = ty_ref[k] * (here - turned(here, -1, 0))
            fz = tz_ref[k] * (here - turned(here, -1, 1))
            applied = storage * here + (fx - fx_before) + (fy - turned(fy, 1, 0)) + (fz - turned(fz, 1, 1))
            residual = r_ref[k] - applied
            fresh = keep * here + gain * (residual * w_ref[k])
            if REACH <= k < count - REACH:
                so_far = here if step == 0 else p_ref[k]
                p_ref[k] = so_far + fresh
            if step < DEGREE - 1:
                r_ref[k] = residual
                d_ref[k] = fresh
            here, fx_before = after, fx


def window_scratch(count, rows, lanes):
    return [pltpu.VMEM((count, rows, lanes), jnp.float32)] * 7


def pool_kernel(log_ref, source_ref, out_ref, sum_ref):
    layers, rows, lanes = log_ref.shape
    pick = (iota((lanes, lanes // 2), 0) // 2 == iota((lanes, lanes // 2), 1)).astype(jnp.float32)
    for a, ref in enumerate((log_ref, source_ref)):
        for x in range(layers // 2):
            both = []
            for tile in range(lanes // LANES):
                columns = pl.ds(tile * LANES, LANES)
                sum_ref[tile] = ref[2 * x, :, columns] + ref[2 * x + 1, :, columns]
                both.append(
                    sum_ref[tile, pl.ds(0, rows // 2, stride=2), :]
                    + sum_ref[tile, pl.ds(1, rows // 2, stride=2), :]
                )
            both = jnp.concatenate(both, axis=1)
            pooled = jnp.dot(
                both, pick, precision=lax.Precision.HIGHEST, preferred_element_type=jnp.float32
            )
            out_ref[a, x] = pooled * 0.125 if a == 0 else pooled


def pool(log_perm, source):
    layers, rows, lanes = log_perm.shape
    return pl.pallas_call(
        pool_kernel,
        out_shape=jax.ShapeDtypeStruct((2, layers // 2, rows // 2, lanes // 2), jnp.float32),
        in_specs=[VMEM, VMEM],
        out_specs=VMEM,
        scratch_shapes=[pltpu.VMEM((lanes // LANES, rows, LANES), jnp.float32)],
        compiler_params=pltpu.CompilerParams(vmem_limit_bytes=8 << 20),
        cost_estimate=pl.CostEstimate(flops=10_000_000, bytes_accessed=300_000, transcendentals=0),
        name="pool",
    )(log_perm, source)


def coarse_kernel(peers, low_ref, high_ref, all_ref, out_ref, wide_ref, *refs):
    _, _, layers, rows, lanes = all_ref.shape
    ix, iy, iz = (lax.axis_index(axis) for axis in AXES)
    nx, ny, nz = peers
    y_right, y_left = jnp.minimum(iy + 1, ny - 1), jnp.maximum(iy - 1, 0)
    z_right, z_left = jnp.minimum(iz + 1, nz - 1), jnp.maximum(iz - 1, 0)
    tile_right = iota((rows, LANES), 1) < LANES // 2
    rows_right = iota((rows, lanes + LANES), 0) < rows // 2

    def strip(a, block, layer, y):
        x = jnp.clip(ix + block, 0, nx - 1)
        base = (x * ny + y) * nz
        own = all_ref[base + iz, a, layer]
        right = all_ref[base + z_right, a, layer, :, :LANES]
        left = all_ref[base + z_left, a, layer, :, lanes - LANES :]
        return jnp.concatenate([own, jnp.where(tile_right, right, left)], axis=1)

    around = -(-REACH // layers)
    skip = around * layers - REACH
    count = layers + 2 * REACH

    def window(a, k):
        block, layer = (k + skip) // layers - around, (k + skip) % layers
        halo = jnp.where(rows_right, strip(a, block, layer, y_right), strip(a, block, layer, y_left))
        return jnp.concatenate([strip(a, block, layer, iy), halo], axis=0)

    faces = []
    for k in range(count - 1):
        block = (k + skip) // layers - around
        beyond = (k + 1 + skip) // layers - around
        if block == beyond:
            faces.append(4.0)
        else:
            open_face = (ix + beyond <= nx - 1) if beyond > 0 else (ix + block >= 0)
            faces.append(jnp.where(open_face, 4.0, 0.0))
    shape = (2 * rows, lanes + LANES)
    iterate(
        count,
        functools.partial(window, 0),
        functools.partial(window, 1),
        faces,
        numerators(shape, 0, rows, iy, ny, 2.0),
        numerators(shape, 1, lanes, iz, nz, 2.0),
        jnp.full((1, shape[1]), low_ref[0]),
        jnp.full((1, shape[1]), high_ref[0]),
        8.0 * storage_rate,
        refs,
    )
    p_ref = refs[-1]
    widen = (iota((lanes, 2 * lanes), 0) == iota((lanes, 2 * lanes), 1) // 2).astype(jnp.float32)
    for x in range(layers):
        wide = jnp.dot(
            p_ref[REACH + x, :rows, :lanes],
            widen,
            precision=lax.Precision.HIGHEST,
            preferred_element_type=jnp.float32,
        )
        for tile in range(2 * lanes // LANES):
            columns = slice(tile * LANES, (tile + 1) * LANES)
            for half in range(2):
                wide_ref[tile, pl.ds(half, rows, stride=2), :] = wide[:, columns]
            for twin in range(2):
                out_ref[2 * x + twin, :, columns] = wide_ref[tile]


def coarse_level(everyone, low_bound, high_bound, peers):
    _, _, layers, rows, lanes = everyone.shape
    window = (layers + 2 * REACH, 2 * rows, lanes + LANES)
    return pl.pallas_call(
        functools.partial(coarse_kernel, peers),
        out_shape=jax.ShapeDtypeStruct((2 * layers, 2 * rows, 2 * lanes), jnp.float32),
        in_specs=[SMEM, SMEM, VMEM],
        out_specs=VMEM,
        scratch_shapes=[pltpu.VMEM((2 * lanes // LANES, 2 * rows, LANES), jnp.float32)]
        + window_scratch(*window),
        compiler_params=pltpu.CompilerParams(vmem_limit_bytes=24 << 20),
        cost_estimate=pl.CostEstimate(flops=20_000_000, bytes_accessed=4_000_000, transcendentals=0),
        name="coarse_level",
    )(low_bound, high_bound, everyone)


def unpacked(packed, rows, both_sides):
    log_own, source_own = packed[:rows], packed[rows : 2 * rows]
    if both_sides:
        log_halo, source_halo = packed[2 * rows : 2 * rows + 8], packed[2 * rows + 8 :]
    else:
        halo = packed[2 * rows :]
        swapped = turned(halo, REACH, 0)
        first = iota(halo.shape, 0) < REACH
        log_halo, source_halo = jnp.where(first, halo, swapped), jnp.where(first, swapped, halo)
    return (
        jnp.concatenate([log_own, log_halo], axis=0),
        jnp.concatenate([source_own, source_halo], axis=0),
    )


def fine_kernel(
    peers, low_ref, high_ref, left_ref, own_ref, right_ref, tile_ref, spread_ref, fine_ref, diff_ref, *refs
):
    layers, rows, lanes = fine_ref.shape
    ix, iy, iz = (lax.axis_index(axis) for axis in AXES)
    nx, ny, nz = peers
    blocks = (left_ref, own_ref, right_ref)
    count = layers + 2 * REACH
    skip = layers - REACH

    def window(a, k):
        block, layer = (k + skip) // layers, (k + skip) % layers
        core = unpacked(blocks[block][layer], rows, ny > 2)[a]
        tile = unpacked(tile_ref[block, layer], rows, ny > 2)[a]
        return jnp.concatenate([core, tile], axis=1)

    faces = [2.0] * (count - 1)
    faces[REACH - 1] = jnp.where(ix > 0, 2.0, 0.0)
    faces[REACH + layers - 1] = jnp.where(ix < nx - 1, 2.0, 0.0)
    shape = (rows + 2 * REACH, lanes + LANES)
    iterate(
        count,
        functools.partial(window, 0),
        functools.partial(window, 1),
        faces,
        numerators(shape, 0, rows, iy, ny, 1.0),
        numerators(shape, 1, lanes, iz, nz, 1.0),
        jnp.full((1, shape[1]), low_ref[0]),
        jnp.full((1, shape[1]), high_ref[0]),
        storage_rate,
        refs,
    )
    p_ref = refs[-1]
    for x in range(layers):
        fine = p_ref[REACH + x, :rows, :lanes]
        fine_ref[x] = fine
        diff_ref[x] = fine - spread_ref[x]


def fine_level(left, own, right, tile, spread, low_bound, high_bound, peers):
    layers, rows, lanes = spread.shape
    window = (layers + 2 * REACH, rows + 2 * REACH, lanes + LANES)
    out = jax.ShapeDtypeStruct(spread.shape, jnp.float32)
    return pl.pallas_call(
        functools.partial(fine_kernel, peers),
        out_shape=(out, out),
        in_specs=[SMEM, SMEM, VMEM, VMEM, VMEM, VMEM, VMEM],
        out_specs=(VMEM, VMEM),
        scratch_shapes=window_scratch(*window),
        compiler_params=pltpu.CompilerParams(vmem_limit_bytes=24 << 20),
        cost_estimate=pl.CostEstimate(flops=20_000_000, bytes_accessed=10_000_000, transcendentals=0),
        name="fine_level",
    )(low_bound, high_bound, left, own, right, tile, spread)


def exchange_rows(log_perm, source, peers):
    rows = log_perm.shape[1]
    last = jnp.concatenate([log_perm[:, rows - REACH :], source[:, rows - REACH :]], axis=1)
    first = jnp.concatenate([log_perm[:, :REACH], source[:, :REACH]], axis=1)
    if peers == 2:
        sent = jnp.where(lax.axis_index("gy") == 0, last, first)
        return lax.ppermute(sent, "gy", [(0, 1), (1, 0)])
    left = lax.ppermute(last, "gy", up_pairs(peers))
    right = lax.ppermute(first, "gy", down_pairs(peers))
    return jnp.concatenate(
        [right[:, :REACH], left[:, :REACH], right[:, REACH:], left[:, REACH:]], axis=1
    )


def exchange_lanes(blocks, peers):
    lanes = blocks[0].shape[-1]
    last = jnp.stack([block[..., lanes - LANES :] for block in blocks])
    first = jnp.stack([block[..., :LANES] for block in blocks])
    if peers == 2:
        sent = jnp.where(lax.axis_index("gz") == 0, last, first)
        return lax.ppermute(sent, "gz", [(0, 1), (1, 0)])
    left = lax.ppermute(last, "gz", up_pairs(peers))
    right = lax.ppermute(first, "gz", down_pairs(peers))
    return jnp.where(iota(left.shape, left.ndim - 1) < LANES // 2, right, left)


def shards(peers, log_perm, source, low_bound, high_bound):
    nx, ny, nz = peers
    everyone = lax.all_gather(pool(log_perm, source), AXES)
    halo = exchange_rows(log_perm, source, ny)
    own = jnp.concatenate([log_perm, source, halo], axis=1)
    left = lax.ppermute(own, "gx", up_pairs(nx))
    right = lax.ppermute(own, "gx", down_pairs(nx))
    tile = exchange_lanes((left, own, right), nz)
    spread = coarse_level(everyone, low_bound, high_bound, peers)
    return fine_level(left, own, right, tile, spread, low_bound, high_bound, peers)


def solution(mesh):
    peers = tuple(mesh.shape[axis] for axis in AXES)
    split = P(("groups", "gx"), "gy", "gz")
    return jax.shard_map(
        functools.partial(shards, peers),
        mesh=mesh,
        in_specs=(split, split, P(), P()),
        out_specs=(split, split),
        check_vma=False,
    )
```

```python
import functools

import jax
import jax.numpy as jnp
from jax import lax
from jax.experimental import pallas as pl
from jax.experimental.pallas import tpu as pltpu
from jax.sharding import PartitionSpec as P

DEGREE = 3
REACH = DEGREE + 1
LANES = 128
SUBLANES = 8
storage_rate = 0.1
AXES = ("gx", "gy", "gz")
VMEM = pl.BlockSpec(memory_space=pltpu.VMEM)
SMEM = pl.BlockSpec(memory_space=pltpu.SMEM)


def iota(shape, dim):
    return lax.broadcasted_iota(jnp.int32, shape, dim)


def turned(value, shift, axis):
    size = value.shape[axis]
    return pltpu.roll(value, shift % size, axis)


def both_ways(pairs):
    return [pair for i, j in pairs for pair in ((i, j), (j, i))]


def swap(axis, peers, right, left):
    even = lax.axis_index(axis) % 2 == 0
    first = lax.ppermute(
        right if right is left else jnp.where(even, right, left),
        axis,
        both_ways([(i, i + 1) for i in range(0, peers - 1, 2)]),
    )
    if peers == 2:
        return (first,)
    second = lax.ppermute(
        left if right is left else jnp.where(even, left, right),
        axis,
        both_ways([(i, i + 1) for i in range(1, peers - 1, 2)]),
    )
    return (first, second)


def far_swap(axis, peers, right, left):
    low = lax.axis_index(axis) % 4 < 2
    pairs = [(i, i + 2) for i in range(peers - 2)]
    near = [pair for pair in pairs if pair[0] % 4 < 2]
    rest = [pair for pair in pairs if pair[0] % 4 >= 2]
    got = []
    for chosen, sent in ((near, (right, left)), (rest, (left, right))):
        if chosen:
            got.append(lax.ppermute(jnp.where(low, *sent), axis, both_ways(chosen)))
    return tuple(got)


def from_right(is_first, got):
    return got[0] if len(got) == 1 else jnp.where(is_first, got[0], got[1])


def from_left(is_first, got):
    return got[0] if len(got) == 1 else jnp.where(is_first, got[1], got[0])


def numerators(shape, dim, own, index, peers, face_scale):
    place = iota(shape, dim)
    right = jnp.where(index < peers - 1, 2.0 * face_scale, 0.0)
    left = jnp.where(index > 0, 2.0 * face_scale, 0.0)
    return jnp.where(
        place == own - 1, right, jnp.where(place == shape[dim] - 1, left, 2.0 * face_scale)
    )


def iterate(count, log_at, source_at, x_faces, y_top, z_top, low, high, storage, refs):
    tx_ref, ty_ref, tz_ref, w_ref, d_ref, r_ref, p_ref = refs
    theta, delta = (high + low) * 0.5, (high - low) * 0.5
    sigma = theta / delta
    rho = 1.0 / sigma
    over_theta = 1.0 / theta
    after = jnp.exp(-log_at(0))
    tx_before = None
    for k in range(count):
        here = after
        if k + 1 < count:
            after = jnp.exp(-log_at(k + 1))
            tx = x_faces[k] / (here + after)
            tx_ref[k] = tx
        if 1 <= k <= count - 2:
            ty = y_top / (here + turned(here, -1, 0))
            tz = z_top / (here + turned(here, -1, 1))
            diagonal = storage + (tx_before + tx) + (ty + turned(ty, 1, 0)) + (tz + turned(tz, 1, 1))
            w = 1.0 / diagonal
            source = source_at(k)
            d_ref[k] = source * (over_theta * w)
            if 2 <= k <= count - 3:
                ty_ref[k] = ty
                tz_ref[k] = tz
                w_ref[k] = w
                r_ref[k] = source
        tx_before = tx
    for step in range(DEGREE):
        first, last = 2 + step, count - 2 - step
        rho_next = 1.0 / (2.0 * sigma - rho)
        keep, gain = rho_next * rho, 2.0 * rho_next / delta
        rho = rho_next
        here = d_ref[first]
        fx_before = tx_ref[first - 1] * (d_ref[first - 1] - here)
        for k in range(first, last):
            after = d_ref[k + 1]
            fx = tx_ref[k] * (here - after)
            fy = ty_ref[k] * (here - turned(here, -1, 0))
            fz = tz_ref[k] * (here - turned(here, -1, 1))
            applied = storage * here + (fx - fx_before) + (fy - turned(fy, 1, 0)) + (fz - turned(fz, 1, 1))
            residual = r_ref[k] - applied
            fresh = keep * here + gain * (residual * w_ref[k])
            if REACH <= k < count - REACH:
                so_far = here if step == 0 else p_ref[k]
                p_ref[k] = so_far + fresh
            if step < DEGREE - 1:
                r_ref[k] = residual
                d_ref[k] = fresh
            here, fx_before = after, fx


def window_scratch(count, rows, lanes):
    return [pltpu.VMEM((count, rows, lanes), jnp.float32)] * 7


def exact_dot(value, zero_one):
    parts = []
    for _ in range(3):
        part = value.astype(jnp.bfloat16)
        parts.append(part)
        value = value - part.astype(jnp.float32)
    rows = value.shape[0]
    out = jnp.dot(jnp.concatenate(parts, axis=0), zero_one, preferred_element_type=jnp.float32)
    return (out[2 * rows :] + out[rows : 2 * rows]) + out[:rows]


def pack_kernel(log_ref, source_ref, *refs):
    *halo_refs, out_ref, sum_ref = refs
    layers, rows, lanes = log_ref.shape
    even = lax.axis_index("gy") % 2 == 0
    starts = lax.axis_index("gy") == 0
    half = lanes // 2
    first_rows = iota((SUBLANES, lanes), 0) < REACH
    wide = len(halo_refs) == 2

    def halo(a, layer):
        got = tuple(ref[a * layers + layer] for ref in halo_refs)
        return from_right(even, got), from_left(even, got)

    slot = 0
    strips = []
    for layer in range(layers):
        tiles = []
        for a in range(2):
            right, left = halo(a, layer)
            tiles.append(jnp.where(first_rows, right, left) if wide else right)
        if wide:
            for tile in tiles:
                out_ref[slot] = tile
                slot += 1
        else:
            out_ref[slot] = jnp.where(first_rows == starts, tiles[0], turned(tiles[1], REACH, 0))
            slot += 1
    pieces = []

    def gather(top, bottom):
        for tile in range(lanes // LANES):
            columns = slice(tile * LANES, (tile + 1) * LANES)
            sum_ref[tile, :SUBLANES] = top[:, columns]
            sum_ref[tile, SUBLANES:] = bottom[:, columns]
        pieces.append(
            jnp.concatenate(
                [
                    sum_ref[tile, pl.ds(0, SUBLANES, stride=2), :]
                    + sum_ref[tile, pl.ds(1, SUBLANES, stride=2), :]
                    for tile in range(lanes // LANES)
                ],
                axis=1,
            )
        )

    for x in range(layers // 2):
        for ref in (log_ref, source_ref):
            both = ref[2 * x] + ref[2 * x + 1]
            gather(both[:SUBLANES], both[SUBLANES:])
    sums = []
    for x in range(layers // 2):
        for a in range(2):
            right, left = zip(halo(a, 2 * x), halo(a, 2 * x + 1))
            sums.append((right[0] + right[1], left[0] + left[1]))
    for x in range(layers // 2):
        if wide:
            continue
        gather(sums[2 * x][0], sums[2 * x + 1][0])
    if wide:
        for a in range(2):
            for x in range(layers // 2):
                gather(*sums[2 * x + a])
    pick = (iota((lanes, half), 0) // 2 == iota((lanes, half), 1)).astype(jnp.bfloat16)
    pooled = exact_dot(jnp.concatenate(pieces, axis=0), pick)
    tile = [pooled[SUBLANES * i : SUBLANES * (i + 1)] for i in range(len(pieces))]
    for x in range(layers // 2):
        tile[2 * x] = tile[2 * x] * 0.125
    if wide:
        for x in range(layers // 2):
            tile[layers + x] = tile[layers + x] * 0.125
    else:
        scale = jnp.where(iota((SUBLANES, half), 0) < REACH, 0.125, 1.0)
        for x in range(layers // 2):
            tile[layers + x] = tile[layers + x] * scale
    for i in range(0, len(tile), 2):
        out_ref[slot] = jnp.concatenate(tile[i : i + 2], axis=1)
        slot += 1


def pack(log_perm, source, got):
    layers, rows, lanes = log_perm.shape
    slots = len(got) * layers + 2 + len(got)
    return pl.pallas_call(
        pack_kernel,
        out_shape=jax.ShapeDtypeStruct((slots, SUBLANES, lanes), jnp.float32),
        in_specs=[VMEM] * (2 + len(got)),
        out_specs=VMEM,
        scratch_shapes=[pltpu.VMEM((lanes // LANES, 2 * SUBLANES, LANES), jnp.float32)],
        compiler_params=pltpu.CompilerParams(vmem_limit_bytes=8 << 20),
        cost_estimate=pl.CostEstimate(flops=5_000_000, bytes_accessed=700_000, transcendentals=0),
        name="pack",
    )(log_perm, source, *got)


def halves(both_sides, packed, partner):
    if both_sides:
        return packed, partner
    swapped = turned(packed, REACH, 0)
    return packed, swapped


def coarse_kernel(peers, slots, n_far, low_ref, high_ref, own_ref, *refs):
    near_refs, far_refs = refs[:2], refs[2 : 2 + n_far]
    tile_ref, out_ref, wide_ref, *scratch = refs[2 + n_far :]
    ix, iy, iz = (lax.axis_index(axis) for axis in AXES)
    nx, ny, nz = peers
    both_sides = ny > 2
    lanes = own_ref.shape[2] // 2
    rows = SUBLANES
    even, low = ix % 2 == 0, ix % 4 < 2
    strips, own_rows, near_rows, far_rows = slots
    top = iota((rows, lanes + LANES), 0) < REACH

    def packed(side, slot, half):
        columns = slice(half * lanes, (half + 1) * lanes)
        if side == 0:
            core = own_ref[strips + slot, :, columns]
            start = own_rows
        else:
            pick = from_left if side < 0 else from_right
            core = pick(even, tuple(ref[strips + slot, :, columns] for ref in near_refs))
            start = pick(even, tuple(near_rows))
        row = pl.multiple_of(start + (2 * slot + half) * rows, rows)
        return jnp.concatenate([core, tile_ref[pl.ds(row, rows), :]], axis=1)

    def far(side, slot, half):
        columns = slice(half * lanes, (half + 1) * lanes)
        pick = from_left if side < 0 else from_right
        core = pick(low, tuple(ref[slot, :, columns] for ref in far_refs))
        start = pick(low, tuple(far_rows))
        return jnp.concatenate([core, tile_ref[pl.ds(pl.multiple_of(start, rows), rows), :]], axis=1)

    def window(a, k):
        block, layer = k // 2 - 2, k % 2
        if abs(block) == 2:
            nearest = layer == (1 if block < 0 else 0)
            if a == 1:
                core = far(block, 1, 0)
                return jnp.concatenate([core, jnp.zeros_like(core)], axis=0)
            core = far(block, 0, 0 if nearest else 1)
            halo = far(block, 1, 1)
            if not both_sides:
                halo = jnp.where(top, halo, turned(halo, REACH, 0))
            return jnp.concatenate([core, halo], axis=0)
        core = packed(block, layer, a)
        if both_sides:
            halo = packed(block, 2 + a, layer)
        else:
            tile = packed(block, 2, layer)
            other = turned(tile, REACH, 0)
            halo = jnp.where(top, tile, other) if a == 0 else jnp.where(top, other, tile)
        return jnp.concatenate([core, halo], axis=0)

    def open_face(inside):
        return jnp.where(inside, 4.0, 0.0)

    faces = [4.0] * 9
    faces[1], faces[3] = open_face(ix > 1), open_face(ix > 0)
    faces[5], faces[7] = open_face(ix < nx - 1), open_face(ix < nx - 2)
    shape = (2 * rows, lanes + LANES)
    iterate(
        2 + 2 * REACH,
        functools.partial(window, 0),
        functools.partial(window, 1),
        faces,
        numerators(shape, 0, rows, iy, ny, 2.0),
        numerators(shape, 1, lanes, iz, nz, 2.0),
        jnp.full((1, shape[1]), low_ref[0]),
        jnp.full((1, shape[1]), high_ref[0]),
        8.0 * storage_rate,
        scratch,
    )
    p_ref = scratch[-1]
    widen = (iota((lanes, 2 * lanes), 0) == iota((lanes, 2 * lanes), 1) // 2).astype(jnp.bfloat16)
    pressure = jnp.concatenate([p_ref[REACH + x, :rows, :lanes] for x in range(2)], axis=0)
    wide = exact_dot(pressure, widen)
    for x in range(2):
        for tile in range(2 * lanes // LANES):
            columns = slice(tile * LANES, (tile + 1) * LANES)
            for half in range(2):
                wide_ref[tile, pl.ds(half, rows, stride=2), :] = wide[x * rows : (x + 1) * rows, columns]
            for twin in range(2):
                out_ref[2 * x + twin, :, columns] = wide_ref[tile]


def coarse_level(low_bound, high_bound, own, near, far, tile, slots, peers):
    lanes = own.shape[2] // 2
    window = (2 + 2 * REACH, 2 * SUBLANES, lanes + LANES)
    return pl.pallas_call(
        functools.partial(coarse_kernel, peers, slots, len(far)),
        out_shape=jax.ShapeDtypeStruct((REACH, 2 * SUBLANES, 2 * lanes), jnp.float32),
        in_specs=[SMEM, SMEM] + [VMEM] * (4 + len(far)),
        out_specs=VMEM,
        scratch_shapes=[pltpu.VMEM((2 * lanes // LANES, 2 * SUBLANES, LANES), jnp.float32)]
        + window_scratch(*window),
        compiler_params=pltpu.CompilerParams(vmem_limit_bytes=24 << 20),
        cost_estimate=pl.CostEstimate(flops=20_000_000, bytes_accessed=4_000_000, transcendentals=0),
        name="coarse_level",
    )(low_bound, high_bound, own, *near, *far, tile)


def fine_kernel(
    peers,
    slots,
    low_ref,
    high_ref,
    log_ref,
    source_ref,
    own_ref,
    first_ref,
    second_ref,
    first_pack_ref,
    second_pack_ref,
    tile_ref,
    spread_ref,
    fine_ref,
    diff_ref,
    *refs,
):
    layers, rows, lanes = fine_ref.shape
    ix, iy, iz = (lax.axis_index(axis) for axis in AXES)
    nx, ny, nz = peers
    both_sides = ny > 2
    even = ix % 2 == 0
    count = 3 * layers
    own_rows, own_strip_rows, raw_rows, strip_rows = slots

    def lane_tile(start, size):
        return tile_ref[pl.ds(pl.multiple_of(start, SUBLANES), size), :]

    def window(a, k):
        side, layer = k // layers - 1, k % layers
        if side == 0:
            core = (log_ref, source_ref)[a][layer]
            core_tile = lane_tile(own_rows + (a * layers + layer) * rows, rows)
            strip = lambda slot: own_ref[slot]
            strip_start = own_strip_rows
        else:
            pick = from_left if side < 0 else from_right
            slot = layer if a == 0 else layers + layer - (1 if side < 0 else 0)
            core = pick(even, (first_ref[slot], second_ref[slot]))
            core_tile = lane_tile(pick(even, tuple(raw_rows)) + slot * rows, rows)
            strip = lambda slot: pick(even, (first_pack_ref[slot], second_pack_ref[slot]))
            strip_start = pick(even, tuple(strip_rows))
        if both_sides:
            slot = 2 * layer + a
        else:
            slot = layer
        halo = jnp.concatenate(
            [strip(slot), lane_tile(strip_start + slot * SUBLANES, SUBLANES)], axis=1
        )
        if a == 1 and not both_sides:
            halo = turned(halo, REACH, 0)
        return jnp.concatenate([jnp.concatenate([core, core_tile], axis=1), halo], axis=0)

    faces = [2.0] * (count - 1)
    faces[layers - 1] = jnp.where(ix > 0, 2.0, 0.0)
    faces[2 * layers - 1] = jnp.where(ix < nx - 1, 2.0, 0.0)
    shape = (rows + 2 * REACH, lanes + LANES)
    iterate(
        count,
        functools.partial(window, 0),
        functools.partial(window, 1),
        faces,
        numerators(shape, 0, rows, iy, ny, 1.0),
        numerators(shape, 1, lanes, iz, nz, 1.0),
        jnp.full((1, shape[1]), low_ref[0]),
        jnp.full((1, shape[1]), high_ref[0]),
        storage_rate,
        refs,
    )
    p_ref = refs[-1]
    for x in range(layers):
        fine = p_ref[REACH + x, :rows, :lanes]
        fine_ref[x] = fine
        diff_ref[x] = fine - spread_ref[x]


def fine_level(low_bound, high_bound, log_perm, source, own, raw, near, tile, spread, slots, peers):
    layers, rows, lanes = log_perm.shape
    window = (layers + 2 * REACH, rows + 2 * REACH, lanes + LANES)
    out = jax.ShapeDtypeStruct(log_perm.shape, jnp.float32)
    return pl.pallas_call(
        functools.partial(fine_kernel, peers, slots),
        out_shape=(out, out),
        in_specs=[SMEM, SMEM] + [VMEM] * 9,
        out_specs=(VMEM, VMEM),
        scratch_shapes=window_scratch(*window),
        compiler_params=pltpu.CompilerParams(vmem_limit_bytes=24 << 20),
        cost_estimate=pl.CostEstimate(flops=20_000_000, bytes_accessed=10_000_000, transcendentals=0),
        name="fine_level",
    )(low_bound, high_bound, log_perm, source, own, *raw, *near, tile, spread)


def shards(peers, log_perm, source, low_bound, high_bound):
    nx, ny, nz = peers
    layers, rows, lanes = log_perm.shape
    assert layers == REACH and rows == 2 * SUBLANES and nx > 2
    half = lanes // 2
    stacked = jnp.concatenate([log_perm, source], axis=0)
    got_rows = swap("gy", ny, stacked[:, rows - SUBLANES :], stacked[:, :SUBLANES])
    raw = swap("gx", nx, jnp.concatenate([log_perm, source[1:]]), jnp.concatenate([log_perm, source[:-1]]))
    own = pack(log_perm, source, got_rows)
    near = swap("gx", nx, own, own)
    strips = len(got_rows) * layers
    pooled = own[strips:]
    left_half, right_half = pooled[..., :half], pooled[..., half:]

    def far_pack(inner, outer):
        halo = (left_half, right_half)[inner][2]
        return jnp.stack(
            [
                jnp.concatenate([left_half[inner], left_half[outer]], axis=1),
                jnp.concatenate([right_half[inner], halo], axis=1),
            ]
        )

    far = far_swap("gx", nx, far_pack(1, 0), far_pack(0, 1))
    offset, edges = 0, []

    def add(array, columns):
        nonlocal offset
        start = offset
        flat = array.reshape(-1, array.shape[-1])[:, columns]
        edges.append(flat)
        offset += flat.shape[0]
        return start

    whole = slice(0, lanes)

    def add_pooled(array):
        return add(array[strips:].reshape(-1, SUBLANES, 2, half).swapaxes(1, 2), slice(0, half))

    own_rows = add(stacked, whole)
    raw_rows = [add(block, whole) for block in raw]
    own_strip_rows = add(own[:strips], whole)
    strip_rows = [add(block[:strips], whole) for block in near]
    own_pooled = add_pooled(own)
    near_pooled = [add_pooled(block) for block in near]
    far_rows = [add(block[0], slice(0, half)) for block in far]
    last = jnp.concatenate([flat[:, -LANES:] for flat in edges])
    first = jnp.concatenate([flat[:, :LANES] for flat in edges])
    if nz == 2:
        sent = jnp.where(lax.axis_index("gz") == 0, last, first)
        tile = lax.ppermute(sent, "gz", [(0, 1), (1, 0)])
    else:
        even = lax.axis_index("gz") % 2 == 0
        got = swap("gz", nz, last, first)
        tile = jnp.where(
            iota(last.shape, 1) < LANES // 2, from_right(even, got), from_left(even, got)
        )
    spread = coarse_level(
        low_bound,
        high_bound,
        own,
        near,
        far,
        tile,
        (strips, own_pooled, near_pooled, far_rows),
        peers,
    )
    return fine_level(
        low_bound,
        high_bound,
        log_perm,
        source,
        own,
        raw,
        near,
        tile,
        spread,
        (own_rows, own_strip_rows, raw_rows, strip_rows),
        peers,
    )


def solution(mesh):
    peers = tuple(mesh.shape[axis] for axis in AXES)
    split = P(("groups", "gx"), "gy", "gz")
    return jax.shard_map(
        functools.partial(shards, peers),
        mesh=mesh,
        in_specs=(split, split, P(), P()),
        out_specs=(split, split),
        check_vma=False,
    )
```

```python
import functools

import jax
import jax.numpy as jnp
from jax import lax
from jax.experimental import pallas as pl
from jax.experimental.pallas import tpu as pltpu
from jax.sharding import PartitionSpec as P

DEGREE = 3
REACH = DEGREE + 1
LANES = 128
SUBLANES = 8
storage_rate = 0.1
AXES = ("gx", "gy", "gz")
VMEM = pl.BlockSpec(memory_space=pltpu.VMEM)
SMEM = pl.BlockSpec(memory_space=pltpu.SMEM)


def iota(shape, dim):
    return lax.broadcasted_iota(jnp.int32, shape, dim)


def turned(value, shift, axis):
    size = value.shape[axis]
    return pltpu.roll(value, shift % size, axis)


def both_ways(peers, pairs):
    partner = list(range(peers))
    for i, j in pairs:
        partner[i], partner[j] = j, i
    return list(enumerate(partner))


def swap(axis, peers, right, left):
    even = lax.axis_index(axis) % 2 == 0
    first = lax.ppermute(
        right if right is left else jnp.where(even, right, left),
        axis,
        both_ways(peers, [(i, i + 1) for i in range(0, peers - 1, 2)]),
    )
    if peers == 2:
        return (first,)
    second = lax.ppermute(
        left if right is left else jnp.where(even, left, right),
        axis,
        both_ways(peers, [(i, i + 1) for i in range(1, peers - 1, 2)]),
    )
    return (first, second)


def far_swap(axis, peers, right, left):
    low = lax.axis_index(axis) % 4 < 2
    pairs = [(i, i + 2) for i in range(peers - 2)]
    near = [pair for pair in pairs if pair[0] % 4 < 2]
    rest = [pair for pair in pairs if pair[0] % 4 >= 2]
    got = []
    for chosen, sent in ((near, (right, left)), (rest, (left, right))):
        if chosen:
            got.append(lax.ppermute(jnp.where(low, *sent), axis, both_ways(peers, chosen)))
    return tuple(got)


def from_right(is_first, got):
    return got[0] if len(got) == 1 else jnp.where(is_first, got[0], got[1])


def from_left(is_first, got):
    return got[0] if len(got) == 1 else jnp.where(is_first, got[1], got[0])


def numerators(shape, dim, own, index, peers, face_scale):
    place = iota(shape, dim)
    right = jnp.where(index < peers - 1, 2.0 * face_scale, 0.0)
    left = jnp.where(index > 0, 2.0 * face_scale, 0.0)
    return jnp.where(
        place == own - 1, right, jnp.where(place == shape[dim] - 1, left, 2.0 * face_scale)
    )


def iterate(count, log_at, source_at, x_faces, y_top, z_top, low, high, storage, refs):
    tx_ref, ty_ref, tz_ref, w_ref, d_ref, r_ref, p_ref = refs
    theta, delta = (high + low) * 0.5, (high - low) * 0.5
    sigma = theta / delta
    rho = 1.0 / sigma
    over_theta = 1.0 / theta
    after = jnp.exp(-log_at(0))
    tx_before = None
    for k in range(count):
        here = after
        if k + 1 < count:
            after = jnp.exp(-log_at(k + 1))
            tx = x_faces[k] / (here + after)
            tx_ref[k] = tx
        if 1 <= k <= count - 2:
            ty = y_top / (here + turned(here, -1, 0))
            tz = z_top / (here + turned(here, -1, 1))
            diagonal = storage + (tx_before + tx) + (ty + turned(ty, 1, 0)) + (tz + turned(tz, 1, 1))
            w = 1.0 / diagonal
            source = source_at(k)
            d_ref[k] = source * (over_theta * w)
            if 2 <= k <= count - 3:
                ty_ref[k] = ty
                tz_ref[k] = tz
                w_ref[k] = w
                r_ref[k] = source
        tx_before = tx
    for step in range(DEGREE):
        first, last = 2 + step, count - 2 - step
        rho_next = 1.0 / (2.0 * sigma - rho)
        keep, gain = rho_next * rho, 2.0 * rho_next / delta
        rho = rho_next
        here = d_ref[first]
        fx_before = tx_ref[first - 1] * (d_ref[first - 1] - here)
        for k in range(first, last):
            after = d_ref[k + 1]
            fx = tx_ref[k] * (here - after)
            fy = ty_ref[k] * (here - turned(here, -1, 0))
            fz = tz_ref[k] * (here - turned(here, -1, 1))
            applied = storage * here + (fx - fx_before) + (fy - turned(fy, 1, 0)) + (fz - turned(fz, 1, 1))
            residual = r_ref[k] - applied
            fresh = keep * here + gain * (residual * w_ref[k])
            if REACH <= k < count - REACH:
                so_far = here if step == 0 else p_ref[k]
                p_ref[k] = so_far + fresh
            if step < DEGREE - 1:
                r_ref[k] = residual
                d_ref[k] = fresh
            here, fx_before = after, fx


def window_scratch(count, rows, lanes):
    return [pltpu.VMEM((count, rows, lanes), jnp.float32)] * 7


def exact_dot(value, zero_one):
    parts = []
    for _ in range(3):
        part = value.astype(jnp.bfloat16)
        parts.append(part)
        value = value - part.astype(jnp.float32)
    rows = value.shape[0]
    out = jnp.dot(jnp.concatenate(parts, axis=0), zero_one, preferred_element_type=jnp.float32)
    return (out[2 * rows :] + out[rows : 2 * rows]) + out[:rows]


def pack_kernel(log_ref, source_ref, *refs):
    *halo_refs, out_ref, sum_ref = refs
    layers, rows, lanes = log_ref.shape
    even = lax.axis_index("gy") % 2 == 0
    starts = lax.axis_index("gy") == 0
    half = lanes // 2
    first_rows = iota((SUBLANES, lanes), 0) < REACH
    wide = len(halo_refs) == 2

    def halo(a, layer):
        got = tuple(ref[a * layers + layer] for ref in halo_refs)
        return from_right(even, got), from_left(even, got)

    slot = 0
    strips = []
    for layer in range(layers):
        tiles = []
        for a in range(2):
            right, left = halo(a, layer)
            tiles.append(jnp.where(first_rows, right, left) if wide else right)
        if wide:
            for tile in tiles:
                out_ref[slot] = tile
                slot += 1
        else:
            out_ref[slot] = jnp.where(first_rows == starts, tiles[0], turned(tiles[1], REACH, 0))
            slot += 1
    pieces = []

    def gather(top, bottom):
        for tile in range(lanes // LANES):
            columns = slice(tile * LANES, (tile + 1) * LANES)
            sum_ref[tile, :SUBLANES] = top[:, columns]
            sum_ref[tile, SUBLANES:] = bottom[:, columns]
        pieces.append(
            jnp.concatenate(
                [
                    sum_ref[tile, pl.ds(0, SUBLANES, stride=2), :]
                    + sum_ref[tile, pl.ds(1, SUBLANES, stride=2), :]
                    for tile in range(lanes // LANES)
                ],
                axis=1,
            )
        )

    for x in range(layers // 2):
        for ref in (log_ref, source_ref):
            both = ref[2 * x] + ref[2 * x + 1]
            gather(both[:SUBLANES], both[SUBLANES:])
    sums = []
    for x in range(layers // 2):
        for a in range(2):
            right, left = zip(halo(a, 2 * x), halo(a, 2 * x + 1))
            sums.append((right[0] + right[1], left[0] + left[1]))
    for x in range(layers // 2):
        if wide:
            continue
        gather(sums[2 * x][0], sums[2 * x + 1][0])
    if wide:
        for a in range(2):
            for x in range(layers // 2):
                gather(*sums[2 * x + a])
    pick = (iota((lanes, half), 0) // 2 == iota((lanes, half), 1)).astype(jnp.bfloat16)
    pooled = exact_dot(jnp.concatenate(pieces, axis=0), pick)
    tile = [pooled[SUBLANES * i : SUBLANES * (i + 1)] for i in range(len(pieces))]
    for x in range(layers // 2):
        tile[2 * x] = tile[2 * x] * 0.125
    if wide:
        for x in range(layers // 2):
            tile[layers + x] = tile[layers + x] * 0.125
    else:
        scale = jnp.where(iota((SUBLANES, half), 0) < REACH, 0.125, 1.0)
        for x in range(layers // 2):
            tile[layers + x] = tile[layers + x] * scale
    for i in range(0, len(tile), 2):
        out_ref[slot] = jnp.concatenate(tile[i : i + 2], axis=1)
        slot += 1


def pack(log_perm, source, got):
    layers, rows, lanes = log_perm.shape
    slots = len(got) * layers + 2 + len(got)
    return pl.pallas_call(
        pack_kernel,
        out_shape=jax.ShapeDtypeStruct((slots, SUBLANES, lanes), jnp.float32),
        in_specs=[VMEM] * (2 + len(got)),
        out_specs=VMEM,
        scratch_shapes=[pltpu.VMEM((lanes // LANES, 2 * SUBLANES, LANES), jnp.float32)],
        compiler_params=pltpu.CompilerParams(vmem_limit_bytes=8 << 20),
        cost_estimate=pl.CostEstimate(flops=5_000_000, bytes_accessed=700_000, transcendentals=0),
        name="pack",
    )(log_perm, source, *got)


def halves(both_sides, packed, partner):
    if both_sides:
        return packed, partner
    swapped = turned(packed, REACH, 0)
    return packed, swapped


def coarse_kernel(peers, slots, n_far, low_ref, high_ref, own_ref, *refs):
    near_refs, far_refs = refs[:2], refs[2 : 2 + n_far]
    tile_ref, out_ref, wide_ref, *scratch = refs[2 + n_far :]
    ix, iy, iz = (lax.axis_index(axis) for axis in AXES)
    nx, ny, nz = peers
    both_sides = ny > 2
    lanes = own_ref.shape[2] // 2
    rows = SUBLANES
    even, low = ix % 2 == 0, ix % 4 < 2
    strips, own_rows, near_rows, far_rows = slots
    top = iota((rows, lanes + LANES), 0) < REACH

    def packed(side, slot, half):
        columns = slice(half * lanes, (half + 1) * lanes)
        if side == 0:
            core = own_ref[strips + slot, :, columns]
            start = own_rows
        else:
            pick = from_left if side < 0 else from_right
            core = pick(even, tuple(ref[strips + slot, :, columns] for ref in near_refs))
            start = pick(even, tuple(near_rows))
        row = pl.multiple_of(start + (2 * slot + half) * rows, rows)
        return jnp.concatenate([core, tile_ref[pl.ds(row, rows), :]], axis=1)

    def far(side, slot, half):
        columns = slice(half * lanes, (half + 1) * lanes)
        pick = from_left if side < 0 else from_right
        core = pick(low, tuple(ref[slot, :, columns] for ref in far_refs))
        start = pick(low, tuple(far_rows))
        return jnp.concatenate([core, tile_ref[pl.ds(pl.multiple_of(start, rows), rows), :]], axis=1)

    def window(a, k):
        block, layer = k // 2 - 2, k % 2
        if abs(block) == 2:
            nearest = layer == (1 if block < 0 else 0)
            if a == 1:
                core = far(block, 1, 0)
                return jnp.concatenate([core, jnp.zeros_like(core)], axis=0)
            core = far(block, 0, 0 if nearest else 1)
            halo = far(block, 1, 1)
            if not both_sides:
                halo = jnp.where(top, halo, turned(halo, REACH, 0))
            return jnp.concatenate([core, halo], axis=0)
        core = packed(block, layer, a)
        if both_sides:
            halo = packed(block, 2 + a, layer)
        else:
            tile = packed(block, 2, layer)
            other = turned(tile, REACH, 0)
            halo = jnp.where(top, tile, other) if a == 0 else jnp.where(top, other, tile)
        return jnp.concatenate([core, halo], axis=0)

    def open_face(inside):
        return jnp.where(inside, 4.0, 0.0)

    faces = [4.0] * 9
    faces[1], faces[3] = open_face(ix > 1), open_face(ix > 0)
    faces[5], faces[7] = open_face(ix < nx - 1), open_face(ix < nx - 2)
    shape = (2 * rows, lanes + LANES)
    iterate(
        2 + 2 * REACH,
        functools.partial(window, 0),
        functools.partial(window, 1),
        faces,
        numerators(shape, 0, rows, iy, ny, 2.0),
        numerators(shape, 1, lanes, iz, nz, 2.0),
        jnp.full((1, shape[1]), low_ref[0]),
        jnp.full((1, shape[1]), high_ref[0]),
        8.0 * storage_rate,
        scratch,
    )
    p_ref = scratch[-1]
    widen = (iota((lanes, 2 * lanes), 0) == iota((lanes, 2 * lanes), 1) // 2).astype(jnp.bfloat16)
    pressure = jnp.concatenate([p_ref[REACH + x, :rows, :lanes] for x in range(2)], axis=0)
    wide = exact_dot(pressure, widen)
    for x in range(2):
        for tile in range(2 * lanes // LANES):
            columns = slice(tile * LANES, (tile + 1) * LANES)
            for half in range(2):
                wide_ref[tile, pl.ds(half, rows, stride=2), :] = wide[x * rows : (x + 1) * rows, columns]
            for twin in range(2):
                out_ref[2 * x + twin, :, columns] = wide_ref[tile]


def coarse_level(low_bound, high_bound, own, near, far, tile, slots, peers):
    lanes = own.shape[2] // 2
    window = (2 + 2 * REACH, 2 * SUBLANES, lanes + LANES)
    return pl.pallas_call(
        functools.partial(coarse_kernel, peers, slots, len(far)),
        out_shape=jax.ShapeDtypeStruct((REACH, 2 * SUBLANES, 2 * lanes), jnp.float32),
        in_specs=[SMEM, SMEM] + [VMEM] * (4 + len(far)),
        out_specs=VMEM,
        scratch_shapes=[pltpu.VMEM((2 * lanes // LANES, 2 * SUBLANES, LANES), jnp.float32)]
        + window_scratch(*window),
        compiler_params=pltpu.CompilerParams(vmem_limit_bytes=24 << 20),
        cost_estimate=pl.CostEstimate(flops=20_000_000, bytes_accessed=4_000_000, transcendentals=0),
        name="coarse_level",
    )(low_bound, high_bound, own, *near, *far, tile)


def fine_kernel(
    peers,
    slots,
    low_ref,
    high_ref,
    log_ref,
    source_ref,
    own_ref,
    first_ref,
    second_ref,
    first_pack_ref,
    second_pack_ref,
    tile_ref,
    spread_ref,
    fine_ref,
    diff_ref,
    *refs,
):
    layers, rows, lanes = fine_ref.shape
    ix, iy, iz = (lax.axis_index(axis) for axis in AXES)
    nx, ny, nz = peers
    both_sides = ny > 2
    even = ix % 2 == 0
    count = 3 * layers
    own_rows, own_strip_rows, raw_rows, strip_rows = slots

    def lane_tile(start, size):
        return tile_ref[pl.ds(pl.multiple_of(start, SUBLANES), size), :]

    def window(a, k):
        side, layer = k // layers - 1, k % layers
        if side == 0:
            core = (log_ref, source_ref)[a][layer]
            core_tile = lane_tile(own_rows + (a * layers + layer) * rows, rows)
            strip = lambda slot: own_ref[slot]
            strip_start = own_strip_rows
        else:
            pick = from_left if side < 0 else from_right
            slot = layer if a == 0 else layers + layer - (1 if side < 0 else 0)
            core = pick(even, (first_ref[slot], second_ref[slot]))
            core_tile = lane_tile(pick(even, tuple(raw_rows)) + slot * rows, rows)
            strip = lambda slot: pick(even, (first_pack_ref[slot], second_pack_ref[slot]))
            strip_start = pick(even, tuple(strip_rows))
        if both_sides:
            slot = 2 * layer + a
        else:
            slot = layer
        halo = jnp.concatenate(
            [strip(slot), lane_tile(strip_start + slot * SUBLANES, SUBLANES)], axis=1
        )
        if a == 1 and not both_sides:
            halo = turned(halo, REACH, 0)
        return jnp.concatenate([jnp.concatenate([core, core_tile], axis=1), halo], axis=0)

    faces = [2.0] * (count - 1)
    faces[layers - 1] = jnp.where(ix > 0, 2.0, 0.0)
    faces[2 * layers - 1] = jnp.where(ix < nx - 1, 2.0, 0.0)
    shape = (rows + 2 * REACH, lanes + LANES)
    iterate(
        count,
        functools.partial(window, 0),
        functools.partial(window, 1),
        faces,
        numerators(shape, 0, rows, iy, ny, 1.0),
        numerators(shape, 1, lanes, iz, nz, 1.0),
        jnp.full((1, shape[1]), low_ref[0]),
        jnp.full((1, shape[1]), high_ref[0]),
        storage_rate,
        refs,
    )
    p_ref = refs[-1]
    for x in range(layers):
        fine = p_ref[REACH + x, :rows, :lanes]
        fine_ref[x] = fine
        diff_ref[x] = fine - spread_ref[x]


def fine_level(low_bound, high_bound, log_perm, source, own, raw, near, tile, spread, slots, peers):
    layers, rows, lanes = log_perm.shape
    window = (layers + 2 * REACH, rows + 2 * REACH, lanes + LANES)
    out = jax.ShapeDtypeStruct(log_perm.shape, jnp.float32)
    return pl.pallas_call(
        functools.partial(fine_kernel, peers, slots),
        out_shape=(out, out),
        in_specs=[SMEM, SMEM] + [VMEM] * 9,
        out_specs=(VMEM, VMEM),
        scratch_shapes=window_scratch(*window),
        compiler_params=pltpu.CompilerParams(vmem_limit_bytes=24 << 20),
        cost_estimate=pl.CostEstimate(flops=20_000_000, bytes_accessed=10_000_000, transcendentals=0),
        name="fine_level",
    )(low_bound, high_bound, log_perm, source, own, *raw, *near, tile, spread)


def shards(peers, log_perm, source, low_bound, high_bound):
    nx, ny, nz = peers
    layers, rows, lanes = log_perm.shape
    assert layers == REACH and rows == 2 * SUBLANES and nx > 2
    half = lanes // 2
    stacked = jnp.concatenate([log_perm, source], axis=0)
    got_rows = swap("gy", ny, stacked[:, rows - SUBLANES :], stacked[:, :SUBLANES])
    raw = swap("gx", nx, jnp.concatenate([log_perm, source[1:]]), jnp.concatenate([log_perm, source[:-1]]))
    own = pack(log_perm, source, got_rows)
    near = swap("gx", nx, own, own)
    strips = len(got_rows) * layers
    pooled = own[strips:]
    left_half, right_half = pooled[..., :half], pooled[..., half:]

    def far_pack(inner, outer):
        halo = (left_half, right_half)[inner][2]
        return jnp.stack(
            [
                jnp.concatenate([left_half[inner], left_half[outer]], axis=1),
                jnp.concatenate([right_half[inner], halo], axis=1),
            ]
        )

    far = far_swap("gx", nx, far_pack(1, 0), far_pack(0, 1))
    offset, edges = 0, []

    def add(array, columns):
        nonlocal offset
        start = offset
        flat = array.reshape(-1, array.shape[-1])[:, columns]
        edges.append(flat)
        offset += flat.shape[0]
        return start

    whole = slice(0, lanes)

    def add_pooled(array):
        return add(array[strips:].reshape(-1, SUBLANES, 2, half).swapaxes(1, 2), slice(0, half))

    own_rows = add(stacked, whole)
    raw_rows = [add(block, whole) for block in raw]
    own_strip_rows = add(own[:strips], whole)
    strip_rows = [add(block[:strips], whole) for block in near]
    own_pooled = add_pooled(own)
    near_pooled = [add_pooled(block) for block in near]
    far_rows = [add(block[0], slice(0, half)) for block in far]
    last = jnp.concatenate([flat[:, -LANES:] for flat in edges])
    first = jnp.concatenate([flat[:, :LANES] for flat in edges])
    if nz == 2:
        sent = jnp.where(lax.axis_index("gz") == 0, last, first)
        tile = lax.ppermute(sent, "gz", [(0, 1), (1, 0)])
    else:
        even = lax.axis_index("gz") % 2 == 0
        got = swap("gz", nz, last, first)
        tile = jnp.where(
            iota(last.shape, 1) < LANES // 2, from_right(even, got), from_left(even, got)
        )
    spread = coarse_level(
        low_bound,
        high_bound,
        own,
        near,
        far,
        tile,
        (strips, own_pooled, near_pooled, far_rows),
        peers,
    )
    return fine_level(
        low_bound,
        high_bound,
        log_perm,
        source,
        own,
        raw,
        near,
        tile,
        spread,
        (own_rows, own_strip_rows, raw_rows, strip_rows),
        peers,
    )


def solution(mesh):
    peers = tuple(mesh.shape[axis] for axis in AXES)
    split = P(("groups", "gx"), "gy", "gz")
    return jax.shard_map(
        functools.partial(shards, peers),
        mesh=mesh,
        in_specs=(split, split, P(), P()),
        out_specs=(split, split),
        check_vma=False,
    )
```

```python
import functools

import jax
import jax.numpy as jnp
from jax import lax
from jax.experimental import pallas as pl
from jax.experimental.pallas import tpu as pltpu
from jax.sharding import PartitionSpec as P

DEGREE = 3
REACH = DEGREE + 1
LANES = 128
SUBLANES = 8
storage_rate = 0.1
AXES = ("gx", "gy", "gz")
VMEM = pl.BlockSpec(memory_space=pltpu.VMEM)
SMEM = pl.BlockSpec(memory_space=pltpu.SMEM)


def iota(shape, dim):
    return lax.broadcasted_iota(jnp.int32, shape, dim)


def turned(value, shift, axis):
    size = value.shape[axis]
    return pltpu.roll(value, shift % size, axis)


def permute(value, axis, peers, pairs):
    cores = lax.axis_size("gz")
    if axis == "gz" or cores % 2:
        return lax.ppermute(value, axis, [pair for i, j in pairs for pair in ((i, j), (j, i))])
    partner = {}
    for i, j in pairs:
        partner[i], partner[j] = j, i
    moves = [
        (i * cores + core, partner[i] * cores + core if i in partner else i * cores + (core ^ 1))
        for i in range(peers)
        for core in range(cores)
    ]
    return lax.ppermute(value, (axis, "gz"), moves)


def swap(axis, peers, right, left):
    even = lax.axis_index(axis) % 2 == 0
    first = permute(
        right if right is left else jnp.where(even, right, left),
        axis,
        peers,
        [(i, i + 1) for i in range(0, peers - 1, 2)],
    )
    if peers == 2:
        return (first,)
    second = permute(
        left if right is left else jnp.where(even, left, right),
        axis,
        peers,
        [(i, i + 1) for i in range(1, peers - 1, 2)],
    )
    return (first, second)


def far_swap(axis, peers, right, left):
    low = lax.axis_index(axis) % 4 < 2
    pairs = [(i, i + 2) for i in range(peers - 2)]
    near = [pair for pair in pairs if pair[0] % 4 < 2]
    rest = [pair for pair in pairs if pair[0] % 4 >= 2]
    got = []
    for chosen, sent in ((near, (right, left)), (rest, (left, right))):
        if chosen:
            got.append(permute(jnp.where(low, *sent), axis, peers, chosen))
    return tuple(got)


def from_right(is_first, got):
    return got[0] if len(got) == 1 else jnp.where(is_first, got[0], got[1])


def from_left(is_first, got):
    return got[0] if len(got) == 1 else jnp.where(is_first, got[1], got[0])


def numerators(shape, dim, own, index, peers, face_scale):
    place = iota(shape, dim)
    right = jnp.where(index < peers - 1, 2.0 * face_scale, 0.0)
    left = jnp.where(index > 0, 2.0 * face_scale, 0.0)
    return jnp.where(
        place == own - 1, right, jnp.where(place == shape[dim] - 1, left, 2.0 * face_scale)
    )


def iterate(count, log_at, source_at, x_faces, y_top, z_top, low, high, storage, refs):
    tx_ref, ty_ref, tz_ref, w_ref, d_ref, r_ref, p_ref = refs
    theta, delta = (high + low) * 0.5, (high - low) * 0.5
    sigma = theta / delta
    rho = 1.0 / sigma
    over_theta = 1.0 / theta
    after = jnp.exp(-log_at(0))
    tx_before = None
    for k in range(count):
        here = after
        if k + 1 < count:
            after = jnp.exp(-log_at(k + 1))
            tx = x_faces[k] / (here + after)
            tx_ref[k] = tx
        if 1 <= k <= count - 2:
            ty = y_top / (here + turned(here, -1, 0))
            tz = z_top / (here + turned(here, -1, 1))
            diagonal = storage + (tx_before + tx) + (ty + turned(ty, 1, 0)) + (tz + turned(tz, 1, 1))
            w = 1.0 / diagonal
            source = source_at(k)
            d_ref[k] = source * (over_theta * w)
            if 2 <= k <= count - 3:
                ty_ref[k] = ty
                tz_ref[k] = tz
                w_ref[k] = w
                r_ref[k] = source
        tx_before = tx
    for step in range(DEGREE):
        first, last = 2 + step, count - 2 - step
        rho_next = 1.0 / (2.0 * sigma - rho)
        keep, gain = rho_next * rho, 2.0 * rho_next / delta
        rho = rho_next
        here = d_ref[first]
        fx_before = tx_ref[first - 1] * (d_ref[first - 1] - here)
        for k in range(first, last):
            after = d_ref[k + 1]
            fx = tx_ref[k] * (here - after)
            fy = ty_ref[k] * (here - turned(here, -1, 0))
            fz = tz_ref[k] * (here - turned(here, -1, 1))
            applied = storage * here + (fx - fx_before) + (fy - turned(fy, 1, 0)) + (fz - turned(fz, 1, 1))
            residual = r_ref[k] - applied
            fresh = keep * here + gain * (residual * w_ref[k])
            if REACH <= k < count - REACH:
                so_far = here if step == 0 else p_ref[k]
                p_ref[k] = so_far + fresh
            if step < DEGREE - 1:
                r_ref[k] = residual
                d_ref[k] = fresh
            here, fx_before = after, fx


def window_scratch(count, rows, lanes):
    return [pltpu.VMEM((count, rows, lanes), jnp.float32)] * 7


def exact_dot(value, zero_one):
    parts = []
    for _ in range(3):
        part = value.astype(jnp.bfloat16)
        parts.append(part)
        value = value - part.astype(jnp.float32)
    rows = value.shape[0]
    out = jnp.dot(jnp.concatenate(parts, axis=0), zero_one, preferred_element_type=jnp.float32)
    return (out[2 * rows :] + out[rows : 2 * rows]) + out[:rows]


def pack_kernel(log_ref, source_ref, *refs):
    *halo_refs, out_ref, sum_ref = refs
    layers, rows, lanes = log_ref.shape
    even = lax.axis_index("gy") % 2 == 0
    starts = lax.axis_index("gy") == 0
    half = lanes // 2
    first_rows = iota((SUBLANES, lanes), 0) < REACH
    wide = len(halo_refs) == 2

    def halo(a, layer):
        got = tuple(ref[a * layers + layer] for ref in halo_refs)
        return from_right(even, got), from_left(even, got)

    slot = 0
    strips = []
    for layer in range(layers):
        tiles = []
        for a in range(2):
            right, left = halo(a, layer)
            tiles.append(jnp.where(first_rows, right, left) if wide else right)
        if wide:
            for tile in tiles:
                out_ref[slot] = tile
                slot += 1
        else:
            out_ref[slot] = jnp.where(first_rows == starts, tiles[0], turned(tiles[1], REACH, 0))
            slot += 1
    pieces = []

    def gather(top, bottom):
        for tile in range(lanes // LANES):
            columns = slice(tile * LANES, (tile + 1) * LANES)
            sum_ref[tile, :SUBLANES] = top[:, columns]
            sum_ref[tile, SUBLANES:] = bottom[:, columns]
        pieces.append(
            jnp.concatenate(
                [
                    sum_ref[tile, pl.ds(0, SUBLANES, stride=2), :]
                    + sum_ref[tile, pl.ds(1, SUBLANES, stride=2), :]
                    for tile in range(lanes // LANES)
                ],
                axis=1,
            )
        )

    for x in range(layers // 2):
        for ref in (log_ref, source_ref):
            both = ref[2 * x] + ref[2 * x + 1]
            gather(both[:SUBLANES], both[SUBLANES:])
    sums = []
    for x in range(layers // 2):
        for a in range(2):
            right, left = zip(halo(a, 2 * x), halo(a, 2 * x + 1))
            sums.append((right[0] + right[1], left[0] + left[1]))
    for x in range(layers // 2):
        if wide:
            continue
        gather(sums[2 * x][0], sums[2 * x + 1][0])
    if wide:
        for a in range(2):
            for x in range(layers // 2):
                gather(*sums[2 * x + a])
    pick = (iota((lanes, half), 0) // 2 == iota((lanes, half), 1)).astype(jnp.bfloat16)
    pooled = exact_dot(jnp.concatenate(pieces, axis=0), pick)
    tile = [pooled[SUBLANES * i : SUBLANES * (i + 1)] for i in range(len(pieces))]
    for x in range(layers // 2):
        tile[2 * x] = tile[2 * x] * 0.125
    if wide:
        for x in range(layers // 2):
            tile[layers + x] = tile[layers + x] * 0.125
    else:
        scale = jnp.where(iota((SUBLANES, half), 0) < REACH, 0.125, 1.0)
        for x in range(layers // 2):
            tile[layers + x] = tile[layers + x] * scale
    for i in range(0, len(tile), 2):
        out_ref[slot] = jnp.concatenate(tile[i : i + 2], axis=1)
        slot += 1


def pack(log_perm, source, got):
    layers, rows, lanes = log_perm.shape
    slots = len(got) * layers + 2 + len(got)
    return pl.pallas_call(
        pack_kernel,
        out_shape=jax.ShapeDtypeStruct((slots, SUBLANES, lanes), jnp.float32),
        in_specs=[VMEM] * (2 + len(got)),
        out_specs=VMEM,
        scratch_shapes=[pltpu.VMEM((lanes // LANES, 2 * SUBLANES, LANES), jnp.float32)],
        compiler_params=pltpu.CompilerParams(vmem_limit_bytes=8 << 20),
        cost_estimate=pl.CostEstimate(flops=5_000_000, bytes_accessed=700_000, transcendentals=0),
        name="pack",
    )(log_perm, source, *got)


def halves(both_sides, packed, partner):
    if both_sides:
        return packed, partner
    swapped = turned(packed, REACH, 0)
    return packed, swapped


def coarse_kernel(peers, slots, n_far, low_ref, high_ref, own_ref, *refs):
    near_refs, far_refs = refs[:2], refs[2 : 2 + n_far]
    tile_ref, out_ref, wide_ref, *scratch = refs[2 + n_far :]
    ix, iy, iz = (lax.axis_index(axis) for axis in AXES)
    nx, ny, nz = peers
    both_sides = ny > 2
    lanes = own_ref.shape[2] // 2
    rows = SUBLANES
    even, low = ix % 2 == 0, ix % 4 < 2
    strips, own_rows, near_rows, far_rows = slots
    top = iota((rows, lanes + LANES), 0) < REACH

    def packed(side, slot, half):
        columns = slice(half * lanes, (half + 1) * lanes)
        if side == 0:
            core = own_ref[strips + slot, :, columns]
            start = own_rows
        else:
            pick = from_left if side < 0 else from_right
            core = pick(even, tuple(ref[strips + slot, :, columns] for ref in near_refs))
            start = pick(even, tuple(near_rows))
        row = pl.multiple_of(start + (2 * slot + half) * rows, rows)
        return jnp.concatenate([core, tile_ref[pl.ds(row, rows), :]], axis=1)

    def far(side, slot, half):
        columns = slice(half * lanes, (half + 1) * lanes)
        pick = from_left if side < 0 else from_right
        core = pick(low, tuple(ref[slot, :, columns] for ref in far_refs))
        start = pick(low, tuple(far_rows))
        return jnp.concatenate([core, tile_ref[pl.ds(pl.multiple_of(start, rows), rows), :]], axis=1)

    def window(a, k):
        block, layer = k // 2 - 2, k % 2
        if abs(block) == 2:
            nearest = layer == (1 if block < 0 else 0)
            if a == 1:
                core = far(block, 1, 0)
                return jnp.concatenate([core, jnp.zeros_like(core)], axis=0)
            core = far(block, 0, 0 if nearest else 1)
            halo = far(block, 1, 1)
            if not both_sides:
                halo = jnp.where(top, halo, turned(halo, REACH, 0))
            return jnp.concatenate([core, halo], axis=0)
        core = packed(block, layer, a)
        if both_sides:
            halo = packed(block, 2 + a, layer)
        else:
            tile = packed(block, 2, layer)
            other = turned(tile, REACH, 0)
            halo = jnp.where(top, tile, other) if a == 0 else jnp.where(top, other, tile)
        return jnp.concatenate([core, halo], axis=0)

    def open_face(inside):
        return jnp.where(inside, 4.0, 0.0)

    faces = [4.0] * 9
    faces[1], faces[3] = open_face(ix > 1), open_face(ix > 0)
    faces[5], faces[7] = open_face(ix < nx - 1), open_face(ix < nx - 2)
    shape = (2 * rows, lanes + LANES)
    iterate(
        2 + 2 * REACH,
        functools.partial(window, 0),
        functools.partial(window, 1),
        faces,
        numerators(shape, 0, rows, iy, ny, 2.0),
        numerators(shape, 1, lanes, iz, nz, 2.0),
        jnp.full((1, shape[1]), low_ref[0]),
        jnp.full((1, shape[1]), high_ref[0]),
        8.0 * storage_rate,
        scratch,
    )
    p_ref = scratch[-1]
    widen = (iota((lanes, 2 * lanes), 0) == iota((lanes, 2 * lanes), 1) // 2).astype(jnp.bfloat16)
    pressure = jnp.concatenate([p_ref[REACH + x, :rows, :lanes] for x in range(2)], axis=0)
    wide = exact_dot(pressure, widen)
    for x in range(2):
        for tile in range(2 * lanes // LANES):
            columns = slice(tile * LANES, (tile + 1) * LANES)
            for half in range(2):
                wide_ref[tile, pl.ds(half, rows, stride=2), :] = wide[x * rows : (x + 1) * rows, columns]
            for twin in range(2):
                out_ref[2 * x + twin, :, columns] = wide_ref[tile]


def coarse_level(low_bound, high_bound, own, near, far, tile, slots, peers):
    lanes = own.shape[2] // 2
    window = (2 + 2 * REACH, 2 * SUBLANES, lanes + LANES)
    return pl.pallas_call(
        functools.partial(coarse_kernel, peers, slots, len(far)),
        out_shape=jax.ShapeDtypeStruct((REACH, 2 * SUBLANES, 2 * lanes), jnp.float32),
        in_specs=[SMEM, SMEM] + [VMEM] * (4 + len(far)),
        out_specs=VMEM,
        scratch_shapes=[pltpu.VMEM((2 * lanes // LANES, 2 * SUBLANES, LANES), jnp.float32)]
        + window_scratch(*window),
        compiler_params=pltpu.CompilerParams(vmem_limit_bytes=24 << 20),
        cost_estimate=pl.CostEstimate(flops=20_000_000, bytes_accessed=4_000_000, transcendentals=0),
        name="coarse_level",
    )(low_bound, high_bound, own, *near, *far, tile)


def fine_kernel(
    peers,
    slots,
    low_ref,
    high_ref,
    log_ref,
    source_ref,
    own_ref,
    first_ref,
    second_ref,
    first_pack_ref,
    second_pack_ref,
    tile_ref,
    spread_ref,
    fine_ref,
    diff_ref,
    *refs,
):
    layers, rows, lanes = fine_ref.shape
    ix, iy, iz = (lax.axis_index(axis) for axis in AXES)
    nx, ny, nz = peers
    both_sides = ny > 2
    even = ix % 2 == 0
    count = 3 * layers
    own_rows, own_strip_rows, raw_rows, strip_rows = slots

    def lane_tile(start, size):
        return tile_ref[pl.ds(pl.multiple_of(start, SUBLANES), size), :]

    def window(a, k):
        side, layer = k // layers - 1, k % layers
        if side == 0:
            core = (log_ref, source_ref)[a][layer]
            core_tile = lane_tile(own_rows + (a * layers + layer) * rows, rows)
            strip = lambda slot: own_ref[slot]
            strip_start = own_strip_rows
        else:
            pick = from_left if side < 0 else from_right
            slot = layer if a == 0 else layers + layer - (1 if side < 0 else 0)
            core = pick(even, (first_ref[slot], second_ref[slot]))
            core_tile = lane_tile(pick(even, tuple(raw_rows)) + slot * rows, rows)
            strip = lambda slot: pick(even, (first_pack_ref[slot], second_pack_ref[slot]))
            strip_start = pick(even, tuple(strip_rows))
        if both_sides:
            slot = 2 * layer + a
        else:
            slot = layer
        halo = jnp.concatenate(
            [strip(slot), lane_tile(strip_start + slot * SUBLANES, SUBLANES)], axis=1
        )
        if a == 1 and not both_sides:
            halo = turned(halo, REACH, 0)
        return jnp.concatenate([jnp.concatenate([core, core_tile], axis=1), halo], axis=0)

    faces = [2.0] * (count - 1)
    faces[layers - 1] = jnp.where(ix > 0, 2.0, 0.0)
    faces[2 * layers - 1] = jnp.where(ix < nx - 1, 2.0, 0.0)
    shape = (rows + 2 * REACH, lanes + LANES)
    iterate(
        count,
        functools.partial(window, 0),
        functools.partial(window, 1),
        faces,
        numerators(shape, 0, rows, iy, ny, 1.0),
        numerators(shape, 1, lanes, iz, nz, 1.0),
        jnp.full((1, shape[1]), low_ref[0]),
        jnp.full((1, shape[1]), high_ref[0]),
        storage_rate,
        refs,
    )
    p_ref = refs[-1]
    for x in range(layers):
        fine = p_ref[REACH + x, :rows, :lanes]
        fine_ref[x] = fine
        diff_ref[x] = fine - spread_ref[x]


def fine_level(low_bound, high_bound, log_perm, source, own, raw, near, tile, spread, slots, peers):
    layers, rows, lanes = log_perm.shape
    window = (layers + 2 * REACH, rows + 2 * REACH, lanes + LANES)
    out = jax.ShapeDtypeStruct(log_perm.shape, jnp.float32)
    return pl.pallas_call(
        functools.partial(fine_kernel, peers, slots),
        out_shape=(out, out),
        in_specs=[SMEM, SMEM] + [VMEM] * 9,
        out_specs=(VMEM, VMEM),
        scratch_shapes=window_scratch(*window),
        compiler_params=pltpu.CompilerParams(vmem_limit_bytes=24 << 20),
        cost_estimate=pl.CostEstimate(flops=20_000_000, bytes_accessed=10_000_000, transcendentals=0),
        name="fine_level",
    )(low_bound, high_bound, log_perm, source, own, *raw, *near, tile, spread)


def shards(peers, log_perm, source, low_bound, high_bound):
    nx, ny, nz = peers
    layers, rows, lanes = log_perm.shape
    assert layers == REACH and rows == 2 * SUBLANES and nx > 2
    half = lanes // 2
    stacked = jnp.concatenate([log_perm, source], axis=0)
    got_rows = swap("gy", ny, stacked[:, rows - SUBLANES :], stacked[:, :SUBLANES])
    raw = swap("gx", nx, jnp.concatenate([log_perm, source[1:]]), jnp.concatenate([log_perm, source[:-1]]))
    own = pack(log_perm, source, got_rows)
    near = swap("gx", nx, own, own)
    strips = len(got_rows) * layers
    pooled = own[strips:]
    left_half, right_half = pooled[..., :half], pooled[..., half:]

    def far_pack(inner, outer):
        halo = (left_half, right_half)[inner][2]
        return jnp.stack(
            [
                jnp.concatenate([left_half[inner], left_half[outer]], axis=1),
                jnp.concatenate([right_half[inner], halo], axis=1),
            ]
        )

    far = far_swap("gx", nx, far_pack(1, 0), far_pack(0, 1))
    offset, edges = 0, []

    def add(array, columns):
        nonlocal offset
        start = offset
        flat = array.reshape(-1, array.shape[-1])[:, columns]
        edges.append(flat)
        offset += flat.shape[0]
        return start

    whole = slice(0, lanes)

    def add_pooled(array):
        return add(array[strips:].reshape(-1, SUBLANES, 2, half).swapaxes(1, 2), slice(0, half))

    own_rows = add(stacked, whole)
    raw_rows = [add(block, whole) for block in raw]
    own_strip_rows = add(own[:strips], whole)
    strip_rows = [add(block[:strips], whole) for block in near]
    own_pooled = add_pooled(own)
    near_pooled = [add_pooled(block) for block in near]
    far_rows = [add(block[0], slice(0, half)) for block in far]
    last = jnp.concatenate([flat[:, -LANES:] for flat in edges])
    first = jnp.concatenate([flat[:, :LANES] for flat in edges])
    if nz == 2:
        sent = jnp.where(lax.axis_index("gz") == 0, last, first)
        tile = lax.ppermute(sent, "gz", [(0, 1), (1, 0)])
    else:
        even = lax.axis_index("gz") % 2 == 0
        got = swap("gz", nz, last, first)
        tile = jnp.where(
            iota(last.shape, 1) < LANES // 2, from_right(even, got), from_left(even, got)
        )
    spread = coarse_level(
        low_bound,
        high_bound,
        own,
        near,
        far,
        tile,
        (strips, own_pooled, near_pooled, far_rows),
        peers,
    )
    return fine_level(
        low_bound,
        high_bound,
        log_perm,
        source,
        own,
        raw,
        near,
        tile,
        spread,
        (own_rows, own_strip_rows, raw_rows, strip_rows),
        peers,
    )


def solution(mesh):
    peers = tuple(mesh.shape[axis] for axis in AXES)
    split = P(("groups", "gx"), "gy", "gz")
    return jax.shard_map(
        functools.partial(shards, peers),
        mesh=mesh,
        in_specs=(split, split, P(), P()),
        out_specs=(split, split),
        check_vma=False,
    )
```

```python
import functools

import jax
import jax.numpy as jnp
from jax import lax
from jax.experimental import pallas as pl
from jax.experimental.pallas import tpu as pltpu
from jax.sharding import PartitionSpec as P

DEGREE = 3
REACH = DEGREE + 1
LANES = 128
SUBLANES = 8
storage_rate = 0.1
AXES = ("gx", "gy", "gz")
VMEM = pl.BlockSpec(memory_space=pltpu.VMEM)
SMEM = pl.BlockSpec(memory_space=pltpu.SMEM)


def iota(shape, dim):
    return lax.broadcasted_iota(jnp.int32, shape, dim)


def turned(value, shift, axis):
    size = value.shape[axis]
    return pltpu.roll(value, shift % size, axis)


def permute(value, axis, peers, pairs):
    cores = lax.axis_size("gz")
    if axis == "gz" or cores % 2:
        return lax.ppermute(value, axis, [pair for i, j in pairs for pair in ((i, j), (j, i))])
    partner = {}
    for i, j in pairs:
        partner[i], partner[j] = j, i
    moves = [
        (i * cores + core, partner[i] * cores + core if i in partner else i * cores + (core ^ 1))
        for i in range(peers)
        for core in range(cores)
    ]
    return lax.ppermute(value, (axis, "gz"), moves)


def neighbour_pairs(peers, start):
    return [(i, i + 1) for i in range(start, peers - 1, 2)]


def first_swap(axis, peers, right, left):
    even = lax.axis_index(axis) % 2 == 0
    return permute(jnp.where(even, right, left), axis, peers, neighbour_pairs(peers, 0))


def second_swap(axis, peers, right, left):
    even = lax.axis_index(axis) % 2 == 0
    return permute(jnp.where(even, left, right), axis, peers, neighbour_pairs(peers, 1))


def swap(axis, peers, right, left):
    got = (first_swap(axis, peers, right, left),)
    return got if peers == 2 else got + (second_swap(axis, peers, right, left),)


def far_pairs(peers):
    pairs = [(i, i + 2) for i in range(peers - 2)]
    groups = [[pair for pair in pairs if pair[0] % 4 < 2], [pair for pair in pairs if pair[0] % 4 >= 2]]
    return [group for group in groups if group]


def from_right(is_first, got):
    return got[0] if len(got) == 1 else jnp.where(is_first, got[0], got[1])


def from_left(is_first, got):
    return got[0] if len(got) == 1 else jnp.where(is_first, got[1], got[0])


def numerators(shape, dim, own, index, peers, face_scale):
    place = iota(shape, dim)
    right = jnp.where(index < peers - 1, 2.0 * face_scale, 0.0)
    left = jnp.where(index > 0, 2.0 * face_scale, 0.0)
    return jnp.where(
        place == own - 1, right, jnp.where(place == shape[dim] - 1, left, 2.0 * face_scale)
    )


def iterate(count, log_at, source_at, x_faces, y_top, z_top, low, high, storage, refs):
    tx_ref, ty_ref, tz_ref, w_ref, d_ref, r_ref, p_ref = refs
    theta, delta = (high + low) * 0.5, (high - low) * 0.5
    sigma = theta / delta
    rho = 1.0 / sigma
    over_theta = 1.0 / theta
    after = jnp.exp(-log_at(0))
    tx_before = None
    for k in range(count):
        here = after
        if k + 1 < count:
            after = jnp.exp(-log_at(k + 1))
            tx = x_faces[k] / (here + after)
            tx_ref[k] = tx
        if 1 <= k <= count - 2:
            ty = y_top / (here + turned(here, -1, 0))
            tz = z_top / (here + turned(here, -1, 1))
            diagonal = storage + (tx_before + tx) + (ty + turned(ty, 1, 0)) + (tz + turned(tz, 1, 1))
            w = 1.0 / diagonal
            source = source_at(k)
            d_ref[k] = source * (over_theta * w)
            if 2 <= k <= count - 3:
                ty_ref[k] = ty
                tz_ref[k] = tz
                w_ref[k] = w
                r_ref[k] = source
        tx_before = tx
    for step in range(DEGREE):
        first, last = 2 + step, count - 2 - step
        rho_next = 1.0 / (2.0 * sigma - rho)
        keep, gain = rho_next * rho, 2.0 * rho_next / delta
        rho = rho_next
        here = d_ref[first]
        fx_before = tx_ref[first - 1] * (d_ref[first - 1] - here)
        for k in range(first, last):
            after = d_ref[k + 1]
            fx = tx_ref[k] * (here - after)
            fy = ty_ref[k] * (here - turned(here, -1, 0))
            fz = tz_ref[k] * (here - turned(here, -1, 1))
            applied = storage * here + (fx - fx_before) + (fy - turned(fy, 1, 0)) + (fz - turned(fz, 1, 1))
            residual = r_ref[k] - applied
            fresh = keep * here + gain * (residual * w_ref[k])
            if REACH <= k < count - REACH:
                so_far = here if step == 0 else p_ref[k]
                p_ref[k] = so_far + fresh
            if step < DEGREE - 1:
                r_ref[k] = residual
                d_ref[k] = fresh
            here, fx_before = after, fx


def window_scratch(count, rows, lanes):
    return [pltpu.VMEM((count, rows, lanes), jnp.float32)] * 7


def exact_dot(value, zero_one):
    parts = []
    for _ in range(3):
        part = value.astype(jnp.bfloat16)
        parts.append(part)
        value = value - part.astype(jnp.float32)
    rows = value.shape[0]
    out = jnp.dot(jnp.concatenate(parts, axis=0), zero_one, preferred_element_type=jnp.float32)
    return (out[2 * rows :] + out[rows : 2 * rows]) + out[:rows]


def row_pairs(top, bottom, sum_ref):
    tiles = top.shape[1] // LANES
    for tile in range(tiles):
        columns = slice(tile * LANES, (tile + 1) * LANES)
        sum_ref[tile, :SUBLANES] = top[:, columns]
        sum_ref[tile, SUBLANES:] = bottom[:, columns]
    return jnp.concatenate(
        [
            sum_ref[tile, pl.ds(0, SUBLANES, stride=2), :] + sum_ref[tile, pl.ds(1, SUBLANES, stride=2), :]
            for tile in range(tiles)
        ],
        axis=1,
    )


def lane_pairs(pieces):
    lanes = pieces[0].shape[1]
    pick = (iota((lanes, lanes // 2), 0) // 2 == iota((lanes, lanes // 2), 1)).astype(jnp.bfloat16)
    pooled = exact_dot(jnp.concatenate(pieces, axis=0), pick)
    return [pooled[SUBLANES * i : SUBLANES * (i + 1)] for i in range(len(pieces))]


def join_halo(near, beyond, starts):
    row = iota(near.shape, 0)
    up, down = turned(beyond, 3, 0), turned(beyond, -3, 0)
    right = jnp.where((row == 3) | (row == 7), up, jnp.where(row == 6, turned(beyond, 5, 0), near))
    left = jnp.where((row == 0) | (row == 4), down, jnp.where(row == 5, up, near))
    return jnp.where(starts, right, left)


def beyond_halo(joined, starts):
    row = iota(joined.shape, 0)
    up, down = turned(joined, 3, 0), turned(joined, -3, 0)
    right = jnp.where(row == 1, turned(joined, -5, 0), down)
    left = jnp.where(row == 2, down, up)
    return jnp.where(starts, right, left)


def join_third(near, third):
    row = iota(near.shape, 0)
    return jnp.where(
        row == 3, turned(third, 3, 0), jnp.where(row == 4, turned(third, -3, 0), near)
    )


def third_halo(joined):
    return jnp.where(iota(joined.shape, 0) < REACH, turned(joined, -3, 0), turned(joined, 3, 0))


def pack_kernel(n_far, log_ref, source_ref, *refs):
    *halo_refs, own_ref, first_ref, second_ref, far_ref, sum_ref = refs
    layers, rows, lanes = log_ref.shape
    ix, iy = lax.axis_index("gx"), lax.axis_index("gy")
    even, starts, low = iy % 2 == 0, iy == 0, ix % 4 < 2
    half = lanes // 2
    upper = iota((SUBLANES, lanes), 0) < REACH
    wide = len(halo_refs) == 2

    def halo(a, layer):
        got = tuple(ref[a * layers + layer] for ref in halo_refs)
        return from_right(even, got), from_left(even, got)

    def rows_of(a, layer):
        right, left = halo(a, layer)
        return jnp.where(upper, right, left) if wide else right

    def join(log_tile, source_tile):
        if wide:
            return [log_tile, source_tile]
        return [jnp.where(upper == starts, log_tile, turned(source_tile, REACH, 0))]

    log_rows, source_rows = ([rows_of(a, layer) for layer in range(layers)] for a in range(2))
    own = []
    for layer in range(layers):
        own += join(log_rows[layer], source_rows[layer])
    pieces = []
    for x in range(2):
        for ref in (log_ref, source_ref):
            both = ref[2 * x] + ref[2 * x + 1]
            pieces.append(row_pairs(both[:SUBLANES], both[SUBLANES:], sum_ref))
    sums = []
    for a in range(2):
        for x in range(2):
            near, beyond = halo(a, 2 * x), halo(a, 2 * x + 1)
            sums.append((near[0] + beyond[0], near[1] + beyond[1]))
    if wide:
        pieces += [row_pairs(*both, sum_ref) for both in sums]
    else:
        pieces += [row_pairs(sums[x][0], sums[2 + x][0], sum_ref) for x in range(2)]
    log0, source0, log1, source1, *halos = lane_pairs(pieces)
    logs, sources = (log0 * 0.125, log1 * 0.125), (source0, source1)
    if wide:
        halos = [halos[0] * 0.125, halos[1] * 0.125, halos[2], halos[3]]
    else:
        scale = jnp.where(iota((SUBLANES, half), 0) < REACH, 0.125, 1.0)
        halos = [tile * scale for tile in halos]

    def pair(left, right):
        return jnp.concatenate([left, right], axis=1)

    own += [pair(logs[x], sources[x]) for x in range(2)]
    own += [pair(halos[i], halos[i + 1]) for i in range(0, len(halos), 2)]
    for i, tile in enumerate(own):
        own_ref[i] = tile

    def near_tiles(order):
        near, beyond = order[0] // 2, order[-1] // 2
        tiles = join(join_third(log_rows[order[0]], log_rows[order[2]]), source_rows[order[0]])
        tiles += join(log_rows[order[1]], source_rows[order[1]])
        if wide:
            tiles += [
                pair(halos[near], halos[beyond]),
                pair(halos[2 + near], halos[2 + beyond]),
                pair(sources[beyond], sources[beyond]),
            ]
        else:
            tiles += [pair(join_halo(halos[near], halos[beyond], starts), sources[beyond])]
        return tiles

    forward = list(range(layers))
    for i, (right, left) in enumerate(zip(near_tiles(forward[::-1]), near_tiles(forward))):
        first_ref[i] = jnp.where(ix % 2 == 0, right, left)
        second_ref[i] = jnp.where(ix % 2 == 0, left, right)
    for x, inner, outer in ((0, 1, 0), (1, 0, 1)):
        tiles = (pair(logs[inner], logs[outer]), pair(sources[inner], halos[inner]))
        if x == 0:
            right = tiles
    for i in range(2):
        far_ref[0, i] = jnp.where(low, right[i], tiles[i])
        if n_far == 2:
            far_ref[1, i] = jnp.where(low, tiles[i], right[i])


def pack(log_perm, source, got, n_far):
    layers, rows, lanes = log_perm.shape
    wide = len(got) == 2

    def tiles(*count):
        return jax.ShapeDtypeStruct((*count, SUBLANES, lanes), jnp.float32)

    near = 7 if wide else 3
    return pl.pallas_call(
        functools.partial(pack_kernel, n_far),
        out_shape=(tiles(len(got) * (layers + 1) + 2), tiles(near), tiles(near), tiles(n_far, 2)),
        in_specs=[VMEM] * (2 + len(got)),
        out_specs=(VMEM,) * 4,
        scratch_shapes=[pltpu.VMEM((lanes // LANES, 2 * SUBLANES, LANES), jnp.float32)],
        compiler_params=pltpu.CompilerParams(vmem_limit_bytes=8 << 20),
        cost_estimate=pl.CostEstimate(flops=5_000_000, bytes_accessed=700_000, transcendentals=0),
        name="pack",
    )(log_perm, source, *got)


def pool_kernel(first_ref, second_ref, out_ref, sum_ref):
    layers = REACH
    even = lax.axis_index("gx") % 2 == 0
    pieces = []
    for ref, on_right in ((first_ref, even), (second_ref, jnp.logical_not(even))):
        for x in range(2):
            both = ref[2 * x] + ref[2 * x + 1]
            pieces.append(row_pairs(both[:SUBLANES], both[SUBLANES:], sum_ref))
        both = ref[layers + 1] + jnp.where(on_right, ref[layers], ref[layers + 2])
        pieces.append(row_pairs(both[:SUBLANES], both[SUBLANES:], sum_ref))
    tiles = lane_pairs(pieces)
    for block in range(2):
        log0, log1, source = tiles[3 * block : 3 * block + 3]
        out_ref[block, 0] = jnp.concatenate([log0 * 0.125, log1 * 0.125], axis=1)
        out_ref[block, 1] = jnp.concatenate([source, source], axis=1)


def pool(first, second):
    _, rows, lanes = first.shape
    return pl.pallas_call(
        pool_kernel,
        out_shape=jax.ShapeDtypeStruct((2, 2, SUBLANES, lanes), jnp.float32),
        in_specs=[VMEM] * 2,
        out_specs=VMEM,
        scratch_shapes=[pltpu.VMEM((lanes // LANES, 2 * SUBLANES, LANES), jnp.float32)],
        compiler_params=pltpu.CompilerParams(vmem_limit_bytes=8 << 20),
        cost_estimate=pl.CostEstimate(flops=5_000_000, bytes_accessed=600_000, transcendentals=0),
        name="pool",
    )(first, second)


def lane_rows(ref, start, size):
    return ref[pl.ds(pl.multiple_of(start, SUBLANES), size), :]


def coarse_kernel(peers, places, n_far, low_ref, high_ref, own_ref, pool_ref, *refs):
    near_refs, far_refs = refs[:2], refs[2 : 2 + n_far]
    early_ref, late_ref, out_ref, wide_ref, *scratch = refs[2 + n_far :]
    ix, iy, iz = (lax.axis_index(axis) for axis in AXES)
    nx, ny, nz = peers
    both_sides = ny > 2
    lanes = own_ref.shape[2] // 2
    rows = SUBLANES
    even, low, starts = ix % 2 == 0, ix % 4 < 2, iy == 0
    strips = (2 if both_sides else 1) * REACH
    near_strips = 4 if both_sides else 2
    top = iota((rows, lanes + LANES), 0) < REACH

    def with_lanes(core, ref, start):
        return jnp.concatenate([core, lane_rows(ref, start, rows)], axis=1)

    def columns(half):
        return slice(half * lanes, (half + 1) * lanes)

    def own(slot, half):
        start = places["own_pooled"] + (2 * slot + half) * rows
        return with_lanes(own_ref[strips + slot, :, columns(half)], early_ref, start)

    def pooled(side, slot, half):
        block = jnp.where(even, 0, 1) if side > 0 else jnp.where(even, 1, 0)
        start = places["pooled"] + block * (4 * rows) + (2 * slot + half) * rows
        return with_lanes(pool_ref[block, slot, :, columns(half)], early_ref, start)

    def near(side, slot, half):
        pick = from_left if side < 0 else from_right
        core = pick(even, tuple(ref[near_strips + slot, :, columns(half)] for ref in near_refs))
        start = pick(even, tuple(places["near_pooled"])) + (2 * slot + half) * rows
        return with_lanes(core, late_ref, start)

    def far(side, slot, half):
        pick = from_left if side < 0 else from_right
        core = pick(low, tuple(ref[slot, :, columns(half)] for ref in far_refs))
        return with_lanes(core, late_ref, pick(low, tuple(places["far"])))

    def split(tile, a):
        other = turned(tile, REACH, 0)
        return jnp.where(top, tile, other) if a == 0 else jnp.where(top, other, tile)

    def window(a, k):
        block, layer = k // 2 - 2, k % 2
        nearest = layer == (1 if block < 0 else 0)
        if abs(block) == 2:
            if a == 1:
                core = far(block, 1, 0)
                return jnp.concatenate([core, jnp.zeros_like(core)], axis=0)
            halo = far(block, 1, 1)
            halo = halo if both_sides else split(halo, 0)
            return jnp.concatenate([far(block, 0, 0 if nearest else 1), halo], axis=0)
        if block == 0:
            core = own(layer, a)
            halo = own(2 + a, layer) if both_sides else split(own(2, layer), a)
            return jnp.concatenate([core, halo], axis=0)
        if a == 0:
            core = pooled(block, 0, layer)
        elif nearest:
            core = pooled(block, 1, 0)
        else:
            core = near(block, 2, 0) if both_sides else near(block, 0, 1)
        if both_sides:
            halo = near(block, a, 0 if nearest else 1)
        else:
            joined = near(block, 0, 0)
            halo = split(joined if nearest else beyond_halo(joined, starts), a)
        return jnp.concatenate([core, halo], axis=0)

    def open_face(inside):
        return jnp.where(inside, 4.0, 0.0)

    faces = [4.0] * 9
    faces[1], faces[3] = open_face(ix > 1), open_face(ix > 0)
    faces[5], faces[7] = open_face(ix < nx - 1), open_face(ix < nx - 2)
    shape = (2 * rows, lanes + LANES)
    iterate(
        2 + 2 * REACH,
        functools.partial(window, 0),
        functools.partial(window, 1),
        faces,
        numerators(shape, 0, rows, iy, ny, 2.0),
        numerators(shape, 1, lanes, iz, nz, 2.0),
        jnp.full((1, shape[1]), low_ref[0]),
        jnp.full((1, shape[1]), high_ref[0]),
        8.0 * storage_rate,
        scratch,
    )
    p_ref = scratch[-1]
    widen = (iota((lanes, 2 * lanes), 0) == iota((lanes, 2 * lanes), 1) // 2).astype(jnp.bfloat16)
    pressure = jnp.concatenate([p_ref[REACH + x, :rows, :lanes] for x in range(2)], axis=0)
    wide = exact_dot(pressure, widen)
    for x in range(2):
        for tile in range(2 * lanes // LANES):
            part = slice(tile * LANES, (tile + 1) * LANES)
            for half in range(2):
                wide_ref[tile, pl.ds(half, rows, stride=2), :] = wide[x * rows : (x + 1) * rows, part]
            for twin in range(2):
                out_ref[2 * x + twin, :, part] = wide_ref[tile]


def coarse_level(low_bound, high_bound, own, pooled, near, far, early, late, places, peers):
    lanes = own.shape[2] // 2
    window = (2 + 2 * REACH, 2 * SUBLANES, lanes + LANES)
    return pl.pallas_call(
        functools.partial(coarse_kernel, peers, places, len(far)),
        out_shape=jax.ShapeDtypeStruct((REACH, 2 * SUBLANES, 2 * lanes), jnp.float32),
        in_specs=[SMEM, SMEM] + [VMEM] * (6 + len(far)),
        out_specs=VMEM,
        scratch_shapes=[pltpu.VMEM((2 * lanes // LANES, 2 * SUBLANES, LANES), jnp.float32)]
        + window_scratch(*window),
        compiler_params=pltpu.CompilerParams(vmem_limit_bytes=24 << 20),
        cost_estimate=pl.CostEstimate(flops=20_000_000, bytes_accessed=4_000_000, transcendentals=0),
        name="coarse_level",
    )(low_bound, high_bound, own, pooled, *near, *far, early, late)


def fine_kernel(
    peers,
    places,
    low_ref,
    high_ref,
    log_ref,
    source_ref,
    own_ref,
    first_ref,
    second_ref,
    first_near_ref,
    second_near_ref,
    early_ref,
    late_ref,
    spread_ref,
    fine_ref,
    diff_ref,
    *refs,
):
    layers, rows, lanes = fine_ref.shape
    ix, iy, iz = (lax.axis_index(axis) for axis in AXES)
    nx, ny, nz = peers
    both_sides = ny > 2
    even = ix % 2 == 0
    count = 3 * layers

    def with_lanes(core, ref, start):
        return jnp.concatenate([core, lane_rows(ref, start, core.shape[0])], axis=1)

    def near(side, slot):
        pick = from_left if side < 0 else from_right
        core = pick(even, (first_near_ref[slot], second_near_ref[slot]))
        return with_lanes(core, late_ref, pick(even, tuple(places["near_strips"])) + slot * SUBLANES)

    def window(a, k):
        side, layer = k // layers - 1, k % layers
        if side == 0:
            core = (log_ref, source_ref)[a][layer]
            core = with_lanes(core, early_ref, places["own"] + (a * layers + layer) * rows)
            slot = 2 * layer + a if both_sides else layer
            halo = with_lanes(own_ref[slot], early_ref, places["own_strips"] + slot * SUBLANES)
            if a == 1 and not both_sides:
                halo = turned(halo, REACH, 0)
        else:
            pick = from_left if side < 0 else from_right
            slot = layer if a == 0 else layers + layer - (1 if side < 0 else 0)
            core = pick(even, (first_ref[slot], second_ref[slot]))
            core = with_lanes(core, early_ref, pick(even, tuple(places["raw"])) + slot * rows)
            distance = layers - layer if side < 0 else layer + 1
            if both_sides:
                halo = near(side, (2 if distance == 2 else 0) + a)
            else:
                halo = near(side, 1 if distance == 2 else 0)
                if a == 1:
                    halo = turned(halo, REACH, 0)
            if a == 0 and distance > 2:
                halo = third_halo(halo)
        return jnp.concatenate([core, halo], axis=0)

    faces = [2.0] * (count - 1)
    faces[layers - 1] = jnp.where(ix > 0, 2.0, 0.0)
    faces[2 * layers - 1] = jnp.where(ix < nx - 1, 2.0, 0.0)
    shape = (rows + 2 * REACH, lanes + LANES)
    iterate(
        count,
        functools.partial(window, 0),
        functools.partial(window, 1),
        faces,
        numerators(shape, 0, rows, iy, ny, 1.0),
        numerators(shape, 1, lanes, iz, nz, 1.0),
        jnp.full((1, shape[1]), low_ref[0]),
        jnp.full((1, shape[1]), high_ref[0]),
        storage_rate,
        refs,
    )
    p_ref = refs[-1]
    for x in range(layers):
        fine = p_ref[REACH + x, :rows, :lanes]
        fine_ref[x] = fine
        diff_ref[x] = fine - spread_ref[x]


def fine_level(low_bound, high_bound, log_perm, source, own, raw, near, early, late, spread, places, peers):
    layers, rows, lanes = log_perm.shape
    window = (layers + 2 * REACH, rows + 2 * REACH, lanes + LANES)
    out = jax.ShapeDtypeStruct(log_perm.shape, jnp.float32)
    return pl.pallas_call(
        functools.partial(fine_kernel, peers, places),
        out_shape=(out, out),
        in_specs=[SMEM, SMEM] + [VMEM] * 10,
        out_specs=(VMEM, VMEM),
        scratch_shapes=window_scratch(*window),
        compiler_params=pltpu.CompilerParams(vmem_limit_bytes=24 << 20),
        cost_estimate=pl.CostEstimate(flops=20_000_000, bytes_accessed=10_000_000, transcendentals=0),
        name="fine_level",
    )(low_bound, high_bound, log_perm, source, own, *raw, *near, early, late, spread)


class LaneTiles:
    def __init__(self):
        self.offset, self.parts = 0, []

    def add(self, array):
        start = self.offset
        self.parts.append(array.reshape(-1, array.shape[-1]))
        self.offset += self.parts[-1].shape[0]
        return start

    def add_halves(self, array):
        half = array.shape[-1] // 2
        return self.add(array.reshape(-1, SUBLANES, 2, half).swapaxes(1, 2))

    def swapped(self, peers):
        last = jnp.concatenate([part[:, -LANES:] for part in self.parts])
        first = jnp.concatenate([part[:, :LANES] for part in self.parts])
        got = swap("gz", peers, last, first)
        if len(got) == 1:
            return got[0]
        even = lax.axis_index("gz") % 2 == 0
        return jnp.where(iota(last.shape, 1) < LANES // 2, from_right(even, got), from_left(even, got))


def shards(peers, log_perm, source, low_bound, high_bound):
    nx, ny, nz = peers
    layers, rows, lanes = log_perm.shape
    assert layers == REACH and rows == 2 * SUBLANES and nx > 2
    to_right, to_left = jnp.concatenate([log_perm, source[1:]]), jnp.concatenate([log_perm, source[:-1]])
    second = second_swap("gx", nx, to_right, to_left)
    stacked = jnp.concatenate([log_perm, source])
    got_rows = swap("gy", ny, stacked[:, rows - SUBLANES :], stacked[:, :SUBLANES])
    raw = (first_swap("gx", nx, to_right, to_left), second)
    far_groups = far_pairs(nx)
    own, for_first, for_second, for_far = pack(log_perm, source, got_rows, len(far_groups))
    second = permute(for_second, "gx", nx, neighbour_pairs(nx, 1))
    near = (permute(for_first, "gx", nx, neighbour_pairs(nx, 0)), second)
    far = tuple(permute(for_far[i], "gx", nx, group) for i, group in enumerate(far_groups))
    pooled = pool(*raw)
    strips = len(got_rows) * layers
    near_strips = 2 * len(got_rows)
    places, early, late = {}, LaneTiles(), LaneTiles()
    places["own"] = early.add(stacked)
    places["own_strips"] = early.add(own[:strips])
    places["own_pooled"] = early.add_halves(own[strips:])
    places["raw"] = [early.add(block) for block in raw]
    places["pooled"] = early.add_halves(pooled)
    places["near_strips"] = [late.add(block[:near_strips]) for block in near]
    places["near_pooled"] = [late.add_halves(block[near_strips:]) for block in near]
    places["far"] = [late.add(block[0, :, : lanes // 2]) for block in far]
    early, late = early.swapped(nz), late.swapped(nz)
    spread = coarse_level(low_bound, high_bound, own, pooled, near, far, early, late, places, peers)
    return fine_level(
        low_bound, high_bound, log_perm, source, own, raw, near, early, late, spread, places, peers
    )


def solution(mesh):
    peers = tuple(mesh.shape[axis] for axis in AXES)
    split = P(("groups", "gx"), "gy", "gz")
    return jax.shard_map(
        functools.partial(shards, peers),
        mesh=mesh,
        in_specs=(split, split, P(), P()),
        out_specs=(split, split),
        check_vma=False,
    )
```

```python
import functools

import jax
import jax.numpy as jnp
from jax import lax
from jax.experimental import pallas as pl
from jax.experimental.pallas import tpu as pltpu
from jax.sharding import PartitionSpec as P

DEGREE = 3
REACH = DEGREE + 1
LANES = 128
SUBLANES = 8
storage_rate = 0.1
AXES = ("gx", "gy", "gz")
VMEM = pl.BlockSpec(memory_space=pltpu.VMEM)
SMEM = pl.BlockSpec(memory_space=pltpu.SMEM)


def iota(shape, dim):
    return lax.broadcasted_iota(jnp.int32, shape, dim)


def turned(value, shift, axis):
    size = value.shape[axis]
    return pltpu.roll(value, shift % size, axis)


def permute(value, axis, peers, pairs):
    cores = lax.axis_size("gz")
    if axis == "gz" or cores % 2:
        return lax.ppermute(value, axis, [pair for i, j in pairs for pair in ((i, j), (j, i))])
    partner = {}
    for i, j in pairs:
        partner[i], partner[j] = j, i
    moves = [
        (i * cores + core, partner[i] * cores + core if i in partner else i * cores + (core ^ 1))
        for i in range(peers)
        for core in range(cores)
    ]
    return lax.ppermute(value, (axis, "gz"), moves)


def neighbour_pairs(peers, start):
    return [(i, i + 1) for i in range(start, peers - 1, 2)]


def first_swap(axis, peers, right, left):
    even = lax.axis_index(axis) % 2 == 0
    return permute(jnp.where(even, right, left), axis, peers, neighbour_pairs(peers, 0))


def second_swap(axis, peers, right, left):
    even = lax.axis_index(axis) % 2 == 0
    return permute(jnp.where(even, left, right), axis, peers, neighbour_pairs(peers, 1))


def swap(axis, peers, right, left):
    got = (first_swap(axis, peers, right, left),)
    return got if peers == 2 else got + (second_swap(axis, peers, right, left),)


def far_pairs(peers):
    pairs = [(i, i + 2) for i in range(peers - 2)]
    groups = [[pair for pair in pairs if pair[0] % 4 < 2], [pair for pair in pairs if pair[0] % 4 >= 2]]
    return [group for group in groups if group]


def from_right(is_first, got):
    return got[0] if len(got) == 1 else jnp.where(is_first, got[0], got[1])


def from_left(is_first, got):
    return got[0] if len(got) == 1 else jnp.where(is_first, got[1], got[0])


def numerators(shape, dim, own, index, peers, face_scale):
    place = iota(shape, dim)
    right = jnp.where(index < peers - 1, 2.0 * face_scale, 0.0)
    left = jnp.where(index > 0, 2.0 * face_scale, 0.0)
    return jnp.where(
        place == own - 1, right, jnp.where(place == shape[dim] - 1, left, 2.0 * face_scale)
    )


def iterate(count, log_at, source_at, x_faces, y_top, z_top, low, high, storage, refs):
    tx_ref, ty_ref, tz_ref, w_ref, d_ref, r_ref, p_ref = refs
    theta, delta = (high + low) * 0.5, (high - low) * 0.5
    sigma = theta / delta
    rho = 1.0 / sigma
    over_theta = 1.0 / theta
    after = jnp.exp(-log_at(0))
    tx_before = None
    for k in range(count):
        here = after
        if k + 1 < count:
            after = jnp.exp(-log_at(k + 1))
            tx = x_faces[k] / (here + after)
            tx_ref[k] = tx
        if 1 <= k <= count - 2:
            ty = y_top / (here + turned(here, -1, 0))
            tz = z_top / (here + turned(here, -1, 1))
            diagonal = storage + (tx_before + tx) + (ty + turned(ty, 1, 0)) + (tz + turned(tz, 1, 1))
            w = 1.0 / diagonal
            source = source_at(k)
            d_ref[k] = source * (over_theta * w)
            if 2 <= k <= count - 3:
                ty_ref[k] = ty
                tz_ref[k] = tz
                w_ref[k] = w
                r_ref[k] = source
        tx_before = tx
    for step in range(DEGREE):
        first, last = 2 + step, count - 2 - step
        rho_next = 1.0 / (2.0 * sigma - rho)
        keep, gain = rho_next * rho, 2.0 * rho_next / delta
        rho = rho_next
        here = d_ref[first]
        fx_before = tx_ref[first - 1] * (d_ref[first - 1] - here)
        for k in range(first, last):
            after = d_ref[k + 1]
            fx = tx_ref[k] * (here - after)
            fy = ty_ref[k] * (here - turned(here, -1, 0))
            fz = tz_ref[k] * (here - turned(here, -1, 1))
            applied = storage * here + (fx - fx_before) + (fy - turned(fy, 1, 0)) + (fz - turned(fz, 1, 1))
            residual = r_ref[k] - applied
            fresh = keep * here + gain * (residual * w_ref[k])
            if REACH <= k < count - REACH:
                so_far = here if step == 0 else p_ref[k]
                p_ref[k] = so_far + fresh
            if step < DEGREE - 1:
                r_ref[k] = residual
                d_ref[k] = fresh
            here, fx_before = after, fx


def window_scratch(count, rows, lanes):
    return [pltpu.VMEM((count, rows, lanes), jnp.float32)] * 7


def exact_dot(value, zero_one):
    parts = []
    for _ in range(3):
        part = value.astype(jnp.bfloat16)
        parts.append(part)
        value = value - part.astype(jnp.float32)
    rows = value.shape[0]
    out = jnp.dot(jnp.concatenate(parts, axis=0), zero_one, preferred_element_type=jnp.float32)
    return (out[2 * rows :] + out[rows : 2 * rows]) + out[:rows]


def row_pairs(top, bottom, sum_ref):
    tiles = top.shape[1] // LANES
    for tile in range(tiles):
        columns = slice(tile * LANES, (tile + 1) * LANES)
        sum_ref[tile, :SUBLANES] = top[:, columns]
        sum_ref[tile, SUBLANES:] = bottom[:, columns]
    return jnp.concatenate(
        [
            sum_ref[tile, pl.ds(0, SUBLANES, stride=2), :] + sum_ref[tile, pl.ds(1, SUBLANES, stride=2), :]
            for tile in range(tiles)
        ],
        axis=1,
    )


def lane_pairs(pieces):
    lanes = pieces[0].shape[1]
    pick = (iota((lanes, lanes // 2), 0) // 2 == iota((lanes, lanes // 2), 1)).astype(jnp.bfloat16)
    pooled = exact_dot(jnp.concatenate(pieces, axis=0), pick)
    return [pooled[SUBLANES * i : SUBLANES * (i + 1)] for i in range(len(pieces))]


def join_halo(near, beyond, starts):
    row = iota(near.shape, 0)
    up, down = turned(beyond, 3, 0), turned(beyond, -3, 0)
    right = jnp.where((row == 3) | (row == 7), up, jnp.where(row == 6, turned(beyond, 5, 0), near))
    left = jnp.where((row == 0) | (row == 4), down, jnp.where(row == 5, up, near))
    return jnp.where(starts, right, left)


def beyond_halo(joined, starts):
    row = iota(joined.shape, 0)
    up, down = turned(joined, 3, 0), turned(joined, -3, 0)
    right = jnp.where(row == 1, turned(joined, -5, 0), down)
    left = jnp.where(row == 2, down, up)
    return jnp.where(starts, right, left)


def join_third(near, third):
    row = iota(near.shape, 0)
    return jnp.where(
        row == 3, turned(third, 3, 0), jnp.where(row == 4, turned(third, -3, 0), near)
    )


def third_halo(joined):
    return jnp.where(iota(joined.shape, 0) < REACH, turned(joined, -3, 0), turned(joined, 3, 0))


def prep_kernel(log_ref, source_ref, pooled_ref, left_ref, right_ref, sum_ref):
    layers, rows, lanes = log_ref.shape
    half = lanes // 2
    upper = iota((SUBLANES, lanes), 0) < REACH
    pieces = []
    for x in range(2):
        for ref in (log_ref, source_ref):
            both = ref[2 * x] + ref[2 * x + 1]
            pieces.append(row_pairs(both[:SUBLANES], both[SUBLANES:], sum_ref))
    log0, source0, log1, source1 = lane_pairs(pieces)
    log0, log1 = log0 * 0.125, log1 * 0.125
    pooled_ref[0] = jnp.concatenate([log0, source0], axis=1)
    pooled_ref[1] = jnp.concatenate([log1, source1], axis=1)
    for layer in range(layers):
        left_ref[layer] = jnp.where(
            upper, log_ref[layer, :SUBLANES], turned(source_ref[layer, :SUBLANES], REACH, 0)
        )
        right_ref[layer] = jnp.where(
            upper, turned(source_ref[layer, SUBLANES:], REACH, 0), log_ref[layer, SUBLANES:]
        )
    pair = iota((SUBLANES, half), 0) // 2

    def four(*tiles):
        merged = jnp.where(
            pair == 0, tiles[0], jnp.where(pair == 1, tiles[1], jnp.where(pair == 2, tiles[2], tiles[3]))
        )
        return jnp.concatenate([merged, merged], axis=1)

    left_ref[layers] = four(turned(log1, -2, 0), log0, turned(source1, 2, 0), turned(source0, 4, 0))
    right_ref[layers] = four(turned(log0, -4, 0), turned(log1, -2, 0), source0, turned(source1, 2, 0))


def prep(log_perm, source):
    layers, rows, lanes = log_perm.shape

    def tiles(count):
        return jax.ShapeDtypeStruct((count, SUBLANES, lanes), jnp.float32)

    return pl.pallas_call(
        prep_kernel,
        out_shape=(tiles(2), tiles(layers + 1), tiles(layers + 1)),
        in_specs=[VMEM] * 2,
        out_specs=(VMEM,) * 3,
        scratch_shapes=[pltpu.VMEM((lanes // LANES, 2 * SUBLANES, LANES), jnp.float32)],
        compiler_params=pltpu.CompilerParams(vmem_limit_bytes=8 << 20),
        cost_estimate=pl.CostEstimate(flops=5_000_000, bytes_accessed=700_000, transcendentals=0),
        name="prep",
    )(log_perm, source)


def pack_kernel(wide, n_far, pooled_ref, *refs):
    *got_refs, halo_ref, first_ref, second_ref, far_ref, sum_ref = refs
    layers, lanes = got_refs[0].shape[0] - 1, got_refs[0].shape[2]
    ix, iy = lax.axis_index("gx"), lax.axis_index("gy")
    even, starts, low = iy % 2 == 0, iy == 0, ix % 4 < 2
    half = lanes // 2
    upper = iota((SUBLANES, lanes), 0) < REACH
    row = iota((SUBLANES, half), 0)

    def got(slot):
        tiles = tuple(ref[slot] for ref in got_refs)
        return from_right(even, tiles), from_left(even, tiles)

    strips = [got(layer) for layer in range(layers)]
    extra = [tile[:, :half] for tile in got(layers)]
    pieces = []
    for side in range(2 if wide else 1):
        both = [strips[2 * x][side] + strips[2 * x + 1][side] for x in range(2)]
        pieces.append(row_pairs(*both, sum_ref))
    fine_rows = lane_pairs(pieces)

    def right_halos(rows, extra):
        rows = jnp.where(row % 4 < 2, rows * 0.125, rows)
        return [
            jnp.where(row < 2, near, jnp.where((row == 4) | (row == 5), far, more))
            for near, far, more in (
                (rows, turned(rows, 2, 0), extra),
                (turned(rows, 4, 0), turned(rows, -2, 0), turned(extra, 2, 0)),
            )
        ]

    def left_halos(rows, extra):
        rows = jnp.where(row % 4 >= 2, rows * 0.125, rows)
        return [
            jnp.where((row == 2) | (row == 3), near, jnp.where(row >= 6, far, more))
            for near, far, more in (
                (rows, turned(rows, -2, 0), extra),
                (turned(rows, 4, 0), turned(rows, 2, 0), turned(extra, -2, 0)),
            )
        ]

    right, left = right_halos(fine_rows[0], extra[0]), left_halos(fine_rows[-1], extra[1])
    if wide:
        top = row < REACH
        halos = [jnp.where(top, right[x], turned(left[x], REACH, 0)) for x in range(2)]
        halos += [jnp.where(top, turned(right[x], REACH, 0), left[x]) for x in range(2)]
    else:
        halos = [jnp.where(starts, right[x], left[x]) for x in range(2)]

    def pair(left, right):
        return jnp.concatenate([left, right], axis=1)

    for i in range(len(halos) // 2):
        halo_ref[i] = pair(halos[2 * i], halos[2 * i + 1])
    logs = [pooled_ref[x, :, :half] for x in range(2)]
    sources = [pooled_ref[x, :, half:] for x in range(2)]

    def near_tiles(order):
        near, beyond = order[0] // 2, order[-1] // 2
        if wide:
            log_rows = [jnp.where(upper, *strips[layer]) for layer in range(layers)]
            source_rows = [turned(jnp.where(upper, *strips[layer][::-1]), REACH, 0) for layer in range(layers)]
            return [
                join_third(log_rows[order[0]], log_rows[order[2]]),
                source_rows[order[0]],
                log_rows[order[1]],
                source_rows[order[1]],
                pair(halos[near], halos[beyond]),
                pair(halos[2 + near], halos[2 + beyond]),
                pair(sources[beyond], sources[beyond]),
            ]
        nearest, third = strips[order[0]][0], strips[order[2]][0]
        place = iota((SUBLANES, lanes), 0)
        joined = jnp.where(
            starts,
            jnp.where(place == 3, turned(third, 3, 0), nearest),
            jnp.where(place == 4, turned(third, -3, 0), nearest),
        )
        return [
            joined,
            strips[order[1]][0],
            pair(join_halo(halos[near], halos[beyond], starts), sources[beyond]),
        ]

    forward = list(range(layers))
    for i, (right, left) in enumerate(zip(near_tiles(forward[::-1]), near_tiles(forward))):
        first_ref[i] = jnp.where(ix % 2 == 0, right, left)
        second_ref[i] = jnp.where(ix % 2 == 0, left, right)
    far = [
        (pair(logs[inner], logs[1 - inner]), pair(sources[inner], halos[inner])) for inner in (1, 0)
    ]
    for i in range(2):
        far_ref[0, i] = jnp.where(low, far[0][i], far[1][i])
        if n_far == 2:
            far_ref[1, i] = jnp.where(low, far[1][i], far[0][i])


def pack(pooled, got, n_far):
    slots, rows, lanes = got[0].shape
    wide = len(got) == 2

    def tiles(*count):
        return jax.ShapeDtypeStruct((*count, SUBLANES, lanes), jnp.float32)

    near = 7 if wide else 3
    return pl.pallas_call(
        functools.partial(pack_kernel, wide, n_far),
        out_shape=(tiles(len(got)), tiles(near), tiles(near), tiles(n_far, 2)),
        in_specs=[VMEM] * (1 + len(got)),
        out_specs=(VMEM,) * 4,
        scratch_shapes=[pltpu.VMEM((lanes // LANES, 2 * SUBLANES, LANES), jnp.float32)],
        compiler_params=pltpu.CompilerParams(vmem_limit_bytes=8 << 20),
        cost_estimate=pl.CostEstimate(flops=5_000_000, bytes_accessed=700_000, transcendentals=0),
        name="pack",
    )(pooled, *got)


def pool_kernel(first_ref, second_ref, out_ref, sum_ref):
    layers = REACH
    even = lax.axis_index("gx") % 2 == 0
    pieces = []
    for ref, on_right in ((first_ref, even), (second_ref, jnp.logical_not(even))):
        for x in range(2):
            both = ref[2 * x] + ref[2 * x + 1]
            pieces.append(row_pairs(both[:SUBLANES], both[SUBLANES:], sum_ref))
        both = ref[layers + 1] + jnp.where(on_right, ref[layers], ref[layers + 2])
        pieces.append(row_pairs(both[:SUBLANES], both[SUBLANES:], sum_ref))
    tiles = lane_pairs(pieces)
    for block in range(2):
        log0, log1, source = tiles[3 * block : 3 * block + 3]
        out_ref[block, 0] = jnp.concatenate([log0 * 0.125, log1 * 0.125], axis=1)
        out_ref[block, 1] = jnp.concatenate([source, source], axis=1)


def pool(first, second):
    _, rows, lanes = first.shape
    return pl.pallas_call(
        pool_kernel,
        out_shape=jax.ShapeDtypeStruct((2, 2, SUBLANES, lanes), jnp.float32),
        in_specs=[VMEM] * 2,
        out_specs=VMEM,
        scratch_shapes=[pltpu.VMEM((lanes // LANES, 2 * SUBLANES, LANES), jnp.float32)],
        compiler_params=pltpu.CompilerParams(vmem_limit_bytes=8 << 20),
        cost_estimate=pl.CostEstimate(flops=5_000_000, bytes_accessed=600_000, transcendentals=0),
        name="pool",
    )(first, second)


def lane_rows(ref, start, size):
    return ref[pl.ds(pl.multiple_of(start, SUBLANES), size), :]


def coarse_kernel(peers, places, n_far, low_ref, high_ref, own_ref, halo_ref, pool_ref, *refs):
    near_refs, far_refs = refs[:2], refs[2 : 2 + n_far]
    early_ref, late_ref, out_ref, wide_ref, *scratch = refs[2 + n_far :]
    ix, iy, iz = (lax.axis_index(axis) for axis in AXES)
    nx, ny, nz = peers
    both_sides = ny > 2
    lanes = own_ref.shape[2] // 2
    rows = SUBLANES
    even, low, starts = ix % 2 == 0, ix % 4 < 2, iy == 0
    near_strips = 4 if both_sides else 2
    top = iota((rows, lanes + LANES), 0) < REACH

    def with_lanes(core, ref, start):
        return jnp.concatenate([core, lane_rows(ref, start, rows)], axis=1)

    def columns(half):
        return slice(half * lanes, (half + 1) * lanes)

    def own(slot, half):
        ref, start = (own_ref, places["own_pooled"]) if slot < 2 else (halo_ref, places["own_halos"])
        slot = slot % 2
        start = start + (2 * slot + half) * rows
        return with_lanes(ref[slot, :, columns(half)], early_ref, start)

    def pooled(side, slot, half):
        block = jnp.where(even, 0, 1) if side > 0 else jnp.where(even, 1, 0)
        start = places["pooled"] + block * (4 * rows) + (2 * slot + half) * rows
        return with_lanes(pool_ref[block, slot, :, columns(half)], early_ref, start)

    def near(side, slot, half):
        pick = from_left if side < 0 else from_right
        core = pick(even, tuple(ref[near_strips + slot, :, columns(half)] for ref in near_refs))
        start = pick(even, tuple(places["near_pooled"])) + (2 * slot + half) * rows
        return with_lanes(core, late_ref, start)

    def far(side, slot, half):
        pick = from_left if side < 0 else from_right
        core = pick(low, tuple(ref[slot, :, columns(half)] for ref in far_refs))
        return with_lanes(core, late_ref, pick(low, tuple(places["far"])))

    def split(tile, a):
        other = turned(tile, REACH, 0)
        return jnp.where(top, tile, other) if a == 0 else jnp.where(top, other, tile)

    def window(a, k):
        block, layer = k // 2 - 2, k % 2
        nearest = layer == (1 if block < 0 else 0)
        if abs(block) == 2:
            if a == 1:
                core = far(block, 1, 0)
                return jnp.concatenate([core, jnp.zeros_like(core)], axis=0)
            halo = far(block, 1, 1)
            halo = halo if both_sides else split(halo, 0)
            return jnp.concatenate([far(block, 0, 0 if nearest else 1), halo], axis=0)
        if block == 0:
            core = own(layer, a)
            halo = own(2 + a, layer) if both_sides else split(own(2, layer), a)
            return jnp.concatenate([core, halo], axis=0)
        if a == 0:
            core = pooled(block, 0, layer)
        elif nearest:
            core = pooled(block, 1, 0)
        else:
            core = near(block, 2, 0) if both_sides else near(block, 0, 1)
        if both_sides:
            halo = near(block, a, 0 if nearest else 1)
        else:
            joined = near(block, 0, 0)
            halo = split(joined if nearest else beyond_halo(joined, starts), a)
        return jnp.concatenate([core, halo], axis=0)

    def open_face(inside):
        return jnp.where(inside, 4.0, 0.0)

    faces = [4.0] * 9
    faces[1], faces[3] = open_face(ix > 1), open_face(ix > 0)
    faces[5], faces[7] = open_face(ix < nx - 1), open_face(ix < nx - 2)
    shape = (2 * rows, lanes + LANES)
    iterate(
        2 + 2 * REACH,
        functools.partial(window, 0),
        functools.partial(window, 1),
        faces,
        numerators(shape, 0, rows, iy, ny, 2.0),
        numerators(shape, 1, lanes, iz, nz, 2.0),
        jnp.full((1, shape[1]), low_ref[0]),
        jnp.full((1, shape[1]), high_ref[0]),
        8.0 * storage_rate,
        scratch,
    )
    p_ref = scratch[-1]
    widen = (iota((lanes, 2 * lanes), 0) == iota((lanes, 2 * lanes), 1) // 2).astype(jnp.bfloat16)
    pressure = jnp.concatenate([p_ref[REACH + x, :rows, :lanes] for x in range(2)], axis=0)
    wide = exact_dot(pressure, widen)
    for x in range(2):
        for tile in range(2 * lanes // LANES):
            part = slice(tile * LANES, (tile + 1) * LANES)
            for half in range(2):
                wide_ref[tile, pl.ds(half, rows, stride=2), :] = wide[x * rows : (x + 1) * rows, part]
            for twin in range(2):
                out_ref[2 * x + twin, :, part] = wide_ref[tile]


def coarse_level(low_bound, high_bound, own, halos, pooled, near, far, early, late, places, peers):
    lanes = own.shape[2] // 2
    window = (2 + 2 * REACH, 2 * SUBLANES, lanes + LANES)
    return pl.pallas_call(
        functools.partial(coarse_kernel, peers, places, len(far)),
        out_shape=jax.ShapeDtypeStruct((REACH, 2 * SUBLANES, 2 * lanes), jnp.float32),
        in_specs=[SMEM, SMEM] + [VMEM] * (7 + len(far)),
        out_specs=VMEM,
        scratch_shapes=[pltpu.VMEM((2 * lanes // LANES, 2 * SUBLANES, LANES), jnp.float32)]
        + window_scratch(*window),
        compiler_params=pltpu.CompilerParams(vmem_limit_bytes=24 << 20),
        cost_estimate=pl.CostEstimate(flops=20_000_000, bytes_accessed=4_000_000, transcendentals=0),
        name="coarse_level",
    )(low_bound, high_bound, own, halos, pooled, *near, *far, early, late)


def fine_kernel(
    peers,
    places,
    low_ref,
    high_ref,
    log_ref,
    source_ref,
    first_ref,
    second_ref,
    first_near_ref,
    second_near_ref,
    early_ref,
    late_ref,
    spread_ref,
    *refs,
):
    *got_refs, fine_ref, diff_ref = refs[:-7]
    refs = refs[-7:]
    layers, rows, lanes = fine_ref.shape
    ix, iy, iz = (lax.axis_index(axis) for axis in AXES)
    nx, ny, nz = peers
    both_sides = ny > 2
    even = ix % 2 == 0
    count = 3 * layers

    def with_lanes(core, ref, start):
        return jnp.concatenate([core, lane_rows(ref, start, core.shape[0])], axis=1)

    def near(side, slot):
        pick = from_left if side < 0 else from_right
        core = pick(even, (first_near_ref[slot], second_near_ref[slot]))
        return with_lanes(core, late_ref, pick(even, tuple(places["near_strips"])) + slot * SUBLANES)

    def window(a, k):
        side, layer = k // layers - 1, k % layers
        if side == 0:
            core = (log_ref, source_ref)[a][layer]
            core = with_lanes(core, early_ref, places["own"] + (a * layers + layer) * rows)
            tiles = tuple(
                with_lanes(ref[layer], early_ref, start + layer * SUBLANES)
                for ref, start in zip(got_refs, places["own_strips"])
            )
            halo = tiles[0]
            if both_sides:
                sides = from_right(iy % 2 == 0, tiles), from_left(iy % 2 == 0, tiles)
                upper = iota(halo.shape, 0) < REACH
                halo = jnp.where(upper, *(sides if a == 0 else sides[::-1]))
            if a == 1:
                halo = turned(halo, REACH, 0)
        else:
            pick = from_left if side < 0 else from_right
            slot = layer if a == 0 else layers + layer - (1 if side < 0 else 0)
            core = pick(even, (first_ref[slot], second_ref[slot]))
            core = with_lanes(core, early_ref, pick(even, tuple(places["raw"])) + slot * rows)
            distance = layers - layer if side < 0 else layer + 1
            if both_sides:
                halo = near(side, (2 if distance == 2 else 0) + a)
            else:
                halo = near(side, 1 if distance == 2 else 0)
                if a == 1:
                    halo = turned(halo, REACH, 0)
            if a == 0 and distance > 2:
                halo = third_halo(halo)
        return jnp.concatenate([core, halo], axis=0)

    faces = [2.0] * (count - 1)
    faces[layers - 1] = jnp.where(ix > 0, 2.0, 0.0)
    faces[2 * layers - 1] = jnp.where(ix < nx - 1, 2.0, 0.0)
    shape = (rows + 2 * REACH, lanes + LANES)
    iterate(
        count,
        functools.partial(window, 0),
        functools.partial(window, 1),
        faces,
        numerators(shape, 0, rows, iy, ny, 1.0),
        numerators(shape, 1, lanes, iz, nz, 1.0),
        jnp.full((1, shape[1]), low_ref[0]),
        jnp.full((1, shape[1]), high_ref[0]),
        storage_rate,
        refs,
    )
    p_ref = refs[-1]
    for x in range(layers):
        fine = p_ref[REACH + x, :rows, :lanes]
        fine_ref[x] = fine
        diff_ref[x] = fine - spread_ref[x]


def fine_level(low_bound, high_bound, log_perm, source, got, raw, near, early, late, spread, places, peers):
    layers, rows, lanes = log_perm.shape
    window = (layers + 2 * REACH, rows + 2 * REACH, lanes + LANES)
    out = jax.ShapeDtypeStruct(log_perm.shape, jnp.float32)
    return pl.pallas_call(
        functools.partial(fine_kernel, peers, places),
        out_shape=(out, out),
        in_specs=[SMEM, SMEM] + [VMEM] * (9 + len(got)),
        out_specs=(VMEM, VMEM),
        scratch_shapes=window_scratch(*window),
        compiler_params=pltpu.CompilerParams(vmem_limit_bytes=24 << 20),
        cost_estimate=pl.CostEstimate(flops=20_000_000, bytes_accessed=10_000_000, transcendentals=0),
        name="fine_level",
    )(low_bound, high_bound, log_perm, source, *raw, *near, early, late, spread, *got)


class LaneTiles:
    def __init__(self):
        self.offset, self.parts = 0, []

    def add(self, array):
        start = self.offset
        self.parts.append(array.reshape(-1, array.shape[-1]))
        self.offset += self.parts[-1].shape[0]
        return start

    def add_halves(self, array):
        half = array.shape[-1] // 2
        return self.add(array.reshape(-1, SUBLANES, 2, half).swapaxes(1, 2))

    def swapped(self, peers):
        last = jnp.concatenate([part[:, -LANES:] for part in self.parts])
        first = jnp.concatenate([part[:, :LANES] for part in self.parts])
        got = swap("gz", peers, last, first)
        if len(got) == 1:
            return got[0]
        even = lax.axis_index("gz") % 2 == 0
        return jnp.where(iota(last.shape, 1) < LANES // 2, from_right(even, got), from_left(even, got))


def shards(peers, log_perm, source, low_bound, high_bound):
    nx, ny, nz = peers
    layers, rows, lanes = log_perm.shape
    assert layers == REACH and rows == 2 * SUBLANES and nx > 2
    own, rows_left, rows_right = prep(log_perm, source)
    got = swap("gy", ny, rows_right, rows_left)
    to_right, to_left = jnp.concatenate([log_perm, source[1:]]), jnp.concatenate([log_perm, source[:-1]])
    second = second_swap("gx", nx, to_right, to_left)
    raw = (first_swap("gx", nx, to_right, to_left), second)
    far_groups = far_pairs(nx)
    halos, for_first, for_second, for_far = pack(own, got, len(far_groups))
    far = tuple(permute(for_far[i], "gx", nx, group) for i, group in enumerate(far_groups))
    second = permute(for_second, "gx", nx, neighbour_pairs(nx, 1))
    near = (permute(for_first, "gx", nx, neighbour_pairs(nx, 0)), second)
    pooled = pool(*raw)
    near_strips = 2 * len(got)
    places, early, late = {}, LaneTiles(), LaneTiles()
    places["own"] = early.add(jnp.concatenate([log_perm, source]))
    places["own_strips"] = [early.add(tiles[:layers]) for tiles in got]
    places["own_pooled"] = early.add_halves(own)
    places["own_halos"] = early.add_halves(halos)
    places["raw"] = [early.add(block) for block in raw]
    places["pooled"] = early.add_halves(pooled)
    places["near_strips"] = [late.add(block[:near_strips]) for block in near]
    places["near_pooled"] = [late.add_halves(block[near_strips:]) for block in near]
    places["far"] = [late.add(block[0, :, : lanes // 2]) for block in far]
    early, late = early.swapped(nz), late.swapped(nz)
    spread = coarse_level(
        low_bound, high_bound, own, halos, pooled, near, far, early, late, places, peers
    )
    return fine_level(
        low_bound, high_bound, log_perm, source, got, raw, near, early, late, spread, places, peers
    )


def solution(mesh):
    peers = tuple(mesh.shape[axis] for axis in AXES)
    split = P(("groups", "gx"), "gy", "gz")
    return jax.shard_map(
        functools.partial(shards, peers),
        mesh=mesh,
        in_specs=(split, split, P(), P()),
        out_specs=(split, split),
        check_vma=False,
    )
```

```python
import functools

import jax
import jax.numpy as jnp
from jax import lax
from jax.experimental import pallas as pl
from jax.experimental.pallas import tpu as pltpu
from jax.sharding import PartitionSpec as P

DEGREE = 3
REACH = DEGREE + 1
LANES = 128
SUBLANES = 8
storage_rate = 0.1
AXES = ("gx", "gy", "gz")
VMEM = pl.BlockSpec(memory_space=pltpu.VMEM)
ANY = pl.BlockSpec(memory_space=pl.ANY)


AHEAD = pl.CostEstimate(flops=50_000_000_000, bytes_accessed=1_000_000, transcendentals=0)


def iota(shape, dim):
    return lax.broadcasted_iota(jnp.int32, shape, dim)


def turned(value, shift, axis):
    size = value.shape[axis]
    return pltpu.roll(value, shift % size, axis)


def permute(value, axis, peers, pairs):
    cores = lax.axis_size("gz")
    if axis == "gz" or cores % 2:
        return lax.ppermute(value, axis, [pair for i, j in pairs for pair in ((i, j), (j, i))])
    partner = {}
    for i, j in pairs:
        partner[i], partner[j] = j, i
    moves = [
        (i * cores + core, partner[i] * cores + core if i in partner else i * cores + (core ^ 1))
        for i in range(peers)
        for core in range(cores)
    ]
    return lax.ppermute(value, (axis, "gz"), moves)


def neighbour_pairs(peers, start):
    return [(i, i + 1) for i in range(start, peers - 1, 2)]


def first_swap(axis, peers, right, left):
    even = lax.axis_index(axis) % 2 == 0
    return permute(jnp.where(even, right, left), axis, peers, neighbour_pairs(peers, 0))


def second_swap(axis, peers, right, left):
    even = lax.axis_index(axis) % 2 == 0
    return permute(jnp.where(even, left, right), axis, peers, neighbour_pairs(peers, 1))


def swap(axis, peers, right, left):
    got = (first_swap(axis, peers, right, left),)
    return got if peers == 2 else got + (second_swap(axis, peers, right, left),)


def far_pairs(peers):
    pairs = [(i, i + 2) for i in range(peers - 2)]
    groups = [[pair for pair in pairs if pair[0] % 4 < 2], [pair for pair in pairs if pair[0] % 4 >= 2]]
    return [group for group in groups if group]


def from_right(is_first, got):
    return got[0] if len(got) == 1 else jnp.where(is_first, got[0], got[1])


def from_left(is_first, got):
    return got[0] if len(got) == 1 else jnp.where(is_first, got[1], got[0])


def inverse(value):
    guess = pl.reciprocal(value, approx=True)
    return guess * (2.0 - value * guess)


def numerators(shape, dim, own, index, peers, face_scale):
    place = iota(shape, dim)
    right = jnp.where(index < peers - 1, 2.0 * face_scale, 0.0)
    left = jnp.where(index > 0, 2.0 * face_scale, 0.0)
    return jnp.where(
        place == own - 1, right, jnp.where(place == shape[dim] - 1, left, 2.0 * face_scale)
    )


def iterate(count, log_at, source_at, x_faces, y_top, z_top, coef_ref, storage, refs):
    tx_ref, ty_ref, tz_ref, w_ref, d_ref, r_ref, p_ref = refs
    rows, lanes = y_top.shape

    def coefficient(i):
        return jnp.concatenate(
            [jnp.concatenate([coef_ref[i]] * (lanes // LANES), axis=1)] * (rows // SUBLANES), axis=0
        )

    over_theta = coefficient(0)
    after = jnp.exp(-log_at(0))
    tx_before = None
    for k in range(count):
        here = after
        if k + 1 < count:
            after = jnp.exp(-log_at(k + 1))
            tx = x_faces[k] * inverse(here + after)
            tx_ref[k] = tx
        if 1 <= k <= count - 2:
            ty = y_top * inverse(here + turned(here, -1, 0))
            tz = z_top * inverse(here + turned(here, -1, 1))
            diagonal = storage + (tx_before + tx) + (ty + turned(ty, 1, 0)) + (tz + turned(tz, 1, 1))
            w = inverse(diagonal)
            source = source_at(k)
            d_ref[k] = source * (over_theta * w)
            if 2 <= k <= count - 3:
                ty_ref[k] = ty
                tz_ref[k] = tz
                w_ref[k] = w
                r_ref[k] = source
        tx_before = tx
    for step in range(DEGREE):
        first, last = 2 + step, count - 2 - step
        keep, gain = coefficient(1 + 2 * step), coefficient(2 + 2 * step)
        here = d_ref[first]
        fx_before = tx_ref[first - 1] * (d_ref[first - 1] - here)
        for k in range(first, last):
            after = d_ref[k + 1]
            fx = tx_ref[k] * (here - after)
            fy = ty_ref[k] * (here - turned(here, -1, 0))
            fz = tz_ref[k] * (here - turned(here, -1, 1))
            applied = storage * here + (fx - fx_before) + (fy - turned(fy, 1, 0)) + (fz - turned(fz, 1, 1))
            residual = r_ref[k] - applied
            fresh = keep * here + gain * (residual * w_ref[k])
            if REACH <= k < count - REACH:
                so_far = here if step == 0 else p_ref[k]
                p_ref[k] = so_far + fresh
            if step < DEGREE - 1:
                r_ref[k] = residual
                d_ref[k] = fresh
            here, fx_before = after, fx


def coefficients_kernel(low_ref, high_ref, after_ref, coef_ref, bounds_ref, sems):
    copies = [
        pltpu.make_async_copy(ref, bounds_ref.at[i], sems.at[i]) for i, ref in enumerate((low_ref, high_ref))
    ]
    for copy in copies:
        copy.start()
    for copy in copies:
        copy.wait()
    low, high = (jnp.full((SUBLANES, LANES), bounds_ref[i, 0]) for i in range(2))
    theta, delta = (high + low) * 0.5, (high - low) * 0.5
    sigma = theta / delta
    rho = 1.0 / sigma
    coef_ref[0] = 1.0 / theta
    for step in range(DEGREE):
        rho_next = 1.0 / (2.0 * sigma - rho)
        coef_ref[1 + 2 * step] = rho_next * rho
        coef_ref[2 + 2 * step] = 2.0 * rho_next / delta
        rho = rho_next


def chebyshev_coefficients(low_bound, high_bound, after):
    return pl.pallas_call(
        coefficients_kernel,
        out_shape=jax.ShapeDtypeStruct((1 + 2 * DEGREE, SUBLANES, LANES), jnp.float32),
        in_specs=[pl.BlockSpec(memory_space=pltpu.HBM)] * 2 + [ANY],
        out_specs=VMEM,
        scratch_shapes=[pltpu.SMEM((2, 1), jnp.float32), pltpu.SemaphoreType.DMA((2,))],
        compiler_params=pltpu.CompilerParams(vmem_limit_bytes=4 << 20),
        cost_estimate=pl.CostEstimate(flops=1_000_000, bytes_accessed=100_000, transcendentals=0),
        name="coefficients",
    )(low_bound, high_bound, after)


def put(ref, tile, value):
    for i in range(value.shape[1] // LANES):
        ref[(tile + i) * SUBLANES : (tile + i + 1) * SUBLANES, :] = value[:, i * LANES : (i + 1) * LANES]


def take(ref, tile, count):
    tiles = [ref[(tile + i) * SUBLANES : (tile + i + 1) * SUBLANES, :] for i in range(count)]
    return tiles[0] if count == 1 else jnp.concatenate(tiles, axis=1)


def edges(value):
    lanes = value.shape[-1]
    value = value if isinstance(value, jax.Array) else value.at
    return value[:, lanes - LANES :], value[:, :LANES]


def write_lanes(ref, pairs):
    starts = lax.axis_index("gz") == 0
    each = LANES // SUBLANES
    group = iota((SUBLANES, LANES), 1) // SUBLANES
    for base in range(0, len(pairs), each):
        merged = None
        for j, (last, first) in enumerate(pairs[base : base + each]):
            moved = turned(jnp.where(starts, last, first), SUBLANES * j, 1)
            place = jnp.where(starts, (j - 1) % each, j)
            merged = moved if merged is None else jnp.where(group == place, moved, merged)
        row = base // each * SUBLANES
        ref[row : row + SUBLANES, :] = merged


def read_lanes(ref, slot):
    each = LANES // SUBLANES
    row = slot // each * SUBLANES
    return turned(ref[row : row + SUBLANES, :], -SUBLANES * (slot % each), 1)


def early_slots(layers, row_tiles, n_got):
    keys = [("own", a, layer, i) for a in range(2) for layer in range(layers) for i in range(row_tiles)]
    keys += [("got", g, layer) for g in range(n_got) for layer in range(layers)]
    keys += [("pooled", x, a) for x in range(2) for a in range(2)]
    keys += [("halo", i, half) for i in range(n_got) for half in range(2)]
    keys += [
        ("raw", side, slot, i)
        for side in range(2)
        for slot in range(2 * layers - 1)
        for i in range(row_tiles)
    ]
    keys += [("near", side, i) for side in range(2) for i in range(3)]
    return {key: i for i, key in enumerate(keys)}


def near_layout(lanes, wide):
    whole, half = lanes // LANES, lanes // LANES // 2
    if wide:
        parts = [("log1", whole), ("source1", whole), ("log2", whole), ("source2", whole)]
        parts += [(name, half) for name in ("halo0", "halo1", "halo2", "halo3", "source")]
    else:
        parts = [("strip", whole), ("halo", half), ("source", half), ("row", 1)]
    layout, start = {}, 0
    for name, count in parts:
        layout[name] = (start, count)
        start += count
    return layout, start


def late_slots(lanes, wide):
    names = list(near_layout(lanes, wide)[0])
    keys = [(side, name) for side in range(2) for name in names] + [(side, "far") for side in range(2)]
    return {key: i for i, key in enumerate(keys)}


def rows_to_lanes(row_tile, count):
    return jnp.concatenate(
        [jnp.broadcast_to(row_tile[j : j + 1], (SUBLANES, LANES)) for j in range(count)], axis=1
    )


def packed_rows(slots):
    each = LANES // SUBLANES
    return jax.ShapeDtypeStruct((-(-len(slots) // each) * SUBLANES, LANES), jnp.float32)


def window_scratch(count, rows, lanes):
    return [pltpu.VMEM((count, rows, lanes), jnp.float32)] * 7


def exact_dot(value, zero_one):
    parts = []
    for _ in range(3):
        part = value.astype(jnp.bfloat16)
        parts.append(part)
        value = value - part.astype(jnp.float32)
    rows = value.shape[0]
    out = jnp.dot(jnp.concatenate(parts, axis=0), zero_one, preferred_element_type=jnp.float32)
    return (out[2 * rows :] + out[rows : 2 * rows]) + out[:rows]


def row_pairs(top, bottom, sum_ref):
    tiles = top.shape[1] // LANES
    for tile in range(tiles):
        columns = slice(tile * LANES, (tile + 1) * LANES)
        sum_ref[tile, :SUBLANES] = top[:, columns]
        sum_ref[tile, SUBLANES:] = bottom[:, columns]
    return jnp.concatenate(
        [
            sum_ref[tile, pl.ds(0, SUBLANES, stride=2), :] + sum_ref[tile, pl.ds(1, SUBLANES, stride=2), :]
            for tile in range(tiles)
        ],
        axis=1,
    )


def lane_pairs(pieces):
    lanes = pieces[0].shape[1]
    pick = (iota((lanes, lanes // 2), 0) // 2 == iota((lanes, lanes // 2), 1)).astype(jnp.bfloat16)
    pooled = exact_dot(jnp.concatenate(pieces, axis=0), pick)
    return [pooled[SUBLANES * i : SUBLANES * (i + 1)] for i in range(len(pieces))]


def join_halo(near, beyond, starts):
    row = iota(near.shape, 0)
    up, down = turned(beyond, 3, 0), turned(beyond, -3, 0)
    right = jnp.where((row == 3) | (row == 7), up, jnp.where(row == 6, turned(beyond, 5, 0), near))
    left = jnp.where((row == 0) | (row == 4), down, jnp.where(row == 5, up, near))
    return jnp.where(starts, right, left)


def beyond_halo(joined, starts):
    row = iota(joined.shape, 0)
    up, down = turned(joined, 3, 0), turned(joined, -3, 0)
    right = jnp.where(row == 1, turned(joined, -5, 0), down)
    left = jnp.where(row == 2, down, up)
    return jnp.where(starts, right, left)


def join_third(near, third):
    row = iota(near.shape, 0)
    return jnp.where(
        row == 3, turned(third, 3, 0), jnp.where(row == 4, turned(third, -3, 0), near)
    )


def third_halo(joined):
    return jnp.where(iota(joined.shape, 0) < REACH, turned(joined, -3, 0), turned(joined, 3, 0))


def prep_kernel(log_ref, source_ref, pooled_ref, *refs):
    *out_refs, sum_ref = refs
    layers, rows, lanes = log_ref.shape
    starts = lax.axis_index("gy") == 0

    def put(slot, left, right):
        if len(out_refs) == 1:
            out_refs[0][slot] = jnp.where(starts, right, left)
        else:
            out_refs[0][slot], out_refs[1][slot] = left, right

    half = lanes // 2
    upper = iota((SUBLANES, lanes), 0) < REACH
    pieces = []
    for x in range(2):
        for ref in (log_ref, source_ref):
            both = ref[2 * x] + ref[2 * x + 1]
            pieces.append(row_pairs(both[:SUBLANES], both[SUBLANES:], sum_ref))
    log0, source0, log1, source1 = lane_pairs(pieces)
    log0, log1 = log0 * 0.125, log1 * 0.125
    pooled_ref[0] = jnp.concatenate([log0, source0], axis=1)
    pooled_ref[1] = jnp.concatenate([log1, source1], axis=1)
    for layer in range(layers):
        put(
            layer,
            jnp.where(upper, log_ref[layer, :SUBLANES], turned(source_ref[layer, :SUBLANES], REACH, 0)),
            jnp.where(upper, turned(source_ref[layer, SUBLANES:], REACH, 0), log_ref[layer, SUBLANES:]),
        )
    pair = iota((SUBLANES, half), 0) // 2

    def four(*tiles):
        merged = jnp.where(
            pair == 0, tiles[0], jnp.where(pair == 1, tiles[1], jnp.where(pair == 2, tiles[2], tiles[3]))
        )
        return jnp.concatenate([merged, merged], axis=1)

    put(
        layers,
        four(turned(log1, -2, 0), log0, turned(source1, 2, 0), turned(source0, 4, 0)),
        four(turned(log0, -4, 0), turned(log1, -2, 0), source0, turned(source1, 2, 0)),
    )


def prep(log_perm, source, ny):
    layers, rows, lanes = log_perm.shape
    outs = 1 if ny == 2 else 2

    def tiles(count):
        return jax.ShapeDtypeStruct((count, SUBLANES, lanes), jnp.float32)

    return pl.pallas_call(
        prep_kernel,
        out_shape=(tiles(2),) + (tiles(layers + 1),) * outs,
        in_specs=[VMEM] * 2,
        out_specs=(VMEM,) * (1 + outs),
        scratch_shapes=[pltpu.VMEM((lanes // LANES, 2 * SUBLANES, LANES), jnp.float32)],
        compiler_params=pltpu.CompilerParams(vmem_limit_bytes=8 << 20),
        cost_estimate=pl.CostEstimate(flops=5_000_000, bytes_accessed=700_000, transcendentals=0),
        name="prep",
    )(log_perm, source)


def raw_kernel(to_right_if_odd, log_ref, source_ref, after_ref, out_ref):
    layers = log_ref.shape[0]
    odd = lax.axis_index("gx") % 2
    skip = odd if to_right_if_odd else 1 - odd
    for layer in range(layers):
        out_ref[layer] = log_ref[layer]
    for layer in range(layers - 1):
        out_ref[layers + layer] = source_ref[layer + skip]


def raw_block(log_perm, source, after, to_right_if_odd):
    layers, rows, lanes = log_perm.shape
    return pl.pallas_call(
        functools.partial(raw_kernel, to_right_if_odd),
        out_shape=jax.ShapeDtypeStruct((2 * layers - 1, rows, lanes), jnp.float32),
        in_specs=[VMEM, VMEM, ANY],
        out_specs=VMEM,
        compiler_params=pltpu.CompilerParams(vmem_limit_bytes=8 << 20),
        cost_estimate=pl.CostEstimate(flops=1_000_000, bytes_accessed=500_000, transcendentals=0),
        name="raw_block",
    )(log_perm, source, after)


def pack_far_kernel(wide, pooled_ref, *refs):
    n_got = 2 if wide else 1
    got_refs, halo_ref, far_refs, sum_ref = refs[:n_got], refs[n_got], refs[n_got + 1 : -1], refs[-1]
    layers, lanes = got_refs[0].shape[0] - 1, got_refs[0].shape[2]
    ix, iy = lax.axis_index("gx"), lax.axis_index("gy")
    even, starts, low = iy % 2 == 0, iy == 0, ix % 4 < 2
    half = lanes // 2
    upper = iota((SUBLANES, lanes), 0) < REACH
    row = iota((SUBLANES, half), 0)

    def got(slot):
        tiles = tuple(ref[slot] for ref in got_refs)
        return from_right(even, tiles), from_left(even, tiles)

    strips = [got(layer) for layer in range(layers)]
    extra = [tile[:, :half] for tile in got(layers)]
    pieces = []
    for side in range(2 if wide else 1):
        both = [strips[2 * x][side] + strips[2 * x + 1][side] for x in range(2)]
        pieces.append(row_pairs(*both, sum_ref))
    fine_rows = lane_pairs(pieces)

    def right_halos(rows, extra):
        rows = jnp.where(row % 4 < 2, rows * 0.125, rows)
        return [
            jnp.where(row < 2, near, jnp.where((row == 4) | (row == 5), far, more))
            for near, far, more in (
                (rows, turned(rows, 2, 0), extra),
                (turned(rows, 4, 0), turned(rows, -2, 0), turned(extra, 2, 0)),
            )
        ]

    def left_halos(rows, extra):
        rows = jnp.where(row % 4 >= 2, rows * 0.125, rows)
        return [
            jnp.where((row == 2) | (row == 3), near, jnp.where(row >= 6, far, more))
            for near, far, more in (
                (rows, turned(rows, -2, 0), extra),
                (turned(rows, 4, 0), turned(rows, 2, 0), turned(extra, -2, 0)),
            )
        ]

    right, left = right_halos(fine_rows[0], extra[0]), left_halos(fine_rows[-1], extra[1])
    if wide:
        top = row < REACH
        halos = [jnp.where(top, right[x], turned(left[x], REACH, 0)) for x in range(2)]
        halos += [jnp.where(top, turned(right[x], REACH, 0), left[x]) for x in range(2)]
    else:
        halos = [jnp.where(starts, right[x], left[x]) for x in range(2)]

    def pair(left, right):
        return jnp.concatenate([left, right], axis=1)

    for i in range(len(halos) // 2):
        halo_ref[i] = pair(halos[2 * i], halos[2 * i + 1])
    logs = [pooled_ref[x, :, :half] for x in range(2)]
    sources = [pooled_ref[x, :, half:] for x in range(2)]

    far = [(logs[inner], logs[1 - inner], sources[inner], halos[inner]) for inner in (1, 0)]
    for group, ref in enumerate(far_refs):
        for i, (right, left) in enumerate(zip(*far)):
            put(ref, i * (half // LANES), jnp.where(low, *((right, left) if group == 0 else (left, right))))
        for spare in range(4 * (half // LANES), ref.shape[0] // SUBLANES):
            put(ref, spare, jnp.zeros((SUBLANES, LANES), jnp.float32))


def pack_far(pooled, got, n_far):
    slots, rows, lanes = got[0].shape
    wide = len(got) == 2
    far_rows = max(2 * lanes // LANES, 0 if wide else near_layout(lanes, wide)[1]) * SUBLANES
    out_shape = (jax.ShapeDtypeStruct((len(got), SUBLANES, lanes), jnp.float32),) + (
        jax.ShapeDtypeStruct((far_rows, LANES), jnp.float32),
    ) * n_far
    halos, *far = pl.pallas_call(
        functools.partial(pack_far_kernel, wide),
        out_shape=out_shape,
        in_specs=[VMEM] * (1 + len(got)),
        out_specs=(VMEM,) * len(out_shape),
        scratch_shapes=[pltpu.VMEM((lanes // LANES, 2 * SUBLANES, LANES), jnp.float32)],
        compiler_params=pltpu.CompilerParams(vmem_limit_bytes=8 << 20),
        cost_estimate=AHEAD,
        name="pack_far",
    )(pooled, *got)
    return halos, far


def pack_near_kernel(wide, pooled_ref, halo_ref, after_ref, *refs):
    *got_refs, first_ref, second_ref = refs
    layers, lanes = got_refs[0].shape[0] - 1, got_refs[0].shape[2]
    ix, iy = lax.axis_index("gx"), lax.axis_index("gy")
    even, starts = iy % 2 == 0, iy == 0
    half = lanes // 2
    upper = iota((SUBLANES, lanes), 0) < REACH

    def got(slot):
        tiles = tuple(ref[slot] for ref in got_refs)
        return from_right(even, tiles), from_left(even, tiles)

    strips = [got(layer) for layer in range(layers)]
    halos = [halo_ref[i // 2, :, (i % 2) * half : (i % 2 + 1) * half] for i in range(4 if wide else 2)]
    sources = [pooled_ref[x, :, half:] for x in range(2)]

    def near_tiles(order):
        near, beyond = order[0] // 2, order[-1] // 2
        if wide:
            log_rows = [jnp.where(upper, *strips[layer]) for layer in range(layers)]
            source_rows = [turned(jnp.where(upper, *strips[layer][::-1]), REACH, 0) for layer in range(layers)]
            return {
                "log1": join_third(log_rows[order[0]], log_rows[order[2]]),
                "source1": source_rows[order[0]],
                "log2": log_rows[order[1]],
                "source2": source_rows[order[1]],
                "halo0": halos[near],
                "halo1": halos[beyond],
                "halo2": halos[2 + near],
                "halo3": halos[2 + beyond],
                "source": sources[beyond],
            }
        first, second, third = (strips[layer][0] for layer in order[:3])
        place = iota((SUBLANES, lanes), 0)
        right = jnp.where(place == 3, turned(third, 3, 0), jnp.where(place >= 6, turned(second, -2, 0), first))
        left = jnp.where(place == 4, turned(third, -3, 0), jnp.where(place < 2, turned(second, 2, 0), first))
        line = jnp.where(starts, second[4:5], second[3:4])
        lines = jnp.zeros((SUBLANES, LANES), jnp.float32)
        for j in range(lanes // LANES):
            lines = jnp.where(iota(lines.shape, 0) == j, line[:, j * LANES : (j + 1) * LANES], lines)
        return {
            "strip": jnp.where(starts, right, left),
            "halo": join_halo(halos[near], halos[beyond], starts),
            "source": sources[beyond],
            "row": lines,
        }

    forward = list(range(layers))
    layout, _ = near_layout(lanes, wide)
    right, left = near_tiles(forward[::-1]), near_tiles(forward)
    for name, (start, _) in layout.items():
        put(first_ref, start, jnp.where(ix % 2 == 0, right[name], left[name]))
        put(second_ref, start, jnp.where(ix % 2 == 0, left[name], right[name]))


def pack_near(pooled, halos, after, got):
    slots, rows, lanes = got[0].shape
    wide = len(got) == 2
    out = jax.ShapeDtypeStruct((near_layout(lanes, wide)[1] * SUBLANES, LANES), jnp.float32)
    return pl.pallas_call(
        functools.partial(pack_near_kernel, wide),
        out_shape=(out, out),
        in_specs=[VMEM, VMEM, ANY] + [VMEM] * len(got),
        out_specs=(VMEM,) * 2,
        compiler_params=pltpu.CompilerParams(vmem_limit_bytes=8 << 20),
        cost_estimate=AHEAD,
        name="pack_near",
    )(pooled, halos, after, *got)


def landed_kernel(after_ref, log_ref, source_ref, pooled_ref, halo_ref, first_ref, second_ref, *refs):
    *got_refs, out_ref, sent_ref, sum_ref = refs
    layers, rows, lanes = log_ref.shape
    half = lanes // 2
    even = lax.axis_index("gx") % 2 == 0
    slots = early_slots(layers, rows // SUBLANES, len(got_refs))
    pairs = {}
    for a, ref in enumerate((log_ref, source_ref)):
        for layer in range(layers):
            for i in range(rows // SUBLANES):
                pairs["own", a, layer, i] = edges(ref.at[layer, i * SUBLANES : (i + 1) * SUBLANES])
    for g, ref in enumerate(got_refs):
        for layer in range(layers):
            pairs["got", g, layer] = edges(ref.at[layer])
    for i in range(2):
        for x in range(2):
            columns = slice(x * half, (x + 1) * half)
            pairs["pooled", i, x] = edges(pooled_ref.at[i, :, columns])
            if i < len(got_refs):
                pairs["halo", i, x] = edges(halo_ref.at[i, :, columns])
    pieces = []
    for side, pick in enumerate((from_left, from_right)):

        def block(slot):
            return pick(even, (first_ref[slot], second_ref[slot]))

        for slot in range(2 * layers - 1):
            for i in range(rows // SUBLANES):
                part = slice(i * SUBLANES, (i + 1) * SUBLANES)
                ends = [edges(ref.at[slot, part]) for ref in (first_ref, second_ref)]
                pairs["raw", side, slot, i] = [
                    pick(even, tuple(end[...] for end in both)) for both in zip(*ends)
                ]
        nearest = layers + 1 if side == 0 else layers
        for top in (0, 2, nearest):
            both = block(top) + block(top + 1)
            pieces.append(row_pairs(both[:SUBLANES], both[SUBLANES:], sum_ref))
    tiles = lane_pairs(pieces)
    for side in range(2):
        for i in range(3):
            tile = tiles[3 * side + i] * (0.125 if i < 2 else 1.0)
            put(out_ref, (3 * side + i) * (half // LANES), tile)
            pairs["near", side, i] = edges(tile)
    write_lanes(sent_ref, [tuple(end[...] for end in pairs[key]) for key in slots])


def landed(after, log_perm, source, pooled, halos, raw, got):
    layers, rows, lanes = log_perm.shape
    slots = early_slots(layers, rows // SUBLANES, len(got))
    return pl.pallas_call(
        landed_kernel,
        out_shape=(
            jax.ShapeDtypeStruct((6 * (lanes // 2 // LANES) * SUBLANES, LANES), jnp.float32),
            packed_rows(slots),
        ),
        in_specs=[ANY] + [VMEM] * (6 + len(got)),
        out_specs=(VMEM,) * 2,
        scratch_shapes=[pltpu.VMEM((lanes // LANES, 2 * SUBLANES, LANES), jnp.float32)],
        compiler_params=pltpu.CompilerParams(vmem_limit_bytes=16 << 20),
        cost_estimate=pl.CostEstimate(flops=1_000_000, bytes_accessed=1_000_000, transcendentals=0),
        name="landed",
    )(after, log_perm, source, pooled, halos, *raw, *got)


def near_part(refs, even, lanes, wide, side, name):
    start, count = near_layout(lanes, wide)[0][name]
    pick = from_left if side == 0 else from_right
    got = pick(even, tuple(take(ref, start, count) for ref in refs))
    return rows_to_lanes(got, lanes // LANES) if name == "row" else got


def far_part(refs, low, lanes, side, i):
    count = lanes // 2 // LANES
    pick = from_left if side == 0 else from_right
    return pick(low, tuple(take(ref, i * count, count) for ref in refs))


def late_kernel(lanes, wide, after_ref, first_ref, second_ref, *refs):
    *far_refs, sent_ref = refs
    even, low = lax.axis_index("gx") % 2 == 0, lax.axis_index("gx") % 4 < 2
    pairs = []
    for side, name in late_slots(lanes, wide):
        if name == "far":
            pairs.append(edges(far_part(far_refs, low, lanes, side, 0)))
        else:
            pairs.append(edges(near_part((first_ref, second_ref), even, lanes, wide, side, name)))
    write_lanes(sent_ref, pairs)


def late_lanes(after, near, far, lanes, wide):
    return pl.pallas_call(
        functools.partial(late_kernel, lanes, wide),
        out_shape=packed_rows(late_slots(lanes, wide)),
        in_specs=[ANY] + [VMEM] * (2 + len(far)),
        out_specs=VMEM,
        compiler_params=pltpu.CompilerParams(vmem_limit_bytes=8 << 20),
        cost_estimate=pl.CostEstimate(flops=1_000_000, bytes_accessed=200_000, transcendentals=0),
        name="late_lanes",
    )(after, *near, *far)


def coarse_kernel(peers, n_far, own_ref, halo_ref, pool_ref, first_ref, second_ref, *refs):
    near_refs, far_refs = (first_ref, second_ref), refs[:n_far]
    early_ref, late_ref, coef_ref, out_ref, wide_ref, *scratch = refs[n_far:]
    ix, iy, iz = (lax.axis_index(axis) for axis in AXES)
    nx, ny, nz = peers
    wide = ny > 2
    fine_lanes = own_ref.shape[2]
    lanes, rows = fine_lanes // 2, SUBLANES
    even, low, starts = ix % 2 == 0, ix % 4 < 2, iy == 0
    top = iota((rows, lanes + LANES), 0) < REACH
    early = early_slots(REACH, 2, 2 if wide else 1)
    late = late_slots(fine_lanes, wide)

    def columns(half):
        return slice(half * lanes, (half + 1) * lanes)

    def with_early(core, *key):
        return jnp.concatenate([core, read_lanes(early_ref, early[key])], axis=1)

    def near(side, name):
        core = near_part(near_refs, even, fine_lanes, wide, side, name)
        return jnp.concatenate([core, read_lanes(late_ref, late[side, name])], axis=1)

    def far(side, i):
        core = far_part(far_refs, low, fine_lanes, side, i)
        return jnp.concatenate([core, read_lanes(late_ref, late[side, "far"])], axis=1)

    def split(tile, a):
        other = turned(tile, REACH, 0)
        return jnp.where(top, tile, other) if a == 0 else jnp.where(top, other, tile)

    def window(a, k):
        block, layer = k // 2 - 2, k % 2
        nearest = layer == (1 if block < 0 else 0)
        side = 0 if block < 0 else 1
        if abs(block) == 2:
            if a == 1:
                core = far(side, 2)
                return jnp.concatenate([core, jnp.zeros_like(core)], axis=0)
            halo = far(side, 3)
            halo = halo if wide else split(halo, 0)
            return jnp.concatenate([far(side, 0 if nearest else 1), halo], axis=0)
        if block == 0:
            core = with_early(own_ref[layer, :, columns(a)], "pooled", layer, a)
            if wide:
                halo = with_early(halo_ref[a, :, columns(layer)], "halo", a, layer)
            else:
                halo = split(with_early(halo_ref[0, :, columns(layer)], "halo", 0, layer), a)
            return jnp.concatenate([core, halo], axis=0)
        if a == 0 or nearest:
            i = layer if a == 0 else 2
            core = take(pool_ref, (3 * side + i) * (lanes // LANES), lanes // LANES)
            core = with_early(core, "near", side, i)
        else:
            core = near(side, "source")
        if wide:
            halo = near(side, f"halo{2 * a + (0 if nearest else 1)}")
        else:
            joined = near(side, "halo")
            halo = split(joined if nearest else beyond_halo(joined, starts), a)
        return jnp.concatenate([core, halo], axis=0)

    def open_face(inside):
        return jnp.where(inside, 4.0, 0.0)

    faces = [4.0] * 9
    faces[1], faces[3] = open_face(ix > 1), open_face(ix > 0)
    faces[5], faces[7] = open_face(ix < nx - 1), open_face(ix < nx - 2)
    shape = (2 * rows, lanes + LANES)
    iterate(
        2 + 2 * REACH,
        functools.partial(window, 0),
        functools.partial(window, 1),
        faces,
        numerators(shape, 0, rows, iy, ny, 2.0),
        numerators(shape, 1, lanes, iz, nz, 2.0),
        coef_ref,
        8.0 * storage_rate,
        scratch,
    )
    p_ref = scratch[-1]
    widen = (iota((lanes, 2 * lanes), 0) == iota((lanes, 2 * lanes), 1) // 2).astype(jnp.bfloat16)
    pressure = jnp.concatenate([p_ref[REACH + x, :rows, :lanes] for x in range(2)], axis=0)
    spread = exact_dot(pressure, widen)
    for x in range(2):
        for tile in range(2 * lanes // LANES):
            part = slice(tile * LANES, (tile + 1) * LANES)
            for half in range(2):
                wide_ref[tile, pl.ds(half, rows, stride=2), :] = spread[x * rows : (x + 1) * rows, part]
            for twin in range(2):
                out_ref[2 * x + twin, :, part] = wide_ref[tile]


def coarse_level(own, halos, pooled, near, far, early, late, coefficients, peers):
    lanes = own.shape[2] // 2
    window = (2 + 2 * REACH, 2 * SUBLANES, lanes + LANES)
    return pl.pallas_call(
        functools.partial(coarse_kernel, peers, len(far)),
        out_shape=jax.ShapeDtypeStruct((REACH, 2 * SUBLANES, 2 * lanes), jnp.float32),
        in_specs=[VMEM] * (8 + len(far)),
        out_specs=VMEM,
        scratch_shapes=[pltpu.VMEM((2 * lanes // LANES, 2 * SUBLANES, LANES), jnp.float32)]
        + window_scratch(*window),
        compiler_params=pltpu.CompilerParams(vmem_limit_bytes=24 << 20),
        cost_estimate=pl.CostEstimate(flops=20_000_000, bytes_accessed=4_000_000, transcendentals=0),
        name="coarse_level",
    )(own, halos, pooled, *near, *far, early, late, coefficients)


def fine_kernel(peers, n_far, log_ref, source_ref, *refs):
    layers, rows, lanes = log_ref.shape
    ix, iy, iz = (lax.axis_index(axis) for axis in AXES)
    nx, ny, nz = peers
    wide = ny > 2
    n_got = 2 if wide else 1
    got_refs, refs = refs[:n_got], refs[n_got:]
    second_ref, first_ref = refs[:2]
    second_near_ref, first_near_ref, early_ref, late_ref, spread_ref = refs[2 + n_far : 7 + n_far]
    coef_ref, fine_ref, diff_ref, *scratch = refs[7 + n_far :]
    even, starts = ix % 2 == 0, iy == 0
    count = 3 * layers
    upper = iota((SUBLANES, lanes + LANES), 0) < REACH
    early = early_slots(layers, rows // SUBLANES, n_got)
    late = late_slots(lanes, wide)

    def with_early(core, *keys):
        tile = jnp.concatenate([read_lanes(early_ref, early[key]) for key in keys], axis=0)
        return jnp.concatenate([core, tile], axis=1)

    def near(side, name):
        core = near_part((first_near_ref, second_near_ref), even, lanes, wide, side, name)
        return jnp.concatenate([core, read_lanes(late_ref, late[side, name])], axis=1)

    def near_halo(a, side, distance):
        if wide:
            tile = near(side, ("log" if a == 0 else "source") + ("2" if distance == 2 else "1"))
        elif a == 1:
            return near(side, "row") if distance == 2 else turned(near(side, "strip"), REACH, 0)
        else:
            tile = near(side, "strip")
            if distance == 2:
                return jnp.where(starts, turned(tile, 2, 0), turned(tile, -2, 0))
        return third_halo(tile) if a == 0 and distance > 2 else tile

    def window(a, k):
        block, layer = k // layers - 1, k % layers
        if block == 0:
            core = (log_ref, source_ref)[a][layer]
            core = with_early(core, *(("own", a, layer, i) for i in range(rows // SUBLANES)))
            tiles = tuple(with_early(ref[layer], ("got", g, layer)) for g, ref in enumerate(got_refs))
            halo = tiles[0]
            if wide:
                sides = from_right(iy % 2 == 0, tiles), from_left(iy % 2 == 0, tiles)
                halo = jnp.where(upper, *(sides if a == 0 else sides[::-1]))
            if a == 1:
                halo = turned(halo, REACH, 0)
            return jnp.concatenate([core, halo], axis=0)
        side, pick = (0, from_left) if block < 0 else (1, from_right)
        slot = layer if a == 0 else layers + layer - (1 if block < 0 else 0)
        core = pick(even, (first_ref[slot], second_ref[slot]))
        core = with_early(core, *(("raw", side, slot, i) for i in range(rows // SUBLANES)))
        halo = near_halo(a, side, layers - layer if block < 0 else layer + 1)
        return jnp.concatenate([core, halo], axis=0)

    faces = [2.0] * (count - 1)
    faces[layers - 1] = jnp.where(ix > 0, 2.0, 0.0)
    faces[2 * layers - 1] = jnp.where(ix < nx - 1, 2.0, 0.0)
    shape = (rows + 2 * REACH, lanes + LANES)
    iterate(
        count,
        functools.partial(window, 0),
        functools.partial(window, 1),
        faces,
        numerators(shape, 0, rows, iy, ny, 1.0),
        numerators(shape, 1, lanes, iz, nz, 1.0),
        coef_ref,
        storage_rate,
        scratch,
    )
    p_ref = scratch[-1]
    for x in range(layers):
        fine = p_ref[REACH + x, :rows, :lanes]
        fine_ref[x] = fine
        diff_ref[x] = fine - spread_ref[x]


def fine_level(log_perm, source, got, raw, far, near, early, late, spread, coefficients, peers):
    layers, rows, lanes = log_perm.shape
    window = (layers + 2 * REACH, rows + 2 * REACH, lanes + LANES)
    out = jax.ShapeDtypeStruct(log_perm.shape, jnp.float32)
    return pl.pallas_call(
        functools.partial(fine_kernel, peers, len(far)),
        out_shape=(out, out),
        in_specs=[VMEM] * (4 + len(got)) + [ANY] * len(far) + [VMEM] * 6,
        out_specs=(VMEM, VMEM),
        scratch_shapes=window_scratch(*window),
        compiler_params=pltpu.CompilerParams(vmem_limit_bytes=24 << 20),
        cost_estimate=pl.CostEstimate(flops=20_000_000, bytes_accessed=10_000_000, transcendentals=0),
        name="fine_level",
    )(log_perm, source, *got, *raw[::-1], *far, *near[::-1], early, late, spread, coefficients)


def shards(peers, log_perm, source, low_bound, high_bound):
    nx, ny, nz = peers
    layers, rows, lanes = log_perm.shape
    assert layers == REACH and rows == 2 * SUBLANES and nx > 2 and nz == 2
    own, *rows_sent = prep(log_perm, source, ny)
    if ny == 2:
        got = (permute(rows_sent[0], "gy", ny, [(0, 1)]),)
    else:
        got = swap("gy", ny, rows_sent[1], rows_sent[0])
    for_second = raw_block(log_perm, source, rows_sent[0], True)
    second = permute(for_second, "gx", nx, neighbour_pairs(nx, 1))
    for_first = raw_block(log_perm, source, for_second, False)
    raw = (permute(for_first, "gx", nx, neighbour_pairs(nx, 0)), second)
    far_groups = far_pairs(nx)
    halos, for_far = pack_far(own, got, len(far_groups))
    far = [permute(tiles, "gx", nx, group) for tiles, group in zip(for_far, far_groups)]
    for_first, for_second = pack_near(own, halos, for_far[0], got)
    second = permute(for_second, "gx", nx, neighbour_pairs(nx, 1))
    near = (permute(for_first, "gx", nx, neighbour_pairs(nx, 0)), second)
    pooled, early_sent = landed(for_first, log_perm, source, own, halos, raw, got)
    early = lax.ppermute(early_sent, "gz", [(0, 1), (1, 0)])
    late_sent = late_lanes(early_sent, near, far, lanes, ny > 2)
    late = lax.ppermute(late_sent, "gz", [(0, 1), (1, 0)])
    coefficients = chebyshev_coefficients(low_bound, high_bound, late_sent)
    spread = coarse_level(own, halos, pooled, near, far, early, late, coefficients, peers)
    return fine_level(log_perm, source, got, raw, far, near, early, late, spread, coefficients, peers)


def solution(mesh):
    peers = tuple(mesh.shape[axis] for axis in AXES)
    split = P(("groups", "gx"), "gy", "gz")
    return jax.shard_map(
        functools.partial(shards, peers),
        mesh=mesh,
        in_specs=(split, split, P(), P()),
        out_specs=(split, split),
        check_vma=False,
    )
```

```python
import functools

import jax
import jax.numpy as jnp
from jax import lax
from jax.experimental import pallas as pl
from jax.experimental.pallas import tpu as pltpu
from jax.sharding import PartitionSpec as P

DEGREE = 3
REACH = DEGREE + 1
LANES = 128
SUBLANES = 8
storage_rate = 0.1
AXES = ("gx", "gy", "gz")
VMEM = pl.BlockSpec(memory_space=pltpu.VMEM)
ANY = pl.BlockSpec(memory_space=pl.ANY)
HBM = pl.BlockSpec(memory_space=pltpu.HBM)


AHEAD = pl.CostEstimate(flops=50_000_000_000, bytes_accessed=1_000_000, transcendentals=0)


def iota(shape, dim):
    return lax.broadcasted_iota(jnp.int32, shape, dim)


def turned(value, shift, axis):
    size = value.shape[axis]
    return pltpu.roll(value, shift % size, axis)


def permute(value, axis, peers, pairs):
    cores = lax.axis_size("gz")
    if axis == "gz" or cores % 2:
        return lax.ppermute(value, axis, [pair for i, j in pairs for pair in ((i, j), (j, i))])
    partner = {}
    for i, j in pairs:
        partner[i], partner[j] = j, i
    moves = [
        (i * cores + core, partner[i] * cores + core if i in partner else i * cores + (core ^ 1))
        for i in range(peers)
        for core in range(cores)
    ]
    return lax.ppermute(value, (axis, "gz"), moves)


def neighbour_pairs(peers, start):
    return [(i, i + 1) for i in range(start, peers - 1, 2)]


def first_swap(axis, peers, right, left):
    even = lax.axis_index(axis) % 2 == 0
    return permute(jnp.where(even, right, left), axis, peers, neighbour_pairs(peers, 0))


def second_swap(axis, peers, right, left):
    even = lax.axis_index(axis) % 2 == 0
    return permute(jnp.where(even, left, right), axis, peers, neighbour_pairs(peers, 1))


def swap(axis, peers, right, left):
    got = (first_swap(axis, peers, right, left),)
    return got if peers == 2 else got + (second_swap(axis, peers, right, left),)


def far_pairs(peers):
    pairs = [(i, i + 2) for i in range(peers - 2)]
    groups = [[pair for pair in pairs if pair[0] % 4 < 2], [pair for pair in pairs if pair[0] % 4 >= 2]]
    return [group for group in groups if group]


def from_right(is_first, got):
    return got[0] if len(got) == 1 else jnp.where(is_first, got[0], got[1])


def from_left(is_first, got):
    return got[0] if len(got) == 1 else jnp.where(is_first, got[1], got[0])


def inverse(value):
    guess = pl.reciprocal(value, approx=True)
    return guess * (2.0 - value * guess)


def numerators(shape, dim, own, index, peers, face_scale):
    place = iota(shape, dim)
    right = jnp.where(index < peers - 1, 2.0 * face_scale, 0.0)
    left = jnp.where(index > 0, 2.0 * face_scale, 0.0)
    return jnp.where(
        place == own - 1, right, jnp.where(place == shape[dim] - 1, left, 2.0 * face_scale)
    )


def iterate(count, log_at, source_at, x_faces, y_top, z_top, coef_ref, storage, refs):
    tx_ref, ty_ref, tz_ref, w_ref, d_ref, r_ref, p_ref = refs
    rows, lanes = y_top.shape

    def coefficient(i):
        return jnp.concatenate(
            [jnp.concatenate([coef_ref[i]] * (lanes // LANES), axis=1)] * (rows // SUBLANES), axis=0
        )

    over_theta = coefficient(0)
    after = jnp.exp(-log_at(0))
    tx_before = None
    for k in range(count):
        here = after
        if k + 1 < count:
            after = jnp.exp(-log_at(k + 1))
            tx = x_faces[k] * inverse(here + after)
            tx_ref[k] = tx
        if 1 <= k <= count - 2:
            ty = y_top * inverse(here + turned(here, -1, 0))
            tz = z_top * inverse(here + turned(here, -1, 1))
            diagonal = storage + (tx_before + tx) + (ty + turned(ty, 1, 0)) + (tz + turned(tz, 1, 1))
            w = inverse(diagonal)
            source = source_at(k)
            d_ref[k] = source * (over_theta * w)
            if 2 <= k <= count - 3:
                ty_ref[k] = ty
                tz_ref[k] = tz
                w_ref[k] = w
                r_ref[k] = source
        tx_before = tx
    for step in range(DEGREE):
        first, last = 2 + step, count - 2 - step
        keep, gain = coefficient(1 + 2 * step), coefficient(2 + 2 * step)
        here = d_ref[first]
        fx_before = tx_ref[first - 1] * (d_ref[first - 1] - here)
        for k in range(first, last):
            after = d_ref[k + 1]
            fx = tx_ref[k] * (here - after)
            fy = ty_ref[k] * (here - turned(here, -1, 0))
            fz = tz_ref[k] * (here - turned(here, -1, 1))
            applied = storage * here + (fx - fx_before) + (fy - turned(fy, 1, 0)) + (fz - turned(fz, 1, 1))
            residual = r_ref[k] - applied
            fresh = keep * here + gain * (residual * w_ref[k])
            if REACH <= k < count - REACH:
                so_far = here if step == 0 else p_ref[k]
                p_ref[k] = so_far + fresh
            if step < DEGREE - 1:
                r_ref[k] = residual
                d_ref[k] = fresh
            here, fx_before = after, fx


def coefficients_kernel(low_ref, high_ref, after_ref, coef_ref, bounds_ref, sems):
    copies = [
        pltpu.make_async_copy(ref, bounds_ref.at[i], sems.at[i]) for i, ref in enumerate((low_ref, high_ref))
    ]
    for copy in copies:
        copy.start()
    for copy in copies:
        copy.wait()
    low, high = (jnp.full((SUBLANES, LANES), bounds_ref[i, 0]) for i in range(2))
    theta, delta = (high + low) * 0.5, (high - low) * 0.5
    sigma = theta / delta
    rho = 1.0 / sigma
    coef_ref[0] = 1.0 / theta
    for step in range(DEGREE):
        rho_next = 1.0 / (2.0 * sigma - rho)
        coef_ref[1 + 2 * step] = rho_next * rho
        coef_ref[2 + 2 * step] = 2.0 * rho_next / delta
        rho = rho_next


def chebyshev_coefficients(low_bound, high_bound, after):
    return pl.pallas_call(
        coefficients_kernel,
        out_shape=jax.ShapeDtypeStruct((1 + 2 * DEGREE, SUBLANES, LANES), jnp.float32),
        in_specs=[HBM] * 2 + [ANY],
        out_specs=VMEM,
        scratch_shapes=[pltpu.SMEM((2, 1), jnp.float32), pltpu.SemaphoreType.DMA((2,))],
        compiler_params=pltpu.CompilerParams(vmem_limit_bytes=4 << 20),
        cost_estimate=pl.CostEstimate(flops=1_000_000, bytes_accessed=100_000, transcendentals=0),
        name="coefficients",
    )(low_bound, high_bound, after)


def put(ref, tile, value):
    for i in range(value.shape[1] // LANES):
        ref[(tile + i) * SUBLANES : (tile + i + 1) * SUBLANES, :] = value[:, i * LANES : (i + 1) * LANES]


def take(ref, tile, count):
    tiles = [ref[(tile + i) * SUBLANES : (tile + i + 1) * SUBLANES, :] for i in range(count)]
    return tiles[0] if count == 1 else jnp.concatenate(tiles, axis=1)


def edges(value):
    lanes = value.shape[-1]
    value = value if isinstance(value, jax.Array) else value.at
    return value[:, lanes - LANES :], value[:, :LANES]


def write_lanes(ref, pairs):
    starts = lax.axis_index("gz") == 0
    each = LANES // SUBLANES
    group = iota((SUBLANES, LANES), 1) // SUBLANES
    for base in range(0, len(pairs), each):
        merged = None
        for j, (last, first) in enumerate(pairs[base : base + each]):
            moved = turned(jnp.where(starts, last, first), SUBLANES * j, 1)
            place = jnp.where(starts, (j - 1) % each, j)
            merged = moved if merged is None else jnp.where(group == place, moved, merged)
        row = base // each * SUBLANES
        ref[row : row + SUBLANES, :] = merged


def read_lanes(ref, slot):
    each = LANES // SUBLANES
    row = slot // each * SUBLANES
    return turned(ref[row : row + SUBLANES, :], -SUBLANES * (slot % each), 1)


def early_slots(layers, row_tiles, n_got):
    keys = [("own", a, layer, i) for a in range(2) for layer in range(layers) for i in range(row_tiles)]
    keys += [("got", g, layer) for g in range(n_got) for layer in range(layers)]
    keys += [("pooled", x, a) for x in range(2) for a in range(2)]
    keys += [("halo", i, half) for i in range(n_got) for half in range(2)]
    keys += [
        ("raw", side, slot, i)
        for side in range(2)
        for slot in range(2 * layers - 1)
        for i in range(row_tiles)
    ]
    keys += [("near", side, i) for side in range(2) for i in range(3)]
    return {key: i for i, key in enumerate(keys)}


def near_layout(lanes, wide):
    whole, half = lanes // LANES, lanes // LANES // 2
    if wide:
        parts = [("log1", whole), ("source1", whole), ("log2", whole), ("source2", whole)]
        parts += [(name, half) for name in ("halo0", "halo1", "halo2", "halo3", "source")]
    else:
        parts = [("strip", whole), ("halo", half), ("source", half), ("row", 1)]
    layout, start = {}, 0
    for name, count in parts:
        layout[name] = (start, count)
        start += count
    return layout, start


def late_slots(lanes, wide):
    names = list(near_layout(lanes, wide)[0])
    keys = [(side, name) for side in range(2) for name in names] + [(side, "far") for side in range(2)]
    return {key: i for i, key in enumerate(keys)}


def rows_to_lanes(row_tile, count):
    return jnp.concatenate(
        [jnp.broadcast_to(row_tile[j : j + 1], (SUBLANES, LANES)) for j in range(count)], axis=1
    )


def packed_rows(slots):
    each = LANES // SUBLANES
    return jax.ShapeDtypeStruct((-(-len(slots) // each) * SUBLANES, LANES), jnp.float32)


def window_scratch(count, rows, lanes):
    return [pltpu.VMEM((count, rows, lanes), jnp.float32)] * 7


def exact_dot(value, zero_one):
    parts = []
    for _ in range(3):
        part = value.astype(jnp.bfloat16)
        parts.append(part)
        value = value - part.astype(jnp.float32)
    rows = value.shape[0]
    out = jnp.dot(jnp.concatenate(parts, axis=0), zero_one, preferred_element_type=jnp.float32)
    return (out[2 * rows :] + out[rows : 2 * rows]) + out[:rows]


def row_pairs(top, bottom, sum_ref):
    tiles = top.shape[1] // LANES
    for tile in range(tiles):
        columns = slice(tile * LANES, (tile + 1) * LANES)
        sum_ref[tile, :SUBLANES] = top[:, columns]
        sum_ref[tile, SUBLANES:] = bottom[:, columns]
    return jnp.concatenate(
        [
            sum_ref[tile, pl.ds(0, SUBLANES, stride=2), :] + sum_ref[tile, pl.ds(1, SUBLANES, stride=2), :]
            for tile in range(tiles)
        ],
        axis=1,
    )


def lane_pairs(pieces):
    lanes = pieces[0].shape[1]
    pick = (iota((lanes, lanes // 2), 0) // 2 == iota((lanes, lanes // 2), 1)).astype(jnp.bfloat16)
    pooled = exact_dot(jnp.concatenate(pieces, axis=0), pick)
    return [pooled[SUBLANES * i : SUBLANES * (i + 1)] for i in range(len(pieces))]


def join_halo(near, beyond, starts):
    row = iota(near.shape, 0)
    up, down = turned(beyond, 3, 0), turned(beyond, -3, 0)
    right = jnp.where((row == 3) | (row == 7), up, jnp.where(row == 6, turned(beyond, 5, 0), near))
    left = jnp.where((row == 0) | (row == 4), down, jnp.where(row == 5, up, near))
    return jnp.where(starts, right, left)


def beyond_halo(joined, starts):
    row = iota(joined.shape, 0)
    up, down = turned(joined, 3, 0), turned(joined, -3, 0)
    right = jnp.where(row == 1, turned(joined, -5, 0), down)
    left = jnp.where(row == 2, down, up)
    return jnp.where(starts, right, left)


def join_third(near, third):
    row = iota(near.shape, 0)
    return jnp.where(
        row == 3, turned(third, 3, 0), jnp.where(row == 4, turned(third, -3, 0), near)
    )


def third_halo(joined):
    return jnp.where(iota(joined.shape, 0) < REACH, turned(joined, -3, 0), turned(joined, 3, 0))


def parts(both_ref):
    layers = both_ref.shape[0] // 2
    return both_ref.at[:layers], both_ref.at[layers:]


def prep_kernel(both_ref, pooled_ref, *refs):
    *out_refs, sum_ref = refs
    log_ref, source_ref = parts(both_ref)
    layers, rows, lanes = log_ref.shape
    starts = lax.axis_index("gy") == 0

    def put(slot, left, right):
        if len(out_refs) == 1:
            out_refs[0][slot] = jnp.where(starts, right, left)
        else:
            out_refs[0][slot], out_refs[1][slot] = left, right

    half = lanes // 2
    upper = iota((SUBLANES, lanes), 0) < REACH
    pieces = []
    for x in range(2):
        for ref in (log_ref, source_ref):
            both = ref[2 * x] + ref[2 * x + 1]
            pieces.append(row_pairs(both[:SUBLANES], both[SUBLANES:], sum_ref))
    log0, source0, log1, source1 = lane_pairs(pieces)
    log0, log1 = log0 * 0.125, log1 * 0.125
    pooled_ref[0] = jnp.concatenate([log0, source0], axis=1)
    pooled_ref[1] = jnp.concatenate([log1, source1], axis=1)
    for layer in range(layers):
        put(
            layer,
            jnp.where(upper, log_ref[layer, :SUBLANES], turned(source_ref[layer, :SUBLANES], REACH, 0)),
            jnp.where(upper, turned(source_ref[layer, SUBLANES:], REACH, 0), log_ref[layer, SUBLANES:]),
        )
    pair = iota((SUBLANES, half), 0) // 2

    def four(*tiles):
        merged = jnp.where(
            pair == 0, tiles[0], jnp.where(pair == 1, tiles[1], jnp.where(pair == 2, tiles[2], tiles[3]))
        )
        return jnp.concatenate([merged, merged], axis=1)

    put(
        layers,
        four(turned(log1, -2, 0), log0, turned(source1, 2, 0), turned(source0, 4, 0)),
        four(turned(log0, -4, 0), turned(log1, -2, 0), source0, turned(source1, 2, 0)),
    )


def prep(both, ny):
    layers, rows, lanes = both.shape[0] // 2, *both.shape[1:]
    outs = 1 if ny == 2 else 2

    def tiles(count):
        return jax.ShapeDtypeStruct((count, SUBLANES, lanes), jnp.float32)

    return pl.pallas_call(
        prep_kernel,
        out_shape=(tiles(2),) + (tiles(layers + 1),) * outs,
        in_specs=[VMEM],
        out_specs=(VMEM,) * (1 + outs),
        scratch_shapes=[pltpu.VMEM((lanes // LANES, 2 * SUBLANES, LANES), jnp.float32)],
        compiler_params=pltpu.CompilerParams(vmem_limit_bytes=8 << 20),
        cost_estimate=pl.CostEstimate(flops=5_000_000, bytes_accessed=700_000, transcendentals=0),
        name="prep",
    )(both)


def raw_kernel(to_right_if_odd, both_ref, after_ref, out_ref):
    log_ref, source_ref = parts(both_ref)
    layers = log_ref.shape[0]
    odd = lax.axis_index("gx") % 2
    skip = odd if to_right_if_odd else 1 - odd
    for layer in range(layers):
        out_ref[layer] = log_ref[layer]
    for layer in range(layers - 1):
        out_ref[layers + layer] = source_ref[layer + skip]


def raw_block(both, after, to_right_if_odd):
    layers, rows, lanes = both.shape[0] // 2, *both.shape[1:]
    return pl.pallas_call(
        functools.partial(raw_kernel, to_right_if_odd),
        out_shape=jax.ShapeDtypeStruct((2 * layers - 1, rows, lanes), jnp.float32),
        in_specs=[VMEM, ANY],
        out_specs=VMEM,
        compiler_params=pltpu.CompilerParams(vmem_limit_bytes=8 << 20),
        cost_estimate=pl.CostEstimate(flops=1_000_000, bytes_accessed=500_000, transcendentals=0),
        name="raw_block",
    )(both, after)


def pack_far_kernel(wide, pooled_ref, *refs):
    n_got = 2 if wide else 1
    got_refs, halo_ref, far_refs, sum_ref = refs[:n_got], refs[n_got], refs[n_got + 1 : -1], refs[-1]
    layers, lanes = got_refs[0].shape[0] - 1, got_refs[0].shape[2]
    ix, iy = lax.axis_index("gx"), lax.axis_index("gy")
    even, starts, low = iy % 2 == 0, iy == 0, ix % 4 < 2
    half = lanes // 2
    upper = iota((SUBLANES, lanes), 0) < REACH
    row = iota((SUBLANES, half), 0)

    def got(slot):
        tiles = tuple(ref[slot] for ref in got_refs)
        return from_right(even, tiles), from_left(even, tiles)

    strips = [got(layer) for layer in range(layers)]
    extra = [tile[:, :half] for tile in got(layers)]
    pieces = []
    for side in range(2 if wide else 1):
        both = [strips[2 * x][side] + strips[2 * x + 1][side] for x in range(2)]
        pieces.append(row_pairs(*both, sum_ref))
    fine_rows = lane_pairs(pieces)

    def right_halos(rows, extra):
        rows = jnp.where(row % 4 < 2, rows * 0.125, rows)
        return [
            jnp.where(row < 2, near, jnp.where((row == 4) | (row == 5), far, more))
            for near, far, more in (
                (rows, turned(rows, 2, 0), extra),
                (turned(rows, 4, 0), turned(rows, -2, 0), turned(extra, 2, 0)),
            )
        ]

    def left_halos(rows, extra):
        rows = jnp.where(row % 4 >= 2, rows * 0.125, rows)
        return [
            jnp.where((row == 2) | (row == 3), near, jnp.where(row >= 6, far, more))
            for near, far, more in (
                (rows, turned(rows, -2, 0), extra),
                (turned(rows, 4, 0), turned(rows, 2, 0), turned(extra, -2, 0)),
            )
        ]

    right, left = right_halos(fine_rows[0], extra[0]), left_halos(fine_rows[-1], extra[1])
    if wide:
        top = row < REACH
        halos = [jnp.where(top, right[x], turned(left[x], REACH, 0)) for x in range(2)]
        halos += [jnp.where(top, turned(right[x], REACH, 0), left[x]) for x in range(2)]
    else:
        halos = [jnp.where(starts, right[x], left[x]) for x in range(2)]

    def pair(left, right):
        return jnp.concatenate([left, right], axis=1)

    for i in range(len(halos) // 2):
        halo_ref[i] = pair(halos[2 * i], halos[2 * i + 1])
    logs = [pooled_ref[x, :, :half] for x in range(2)]
    sources = [pooled_ref[x, :, half:] for x in range(2)]

    far = [(logs[inner], logs[1 - inner], sources[inner], halos[inner]) for inner in (1, 0)]
    for group, ref in enumerate(far_refs):
        for i, (right, left) in enumerate(zip(*far)):
            put(ref, i * (half // LANES), jnp.where(low, *((right, left) if group == 0 else (left, right))))
        for spare in range(4 * (half // LANES), ref.shape[0] // SUBLANES):
            put(ref, spare, jnp.zeros((SUBLANES, LANES), jnp.float32))


def pack_far(pooled, got, n_far):
    slots, rows, lanes = got[0].shape
    wide = len(got) == 2
    far_rows = max(2 * lanes // LANES, 0 if wide else near_layout(lanes, wide)[1]) * SUBLANES
    out_shape = (jax.ShapeDtypeStruct((len(got), SUBLANES, lanes), jnp.float32),) + (
        jax.ShapeDtypeStruct((far_rows, LANES), jnp.float32),
    ) * n_far
    halos, *far = pl.pallas_call(
        functools.partial(pack_far_kernel, wide),
        out_shape=out_shape,
        in_specs=[VMEM] * (1 + len(got)),
        out_specs=(VMEM,) * len(out_shape),
        scratch_shapes=[pltpu.VMEM((lanes // LANES, 2 * SUBLANES, LANES), jnp.float32)],
        compiler_params=pltpu.CompilerParams(vmem_limit_bytes=8 << 20),
        cost_estimate=AHEAD,
        name="pack_far",
    )(pooled, *got)
    return halos, far


def pack_near_kernel(wide, pooled_ref, halo_ref, after_ref, *refs):
    *got_refs, first_ref, second_ref = refs
    layers, lanes = got_refs[0].shape[0] - 1, got_refs[0].shape[2]
    ix, iy = lax.axis_index("gx"), lax.axis_index("gy")
    even, starts = iy % 2 == 0, iy == 0
    half = lanes // 2
    upper = iota((SUBLANES, lanes), 0) < REACH

    def got(slot):
        tiles = tuple(ref[slot] for ref in got_refs)
        return from_right(even, tiles), from_left(even, tiles)

    strips = [got(layer) for layer in range(layers)]
    halos = [halo_ref[i // 2, :, (i % 2) * half : (i % 2 + 1) * half] for i in range(4 if wide else 2)]
    sources = [pooled_ref[x, :, half:] for x in range(2)]

    def near_tiles(order):
        near, beyond = order[0] // 2, order[-1] // 2
        if wide:
            log_rows = [jnp.where(upper, *strips[layer]) for layer in range(layers)]
            source_rows = [turned(jnp.where(upper, *strips[layer][::-1]), REACH, 0) for layer in range(layers)]
            return {
                "log1": join_third(log_rows[order[0]], log_rows[order[2]]),
                "source1": source_rows[order[0]],
                "log2": log_rows[order[1]],
                "source2": source_rows[order[1]],
                "halo0": halos[near],
                "halo1": halos[beyond],
                "halo2": halos[2 + near],
                "halo3": halos[2 + beyond],
                "source": sources[beyond],
            }
        first, second, third = (strips[layer][0] for layer in order[:3])
        place = iota((SUBLANES, lanes), 0)
        right = jnp.where(place == 3, turned(third, 3, 0), jnp.where(place >= 6, turned(second, -2, 0), first))
        left = jnp.where(place == 4, turned(third, -3, 0), jnp.where(place < 2, turned(second, 2, 0), first))
        line = jnp.where(starts, second[4:5], second[3:4])
        lines = jnp.zeros((SUBLANES, LANES), jnp.float32)
        for j in range(lanes // LANES):
            lines = jnp.where(iota(lines.shape, 0) == j, line[:, j * LANES : (j + 1) * LANES], lines)
        return {
            "strip": jnp.where(starts, right, left),
            "halo": join_halo(halos[near], halos[beyond], starts),
            "source": sources[beyond],
            "row": lines,
        }

    forward = list(range(layers))
    layout, _ = near_layout(lanes, wide)
    right, left = near_tiles(forward[::-1]), near_tiles(forward)
    for name, (start, _) in layout.items():
        put(first_ref, start, jnp.where(ix % 2 == 0, right[name], left[name]))
        put(second_ref, start, jnp.where(ix % 2 == 0, left[name], right[name]))


def pack_near(pooled, halos, after, got):
    slots, rows, lanes = got[0].shape
    wide = len(got) == 2
    out = jax.ShapeDtypeStruct((near_layout(lanes, wide)[1] * SUBLANES, LANES), jnp.float32)
    return pl.pallas_call(
        functools.partial(pack_near_kernel, wide),
        out_shape=(out, out),
        in_specs=[VMEM, VMEM, ANY] + [VMEM] * len(got),
        out_specs=(VMEM,) * 2,
        compiler_params=pltpu.CompilerParams(vmem_limit_bytes=8 << 20),
        cost_estimate=AHEAD,
        name="pack_near",
    )(pooled, halos, after, *got)


def landed_kernel(after_ref, both_ref, pooled_ref, halo_ref, first_ref, second_ref, *refs):
    *got_refs, out_ref, sent_ref, sum_ref = refs
    log_ref, source_ref = parts(both_ref)
    layers, rows, lanes = log_ref.shape
    half = lanes // 2
    even = lax.axis_index("gx") % 2 == 0
    slots = early_slots(layers, rows // SUBLANES, len(got_refs))
    pairs = {}
    for a, ref in enumerate((log_ref, source_ref)):
        for layer in range(layers):
            for i in range(rows // SUBLANES):
                pairs["own", a, layer, i] = edges(ref.at[layer, i * SUBLANES : (i + 1) * SUBLANES])
    for g, ref in enumerate(got_refs):
        for layer in range(layers):
            pairs["got", g, layer] = edges(ref.at[layer])
    for i in range(2):
        for x in range(2):
            columns = slice(x * half, (x + 1) * half)
            pairs["pooled", i, x] = edges(pooled_ref.at[i, :, columns])
            if i < len(got_refs):
                pairs["halo", i, x] = edges(halo_ref.at[i, :, columns])
    pieces = []
    for side, pick in enumerate((from_left, from_right)):

        def block(slot):
            return pick(even, (first_ref[slot], second_ref[slot]))

        for slot in range(2 * layers - 1):
            for i in range(rows // SUBLANES):
                part = slice(i * SUBLANES, (i + 1) * SUBLANES)
                ends = [edges(ref.at[slot, part]) for ref in (first_ref, second_ref)]
                pairs["raw", side, slot, i] = [
                    pick(even, tuple(end[...] for end in both)) for both in zip(*ends)
                ]
        nearest = layers + 1 if side == 0 else layers
        for top in (0, 2, nearest):
            both = block(top) + block(top + 1)
            pieces.append(row_pairs(both[:SUBLANES], both[SUBLANES:], sum_ref))
    tiles = lane_pairs(pieces)
    for side in range(2):
        for i in range(3):
            tile = tiles[3 * side + i] * (0.125 if i < 2 else 1.0)
            put(out_ref, (3 * side + i) * (half // LANES), tile)
            pairs["near", side, i] = edges(tile)
    write_lanes(sent_ref, [tuple(end[...] for end in pairs[key]) for key in slots])


def landed(after, both, pooled, halos, raw, got):
    layers, rows, lanes = both.shape[0] // 2, *both.shape[1:]
    slots = early_slots(layers, rows // SUBLANES, len(got))
    return pl.pallas_call(
        landed_kernel,
        out_shape=(
            jax.ShapeDtypeStruct((6 * (lanes // 2 // LANES) * SUBLANES, LANES), jnp.float32),
            packed_rows(slots),
        ),
        in_specs=[ANY] + [VMEM] * (5 + len(got)),
        out_specs=(VMEM,) * 2,
        scratch_shapes=[pltpu.VMEM((lanes // LANES, 2 * SUBLANES, LANES), jnp.float32)],
        compiler_params=pltpu.CompilerParams(vmem_limit_bytes=16 << 20),
        cost_estimate=pl.CostEstimate(flops=1_000_000, bytes_accessed=1_000_000, transcendentals=0),
        name="landed",
    )(after, both, pooled, halos, *raw, *got)


def near_part(refs, even, lanes, wide, side, name):
    start, count = near_layout(lanes, wide)[0][name]
    pick = from_left if side == 0 else from_right
    got = pick(even, tuple(take(ref, start, count) for ref in refs))
    return rows_to_lanes(got, lanes // LANES) if name == "row" else got


def far_part(refs, low, lanes, side, i):
    count = lanes // 2 // LANES
    pick = from_left if side == 0 else from_right
    return pick(low, tuple(take(ref, i * count, count) for ref in refs))


def late_kernel(lanes, wide, after_ref, first_ref, second_ref, *refs):
    *far_refs, sent_ref = refs
    even, low = lax.axis_index("gx") % 2 == 0, lax.axis_index("gx") % 4 < 2
    pairs = []
    for side, name in late_slots(lanes, wide):
        if name == "far":
            pairs.append(edges(far_part(far_refs, low, lanes, side, 0)))
        else:
            pairs.append(edges(near_part((first_ref, second_ref), even, lanes, wide, side, name)))
    write_lanes(sent_ref, pairs)


def late_lanes(after, near, far, lanes, wide):
    return pl.pallas_call(
        functools.partial(late_kernel, lanes, wide),
        out_shape=packed_rows(late_slots(lanes, wide)),
        in_specs=[ANY] + [VMEM] * (2 + len(far)),
        out_specs=VMEM,
        compiler_params=pltpu.CompilerParams(vmem_limit_bytes=8 << 20),
        cost_estimate=pl.CostEstimate(flops=1_000_000, bytes_accessed=200_000, transcendentals=0),
        name="late_lanes",
    )(after, *near, *far)


def coarse_kernel(peers, n_far, own_ref, halo_ref, pool_ref, first_ref, second_ref, *refs):
    near_refs, far_refs = (first_ref, second_ref), refs[:n_far]
    early_ref, late_ref, coef_ref, out_ref, wide_ref, *scratch = refs[n_far:]
    ix, iy, iz = (lax.axis_index(axis) for axis in AXES)
    nx, ny, nz = peers
    wide = ny > 2
    fine_lanes = own_ref.shape[2]
    lanes, rows = fine_lanes // 2, SUBLANES
    even, low, starts = ix % 2 == 0, ix % 4 < 2, iy == 0
    top = iota((rows, lanes + LANES), 0) < REACH
    early = early_slots(REACH, 2, 2 if wide else 1)
    late = late_slots(fine_lanes, wide)

    def columns(half):
        return slice(half * lanes, (half + 1) * lanes)

    def with_early(core, *key):
        return jnp.concatenate([core, read_lanes(early_ref, early[key])], axis=1)

    def near(side, name):
        core = near_part(near_refs, even, fine_lanes, wide, side, name)
        return jnp.concatenate([core, read_lanes(late_ref, late[side, name])], axis=1)

    def far(side, i):
        core = far_part(far_refs, low, fine_lanes, side, i)
        return jnp.concatenate([core, read_lanes(late_ref, late[side, "far"])], axis=1)

    def split(tile, a):
        other = turned(tile, REACH, 0)
        return jnp.where(top, tile, other) if a == 0 else jnp.where(top, other, tile)

    def window(a, k):
        block, layer = k // 2 - 2, k % 2
        nearest = layer == (1 if block < 0 else 0)
        side = 0 if block < 0 else 1
        if abs(block) == 2:
            if a == 1:
                core = far(side, 2)
                return jnp.concatenate([core, jnp.zeros_like(core)], axis=0)
            halo = far(side, 3)
            halo = halo if wide else split(halo, 0)
            return jnp.concatenate([far(side, 0 if nearest else 1), halo], axis=0)
        if block == 0:
            core = with_early(own_ref[layer, :, columns(a)], "pooled", layer, a)
            if wide:
                halo = with_early(halo_ref[a, :, columns(layer)], "halo", a, layer)
            else:
                halo = split(with_early(halo_ref[0, :, columns(layer)], "halo", 0, layer), a)
            return jnp.concatenate([core, halo], axis=0)
        if a == 0 or nearest:
            i = layer if a == 0 else 2
            core = take(pool_ref, (3 * side + i) * (lanes // LANES), lanes // LANES)
            core = with_early(core, "near", side, i)
        else:
            core = near(side, "source")
        if wide:
            halo = near(side, f"halo{2 * a + (0 if nearest else 1)}")
        else:
            joined = near(side, "halo")
            halo = split(joined if nearest else beyond_halo(joined, starts), a)
        return jnp.concatenate([core, halo], axis=0)

    def open_face(inside):
        return jnp.where(inside, 4.0, 0.0)

    faces = [4.0] * 9
    faces[1], faces[3] = open_face(ix > 1), open_face(ix > 0)
    faces[5], faces[7] = open_face(ix < nx - 1), open_face(ix < nx - 2)
    shape = (2 * rows, lanes + LANES)
    iterate(
        2 + 2 * REACH,
        functools.partial(window, 0),
        functools.partial(window, 1),
        faces,
        numerators(shape, 0, rows, iy, ny, 2.0),
        numerators(shape, 1, lanes, iz, nz, 2.0),
        coef_ref,
        8.0 * storage_rate,
        scratch,
    )
    p_ref = scratch[-1]
    widen = (iota((lanes, 2 * lanes), 0) == iota((lanes, 2 * lanes), 1) // 2).astype(jnp.bfloat16)
    pressure = jnp.concatenate([p_ref[REACH + x, :rows, :lanes] for x in range(2)], axis=0)
    spread = exact_dot(pressure, widen)
    for x in range(2):
        for tile in range(2 * lanes // LANES):
            part = slice(tile * LANES, (tile + 1) * LANES)
            for half in range(2):
                wide_ref[tile, pl.ds(half, rows, stride=2), :] = spread[x * rows : (x + 1) * rows, part]
            for twin in range(2):
                out_ref[2 * x + twin, :, part] = wide_ref[tile]


def coarse_level(own, halos, pooled, near, far, early, late, coefficients, peers):
    lanes = own.shape[2] // 2
    window = (2 + 2 * REACH, 2 * SUBLANES, lanes + LANES)
    return pl.pallas_call(
        functools.partial(coarse_kernel, peers, len(far)),
        out_shape=jax.ShapeDtypeStruct((REACH, 2 * SUBLANES, 2 * lanes), jnp.float32),
        in_specs=[VMEM] * (8 + len(far)),
        out_specs=VMEM,
        scratch_shapes=[pltpu.VMEM((2 * lanes // LANES, 2 * SUBLANES, LANES), jnp.float32)]
        + window_scratch(*window),
        compiler_params=pltpu.CompilerParams(vmem_limit_bytes=24 << 20),
        cost_estimate=pl.CostEstimate(flops=20_000_000, bytes_accessed=4_000_000, transcendentals=0),
        name="coarse_level",
    )(own, halos, pooled, *near, *far, early, late, coefficients)


def fine_kernel(peers, n_far, both_ref, *refs):
    log_ref, source_ref = parts(both_ref)
    layers, rows, lanes = log_ref.shape
    ix, iy, iz = (lax.axis_index(axis) for axis in AXES)
    nx, ny, nz = peers
    wide = ny > 2
    n_got = 2 if wide else 1
    got_refs, refs = refs[:n_got], refs[n_got:]
    second_ref, first_ref = refs[:2]
    second_near_ref, first_near_ref, early_ref, late_ref, spread_ref = refs[2 + n_far : 7 + n_far]
    coef_ref, fine_ref, diff_ref, *scratch = refs[7 + n_far :]
    even, starts = ix % 2 == 0, iy == 0
    count = 3 * layers
    upper = iota((SUBLANES, lanes + LANES), 0) < REACH
    early = early_slots(layers, rows // SUBLANES, n_got)
    late = late_slots(lanes, wide)

    def with_early(core, *keys):
        tile = jnp.concatenate([read_lanes(early_ref, early[key]) for key in keys], axis=0)
        return jnp.concatenate([core, tile], axis=1)

    def near(side, name):
        core = near_part((first_near_ref, second_near_ref), even, lanes, wide, side, name)
        return jnp.concatenate([core, read_lanes(late_ref, late[side, name])], axis=1)

    def near_halo(a, side, distance):
        if wide:
            tile = near(side, ("log" if a == 0 else "source") + ("2" if distance == 2 else "1"))
        elif a == 1:
            return near(side, "row") if distance == 2 else turned(near(side, "strip"), REACH, 0)
        else:
            tile = near(side, "strip")
            if distance == 2:
                return jnp.where(starts, turned(tile, 2, 0), turned(tile, -2, 0))
        return third_halo(tile) if a == 0 and distance > 2 else tile

    def window(a, k):
        block, layer = k // layers - 1, k % layers
        if block == 0:
            core = (log_ref, source_ref)[a][layer]
            core = with_early(core, *(("own", a, layer, i) for i in range(rows // SUBLANES)))
            tiles = tuple(with_early(ref[layer], ("got", g, layer)) for g, ref in enumerate(got_refs))
            halo = tiles[0]
            if wide:
                sides = from_right(iy % 2 == 0, tiles), from_left(iy % 2 == 0, tiles)
                halo = jnp.where(upper, *(sides if a == 0 else sides[::-1]))
            if a == 1:
                halo = turned(halo, REACH, 0)
            return jnp.concatenate([core, halo], axis=0)
        side, pick = (0, from_left) if block < 0 else (1, from_right)
        slot = layer if a == 0 else layers + layer - (1 if block < 0 else 0)
        core = pick(even, (first_ref[slot], second_ref[slot]))
        core = with_early(core, *(("raw", side, slot, i) for i in range(rows // SUBLANES)))
        halo = near_halo(a, side, layers - layer if block < 0 else layer + 1)
        return jnp.concatenate([core, halo], axis=0)

    faces = [2.0] * (count - 1)
    faces[layers - 1] = jnp.where(ix > 0, 2.0, 0.0)
    faces[2 * layers - 1] = jnp.where(ix < nx - 1, 2.0, 0.0)
    shape = (rows + 2 * REACH, lanes + LANES)
    iterate(
        count,
        functools.partial(window, 0),
        functools.partial(window, 1),
        faces,
        numerators(shape, 0, rows, iy, ny, 1.0),
        numerators(shape, 1, lanes, iz, nz, 1.0),
        coef_ref,
        storage_rate,
        scratch,
    )
    p_ref = scratch[-1]
    for x in range(layers):
        fine = p_ref[REACH + x, :rows, :lanes]
        fine_ref[x] = fine
        diff_ref[x] = fine - spread_ref[x]


def fine_level(both, got, raw, far, near, early, late, spread, coefficients, peers):
    layers, rows, lanes = spread.shape
    window = (layers + 2 * REACH, rows + 2 * REACH, lanes + LANES)
    out = jax.ShapeDtypeStruct(spread.shape, jnp.float32)
    return pl.pallas_call(
        functools.partial(fine_kernel, peers, len(far)),
        out_shape=(out, out),
        in_specs=[VMEM] * (3 + len(got)) + [ANY] * len(far) + [VMEM] * 6,
        out_specs=(VMEM, VMEM),
        scratch_shapes=window_scratch(*window),
        compiler_params=pltpu.CompilerParams(vmem_limit_bytes=24 << 20),
        cost_estimate=pl.CostEstimate(flops=20_000_000, bytes_accessed=10_000_000, transcendentals=0),
        name="fine_level",
    )(both, *got, *raw[::-1], *far, *near[::-1], early, late, spread, coefficients)


def shards(peers, log_perm, source, low_bound, high_bound):
    nx, ny, nz = peers
    layers, rows, lanes = log_perm.shape
    assert layers == REACH and rows == 2 * SUBLANES and nx > 2 and nz == 2
    both = jnp.concatenate([log_perm, source])
    own, *rows_sent = prep(both, ny)
    if ny == 2:
        got = (permute(rows_sent[0], "gy", ny, [(0, 1)]),)
    else:
        got = swap("gy", ny, rows_sent[1], rows_sent[0])
    for_second = raw_block(both, rows_sent[0], True)
    second = permute(for_second, "gx", nx, neighbour_pairs(nx, 1))
    for_first = raw_block(both, for_second, False)
    raw = (permute(for_first, "gx", nx, neighbour_pairs(nx, 0)), second)
    far_groups = far_pairs(nx)
    halos, for_far = pack_far(own, got, len(far_groups))
    far = [permute(tiles, "gx", nx, group) for tiles, group in zip(for_far, far_groups)]
    for_first, for_second = pack_near(own, halos, for_far[0], got)
    second = permute(for_second, "gx", nx, neighbour_pairs(nx, 1))
    near = (permute(for_first, "gx", nx, neighbour_pairs(nx, 0)), second)
    coefficients = chebyshev_coefficients(low_bound, high_bound, for_first)
    pooled, early_sent = landed(coefficients, both, own, halos, raw, got)
    early = lax.ppermute(early_sent, "gz", [(0, 1), (1, 0)])
    late_sent = late_lanes(early_sent, near, far, lanes, ny > 2)
    late = lax.ppermute(late_sent, "gz", [(0, 1), (1, 0)])
    spread = coarse_level(own, halos, pooled, near, far, early, late, coefficients, peers)
    return fine_level(both, got, raw, far, near, early, late, spread, coefficients, peers)


def solution(mesh):
    peers = tuple(mesh.shape[axis] for axis in AXES)
    split = P(("groups", "gx"), "gy", "gz")
    return jax.shard_map(
        functools.partial(shards, peers),
        mesh=mesh,
        in_specs=(split, split, P(), P()),
        out_specs=(split, split),
        check_vma=False,
    )
```

```python
import functools

import jax
import jax.numpy as jnp
from jax import lax
from jax.experimental import pallas as pl
from jax.experimental.pallas import tpu as pltpu
from jax.sharding import PartitionSpec as P

DEGREE = 3
REACH = DEGREE + 1
LANES = 128
SUBLANES = 8
storage_rate = 0.1
AXES = ("gx", "gy", "gz")
VMEM = pl.BlockSpec(memory_space=pltpu.VMEM)
ANY = pl.BlockSpec(memory_space=pl.ANY)
HBM = pl.BlockSpec(memory_space=pltpu.HBM)


AHEAD = pl.CostEstimate(flops=50_000_000_000, bytes_accessed=1_000_000, transcendentals=0)


def iota(shape, dim):
    return lax.broadcasted_iota(jnp.int32, shape, dim)


def turned(value, shift, axis):
    size = value.shape[axis]
    return pltpu.roll(value, shift % size, axis)


def permute(value, axis, peers, pairs):
    cores = lax.axis_size("gz")
    if axis == "gz" or cores % 2:
        return lax.ppermute(value, axis, [pair for i, j in pairs for pair in ((i, j), (j, i))])
    partner = {}
    for i, j in pairs:
        partner[i], partner[j] = j, i
    moves = [
        (i * cores + core, partner[i] * cores + core if i in partner else i * cores + (core ^ 1))
        for i in range(peers)
        for core in range(cores)
    ]
    return lax.ppermute(value, (axis, "gz"), moves)


def neighbour_pairs(peers, start):
    return [(i, i + 1) for i in range(start, peers - 1, 2)]


def first_swap(axis, peers, right, left):
    even = lax.axis_index(axis) % 2 == 0
    return permute(jnp.where(even, right, left), axis, peers, neighbour_pairs(peers, 0))


def second_swap(axis, peers, right, left):
    even = lax.axis_index(axis) % 2 == 0
    return permute(jnp.where(even, left, right), axis, peers, neighbour_pairs(peers, 1))


def swap(axis, peers, right, left):
    got = (first_swap(axis, peers, right, left),)
    return got if peers == 2 else got + (second_swap(axis, peers, right, left),)


def far_pairs(peers):
    pairs = [(i, i + 2) for i in range(peers - 2)]
    groups = [[pair for pair in pairs if pair[0] % 4 < 2], [pair for pair in pairs if pair[0] % 4 >= 2]]
    return [group for group in groups if group]


def from_right(is_first, got):
    return got[0] if len(got) == 1 else jnp.where(is_first, got[0], got[1])


def from_left(is_first, got):
    return got[0] if len(got) == 1 else jnp.where(is_first, got[1], got[0])


def inverse(value):
    guess = pl.reciprocal(value, approx=True)
    return guess * (2.0 - value * guess)


def row_numerators(rows, own, index, peers, face_scale):
    place = iota((rows, LANES), 0)
    right = jnp.where(index < peers - 1, 2.0 * face_scale, 0.0)
    left = jnp.where(index > 0, 2.0 * face_scale, 0.0)
    return jnp.where(place == own - 1, right, jnp.where(place == rows - 1, left, 2.0 * face_scale))


def lane_numerators(rows, index, peers, face_scale):
    place = iota((rows, LANES), 1)
    right = jnp.where(index < peers - 1, 2.0 * face_scale, 0.0)
    left = jnp.where(index > 0, 2.0 * face_scale, 0.0)
    return [jnp.where(place == LANES - 1, side, 2.0 * face_scale) for side in (right, left)]


def lane_tiles(value):
    return [value[:, i : i + LANES] for i in range(0, value.shape[1], LANES)]


def beside(tiles, shift):
    moved = [turned(tile, shift, 1) for tile in tiles]
    lane = iota(tiles[0].shape, 1)
    seam = LANES - 1 if shift < 0 else 0
    return [
        jnp.where(lane == seam, moved[(j - shift) % len(tiles)], moved[j]) for j in range(len(tiles))
    ]


def store_rows(ref, k, j, value):
    rows = value.shape[0]
    ref[k, j, SUBLANES : SUBLANES + rows] = value
    ref[k, j, SUBLANES - 1 : SUBLANES] = value[rows - 1 :]
    ref[k, j, SUBLANES + rows : SUBLANES + rows + 1] = value[:1]


def iterate(count, own_rows, rows, tiles, log_at, source_at, x_faces, y_top, z_top, coef_ref, storage, emit, refs):
    k_ref, tx_ref, ty_ref, tzr_ref, tzl_ref, diag_ref, w_ref, d_ref, r_ref, p_ref = refs
    own_tiles = tiles - 1

    def away(k):
        return max(0, REACH - k, k - (count - 1 - REACH))

    def extent(k, step):
        left = DEGREE - step - away(k)
        return None if left < 0 else (own_rows, own_tiles) if left == 0 else (rows, tiles)

    def coefficient(i, size):
        return jnp.concatenate([coef_ref[i]] * (size // SUBLANES), axis=0)

    z_tops = [z_top[0] if j == own_tiles - 1 else z_top[1] if j == own_tiles else None for j in range(tiles)]

    def resistance(k):
        return [jnp.exp(-tile) for tile in lane_tiles(log_at(k))]

    after = resistance(0)
    tx_before = None
    for k in range(count):
        here = after
        if k + 1 < count:
            after = resistance(k + 1)
            outer = max(away(k), away(k + 1))
            size, number = (rows, tiles) if outer < REACH else (own_rows, own_tiles)
            tx = [x_faces[k] * inverse(here[j][:size] + after[j][:size]) for j in range(number)]
            for j in range(number):
                tx_ref[k, j, :size] = tx[j]
        if away(k) <= DEGREE:
            size, number = extent(k, 0)
            right = beside(here, -1)
            tz = []
            for j in range(tiles):
                scale = z_tops[j][:size] if z_tops[j] is not None else z_top[2]
                tz.append(scale * inverse(here[j][:size] + right[j][:size]))
            tz_left = beside(tz, 1)
            source = lane_tiles(source_at(k))
            for j in range(number):
                store_rows(k_ref, k, j, here[j])
                ty = y_top * inverse(here[j] + k_ref[k, j, SUBLANES + 1 : SUBLANES + 1 + rows])
                store_rows(ty_ref, k, j, ty)
                ty_before = ty_ref[k, j, SUBLANES - 1 : SUBLANES - 1 + size]
                diagonal = storage + (tx_before[j][:size] + tx[j][:size])
                diagonal = diagonal + (ty[:size] + ty_before) + (tz[j] + tz_left[j])
                w = inverse(diagonal)
                direction = source[j][:size] * (coefficient(0, size) * w)
                if (size, number) == (rows, tiles):
                    store_rows(d_ref.at[0], k, j, direction)
                else:
                    d_ref[0, k, j, SUBLANES : SUBLANES + size] = direction
                if extent(k, 1) is not None:
                    tzr_ref[k, j, :size] = tz[j]
                    tzl_ref[k, j, :size] = tz_left[j]
                    diag_ref[k, j, :size] = diagonal
                    w_ref[k, j, :size] = w
                    r_ref[k, j, :size] = source[j][:size]
        tx_before = tx
    for step in range(1, DEGREE + 1):
        old, new = d_ref.at[(step - 1) % 2], d_ref.at[step % 2]
        for k in range(count):
            if extent(k, step) is None:
                continue
            size, number = extent(k, step)
            middle = slice(SUBLANES, SUBLANES + size)
            keep, gain = coefficient(2 * step - 1, size), coefficient(2 * step, size)
            here = [old[k, j, middle] for j in range(tiles)]
            right, left = beside(here, -1), beside(here, 1)
            for j in range(number):
                applied = tx_ref[k, j, :size] * old[k + 1, j, middle] + tx_ref[k - 1, j, :size] * old[k - 1, j, middle]
                applied += (
                    ty_ref[k, j, middle] * old[k, j, SUBLANES + 1 : SUBLANES + 1 + size]
                    + ty_ref[k, j, SUBLANES - 1 : SUBLANES - 1 + size] * old[k, j, SUBLANES - 1 : SUBLANES - 1 + size]
                )
                applied += tzr_ref[k, j, :size] * right[j] + tzl_ref[k, j, :size] * left[j]
                residual = r_ref[k, j, :size] - (diag_ref[k, j, :size] * here[j] - applied)
                fresh = keep * here[j] + gain * (residual * w_ref[k, j, :size])
                if away(k) == 0 and j < own_tiles:
                    so_far = here[j][:own_rows] if step == 1 else p_ref[k, j]
                    total = so_far + fresh[:own_rows]
                    if step == DEGREE:
                        emit(k - REACH, j, total)
                    else:
                        p_ref[k, j] = total
                if step < DEGREE:
                    r_ref[k, j, :size] = residual
                    if (size, number) == (rows, tiles):
                        store_rows(new, k, j, fresh)
                    else:
                        new[k, j, middle] = fresh


def coefficients_kernel(low_ref, high_ref, after_ref, coef_ref, bounds_ref, sems):
    copies = [
        pltpu.make_async_copy(ref, bounds_ref.at[i], sems.at[i]) for i, ref in enumerate((low_ref, high_ref))
    ]
    for copy in copies:
        copy.start()
    for copy in copies:
        copy.wait()
    low, high = (jnp.full((SUBLANES, LANES), bounds_ref[i, 0]) for i in range(2))
    theta, delta = (high + low) * 0.5, (high - low) * 0.5
    sigma = theta / delta
    rho = 1.0 / sigma
    coef_ref[0] = 1.0 / theta
    for step in range(DEGREE):
        rho_next = 1.0 / (2.0 * sigma - rho)
        coef_ref[1 + 2 * step] = rho_next * rho
        coef_ref[2 + 2 * step] = 2.0 * rho_next / delta
        rho = rho_next


def chebyshev_coefficients(low_bound, high_bound, after):
    return pl.pallas_call(
        coefficients_kernel,
        out_shape=jax.ShapeDtypeStruct((1 + 2 * DEGREE, SUBLANES, LANES), jnp.float32),
        in_specs=[HBM] * 2 + [ANY],
        out_specs=VMEM,
        scratch_shapes=[pltpu.SMEM((2, 1), jnp.float32), pltpu.SemaphoreType.DMA((2,))],
        compiler_params=pltpu.CompilerParams(vmem_limit_bytes=4 << 20),
        cost_estimate=pl.CostEstimate(flops=1_000_000, bytes_accessed=100_000, transcendentals=0),
        name="coefficients",
    )(low_bound, high_bound, after)


def put(ref, tile, value):
    for i in range(value.shape[1] // LANES):
        ref[(tile + i) * SUBLANES : (tile + i + 1) * SUBLANES, :] = value[:, i * LANES : (i + 1) * LANES]


def take(ref, tile, count):
    tiles = [ref[(tile + i) * SUBLANES : (tile + i + 1) * SUBLANES, :] for i in range(count)]
    return tiles[0] if count == 1 else jnp.concatenate(tiles, axis=1)


def edges(value):
    lanes = value.shape[-1]
    value = value if isinstance(value, jax.Array) else value.at
    return value[:, lanes - LANES :], value[:, :LANES]


def write_lanes(ref, pairs):
    starts = lax.axis_index("gz") == 0
    each = LANES // SUBLANES
    group = iota((SUBLANES, LANES), 1) // SUBLANES
    for base in range(0, len(pairs), each):
        merged = None
        for j, (last, first) in enumerate(pairs[base : base + each]):
            moved = turned(jnp.where(starts, last, first), SUBLANES * j, 1)
            place = jnp.where(starts, (j - 1) % each, j)
            merged = moved if merged is None else jnp.where(group == place, moved, merged)
        row = base // each * SUBLANES
        ref[row : row + SUBLANES, :] = merged


def read_lanes(ref, slot):
    each = LANES // SUBLANES
    row = slot // each * SUBLANES
    return turned(ref[row : row + SUBLANES, :], -SUBLANES * (slot % each), 1)


def early_slots(layers, row_tiles, n_got):
    keys = [("own", a, layer, i) for a in range(2) for layer in range(layers) for i in range(row_tiles)]
    keys += [("got", g, layer) for g in range(n_got) for layer in range(layers)]
    keys += [("pooled", x, a) for x in range(2) for a in range(2)]
    keys += [("halo", i, half) for i in range(n_got) for half in range(2)]
    keys += [
        ("raw", side, slot, i)
        for side in range(2)
        for slot in range(2 * layers - 1)
        for i in range(row_tiles)
    ]
    keys += [("near", side, i) for side in range(2) for i in range(3)]
    return {key: i for i, key in enumerate(keys)}


def near_layout(lanes, wide):
    whole, half = lanes // LANES, lanes // LANES // 2
    if wide:
        parts = [("log1", whole), ("source1", whole), ("log2", whole), ("source2", whole)]
        parts += [(name, half) for name in ("halo0", "halo1", "halo2", "halo3", "source")]
    else:
        parts = [("strip", whole), ("halo", half), ("source", half), ("row", 1)]
    layout, start = {}, 0
    for name, count in parts:
        layout[name] = (start, count)
        start += count
    return layout, start


def late_slots(lanes, wide):
    names = list(near_layout(lanes, wide)[0])
    keys = [(side, name) for side in range(2) for name in names] + [(side, "far") for side in range(2)]
    return {key: i for i, key in enumerate(keys)}


def rows_to_lanes(row_tile, count):
    return jnp.concatenate(
        [jnp.broadcast_to(row_tile[j : j + 1], (SUBLANES, LANES)) for j in range(count)], axis=1
    )


def packed_rows(slots):
    each = LANES // SUBLANES
    return jax.ShapeDtypeStruct((-(-len(slots) // each) * SUBLANES, LANES), jnp.float32)


def window_scratch(count, own_rows, rows, tiles):
    plain = pltpu.VMEM((count, tiles, rows, LANES), jnp.float32)
    margins = pltpu.VMEM((count, tiles, rows + 2 * SUBLANES, LANES), jnp.float32)
    pair = pltpu.VMEM((2, count, tiles, rows + 2 * SUBLANES, LANES), jnp.float32)
    total = pltpu.VMEM((count, tiles, own_rows, LANES), jnp.float32)
    return [margins, plain, margins, plain, plain, plain, plain, pair, plain, total]


def exact_dot(value, zero_one):
    parts = []
    for _ in range(3):
        part = value.astype(jnp.bfloat16)
        parts.append(part)
        value = value - part.astype(jnp.float32)
    rows = value.shape[0]
    out = jnp.dot(jnp.concatenate(parts, axis=0), zero_one, preferred_element_type=jnp.float32)
    return (out[2 * rows :] + out[rows : 2 * rows]) + out[:rows]


def row_pairs(top, bottom, sum_ref):
    tiles = top.shape[1] // LANES
    for tile in range(tiles):
        columns = slice(tile * LANES, (tile + 1) * LANES)
        sum_ref[tile, :SUBLANES] = top[:, columns]
        sum_ref[tile, SUBLANES:] = bottom[:, columns]
    return jnp.concatenate(
        [
            sum_ref[tile, pl.ds(0, SUBLANES, stride=2), :] + sum_ref[tile, pl.ds(1, SUBLANES, stride=2), :]
            for tile in range(tiles)
        ],
        axis=1,
    )


def lane_pairs(pieces):
    lanes = pieces[0].shape[1]
    pick = (iota((lanes, lanes // 2), 0) // 2 == iota((lanes, lanes // 2), 1)).astype(jnp.bfloat16)
    pooled = exact_dot(jnp.concatenate(pieces, axis=0), pick)
    return [pooled[SUBLANES * i : SUBLANES * (i + 1)] for i in range(len(pieces))]


def join_halo(near, beyond, starts):
    row = iota(near.shape, 0)
    up, down = turned(beyond, 3, 0), turned(beyond, -3, 0)
    right = jnp.where((row == 3) | (row == 7), up, jnp.where(row == 6, turned(beyond, 5, 0), near))
    left = jnp.where((row == 0) | (row == 4), down, jnp.where(row == 5, up, near))
    return jnp.where(starts, right, left)


def beyond_halo(joined, starts):
    row = iota(joined.shape, 0)
    up, down = turned(joined, 3, 0), turned(joined, -3, 0)
    right = jnp.where(row == 1, turned(joined, -5, 0), down)
    left = jnp.where(row == 2, down, up)
    return jnp.where(starts, right, left)


def join_third(near, third):
    row = iota(near.shape, 0)
    return jnp.where(
        row == 3, turned(third, 3, 0), jnp.where(row == 4, turned(third, -3, 0), near)
    )


def third_halo(joined):
    return jnp.where(iota(joined.shape, 0) < REACH, turned(joined, -3, 0), turned(joined, 3, 0))


def parts(both_ref):
    layers = both_ref.shape[0] // 2
    return both_ref.at[:layers], both_ref.at[layers:]


def prep_kernel(both_ref, pooled_ref, *refs):
    *out_refs, sum_ref = refs
    log_ref, source_ref = parts(both_ref)
    layers, rows, lanes = log_ref.shape
    starts = lax.axis_index("gy") == 0

    def put(slot, left, right):
        if len(out_refs) == 1:
            out_refs[0][slot] = jnp.where(starts, right, left)
        else:
            out_refs[0][slot], out_refs[1][slot] = left, right

    half = lanes // 2
    upper = iota((SUBLANES, lanes), 0) < REACH
    pieces = []
    for x in range(2):
        for ref in (log_ref, source_ref):
            both = ref[2 * x] + ref[2 * x + 1]
            pieces.append(row_pairs(both[:SUBLANES], both[SUBLANES:], sum_ref))
    log0, source0, log1, source1 = lane_pairs(pieces)
    log0, log1 = log0 * 0.125, log1 * 0.125
    pooled_ref[0] = jnp.concatenate([log0, source0], axis=1)
    pooled_ref[1] = jnp.concatenate([log1, source1], axis=1)
    for layer in range(layers):
        put(
            layer,
            jnp.where(upper, log_ref[layer, :SUBLANES], turned(source_ref[layer, :SUBLANES], REACH, 0)),
            jnp.where(upper, turned(source_ref[layer, SUBLANES:], REACH, 0), log_ref[layer, SUBLANES:]),
        )
    pair = iota((SUBLANES, half), 0) // 2

    def four(*tiles):
        merged = jnp.where(
            pair == 0, tiles[0], jnp.where(pair == 1, tiles[1], jnp.where(pair == 2, tiles[2], tiles[3]))
        )
        return jnp.concatenate([merged, merged], axis=1)

    put(
        layers,
        four(turned(log1, -2, 0), log0, turned(source1, 2, 0), turned(source0, 4, 0)),
        four(turned(log0, -4, 0), turned(log1, -2, 0), source0, turned(source1, 2, 0)),
    )


def prep(both, ny):
    layers, rows, lanes = both.shape[0] // 2, *both.shape[1:]
    outs = 1 if ny == 2 else 2

    def tiles(count):
        return jax.ShapeDtypeStruct((count, SUBLANES, lanes), jnp.float32)

    return pl.pallas_call(
        prep_kernel,
        out_shape=(tiles(2),) + (tiles(layers + 1),) * outs,
        in_specs=[VMEM],
        out_specs=(VMEM,) * (1 + outs),
        scratch_shapes=[pltpu.VMEM((lanes // LANES, 2 * SUBLANES, LANES), jnp.float32)],
        compiler_params=pltpu.CompilerParams(vmem_limit_bytes=8 << 20),
        cost_estimate=pl.CostEstimate(flops=5_000_000, bytes_accessed=700_000, transcendentals=0),
        name="prep",
    )(both)


def raw_kernel(to_right_if_odd, both_ref, after_ref, out_ref):
    log_ref, source_ref = parts(both_ref)
    layers = log_ref.shape[0]
    odd = lax.axis_index("gx") % 2
    skip = odd if to_right_if_odd else 1 - odd
    for layer in range(layers):
        out_ref[layer] = log_ref[layer]
    for layer in range(layers - 1):
        out_ref[layers + layer] = source_ref[layer + skip]


def raw_block(both, after, to_right_if_odd):
    layers, rows, lanes = both.shape[0] // 2, *both.shape[1:]
    return pl.pallas_call(
        functools.partial(raw_kernel, to_right_if_odd),
        out_shape=jax.ShapeDtypeStruct((2 * layers - 1, rows, lanes), jnp.float32),
        in_specs=[VMEM, ANY],
        out_specs=VMEM,
        compiler_params=pltpu.CompilerParams(vmem_limit_bytes=8 << 20),
        cost_estimate=pl.CostEstimate(flops=1_000_000, bytes_accessed=500_000, transcendentals=0),
        name="raw_block",
    )(both, after)


def pack_far_kernel(wide, pooled_ref, *refs):
    n_got = 2 if wide else 1
    got_refs, halo_ref, far_refs, sum_ref = refs[:n_got], refs[n_got], refs[n_got + 1 : -1], refs[-1]
    layers, lanes = got_refs[0].shape[0] - 1, got_refs[0].shape[2]
    ix, iy = lax.axis_index("gx"), lax.axis_index("gy")
    even, starts, low = iy % 2 == 0, iy == 0, ix % 4 < 2
    half = lanes // 2
    upper = iota((SUBLANES, lanes), 0) < REACH
    row = iota((SUBLANES, half), 0)

    def got(slot):
        tiles = tuple(ref[slot] for ref in got_refs)
        return from_right(even, tiles), from_left(even, tiles)

    strips = [got(layer) for layer in range(layers)]
    extra = [tile[:, :half] for tile in got(layers)]
    pieces = []
    for side in range(2 if wide else 1):
        both = [strips[2 * x][side] + strips[2 * x + 1][side] for x in range(2)]
        pieces.append(row_pairs(*both, sum_ref))
    fine_rows = lane_pairs(pieces)

    def right_halos(rows, extra):
        rows = jnp.where(row % 4 < 2, rows * 0.125, rows)
        return [
            jnp.where(row < 2, near, jnp.where((row == 4) | (row == 5), far, more))
            for near, far, more in (
                (rows, turned(rows, 2, 0), extra),
                (turned(rows, 4, 0), turned(rows, -2, 0), turned(extra, 2, 0)),
            )
        ]

    def left_halos(rows, extra):
        rows = jnp.where(row % 4 >= 2, rows * 0.125, rows)
        return [
            jnp.where((row == 2) | (row == 3), near, jnp.where(row >= 6, far, more))
            for near, far, more in (
                (rows, turned(rows, -2, 0), extra),
                (turned(rows, 4, 0), turned(rows, 2, 0), turned(extra, -2, 0)),
            )
        ]

    right, left = right_halos(fine_rows[0], extra[0]), left_halos(fine_rows[-1], extra[1])
    if wide:
        top = row < REACH
        halos = [jnp.where(top, right[x], turned(left[x], REACH, 0)) for x in range(2)]
        halos += [jnp.where(top, turned(right[x], REACH, 0), left[x]) for x in range(2)]
    else:
        halos = [jnp.where(starts, right[x], left[x]) for x in range(2)]

    def pair(left, right):
        return jnp.concatenate([left, right], axis=1)

    for i in range(len(halos) // 2):
        halo_ref[i] = pair(halos[2 * i], halos[2 * i + 1])
    logs = [pooled_ref[x, :, :half] for x in range(2)]
    sources = [pooled_ref[x, :, half:] for x in range(2)]

    far = [(logs[inner], logs[1 - inner], sources[inner], halos[inner]) for inner in (1, 0)]
    for group, ref in enumerate(far_refs):
        for i, (right, left) in enumerate(zip(*far)):
            put(ref, i * (half // LANES), jnp.where(low, *((right, left) if group == 0 else (left, right))))
        for spare in range(4 * (half // LANES), ref.shape[0] // SUBLANES):
            put(ref, spare, jnp.zeros((SUBLANES, LANES), jnp.float32))


def pack_far(pooled, got, n_far):
    slots, rows, lanes = got[0].shape
    wide = len(got) == 2
    far_rows = max(2 * lanes // LANES, 0 if wide else near_layout(lanes, wide)[1]) * SUBLANES
    out_shape = (jax.ShapeDtypeStruct((len(got), SUBLANES, lanes), jnp.float32),) + (
        jax.ShapeDtypeStruct((far_rows, LANES), jnp.float32),
    ) * n_far
    halos, *far = pl.pallas_call(
        functools.partial(pack_far_kernel, wide),
        out_shape=out_shape,
        in_specs=[VMEM] * (1 + len(got)),
        out_specs=(VMEM,) * len(out_shape),
        scratch_shapes=[pltpu.VMEM((lanes // LANES, 2 * SUBLANES, LANES), jnp.float32)],
        compiler_params=pltpu.CompilerParams(vmem_limit_bytes=8 << 20),
        cost_estimate=AHEAD,
        name="pack_far",
    )(pooled, *got)
    return halos, far


def pack_near_kernel(wide, pooled_ref, halo_ref, after_ref, *refs):
    *got_refs, first_ref, second_ref = refs
    layers, lanes = got_refs[0].shape[0] - 1, got_refs[0].shape[2]
    ix, iy = lax.axis_index("gx"), lax.axis_index("gy")
    even, starts = iy % 2 == 0, iy == 0
    half = lanes // 2
    upper = iota((SUBLANES, lanes), 0) < REACH

    def got(slot):
        tiles = tuple(ref[slot] for ref in got_refs)
        return from_right(even, tiles), from_left(even, tiles)

    strips = [got(layer) for layer in range(layers)]
    halos = [halo_ref[i // 2, :, (i % 2) * half : (i % 2 + 1) * half] for i in range(4 if wide else 2)]
    sources = [pooled_ref[x, :, half:] for x in range(2)]

    def near_tiles(order):
        near, beyond = order[0] // 2, order[-1] // 2
        if wide:
            log_rows = [jnp.where(upper, *strips[layer]) for layer in range(layers)]
            source_rows = [turned(jnp.where(upper, *strips[layer][::-1]), REACH, 0) for layer in range(layers)]
            return {
                "log1": join_third(log_rows[order[0]], log_rows[order[2]]),
                "source1": source_rows[order[0]],
                "log2": log_rows[order[1]],
                "source2": source_rows[order[1]],
                "halo0": halos[near],
                "halo1": halos[beyond],
                "halo2": halos[2 + near],
                "halo3": halos[2 + beyond],
                "source": sources[beyond],
            }
        first, second, third = (strips[layer][0] for layer in order[:3])
        place = iota((SUBLANES, lanes), 0)
        right = jnp.where(place == 3, turned(third, 3, 0), jnp.where(place >= 6, turned(second, -2, 0), first))
        left = jnp.where(place == 4, turned(third, -3, 0), jnp.where(place < 2, turned(second, 2, 0), first))
        line = jnp.where(starts, second[4:5], second[3:4])
        lines = jnp.zeros((SUBLANES, LANES), jnp.float32)
        for j in range(lanes // LANES):
            lines = jnp.where(iota(lines.shape, 0) == j, line[:, j * LANES : (j + 1) * LANES], lines)
        return {
            "strip": jnp.where(starts, right, left),
            "halo": join_halo(halos[near], halos[beyond], starts),
            "source": sources[beyond],
            "row": lines,
        }

    forward = list(range(layers))
    layout, _ = near_layout(lanes, wide)
    right, left = near_tiles(forward[::-1]), near_tiles(forward)
    for name, (start, _) in layout.items():
        put(first_ref, start, jnp.where(ix % 2 == 0, right[name], left[name]))
        put(second_ref, start, jnp.where(ix % 2 == 0, left[name], right[name]))


def pack_near(pooled, halos, after, got):
    slots, rows, lanes = got[0].shape
    wide = len(got) == 2
    out = jax.ShapeDtypeStruct((near_layout(lanes, wide)[1] * SUBLANES, LANES), jnp.float32)
    return pl.pallas_call(
        functools.partial(pack_near_kernel, wide),
        out_shape=(out, out),
        in_specs=[VMEM, VMEM, ANY] + [VMEM] * len(got),
        out_specs=(VMEM,) * 2,
        compiler_params=pltpu.CompilerParams(vmem_limit_bytes=8 << 20),
        cost_estimate=AHEAD,
        name="pack_near",
    )(pooled, halos, after, *got)


def landed_kernel(after_ref, both_ref, pooled_ref, halo_ref, first_ref, second_ref, *refs):
    *got_refs, out_ref, sent_ref, sum_ref = refs
    log_ref, source_ref = parts(both_ref)
    layers, rows, lanes = log_ref.shape
    half = lanes // 2
    even = lax.axis_index("gx") % 2 == 0
    slots = early_slots(layers, rows // SUBLANES, len(got_refs))
    pairs = {}
    for a, ref in enumerate((log_ref, source_ref)):
        for layer in range(layers):
            for i in range(rows // SUBLANES):
                pairs["own", a, layer, i] = edges(ref.at[layer, i * SUBLANES : (i + 1) * SUBLANES])
    for g, ref in enumerate(got_refs):
        for layer in range(layers):
            pairs["got", g, layer] = edges(ref.at[layer])
    for i in range(2):
        for x in range(2):
            columns = slice(x * half, (x + 1) * half)
            pairs["pooled", i, x] = edges(pooled_ref.at[i, :, columns])
            if i < len(got_refs):
                pairs["halo", i, x] = edges(halo_ref.at[i, :, columns])
    pieces = []
    for side, pick in enumerate((from_left, from_right)):

        def block(slot):
            return pick(even, (first_ref[slot], second_ref[slot]))

        for slot in range(2 * layers - 1):
            for i in range(rows // SUBLANES):
                part = slice(i * SUBLANES, (i + 1) * SUBLANES)
                ends = [edges(ref.at[slot, part]) for ref in (first_ref, second_ref)]
                pairs["raw", side, slot, i] = [
                    pick(even, tuple(end[...] for end in both)) for both in zip(*ends)
                ]
        nearest = layers + 1 if side == 0 else layers
        for top in (0, 2, nearest):
            both = block(top) + block(top + 1)
            pieces.append(row_pairs(both[:SUBLANES], both[SUBLANES:], sum_ref))
    tiles = lane_pairs(pieces)
    for side in range(2):
        for i in range(3):
            tile = tiles[3 * side + i] * (0.125 if i < 2 else 1.0)
            put(out_ref, (3 * side + i) * (half // LANES), tile)
            pairs["near", side, i] = edges(tile)
    write_lanes(sent_ref, [tuple(end[...] for end in pairs[key]) for key in slots])


def landed(after, both, pooled, halos, raw, got):
    layers, rows, lanes = both.shape[0] // 2, *both.shape[1:]
    slots = early_slots(layers, rows // SUBLANES, len(got))
    return pl.pallas_call(
        landed_kernel,
        out_shape=(
            jax.ShapeDtypeStruct((6 * (lanes // 2 // LANES) * SUBLANES, LANES), jnp.float32),
            packed_rows(slots),
        ),
        in_specs=[ANY] + [VMEM] * (5 + len(got)),
        out_specs=(VMEM,) * 2,
        scratch_shapes=[pltpu.VMEM((lanes // LANES, 2 * SUBLANES, LANES), jnp.float32)],
        compiler_params=pltpu.CompilerParams(vmem_limit_bytes=16 << 20),
        cost_estimate=pl.CostEstimate(flops=1_000_000, bytes_accessed=1_000_000, transcendentals=0),
        name="landed",
    )(after, both, pooled, halos, *raw, *got)


def near_part(refs, even, lanes, wide, side, name):
    start, count = near_layout(lanes, wide)[0][name]
    pick = from_left if side == 0 else from_right
    got = pick(even, tuple(take(ref, start, count) for ref in refs))
    return rows_to_lanes(got, lanes // LANES) if name == "row" else got


def far_part(refs, low, lanes, side, i):
    count = lanes // 2 // LANES
    pick = from_left if side == 0 else from_right
    return pick(low, tuple(take(ref, i * count, count) for ref in refs))


def late_kernel(lanes, wide, after_ref, first_ref, second_ref, *refs):
    *far_refs, sent_ref = refs
    even, low = lax.axis_index("gx") % 2 == 0, lax.axis_index("gx") % 4 < 2
    pairs = []
    for side, name in late_slots(lanes, wide):
        if name == "far":
            pairs.append(edges(far_part(far_refs, low, lanes, side, 0)))
        else:
            pairs.append(edges(near_part((first_ref, second_ref), even, lanes, wide, side, name)))
    write_lanes(sent_ref, pairs)


def late_lanes(after, near, far, lanes, wide):
    return pl.pallas_call(
        functools.partial(late_kernel, lanes, wide),
        out_shape=packed_rows(late_slots(lanes, wide)),
        in_specs=[ANY] + [VMEM] * (2 + len(far)),
        out_specs=VMEM,
        compiler_params=pltpu.CompilerParams(vmem_limit_bytes=8 << 20),
        cost_estimate=pl.CostEstimate(flops=1_000_000, bytes_accessed=200_000, transcendentals=0),
        name="late_lanes",
    )(after, *near, *far)


def coarse_kernel(peers, n_far, own_ref, halo_ref, pool_ref, first_ref, second_ref, *refs):
    near_refs, far_refs = (first_ref, second_ref), refs[:n_far]
    early_ref, late_ref, coef_ref, out_ref, wide_ref, *scratch = refs[n_far:]
    ix, iy, iz = (lax.axis_index(axis) for axis in AXES)
    nx, ny, nz = peers
    wide = ny > 2
    fine_lanes = own_ref.shape[2]
    lanes, rows = fine_lanes // 2, SUBLANES
    even, low, starts = ix % 2 == 0, ix % 4 < 2, iy == 0
    top = iota((rows, lanes + LANES), 0) < REACH
    early = early_slots(REACH, 2, 2 if wide else 1)
    late = late_slots(fine_lanes, wide)

    def columns(half):
        return slice(half * lanes, (half + 1) * lanes)

    def with_early(core, *key):
        return jnp.concatenate([core, read_lanes(early_ref, early[key])], axis=1)

    def near(side, name):
        core = near_part(near_refs, even, fine_lanes, wide, side, name)
        return jnp.concatenate([core, read_lanes(late_ref, late[side, name])], axis=1)

    def far(side, i):
        core = far_part(far_refs, low, fine_lanes, side, i)
        return jnp.concatenate([core, read_lanes(late_ref, late[side, "far"])], axis=1)

    def split(tile, a):
        other = turned(tile, REACH, 0)
        return jnp.where(top, tile, other) if a == 0 else jnp.where(top, other, tile)

    def window(a, k):
        block, layer = k // 2 - 2, k % 2
        nearest = layer == (1 if block < 0 else 0)
        side = 0 if block < 0 else 1
        if abs(block) == 2:
            if a == 1:
                core = far(side, 2)
                return jnp.concatenate([core, jnp.zeros_like(core)], axis=0)
            halo = far(side, 3)
            halo = halo if wide else split(halo, 0)
            return jnp.concatenate([far(side, 0 if nearest else 1), halo], axis=0)
        if block == 0:
            core = with_early(own_ref[layer, :, columns(a)], "pooled", layer, a)
            if wide:
                halo = with_early(halo_ref[a, :, columns(layer)], "halo", a, layer)
            else:
                halo = split(with_early(halo_ref[0, :, columns(layer)], "halo", 0, layer), a)
            return jnp.concatenate([core, halo], axis=0)
        if a == 0 or nearest:
            i = layer if a == 0 else 2
            core = take(pool_ref, (3 * side + i) * (lanes // LANES), lanes // LANES)
            core = with_early(core, "near", side, i)
        else:
            core = near(side, "source")
        if wide:
            halo = near(side, f"halo{2 * a + (0 if nearest else 1)}")
        else:
            joined = near(side, "halo")
            halo = split(joined if nearest else beyond_halo(joined, starts), a)
        return jnp.concatenate([core, halo], axis=0)

    def open_face(inside):
        return jnp.where(inside, 4.0, 0.0)

    faces = [4.0] * 9
    faces[1], faces[3] = open_face(ix > 1), open_face(ix > 0)
    faces[5], faces[7] = open_face(ix < nx - 1), open_face(ix < nx - 2)
    *scratch, p_ref = scratch

    def emit(layer, tile, value):
        p_ref[layer * rows : (layer + 1) * rows, tile * LANES : (tile + 1) * LANES] = value

    iterate(
        2 + 2 * REACH,
        rows,
        2 * rows,
        lanes // LANES + 1,
        functools.partial(window, 0),
        functools.partial(window, 1),
        faces,
        row_numerators(2 * rows, rows, iy, ny, 2.0),
        lane_numerators(2 * rows, iz, nz, 2.0) + [4.0],
        coef_ref,
        8.0 * storage_rate,
        emit,
        scratch,
    )
    widen = (iota((lanes, 2 * lanes), 0) == iota((lanes, 2 * lanes), 1) // 2).astype(jnp.bfloat16)
    spread = exact_dot(p_ref[...], widen)
    for x in range(2):
        for tile in range(2 * lanes // LANES):
            part = slice(tile * LANES, (tile + 1) * LANES)
            for half in range(2):
                wide_ref[tile, pl.ds(half, rows, stride=2), :] = spread[x * rows : (x + 1) * rows, part]
            for twin in range(2):
                out_ref[2 * x + twin, :, part] = wide_ref[tile]


def coarse_level(own, halos, pooled, near, far, early, late, coefficients, peers):
    lanes = own.shape[2] // 2
    window = (2 + 2 * REACH, SUBLANES, 2 * SUBLANES, lanes // LANES + 1)
    return pl.pallas_call(
        functools.partial(coarse_kernel, peers, len(far)),
        out_shape=jax.ShapeDtypeStruct((REACH, 2 * SUBLANES, 2 * lanes), jnp.float32),
        in_specs=[VMEM] * (8 + len(far)),
        out_specs=VMEM,
        scratch_shapes=[pltpu.VMEM((2 * lanes // LANES, 2 * SUBLANES, LANES), jnp.float32)]
        + window_scratch(*window)
        + [pltpu.VMEM((2 * SUBLANES, lanes), jnp.float32)],
        compiler_params=pltpu.CompilerParams(vmem_limit_bytes=24 << 20),
        cost_estimate=pl.CostEstimate(flops=20_000_000, bytes_accessed=4_000_000, transcendentals=0),
        name="coarse_level",
    )(own, halos, pooled, *near, *far, early, late, coefficients)


def fine_kernel(peers, n_far, both_ref, *refs):
    log_ref, source_ref = parts(both_ref)
    layers, rows, lanes = log_ref.shape
    ix, iy, iz = (lax.axis_index(axis) for axis in AXES)
    nx, ny, nz = peers
    wide = ny > 2
    n_got = 2 if wide else 1
    got_refs, refs = refs[:n_got], refs[n_got:]
    second_ref, first_ref = refs[:2]
    second_near_ref, first_near_ref, early_ref, late_ref, spread_ref = refs[2 + n_far : 7 + n_far]
    coef_ref, fine_ref, diff_ref, *scratch = refs[7 + n_far :]
    even, starts = ix % 2 == 0, iy == 0
    count = 3 * layers
    upper = iota((SUBLANES, lanes + LANES), 0) < REACH
    early = early_slots(layers, rows // SUBLANES, n_got)
    late = late_slots(lanes, wide)

    def with_early(core, *keys):
        tile = jnp.concatenate([read_lanes(early_ref, early[key]) for key in keys], axis=0)
        return jnp.concatenate([core, tile], axis=1)

    def near(side, name):
        core = near_part((first_near_ref, second_near_ref), even, lanes, wide, side, name)
        return jnp.concatenate([core, read_lanes(late_ref, late[side, name])], axis=1)

    def near_halo(a, side, distance):
        if wide:
            tile = near(side, ("log" if a == 0 else "source") + ("2" if distance == 2 else "1"))
        elif a == 1:
            return near(side, "row") if distance == 2 else turned(near(side, "strip"), REACH, 0)
        else:
            tile = near(side, "strip")
            if distance == 2:
                return jnp.where(starts, turned(tile, 2, 0), turned(tile, -2, 0))
        return third_halo(tile) if a == 0 and distance > 2 else tile

    def window(a, k):
        block, layer = k // layers - 1, k % layers
        if block == 0:
            core = (log_ref, source_ref)[a][layer]
            core = with_early(core, *(("own", a, layer, i) for i in range(rows // SUBLANES)))
            tiles = tuple(with_early(ref[layer], ("got", g, layer)) for g, ref in enumerate(got_refs))
            halo = tiles[0]
            if wide:
                sides = from_right(iy % 2 == 0, tiles), from_left(iy % 2 == 0, tiles)
                halo = jnp.where(upper, *(sides if a == 0 else sides[::-1]))
            if a == 1:
                halo = turned(halo, REACH, 0)
            return jnp.concatenate([core, halo], axis=0)
        side, pick = (0, from_left) if block < 0 else (1, from_right)
        slot = layer if a == 0 else layers + layer - (1 if block < 0 else 0)
        core = pick(even, (first_ref[slot], second_ref[slot]))
        core = with_early(core, *(("raw", side, slot, i) for i in range(rows // SUBLANES)))
        halo = near_halo(a, side, layers - layer if block < 0 else layer + 1)
        return jnp.concatenate([core, halo], axis=0)

    faces = [2.0] * (count - 1)
    faces[layers - 1] = jnp.where(ix > 0, 2.0, 0.0)
    faces[2 * layers - 1] = jnp.where(ix < nx - 1, 2.0, 0.0)

    def emit(layer, tile, value):
        part = slice(tile * LANES, (tile + 1) * LANES)
        fine_ref[layer, :, part] = value
        diff_ref[layer, :, part] = value - spread_ref[layer, :, part]

    iterate(
        count,
        rows,
        rows + 2 * REACH,
        lanes // LANES + 1,
        functools.partial(window, 0),
        functools.partial(window, 1),
        faces,
        row_numerators(rows + 2 * REACH, rows, iy, ny, 1.0),
        lane_numerators(rows + 2 * REACH, iz, nz, 1.0) + [2.0],
        coef_ref,
        storage_rate,
        emit,
        scratch,
    )


def fine_level(both, got, raw, far, near, early, late, spread, coefficients, peers):
    layers, rows, lanes = spread.shape
    window = (layers + 2 * REACH, rows, rows + 2 * REACH, lanes // LANES + 1)
    out = jax.ShapeDtypeStruct(spread.shape, jnp.float32)
    return pl.pallas_call(
        functools.partial(fine_kernel, peers, len(far)),
        out_shape=(out, out),
        in_specs=[VMEM] * (3 + len(got)) + [ANY] * len(far) + [VMEM] * 6,
        out_specs=(VMEM, VMEM),
        scratch_shapes=window_scratch(*window),
        compiler_params=pltpu.CompilerParams(vmem_limit_bytes=24 << 20),
        cost_estimate=pl.CostEstimate(flops=20_000_000, bytes_accessed=10_000_000, transcendentals=0),
        name="fine_level",
    )(both, *got, *raw[::-1], *far, *near[::-1], early, late, spread, coefficients)


def shards(peers, log_perm, source, low_bound, high_bound):
    nx, ny, nz = peers
    layers, rows, lanes = log_perm.shape
    assert layers == REACH and rows == 2 * SUBLANES and nx > 2 and nz == 2
    both = jnp.concatenate([log_perm, source])
    own, *rows_sent = prep(both, ny)
    if ny == 2:
        got = (permute(rows_sent[0], "gy", ny, [(0, 1)]),)
    else:
        got = swap("gy", ny, rows_sent[1], rows_sent[0])
    for_second = raw_block(both, rows_sent[0], True)
    second = permute(for_second, "gx", nx, neighbour_pairs(nx, 1))
    for_first = raw_block(both, for_second, False)
    raw = (permute(for_first, "gx", nx, neighbour_pairs(nx, 0)), second)
    far_groups = far_pairs(nx)
    halos, for_far = pack_far(own, got, len(far_groups))
    far = [permute(tiles, "gx", nx, group) for tiles, group in zip(for_far, far_groups)]
    for_first, for_second = pack_near(own, halos, for_far[0], got)
    second = permute(for_second, "gx", nx, neighbour_pairs(nx, 1))
    near = (permute(for_first, "gx", nx, neighbour_pairs(nx, 0)), second)
    coefficients = chebyshev_coefficients(low_bound, high_bound, for_first)
    pooled, early_sent = landed(coefficients, both, own, halos, raw, got)
    early = lax.ppermute(early_sent, "gz", [(0, 1), (1, 0)])
    late_sent = late_lanes(early_sent, near, far, lanes, ny > 2)
    late = lax.ppermute(late_sent, "gz", [(0, 1), (1, 0)])
    spread = coarse_level(own, halos, pooled, near, far, early, late, coefficients, peers)
    return fine_level(both, got, raw, far, near, early, late, spread, coefficients, peers)


def solution(mesh):
    peers = tuple(mesh.shape[axis] for axis in AXES)
    split = P(("groups", "gx"), "gy", "gz")
    return jax.shard_map(
        functools.partial(shards, peers),
        mesh=mesh,
        in_specs=(split, split, P(), P()),
        out_specs=(split, split),
        check_vma=False,
    )
```

```python
import functools

import jax
import jax.numpy as jnp
from jax import lax
from jax.experimental import pallas as pl
from jax.experimental.pallas import tpu as pltpu
from jax.sharding import PartitionSpec as P

DEGREE = 3
REACH = DEGREE + 1
LANES = 128
SUBLANES = 8
storage_rate = 0.1
AXES = ("gx", "gy", "gz")
VMEM = pl.BlockSpec(memory_space=pltpu.VMEM)
ANY = pl.BlockSpec(memory_space=pl.ANY)
HBM = pl.BlockSpec(memory_space=pltpu.HBM)


AHEAD = pl.CostEstimate(flops=50_000_000_000, bytes_accessed=1_000_000, transcendentals=0)


def iota(shape, dim):
    return lax.broadcasted_iota(jnp.int32, shape, dim)


def turned(value, shift, axis):
    size = value.shape[axis]
    return pltpu.roll(value, shift % size, axis)


def permute(value, axis, peers, pairs):
    cores = lax.axis_size("gz")
    if axis == "gz" or cores % 2:
        return lax.ppermute(value, axis, [pair for i, j in pairs for pair in ((i, j), (j, i))])
    partner = {}
    for i, j in pairs:
        partner[i], partner[j] = j, i
    moves = [
        (i * cores + core, partner[i] * cores + core if i in partner else i * cores + (core ^ 1))
        for i in range(peers)
        for core in range(cores)
    ]
    return lax.ppermute(value, (axis, "gz"), moves)


def neighbour_pairs(peers, start):
    return [(i, i + 1) for i in range(start, peers - 1, 2)]


def first_swap(axis, peers, right, left):
    even = lax.axis_index(axis) % 2 == 0
    return permute(jnp.where(even, right, left), axis, peers, neighbour_pairs(peers, 0))


def second_swap(axis, peers, right, left):
    even = lax.axis_index(axis) % 2 == 0
    return permute(jnp.where(even, left, right), axis, peers, neighbour_pairs(peers, 1))


def swap(axis, peers, right, left):
    got = (first_swap(axis, peers, right, left),)
    return got if peers == 2 else got + (second_swap(axis, peers, right, left),)


def far_pairs(peers):
    pairs = [(i, i + 2) for i in range(peers - 2)]
    groups = [[pair for pair in pairs if pair[0] % 4 < 2], [pair for pair in pairs if pair[0] % 4 >= 2]]
    return [group for group in groups if group]


def from_right(is_first, got):
    return got[0] if len(got) == 1 else jnp.where(is_first, got[0], got[1])


def from_left(is_first, got):
    return got[0] if len(got) == 1 else jnp.where(is_first, got[1], got[0])


def inverse(value):
    guess = pl.reciprocal(value, approx=True)
    return guess * (2.0 - value * guess)


def row_numerators(rows, own, index, peers, face_scale):
    place = iota((rows, LANES), 0)
    right = jnp.where(index < peers - 1, 2.0 * face_scale, 0.0)
    left = jnp.where(index > 0, 2.0 * face_scale, 0.0)
    return jnp.where(place == own - 1, right, jnp.where(place == rows - 1, left, 2.0 * face_scale))


def lane_numerators(rows, index, peers, face_scale):
    place = iota((rows, LANES), 1)
    right = jnp.where(index < peers - 1, 2.0 * face_scale, 0.0)
    left = jnp.where(index > 0, 2.0 * face_scale, 0.0)
    return [jnp.where(place == LANES - 1, side, 2.0 * face_scale) for side in (right, left)]


def lane_tiles(value):
    return [value[:, i : i + LANES] for i in range(0, value.shape[1], LANES)]


def beside(tiles, shift):
    moved = [turned(tile, shift, 1) for tile in tiles]
    lane = iota(tiles[0].shape, 1)
    seam = LANES - 1 if shift < 0 else 0
    return [
        jnp.where(lane == seam, moved[(j - shift) % len(tiles)], moved[j]) for j in range(len(tiles))
    ]


def store_rows(ref, k, j, value):
    rows = value.shape[0]
    ref[k, j, SUBLANES : SUBLANES + rows] = value
    ref[k, j, SUBLANES - 1 : SUBLANES] = value[rows - 1 :]
    ref[k, j, SUBLANES + rows : SUBLANES + rows + 1] = value[:1]


def iterate(count, own_rows, rows, tiles, log_at, source_at, x_faces, y_top, z_top, coef_ref, storage, emit, refs):
    k_ref, tx_ref, ty_ref, tzr_ref, tzl_ref, diag_ref, w_ref, d_ref, r_ref, p_ref = refs
    own_tiles = tiles - 1

    def away(k):
        return max(0, REACH - k, k - (count - 1 - REACH))

    def extent(k, step):
        left = DEGREE - step - away(k)
        return None if left < 0 else (own_rows, own_tiles) if left == 0 else (rows, tiles)

    def coefficient(i, size):
        return jnp.concatenate([coef_ref[i]] * (size // SUBLANES), axis=0)

    z_tops = [z_top[0] if j == own_tiles - 1 else z_top[1] if j == own_tiles else None for j in range(tiles)]

    def resistance(k):
        return [jnp.exp(-tile) for tile in lane_tiles(log_at(k))]

    after = resistance(0)
    tx_before = None
    for k in range(count):
        here = after
        if k + 1 < count:
            after = resistance(k + 1)
            outer = max(away(k), away(k + 1))
            size, number = (rows, tiles) if outer < REACH else (own_rows, own_tiles)
            tx = [x_faces[k] * inverse(here[j][:size] + after[j][:size]) for j in range(number)]
            for j in range(number):
                tx_ref[k, j, :size] = tx[j]
        if away(k) <= DEGREE:
            size, number = extent(k, 0)
            right = beside(here, -1)
            tz = []
            for j in range(tiles):
                scale = z_tops[j][:size] if z_tops[j] is not None else z_top[2]
                tz.append(scale * inverse(here[j][:size] + right[j][:size]))
            tz_left = beside(tz, 1)
            source = lane_tiles(source_at(k))
            for j in range(number):
                store_rows(k_ref, k, j, here[j])
                ty = y_top * inverse(here[j] + k_ref[k, j, SUBLANES + 1 : SUBLANES + 1 + rows])
                store_rows(ty_ref, k, j, ty)
                ty_before = ty_ref[k, j, SUBLANES - 1 : SUBLANES - 1 + size]
                diagonal = storage + (tx_before[j][:size] + tx[j][:size])
                diagonal = diagonal + (ty[:size] + ty_before) + (tz[j] + tz_left[j])
                w = inverse(diagonal)
                direction = source[j][:size] * (coefficient(0, size) * w)
                if (size, number) == (rows, tiles):
                    store_rows(d_ref.at[0], k, j, direction)
                else:
                    d_ref[0, k, j, SUBLANES : SUBLANES + size] = direction
                if extent(k, 1) is not None:
                    tzr_ref[k, j, :size] = tz[j]
                    tzl_ref[k, j, :size] = tz_left[j]
                    diag_ref[k, j, :size] = diagonal
                    w_ref[k, j, :size] = w
                    r_ref[k, j, :size] = source[j][:size]
        tx_before = tx
    for step in range(1, DEGREE + 1):
        old, new = d_ref.at[(step - 1) % 2], d_ref.at[step % 2]
        for k in range(count):
            if extent(k, step) is None:
                continue
            size, number = extent(k, step)
            middle = slice(SUBLANES, SUBLANES + size)
            keep, gain = coefficient(2 * step - 1, size), coefficient(2 * step, size)
            here = [old[k, j, middle] for j in range(tiles)]
            right, left = beside(here, -1), beside(here, 1)
            for j in range(number):
                applied = tx_ref[k, j, :size] * old[k + 1, j, middle] + tx_ref[k - 1, j, :size] * old[k - 1, j, middle]
                applied += (
                    ty_ref[k, j, middle] * old[k, j, SUBLANES + 1 : SUBLANES + 1 + size]
                    + ty_ref[k, j, SUBLANES - 1 : SUBLANES - 1 + size] * old[k, j, SUBLANES - 1 : SUBLANES - 1 + size]
                )
                applied += tzr_ref[k, j, :size] * right[j] + tzl_ref[k, j, :size] * left[j]
                residual = r_ref[k, j, :size] - (diag_ref[k, j, :size] * here[j] - applied)
                fresh = keep * here[j] + gain * (residual * w_ref[k, j, :size])
                if away(k) == 0 and j < own_tiles:
                    so_far = here[j][:own_rows] if step == 1 else p_ref[k, j]
                    total = so_far + fresh[:own_rows]
                    if step == DEGREE:
                        emit(k - REACH, j, total)
                    else:
                        p_ref[k, j] = total
                if step < DEGREE:
                    r_ref[k, j, :size] = residual
                    if (size, number) == (rows, tiles):
                        store_rows(new, k, j, fresh)
                    else:
                        new[k, j, middle] = fresh


def coefficients_kernel(low_ref, high_ref, after_ref, coef_ref, bounds_ref, sems):
    copies = [
        pltpu.make_async_copy(ref, bounds_ref.at[i], sems.at[i]) for i, ref in enumerate((low_ref, high_ref))
    ]
    for copy in copies:
        copy.start()
    for copy in copies:
        copy.wait()
    low, high = (jnp.full((SUBLANES, LANES), bounds_ref[i, 0]) for i in range(2))
    theta, delta = (high + low) * 0.5, (high - low) * 0.5
    sigma = theta / delta
    rho = 1.0 / sigma
    coef_ref[0] = 1.0 / theta
    for step in range(DEGREE):
        rho_next = 1.0 / (2.0 * sigma - rho)
        coef_ref[1 + 2 * step] = rho_next * rho
        coef_ref[2 + 2 * step] = 2.0 * rho_next / delta
        rho = rho_next


def chebyshev_coefficients(low_bound, high_bound, after):
    return pl.pallas_call(
        coefficients_kernel,
        out_shape=jax.ShapeDtypeStruct((1 + 2 * DEGREE, SUBLANES, LANES), jnp.float32),
        in_specs=[HBM] * 2 + [ANY],
        out_specs=VMEM,
        scratch_shapes=[pltpu.SMEM((2, 1), jnp.float32), pltpu.SemaphoreType.DMA((2,))],
        compiler_params=pltpu.CompilerParams(vmem_limit_bytes=4 << 20),
        cost_estimate=pl.CostEstimate(flops=1000000, bytes_accessed=500_000, transcendentals=0),
        name="coefficients",
    )(low_bound, high_bound, after)


def put(ref, tile, value):
    for i in range(value.shape[1] // LANES):
        ref[(tile + i) * SUBLANES : (tile + i + 1) * SUBLANES, :] = value[:, i * LANES : (i + 1) * LANES]


def take(ref, tile, count):
    tiles = [ref[(tile + i) * SUBLANES : (tile + i + 1) * SUBLANES, :] for i in range(count)]
    return tiles[0] if count == 1 else jnp.concatenate(tiles, axis=1)


def edges(value):
    lanes = value.shape[-1]
    value = value if isinstance(value, jax.Array) else value.at
    return value[:, lanes - LANES :], value[:, :LANES]


def write_lanes(ref, pairs):
    starts = lax.axis_index("gz") == 0
    each = LANES // SUBLANES
    group = iota((SUBLANES, LANES), 1) // SUBLANES
    for base in range(0, len(pairs), each):
        merged = None
        for j, (last, first) in enumerate(pairs[base : base + each]):
            moved = turned(jnp.where(starts, last, first), SUBLANES * j, 1)
            place = jnp.where(starts, (j - 1) % each, j)
            merged = moved if merged is None else jnp.where(group == place, moved, merged)
        row = base // each * SUBLANES
        ref[row : row + SUBLANES, :] = merged


def read_lanes(ref, slot):
    each = LANES // SUBLANES
    row = slot // each * SUBLANES
    return turned(ref[row : row + SUBLANES, :], -SUBLANES * (slot % each), 1)


def early_slots(layers, row_tiles, n_got):
    keys = [("own", a, layer, i) for a in range(2) for layer in range(layers) for i in range(row_tiles)]
    keys += [("got", g, layer) for g in range(n_got) for layer in range(layers)]
    keys += [("pooled", x, a) for x in range(2) for a in range(2)]
    keys += [("halo", i, half) for i in range(n_got) for half in range(2)]
    keys += [
        ("raw", side, slot, i)
        for side in range(2)
        for slot in range(2 * layers - 1)
        for i in range(row_tiles)
    ]
    keys += [("near", side, i) for side in range(2) for i in range(3)]
    return {key: i for i, key in enumerate(keys)}


def near_layout(lanes, wide):
    whole, half = lanes // LANES, lanes // LANES // 2
    if wide:
        parts = [("log1", whole), ("source1", whole), ("log2", whole), ("source2", whole)]
        parts += [(name, half) for name in ("halo0", "halo1", "halo2", "halo3", "source")]
    else:
        parts = [("strip", whole), ("halo", half), ("source", half), ("row", 1)]
    layout, start = {}, 0
    for name, count in parts:
        layout[name] = (start, count)
        start += count
    return layout, start


def late_slots(lanes, wide):
    names = list(near_layout(lanes, wide)[0])
    keys = [(side, name) for side in range(2) for name in names] + [(side, "far") for side in range(2)]
    return {key: i for i, key in enumerate(keys)}


def rows_to_lanes(row_tile, count):
    return jnp.concatenate(
        [jnp.broadcast_to(row_tile[j : j + 1], (SUBLANES, LANES)) for j in range(count)], axis=1
    )


def packed_rows(slots):
    each = LANES // SUBLANES
    return jax.ShapeDtypeStruct((-(-len(slots) // each) * SUBLANES, LANES), jnp.float32)


def window_scratch(count, own_rows, rows, tiles):
    plain = pltpu.VMEM((count, tiles, rows, LANES), jnp.float32)
    margins = pltpu.VMEM((count, tiles, rows + 2 * SUBLANES, LANES), jnp.float32)
    pair = pltpu.VMEM((2, count, tiles, rows + 2 * SUBLANES, LANES), jnp.float32)
    total = pltpu.VMEM((count, tiles, own_rows, LANES), jnp.float32)
    return [margins, plain, margins, plain, plain, plain, plain, pair, plain, total]


def exact_dot(value, zero_one):
    parts = []
    for _ in range(3):
        part = value.astype(jnp.bfloat16)
        parts.append(part)
        value = value - part.astype(jnp.float32)
    rows = value.shape[0]
    out = jnp.dot(jnp.concatenate(parts, axis=0), zero_one, preferred_element_type=jnp.float32)
    return (out[2 * rows :] + out[rows : 2 * rows]) + out[:rows]


def row_pairs(top, bottom, sum_ref):
    tiles = top.shape[1] // LANES
    for tile in range(tiles):
        columns = slice(tile * LANES, (tile + 1) * LANES)
        sum_ref[tile, :SUBLANES] = top[:, columns]
        sum_ref[tile, SUBLANES:] = bottom[:, columns]
    return jnp.concatenate(
        [
            sum_ref[tile, pl.ds(0, SUBLANES, stride=2), :] + sum_ref[tile, pl.ds(1, SUBLANES, stride=2), :]
            for tile in range(tiles)
        ],
        axis=1,
    )


def lane_pairs(pieces):
    lanes = pieces[0].shape[1]
    pick = (iota((lanes, lanes // 2), 0) // 2 == iota((lanes, lanes // 2), 1)).astype(jnp.bfloat16)
    pooled = exact_dot(jnp.concatenate(pieces, axis=0), pick)
    return [pooled[SUBLANES * i : SUBLANES * (i + 1)] for i in range(len(pieces))]


def join_halo(near, beyond, starts):
    row = iota(near.shape, 0)
    up, down = turned(beyond, 3, 0), turned(beyond, -3, 0)
    right = jnp.where((row == 3) | (row == 7), up, jnp.where(row == 6, turned(beyond, 5, 0), near))
    left = jnp.where((row == 0) | (row == 4), down, jnp.where(row == 5, up, near))
    return jnp.where(starts, right, left)


def beyond_halo(joined, starts):
    row = iota(joined.shape, 0)
    up, down = turned(joined, 3, 0), turned(joined, -3, 0)
    right = jnp.where(row == 1, turned(joined, -5, 0), down)
    left = jnp.where(row == 2, down, up)
    return jnp.where(starts, right, left)


def join_third(near, third):
    row = iota(near.shape, 0)
    return jnp.where(
        row == 3, turned(third, 3, 0), jnp.where(row == 4, turned(third, -3, 0), near)
    )


def third_halo(joined):
    return jnp.where(iota(joined.shape, 0) < REACH, turned(joined, -3, 0), turned(joined, 3, 0))


def parts(both_ref):
    layers = both_ref.shape[0] // 2
    return both_ref.at[:layers], both_ref.at[layers:]


def prep_kernel(both_ref, after_ref, pooled_ref, *refs):
    *out_refs, sum_ref = refs
    log_ref, source_ref = parts(both_ref)
    layers, rows, lanes = log_ref.shape
    starts = lax.axis_index("gy") == 0

    def put(slot, left, right):
        if len(out_refs) == 1:
            out_refs[0][slot] = jnp.where(starts, right, left)
        else:
            out_refs[0][slot], out_refs[1][slot] = left, right

    half = lanes // 2
    upper = iota((SUBLANES, lanes), 0) < REACH
    pieces = []
    for x in range(2):
        for ref in (log_ref, source_ref):
            both = ref[2 * x] + ref[2 * x + 1]
            pieces.append(row_pairs(both[:SUBLANES], both[SUBLANES:], sum_ref))
    log0, source0, log1, source1 = lane_pairs(pieces)
    log0, log1 = log0 * 0.125, log1 * 0.125
    pooled_ref[0] = jnp.concatenate([log0, source0], axis=1)
    pooled_ref[1] = jnp.concatenate([log1, source1], axis=1)
    for layer in range(layers):
        put(
            layer,
            jnp.where(upper, log_ref[layer, :SUBLANES], turned(source_ref[layer, :SUBLANES], REACH, 0)),
            jnp.where(upper, turned(source_ref[layer, SUBLANES:], REACH, 0), log_ref[layer, SUBLANES:]),
        )
    pair = iota((SUBLANES, half), 0) // 2

    def four(*tiles):
        merged = jnp.where(
            pair == 0, tiles[0], jnp.where(pair == 1, tiles[1], jnp.where(pair == 2, tiles[2], tiles[3]))
        )
        return jnp.concatenate([merged, merged], axis=1)

    put(
        layers,
        four(turned(log1, -2, 0), log0, turned(source1, 2, 0), turned(source0, 4, 0)),
        four(turned(log0, -4, 0), turned(log1, -2, 0), source0, turned(source1, 2, 0)),
    )


def prep(both, after, ny):
    layers, rows, lanes = both.shape[0] // 2, *both.shape[1:]
    outs = 1 if ny == 2 else 2

    def tiles(count):
        return jax.ShapeDtypeStruct((count, SUBLANES, lanes), jnp.float32)

    return pl.pallas_call(
        prep_kernel,
        out_shape=(tiles(2),) + (tiles(layers + 1),) * outs,
        in_specs=[VMEM, ANY],
        out_specs=(VMEM,) * (1 + outs),
        scratch_shapes=[pltpu.VMEM((lanes // LANES, 2 * SUBLANES, LANES), jnp.float32)],
        compiler_params=pltpu.CompilerParams(vmem_limit_bytes=8 << 20),
        cost_estimate=pl.CostEstimate(flops=5_000_000, bytes_accessed=700_000, transcendentals=0),
        name="prep",
    )(both, after)


def raw_kernel(to_right_if_odd, both_ref, *refs):
    out_ref = refs[-1]
    log_ref, source_ref = parts(both_ref)
    layers = log_ref.shape[0]
    odd = lax.axis_index("gx") % 2
    skip = odd if to_right_if_odd else 1 - odd
    for layer in range(layers):
        out_ref[layer] = log_ref[layer]
    for layer in range(layers - 1):
        out_ref[layers + layer] = source_ref[layer + skip]


def raw_block(both, to_right_if_odd, *after):
    layers, rows, lanes = both.shape[0] // 2, *both.shape[1:]
    return pl.pallas_call(
        functools.partial(raw_kernel, to_right_if_odd),
        out_shape=jax.ShapeDtypeStruct((2 * layers - 1, rows, lanes), jnp.float32),
        in_specs=[VMEM] + [ANY] * len(after),
        out_specs=VMEM,
        compiler_params=pltpu.CompilerParams(vmem_limit_bytes=8 << 20),
        cost_estimate=pl.CostEstimate(flops=1_000_000, bytes_accessed=500_000, transcendentals=0),
        name="raw_block",
    )(both, *after)


def pack_far_kernel(wide, pooled_ref, *refs):
    n_got = 2 if wide else 1
    got_refs, halo_ref, far_refs, sum_ref = refs[:n_got], refs[n_got], refs[n_got + 1 : -1], refs[-1]
    layers, lanes = got_refs[0].shape[0] - 1, got_refs[0].shape[2]
    ix, iy = lax.axis_index("gx"), lax.axis_index("gy")
    even, starts, low = iy % 2 == 0, iy == 0, ix % 4 < 2
    half = lanes // 2
    upper = iota((SUBLANES, lanes), 0) < REACH
    row = iota((SUBLANES, half), 0)

    def got(slot):
        tiles = tuple(ref[slot] for ref in got_refs)
        return from_right(even, tiles), from_left(even, tiles)

    strips = [got(layer) for layer in range(layers)]
    extra = [tile[:, :half] for tile in got(layers)]
    pieces = []
    for side in range(2 if wide else 1):
        both = [strips[2 * x][side] + strips[2 * x + 1][side] for x in range(2)]
        pieces.append(row_pairs(*both, sum_ref))
    fine_rows = lane_pairs(pieces)

    def right_halos(rows, extra):
        rows = jnp.where(row % 4 < 2, rows * 0.125, rows)
        return [
            jnp.where(row < 2, near, jnp.where((row == 4) | (row == 5), far, more))
            for near, far, more in (
                (rows, turned(rows, 2, 0), extra),
                (turned(rows, 4, 0), turned(rows, -2, 0), turned(extra, 2, 0)),
            )
        ]

    def left_halos(rows, extra):
        rows = jnp.where(row % 4 >= 2, rows * 0.125, rows)
        return [
            jnp.where((row == 2) | (row == 3), near, jnp.where(row >= 6, far, more))
            for near, far, more in (
                (rows, turned(rows, -2, 0), extra),
                (turned(rows, 4, 0), turned(rows, 2, 0), turned(extra, -2, 0)),
            )
        ]

    right, left = right_halos(fine_rows[0], extra[0]), left_halos(fine_rows[-1], extra[1])
    if wide:
        top = row < REACH
        halos = [jnp.where(top, right[x], turned(left[x], REACH, 0)) for x in range(2)]
        halos += [jnp.where(top, turned(right[x], REACH, 0), left[x]) for x in range(2)]
    else:
        halos = [jnp.where(starts, right[x], left[x]) for x in range(2)]

    def pair(left, right):
        return jnp.concatenate([left, right], axis=1)

    for i in range(len(halos) // 2):
        halo_ref[i] = pair(halos[2 * i], halos[2 * i + 1])
    logs = [pooled_ref[x, :, :half] for x in range(2)]
    sources = [pooled_ref[x, :, half:] for x in range(2)]

    far = [(logs[inner], logs[1 - inner], sources[inner], halos[inner]) for inner in (1, 0)]
    for group, ref in enumerate(far_refs):
        for i, (right, left) in enumerate(zip(*far)):
            put(ref, i * (half // LANES), jnp.where(low, *((right, left) if group == 0 else (left, right))))
        for spare in range(4 * (half // LANES), ref.shape[0] // SUBLANES):
            put(ref, spare, jnp.zeros((SUBLANES, LANES), jnp.float32))


def pack_far(pooled, got, n_far):
    slots, rows, lanes = got[0].shape
    wide = len(got) == 2
    far_rows = max(2 * lanes // LANES, 0 if wide else near_layout(lanes, wide)[1]) * SUBLANES
    out_shape = (jax.ShapeDtypeStruct((len(got), SUBLANES, lanes), jnp.float32),) + (
        jax.ShapeDtypeStruct((far_rows, LANES), jnp.float32),
    ) * n_far
    halos, *far = pl.pallas_call(
        functools.partial(pack_far_kernel, wide),
        out_shape=out_shape,
        in_specs=[VMEM] * (1 + len(got)),
        out_specs=(VMEM,) * len(out_shape),
        scratch_shapes=[pltpu.VMEM((lanes // LANES, 2 * SUBLANES, LANES), jnp.float32)],
        compiler_params=pltpu.CompilerParams(vmem_limit_bytes=8 << 20),
        cost_estimate=pl.CostEstimate(flops=1000000, bytes_accessed=500_000, transcendentals=0),
        name="pack_far",
    )(pooled, *got)
    return halos, far


def pack_near_kernel(wide, pooled_ref, halo_ref, after_ref, *refs):
    *got_refs, first_ref, second_ref = refs
    layers, lanes = got_refs[0].shape[0] - 1, got_refs[0].shape[2]
    ix, iy = lax.axis_index("gx"), lax.axis_index("gy")
    even, starts = iy % 2 == 0, iy == 0
    half = lanes // 2
    upper = iota((SUBLANES, lanes), 0) < REACH

    def got(slot):
        tiles = tuple(ref[slot] for ref in got_refs)
        return from_right(even, tiles), from_left(even, tiles)

    strips = [got(layer) for layer in range(layers)]
    halos = [halo_ref[i // 2, :, (i % 2) * half : (i % 2 + 1) * half] for i in range(4 if wide else 2)]
    sources = [pooled_ref[x, :, half:] for x in range(2)]

    def near_tiles(order):
        near, beyond = order[0] // 2, order[-1] // 2
        if wide:
            log_rows = [jnp.where(upper, *strips[layer]) for layer in range(layers)]
            source_rows = [turned(jnp.where(upper, *strips[layer][::-1]), REACH, 0) for layer in range(layers)]
            return {
                "log1": join_third(log_rows[order[0]], log_rows[order[2]]),
                "source1": source_rows[order[0]],
                "log2": log_rows[order[1]],
                "source2": source_rows[order[1]],
                "halo0": halos[near],
                "halo1": halos[beyond],
                "halo2": halos[2 + near],
                "halo3": halos[2 + beyond],
                "source": sources[beyond],
            }
        first, second, third = (strips[layer][0] for layer in order[:3])
        place = iota((SUBLANES, lanes), 0)
        right = jnp.where(place == 3, turned(third, 3, 0), jnp.where(place >= 6, turned(second, -2, 0), first))
        left = jnp.where(place == 4, turned(third, -3, 0), jnp.where(place < 2, turned(second, 2, 0), first))
        line = jnp.where(starts, second[4:5], second[3:4])
        lines = jnp.zeros((SUBLANES, LANES), jnp.float32)
        for j in range(lanes // LANES):
            lines = jnp.where(iota(lines.shape, 0) == j, line[:, j * LANES : (j + 1) * LANES], lines)
        return {
            "strip": jnp.where(starts, right, left),
            "halo": join_halo(halos[near], halos[beyond], starts),
            "source": sources[beyond],
            "row": lines,
        }

    forward = list(range(layers))
    layout, _ = near_layout(lanes, wide)
    right, left = near_tiles(forward[::-1]), near_tiles(forward)
    for name, (start, _) in layout.items():
        put(first_ref, start, jnp.where(ix % 2 == 0, right[name], left[name]))
        put(second_ref, start, jnp.where(ix % 2 == 0, left[name], right[name]))


def pack_near(pooled, halos, after, got):
    slots, rows, lanes = got[0].shape
    wide = len(got) == 2
    out = jax.ShapeDtypeStruct((near_layout(lanes, wide)[1] * SUBLANES, LANES), jnp.float32)
    return pl.pallas_call(
        functools.partial(pack_near_kernel, wide),
        out_shape=(out, out),
        in_specs=[VMEM, VMEM, ANY] + [VMEM] * len(got),
        out_specs=(VMEM,) * 2,
        compiler_params=pltpu.CompilerParams(vmem_limit_bytes=8 << 20),
        cost_estimate=pl.CostEstimate(flops=1000000, bytes_accessed=500_000, transcendentals=0),
        name="pack_near",
    )(pooled, halos, after, *got)


def landed_kernel(after_ref, both_ref, pooled_ref, halo_ref, second_ref, first_ref, *refs):
    *got_refs, out_ref, sent_ref, sum_ref = refs
    log_ref, source_ref = parts(both_ref)
    layers, rows, lanes = log_ref.shape
    half = lanes // 2
    even = lax.axis_index("gx") % 2 == 0
    slots = early_slots(layers, rows // SUBLANES, len(got_refs))
    pairs = {}
    for a, ref in enumerate((log_ref, source_ref)):
        for layer in range(layers):
            for i in range(rows // SUBLANES):
                pairs["own", a, layer, i] = edges(ref.at[layer, i * SUBLANES : (i + 1) * SUBLANES])
    for g, ref in enumerate(got_refs):
        for layer in range(layers):
            pairs["got", g, layer] = edges(ref.at[layer])
    for i in range(2):
        for x in range(2):
            columns = slice(x * half, (x + 1) * half)
            pairs["pooled", i, x] = edges(pooled_ref.at[i, :, columns])
            if i < len(got_refs):
                pairs["halo", i, x] = edges(halo_ref.at[i, :, columns])
    pieces = []
    for side, pick in enumerate((from_left, from_right)):

        def block(slot):
            return pick(even, (first_ref[slot], second_ref[slot]))

        for slot in range(2 * layers - 1):
            for i in range(rows // SUBLANES):
                part = slice(i * SUBLANES, (i + 1) * SUBLANES)
                ends = [edges(ref.at[slot, part]) for ref in (first_ref, second_ref)]
                pairs["raw", side, slot, i] = [
                    pick(even, tuple(end[...] for end in both)) for both in zip(*ends)
                ]
        nearest = layers + 1 if side == 0 else layers
        for top in (0, 2, nearest):
            both = block(top) + block(top + 1)
            pieces.append(row_pairs(both[:SUBLANES], both[SUBLANES:], sum_ref))
    tiles = lane_pairs(pieces)
    for side in range(2):
        for i in range(3):
            tile = tiles[3 * side + i] * (0.125 if i < 2 else 1.0)
            put(out_ref, (3 * side + i) * (half // LANES), tile)
            pairs["near", side, i] = edges(tile)
    write_lanes(sent_ref, [tuple(end[...] for end in pairs[key]) for key in slots])


def landed(after, both, pooled, halos, raw, got):
    layers, rows, lanes = both.shape[0] // 2, *both.shape[1:]
    slots = early_slots(layers, rows // SUBLANES, len(got))
    return pl.pallas_call(
        landed_kernel,
        out_shape=(
            jax.ShapeDtypeStruct((6 * (lanes // 2 // LANES) * SUBLANES, LANES), jnp.float32),
            packed_rows(slots),
        ),
        in_specs=[ANY] + [VMEM] * (5 + len(got)),
        out_specs=(VMEM,) * 2,
        scratch_shapes=[pltpu.VMEM((lanes // LANES, 2 * SUBLANES, LANES), jnp.float32)],
        compiler_params=pltpu.CompilerParams(vmem_limit_bytes=16 << 20),
        cost_estimate=pl.CostEstimate(flops=1_000_000, bytes_accessed=1_000_000, transcendentals=0),
        name="landed",
    )(after, both, pooled, halos, *raw[::-1], *got)


def near_part(refs, even, lanes, wide, side, name):
    start, count = near_layout(lanes, wide)[0][name]
    pick = from_left if side == 0 else from_right
    got = pick(even, tuple(take(ref, start, count) for ref in refs))
    return rows_to_lanes(got, lanes // LANES) if name == "row" else got


def far_part(refs, low, lanes, side, i):
    count = lanes // 2 // LANES
    pick = from_left if side == 0 else from_right
    return pick(low, tuple(take(ref, i * count, count) for ref in refs))


def late_kernel(lanes, wide, after_ref, first_ref, second_ref, *refs):
    *far_refs, sent_ref = refs
    even, low = lax.axis_index("gx") % 2 == 0, lax.axis_index("gx") % 4 < 2
    pairs = []
    for side, name in late_slots(lanes, wide):
        if name == "far":
            pairs.append(edges(far_part(far_refs, low, lanes, side, 0)))
        else:
            pairs.append(edges(near_part((first_ref, second_ref), even, lanes, wide, side, name)))
    write_lanes(sent_ref, pairs)


def late_lanes(after, near, far, lanes, wide):
    return pl.pallas_call(
        functools.partial(late_kernel, lanes, wide),
        out_shape=packed_rows(late_slots(lanes, wide)),
        in_specs=[ANY] + [VMEM] * (2 + len(far)),
        out_specs=VMEM,
        compiler_params=pltpu.CompilerParams(vmem_limit_bytes=8 << 20),
        cost_estimate=pl.CostEstimate(flops=1_000_000, bytes_accessed=200_000, transcendentals=0),
        name="late_lanes",
    )(after, *near, *far)


def coarse_kernel(peers, n_far, own_ref, halo_ref, pool_ref, first_ref, second_ref, *refs):
    near_refs, far_refs = (first_ref, second_ref), refs[:n_far]
    early_ref, late_ref, coef_ref, out_ref, wide_ref, *scratch = refs[n_far:]
    ix, iy, iz = (lax.axis_index(axis) for axis in AXES)
    nx, ny, nz = peers
    wide = ny > 2
    fine_lanes = own_ref.shape[2]
    lanes, rows = fine_lanes // 2, SUBLANES
    even, low, starts = ix % 2 == 0, ix % 4 < 2, iy == 0
    top = iota((rows, lanes + LANES), 0) < REACH
    early = early_slots(REACH, 2, 2 if wide else 1)
    late = late_slots(fine_lanes, wide)

    def columns(half):
        return slice(half * lanes, (half + 1) * lanes)

    def with_early(core, *key):
        return jnp.concatenate([core, read_lanes(early_ref, early[key])], axis=1)

    def near(side, name):
        core = near_part(near_refs, even, fine_lanes, wide, side, name)
        return jnp.concatenate([core, read_lanes(late_ref, late[side, name])], axis=1)

    def far(side, i):
        core = far_part(far_refs, low, fine_lanes, side, i)
        return jnp.concatenate([core, read_lanes(late_ref, late[side, "far"])], axis=1)

    def split(tile, a):
        other = turned(tile, REACH, 0)
        return jnp.where(top, tile, other) if a == 0 else jnp.where(top, other, tile)

    def window(a, k):
        block, layer = k // 2 - 2, k % 2
        nearest = layer == (1 if block < 0 else 0)
        side = 0 if block < 0 else 1
        if abs(block) == 2:
            if a == 1:
                core = far(side, 2)
                return jnp.concatenate([core, jnp.zeros_like(core)], axis=0)
            halo = far(side, 3)
            halo = halo if wide else split(halo, 0)
            return jnp.concatenate([far(side, 0 if nearest else 1), halo], axis=0)
        if block == 0:
            core = with_early(own_ref[layer, :, columns(a)], "pooled", layer, a)
            if wide:
                halo = with_early(halo_ref[a, :, columns(layer)], "halo", a, layer)
            else:
                halo = split(with_early(halo_ref[0, :, columns(layer)], "halo", 0, layer), a)
            return jnp.concatenate([core, halo], axis=0)
        if a == 0 or nearest:
            i = layer if a == 0 else 2
            core = take(pool_ref, (3 * side + i) * (lanes // LANES), lanes // LANES)
            core = with_early(core, "near", side, i)
        else:
            core = near(side, "source")
        if wide:
            halo = near(side, f"halo{2 * a + (0 if nearest else 1)}")
        else:
            joined = near(side, "halo")
            halo = split(joined if nearest else beyond_halo(joined, starts), a)
        return jnp.concatenate([core, halo], axis=0)

    def open_face(inside):
        return jnp.where(inside, 4.0, 0.0)

    faces = [4.0] * 9
    faces[1], faces[3] = open_face(ix > 1), open_face(ix > 0)
    faces[5], faces[7] = open_face(ix < nx - 1), open_face(ix < nx - 2)
    *scratch, p_ref = scratch

    def emit(layer, tile, value):
        p_ref[layer * rows : (layer + 1) * rows, tile * LANES : (tile + 1) * LANES] = value

    iterate(
        2 + 2 * REACH,
        rows,
        2 * rows,
        lanes // LANES + 1,
        functools.partial(window, 0),
        functools.partial(window, 1),
        faces,
        row_numerators(2 * rows, rows, iy, ny, 2.0),
        lane_numerators(2 * rows, iz, nz, 2.0) + [4.0],
        coef_ref,
        8.0 * storage_rate,
        emit,
        scratch,
    )
    widen = (iota((lanes, 2 * lanes), 0) == iota((lanes, 2 * lanes), 1) // 2).astype(jnp.bfloat16)
    spread = exact_dot(p_ref[...], widen)
    for x in range(2):
        for tile in range(2 * lanes // LANES):
            part = slice(tile * LANES, (tile + 1) * LANES)
            for half in range(2):
                wide_ref[tile, pl.ds(half, rows, stride=2), :] = spread[x * rows : (x + 1) * rows, part]
            for twin in range(2):
                out_ref[2 * x + twin, :, part] = wide_ref[tile]


def coarse_level(own, halos, pooled, near, far, early, late, coefficients, peers):
    lanes = own.shape[2] // 2
    window = (2 + 2 * REACH, SUBLANES, 2 * SUBLANES, lanes // LANES + 1)
    return pl.pallas_call(
        functools.partial(coarse_kernel, peers, len(far)),
        out_shape=jax.ShapeDtypeStruct((REACH, 2 * SUBLANES, 2 * lanes), jnp.float32),
        in_specs=[VMEM] * (8 + len(far)),
        out_specs=VMEM,
        scratch_shapes=[pltpu.VMEM((2 * lanes // LANES, 2 * SUBLANES, LANES), jnp.float32)]
        + window_scratch(*window)
        + [pltpu.VMEM((2 * SUBLANES, lanes), jnp.float32)],
        compiler_params=pltpu.CompilerParams(vmem_limit_bytes=24 << 20),
        cost_estimate=pl.CostEstimate(flops=20_000_000, bytes_accessed=4_000_000, transcendentals=0),
        name="coarse_level",
    )(own, halos, pooled, *near, *far, early, late, coefficients)


def fine_kernel(peers, n_far, both_ref, *refs):
    log_ref, source_ref = parts(both_ref)
    layers, rows, lanes = log_ref.shape
    ix, iy, iz = (lax.axis_index(axis) for axis in AXES)
    nx, ny, nz = peers
    wide = ny > 2
    n_got = 2 if wide else 1
    got_refs, refs = refs[:n_got], refs[n_got:]
    second_ref, first_ref = refs[:2]
    second_near_ref, first_near_ref, early_ref, late_ref, spread_ref = refs[2 + n_far : 7 + n_far]
    coef_ref, fine_ref, diff_ref, *scratch = refs[7 + n_far :]
    even, starts = ix % 2 == 0, iy == 0
    count = 3 * layers
    upper = iota((SUBLANES, lanes + LANES), 0) < REACH
    early = early_slots(layers, rows // SUBLANES, n_got)
    late = late_slots(lanes, wide)

    def with_early(core, *keys):
        tile = jnp.concatenate([read_lanes(early_ref, early[key]) for key in keys], axis=0)
        return jnp.concatenate([core, tile], axis=1)

    def near(side, name):
        core = near_part((first_near_ref, second_near_ref), even, lanes, wide, side, name)
        return jnp.concatenate([core, read_lanes(late_ref, late[side, name])], axis=1)

    def near_halo(a, side, distance):
        if wide:
            tile = near(side, ("log" if a == 0 else "source") + ("2" if distance == 2 else "1"))
        elif a == 1:
            return near(side, "row") if distance == 2 else turned(near(side, "strip"), REACH, 0)
        else:
            tile = near(side, "strip")
            if distance == 2:
                return jnp.where(starts, turned(tile, 2, 0), turned(tile, -2, 0))
        return third_halo(tile) if a == 0 and distance > 2 else tile

    def window(a, k):
        block, layer = k // layers - 1, k % layers
        if block == 0:
            core = (log_ref, source_ref)[a][layer]
            core = with_early(core, *(("own", a, layer, i) for i in range(rows // SUBLANES)))
            tiles = tuple(with_early(ref[layer], ("got", g, layer)) for g, ref in enumerate(got_refs))
            halo = tiles[0]
            if wide:
                sides = from_right(iy % 2 == 0, tiles), from_left(iy % 2 == 0, tiles)
                halo = jnp.where(upper, *(sides if a == 0 else sides[::-1]))
            if a == 1:
                halo = turned(halo, REACH, 0)
            return jnp.concatenate([core, halo], axis=0)
        side, pick = (0, from_left) if block < 0 else (1, from_right)
        slot = layer if a == 0 else layers + layer - (1 if block < 0 else 0)
        core = pick(even, (first_ref[slot], second_ref[slot]))
        core = with_early(core, *(("raw", side, slot, i) for i in range(rows // SUBLANES)))
        halo = near_halo(a, side, layers - layer if block < 0 else layer + 1)
        return jnp.concatenate([core, halo], axis=0)

    faces = [2.0] * (count - 1)
    faces[layers - 1] = jnp.where(ix > 0, 2.0, 0.0)
    faces[2 * layers - 1] = jnp.where(ix < nx - 1, 2.0, 0.0)

    def emit(layer, tile, value):
        part = slice(tile * LANES, (tile + 1) * LANES)
        fine_ref[layer, :, part] = value
        diff_ref[layer, :, part] = value - spread_ref[layer, :, part]

    iterate(
        count,
        rows,
        rows + 2 * REACH,
        lanes // LANES + 1,
        functools.partial(window, 0),
        functools.partial(window, 1),
        faces,
        row_numerators(rows + 2 * REACH, rows, iy, ny, 1.0),
        lane_numerators(rows + 2 * REACH, iz, nz, 1.0) + [2.0],
        coef_ref,
        storage_rate,
        emit,
        scratch,
    )


def fine_level(both, got, raw, far, near, early, late, spread, coefficients, peers):
    layers, rows, lanes = spread.shape
    window = (layers + 2 * REACH, rows, rows + 2 * REACH, lanes // LANES + 1)
    out = jax.ShapeDtypeStruct(spread.shape, jnp.float32)
    return pl.pallas_call(
        functools.partial(fine_kernel, peers, len(far)),
        out_shape=(out, out),
        in_specs=[VMEM] * (3 + len(got)) + [ANY] * len(far) + [VMEM] * 6,
        out_specs=(VMEM, VMEM),
        scratch_shapes=window_scratch(*window),
        compiler_params=pltpu.CompilerParams(vmem_limit_bytes=24 << 20),
        cost_estimate=pl.CostEstimate(flops=20_000_000, bytes_accessed=10_000_000, transcendentals=0),
        name="fine_level",
    )(both, *got, *raw[::-1], *far, *near[::-1], early, late, spread, coefficients)


def shards(peers, log_perm, source, low_bound, high_bound):
    nx, ny, nz = peers
    layers, rows, lanes = log_perm.shape
    assert layers == REACH and rows == 2 * SUBLANES and nx > 2 and nz == 2
    both = jnp.concatenate([log_perm, source])
    for_second = raw_block(both, True)
    second = permute(for_second, "gx", nx, neighbour_pairs(nx, 1))
    for_first = raw_block(both, False, for_second)
    raw = (permute(for_first, "gx", nx, neighbour_pairs(nx, 0)), second)
    own, *rows_sent = prep(both, for_first, ny)
    if ny == 2:
        got = (permute(rows_sent[0], "gy", ny, [(0, 1)]),)
    else:
        got = swap("gy", ny, rows_sent[1], rows_sent[0])
    far_groups = far_pairs(nx)
    halos, for_far = pack_far(own, got, len(far_groups))
    far = [permute(tiles, "gx", nx, group) for tiles, group in zip(for_far, far_groups)]
    for_first, for_second = pack_near(own, halos, for_far[0], got)
    second = permute(for_second, "gx", nx, neighbour_pairs(nx, 1))
    near = (permute(for_first, "gx", nx, neighbour_pairs(nx, 0)), second)
    coefficients = chebyshev_coefficients(low_bound, high_bound, for_first)
    pooled, early_sent = landed(coefficients, both, own, halos, raw, got)
    early = lax.ppermute(early_sent, "gz", [(0, 1), (1, 0)])
    late_sent = late_lanes(early_sent, near, far, lanes, ny > 2)
    late = lax.ppermute(late_sent, "gz", [(0, 1), (1, 0)])
    spread = coarse_level(own, halos, pooled, near, far, early, late, coefficients, peers)
    return fine_level(both, got, raw, far, near, early, late, spread, coefficients, peers)


def solution(mesh):
    peers = tuple(mesh.shape[axis] for axis in AXES)
    split = P(("groups", "gx"), "gy", "gz")
    return jax.shard_map(
        functools.partial(shards, peers),
        mesh=mesh,
        in_specs=(split, split, P(), P()),
        out_specs=(split, split),
        check_vma=False,
    )
```

```python
import functools

import jax
import jax.numpy as jnp
from jax import lax
from jax.experimental import pallas as pl
from jax.experimental.pallas import tpu as pltpu
from jax.sharding import PartitionSpec as P

DEGREE = 3
REACH = DEGREE + 1
LANES = 128
SUBLANES = 8
storage_rate = 0.1
AXES = ("gx", "gy", "gz")
VMEM = pl.BlockSpec(memory_space=pltpu.VMEM)
ANY = pl.BlockSpec(memory_space=pl.ANY)
HBM = pl.BlockSpec(memory_space=pltpu.HBM)


AHEAD = pl.CostEstimate(flops=50_000_000_000, bytes_accessed=1_000_000, transcendentals=0)


def iota(shape, dim):
    return lax.broadcasted_iota(jnp.int32, shape, dim)


def turned(value, shift, axis):
    size = value.shape[axis]
    return pltpu.roll(value, shift % size, axis)


def permute(value, axis, peers, pairs):
    cores = lax.axis_size("gz")
    if axis == "gz" or cores % 2:
        return lax.ppermute(value, axis, [pair for i, j in pairs for pair in ((i, j), (j, i))])
    partner = {}
    for i, j in pairs:
        partner[i], partner[j] = j, i
    moves = [
        (i * cores + core, partner[i] * cores + core if i in partner else i * cores + (core ^ 1))
        for i in range(peers)
        for core in range(cores)
    ]
    return lax.ppermute(value, (axis, "gz"), moves)


def neighbour_pairs(peers, start):
    return [(i, i + 1) for i in range(start, peers - 1, 2)]


def first_swap(axis, peers, right, left):
    even = lax.axis_index(axis) % 2 == 0
    return permute(jnp.where(even, right, left), axis, peers, neighbour_pairs(peers, 0))


def second_swap(axis, peers, right, left):
    even = lax.axis_index(axis) % 2 == 0
    return permute(jnp.where(even, left, right), axis, peers, neighbour_pairs(peers, 1))


def swap(axis, peers, right, left):
    got = (first_swap(axis, peers, right, left),)
    return got if peers == 2 else got + (second_swap(axis, peers, right, left),)


def far_pairs(peers):
    pairs = [(i, i + 2) for i in range(peers - 2)]
    groups = [[pair for pair in pairs if pair[0] % 4 < 2], [pair for pair in pairs if pair[0] % 4 >= 2]]
    return [group for group in groups if group]


def from_right(is_first, got):
    return got[0] if len(got) == 1 else jnp.where(is_first, got[0], got[1])


def from_left(is_first, got):
    return got[0] if len(got) == 1 else jnp.where(is_first, got[1], got[0])


def inverse(value):
    guess = pl.reciprocal(value, approx=True)
    return guess * (2.0 - value * guess)


def row_numerators(rows, own, index, peers, face_scale):
    place = iota((rows, LANES), 0)
    right = jnp.where(index < peers - 1, 2.0 * face_scale, 0.0)
    left = jnp.where(index > 0, 2.0 * face_scale, 0.0)
    return jnp.where(place == own - 1, right, jnp.where(place == rows - 1, left, 2.0 * face_scale))


def lane_numerators(rows, index, peers, face_scale):
    place = iota((rows, LANES), 1)
    right = jnp.where(index < peers - 1, 2.0 * face_scale, 0.0)
    left = jnp.where(index > 0, 2.0 * face_scale, 0.0)
    return [jnp.where(place == LANES - 1, side, 2.0 * face_scale) for side in (right, left)]


def lane_tiles(value):
    return [value[:, i : i + LANES] for i in range(0, value.shape[1], LANES)]


def beside(tiles, shift):
    moved = [turned(tile, shift, 1) for tile in tiles]
    lane = iota(tiles[0].shape, 1)
    seam = LANES - 1 if shift < 0 else 0
    return [
        jnp.where(lane == seam, moved[(j - shift) % len(tiles)], moved[j]) for j in range(len(tiles))
    ]


def store_rows(ref, k, j, value):
    rows = value.shape[0]
    ref[k, j, SUBLANES : SUBLANES + rows] = value
    ref[k, j, SUBLANES - 1 : SUBLANES] = value[rows - 1 :]
    ref[k, j, SUBLANES + rows : SUBLANES + rows + 1] = value[:1]


def iterate(count, own_rows, rows, tiles, log_at, source_at, x_faces, y_top, z_top, coef_ref, storage, emit, refs):
    k_ref, tx_ref, ty_ref, tzr_ref, tzl_ref, diag_ref, w_ref, d_ref, r_ref, p_ref = refs
    own_tiles = tiles - 1

    def away(k):
        return max(0, REACH - k, k - (count - 1 - REACH))

    def extent(k, step):
        left = DEGREE - step - away(k)
        return None if left < 0 else (own_rows, own_tiles) if left == 0 else (rows, tiles)

    def coefficient(i, size):
        return jnp.concatenate([coef_ref[i]] * (size // SUBLANES), axis=0)

    z_tops = [z_top[0] if j == own_tiles - 1 else z_top[1] if j == own_tiles else None for j in range(tiles)]

    def resistance(k):
        return [jnp.exp(-tile) for tile in lane_tiles(log_at(k))]

    after = resistance(0)
    tx_before = None
    for k in range(count):
        here = after
        if k + 1 < count:
            after = resistance(k + 1)
            outer = max(away(k), away(k + 1))
            size, number = (rows, tiles) if outer < REACH else (own_rows, own_tiles)
            tx = [x_faces[k] * inverse(here[j][:size] + after[j][:size]) for j in range(number)]
            for j in range(number):
                tx_ref[k, j, :size] = tx[j]
        if away(k) <= DEGREE:
            size, number = extent(k, 0)
            right = beside(here, -1)
            tz = []
            for j in range(tiles):
                scale = z_tops[j][:size] if z_tops[j] is not None else z_top[2]
                tz.append(scale * inverse(here[j][:size] + right[j][:size]))
            tz_left = beside(tz, 1)
            source = lane_tiles(source_at(k))
            for j in range(number):
                store_rows(k_ref, k, j, here[j])
                ty = y_top * inverse(here[j] + k_ref[k, j, SUBLANES + 1 : SUBLANES + 1 + rows])
                store_rows(ty_ref, k, j, ty)
                ty_before = ty_ref[k, j, SUBLANES - 1 : SUBLANES - 1 + size]
                diagonal = storage + (tx_before[j][:size] + tx[j][:size])
                diagonal = diagonal + (ty[:size] + ty_before) + (tz[j] + tz_left[j])
                w = inverse(diagonal)
                direction = source[j][:size] * (coefficient(0, size) * w)
                if (size, number) == (rows, tiles):
                    store_rows(d_ref.at[0], k, j, direction)
                else:
                    d_ref[0, k, j, SUBLANES : SUBLANES + size] = direction
                if extent(k, 1) is not None:
                    tzr_ref[k, j, :size] = tz[j]
                    tzl_ref[k, j, :size] = tz_left[j]
                    diag_ref[k, j, :size] = diagonal
                    w_ref[k, j, :size] = w
                    r_ref[k, j, :size] = source[j][:size]
        tx_before = tx
    for step in range(1, DEGREE + 1):
        old, new = d_ref.at[(step - 1) % 2], d_ref.at[step % 2]
        for k in range(count):
            if extent(k, step) is None:
                continue
            size, number = extent(k, step)
            middle = slice(SUBLANES, SUBLANES + size)
            keep, gain = coefficient(2 * step - 1, size), coefficient(2 * step, size)
            here = [old[k, j, middle] for j in range(tiles)]
            right, left = beside(here, -1), beside(here, 1)
            for j in range(number):
                applied = tx_ref[k, j, :size] * old[k + 1, j, middle] + tx_ref[k - 1, j, :size] * old[k - 1, j, middle]
                applied += (
                    ty_ref[k, j, middle] * old[k, j, SUBLANES + 1 : SUBLANES + 1 + size]
                    + ty_ref[k, j, SUBLANES - 1 : SUBLANES - 1 + size] * old[k, j, SUBLANES - 1 : SUBLANES - 1 + size]
                )
                applied += tzr_ref[k, j, :size] * right[j] + tzl_ref[k, j, :size] * left[j]
                residual = r_ref[k, j, :size] - (diag_ref[k, j, :size] * here[j] - applied)
                fresh = keep * here[j] + gain * (residual * w_ref[k, j, :size])
                if away(k) == 0 and j < own_tiles:
                    so_far = here[j][:own_rows] if step == 1 else p_ref[k, j]
                    total = so_far + fresh[:own_rows]
                    if step == DEGREE:
                        emit(k - REACH, j, total)
                    else:
                        p_ref[k, j] = total
                if step < DEGREE:
                    r_ref[k, j, :size] = residual
                    if (size, number) == (rows, tiles):
                        store_rows(new, k, j, fresh)
                    else:
                        new[k, j, middle] = fresh


def coefficients_kernel(low_ref, high_ref, after_ref, coef_ref, bounds_ref, sems):
    copies = [
        pltpu.make_async_copy(ref, bounds_ref.at[i], sems.at[i]) for i, ref in enumerate((low_ref, high_ref))
    ]
    for copy in copies:
        copy.start()
    for copy in copies:
        copy.wait()
    low, high = (jnp.full((SUBLANES, LANES), bounds_ref[i, 0]) for i in range(2))
    theta, delta = (high + low) * 0.5, (high - low) * 0.5
    sigma = theta / delta
    rho = 1.0 / sigma
    coef_ref[0] = 1.0 / theta
    for step in range(DEGREE):
        rho_next = 1.0 / (2.0 * sigma - rho)
        coef_ref[1 + 2 * step] = rho_next * rho
        coef_ref[2 + 2 * step] = 2.0 * rho_next / delta
        rho = rho_next


def chebyshev_coefficients(low_bound, high_bound, after):
    return pl.pallas_call(
        coefficients_kernel,
        out_shape=jax.ShapeDtypeStruct((1 + 2 * DEGREE, SUBLANES, LANES), jnp.float32),
        in_specs=[HBM] * 2 + [ANY],
        out_specs=VMEM,
        scratch_shapes=[pltpu.SMEM((2, 1), jnp.float32), pltpu.SemaphoreType.DMA((2,))],
        compiler_params=pltpu.CompilerParams(vmem_limit_bytes=4 << 20),
        cost_estimate=pl.CostEstimate(flops=1_000_000, bytes_accessed=100_000, transcendentals=0),
        name="coefficients",
    )(low_bound, high_bound, after)


def put(ref, tile, value):
    for i in range(value.shape[1] // LANES):
        ref[(tile + i) * SUBLANES : (tile + i + 1) * SUBLANES, :] = value[:, i * LANES : (i + 1) * LANES]


def take(ref, tile, count):
    tiles = [ref[(tile + i) * SUBLANES : (tile + i + 1) * SUBLANES, :] for i in range(count)]
    return tiles[0] if count == 1 else jnp.concatenate(tiles, axis=1)


def edges(value):
    lanes = value.shape[-1]
    value = value if isinstance(value, jax.Array) else value.at
    return value[:, lanes - LANES :], value[:, :LANES]


def write_lanes(pairs):
    starts = lax.axis_index("gz") == 0
    each = LANES // REACH
    group = iota((SUBLANES, LANES), 1) // REACH
    merged = None
    for j, (last, first) in enumerate(pairs):
        moved = turned(jnp.where(starts, last, first), REACH * j, 1)
        place = jnp.where(starts, (j - 1) % each, j)
        merged = moved if merged is None else jnp.where(group == place, moved, merged)
    return merged


def read_lanes(tile, slot):
    return turned(tile, -REACH * slot, 1)


def add_lanes(tile, slot, value):
    starts = lax.axis_index("gz") == 0
    group = iota((SUBLANES, LANES), 1) // REACH
    place = jnp.where(starts, slot, (slot - 1) % (LANES // REACH))
    return jnp.where(group == place, turned(value, REACH * slot, 1), tile)


def lane_slots(layers, row_tiles, n_got):
    keys = [("own", a, layer, i) for a in range(2) for layer in range(layers) for i in range(row_tiles)]
    keys += [("pooled", x, a) for x in range(2) for a in range(2)]
    shared = len(keys)
    keys += [("halo", i, half) for i in range(n_got) for half in range(2)]
    keys += [("got", g, layer) for g in range(n_got) for layer in range(layers)]
    return {key: i for i, key in enumerate(keys)}, shared


def near_layout(lanes, wide):
    whole, half = lanes // LANES, lanes // LANES // 2
    if wide:
        parts = [("log1", whole), ("source1", whole), ("log2", whole), ("source2", whole)]
        parts += [(name, half) for name in ("halo0", "halo1", "halo2", "halo3", "source")]
    else:
        parts = [("strip", whole), ("halo", half), ("source", half), ("row", 1)]
    layout, start = {}, 0
    for name, count in parts + [("lanes", 1)]:
        layout[name] = (start, count)
        start += count
    return layout, start


def near_lane_slots(lanes, wide, shared):
    names = [name for name in near_layout(lanes, wide)[0] if name not in ("source", "lanes")]
    return {name: shared + i for i, name in enumerate(names)}


def rows_to_lanes(row_tile, count):
    return jnp.concatenate(
        [jnp.broadcast_to(row_tile[j : j + 1], (SUBLANES, LANES)) for j in range(count)], axis=1
    )


def window_scratch(count, own_rows, rows, tiles):
    plain = pltpu.VMEM((count, tiles, rows, LANES), jnp.float32)
    margins = pltpu.VMEM((count, tiles, rows + 2 * SUBLANES, LANES), jnp.float32)
    pair = pltpu.VMEM((2, count, tiles, rows + 2 * SUBLANES, LANES), jnp.float32)
    total = pltpu.VMEM((count, tiles, own_rows, LANES), jnp.float32)
    return [margins, plain, margins, plain, plain, plain, plain, pair, plain, total]


def exact_dot(value, zero_one):
    parts = []
    for _ in range(3):
        part = value.astype(jnp.bfloat16)
        parts.append(part)
        value = value - part.astype(jnp.float32)
    rows = value.shape[0]
    out = jnp.dot(jnp.concatenate(parts, axis=0), zero_one, preferred_element_type=jnp.float32)
    return (out[2 * rows :] + out[rows : 2 * rows]) + out[:rows]


def row_pairs(top, bottom, sum_ref):
    tiles = top.shape[1] // LANES
    for tile in range(tiles):
        columns = slice(tile * LANES, (tile + 1) * LANES)
        sum_ref[tile, :SUBLANES] = top[:, columns]
        sum_ref[tile, SUBLANES:] = bottom[:, columns]
    return jnp.concatenate(
        [
            sum_ref[tile, pl.ds(0, SUBLANES, stride=2), :] + sum_ref[tile, pl.ds(1, SUBLANES, stride=2), :]
            for tile in range(tiles)
        ],
        axis=1,
    )


def lane_pairs(pieces):
    lanes = pieces[0].shape[1]
    pick = (iota((lanes, lanes // 2), 0) // 2 == iota((lanes, lanes // 2), 1)).astype(jnp.bfloat16)
    pooled = exact_dot(jnp.concatenate(pieces, axis=0), pick)
    return [pooled[SUBLANES * i : SUBLANES * (i + 1)] for i in range(len(pieces))]


def join_halo(near, beyond, starts):
    row = iota(near.shape, 0)
    up, down = turned(beyond, 3, 0), turned(beyond, -3, 0)
    right = jnp.where((row == 3) | (row == 7), up, jnp.where(row == 6, turned(beyond, 5, 0), near))
    left = jnp.where((row == 0) | (row == 4), down, jnp.where(row == 5, up, near))
    return jnp.where(starts, right, left)


def beyond_halo(joined, starts):
    row = iota(joined.shape, 0)
    up, down = turned(joined, 3, 0), turned(joined, -3, 0)
    right = jnp.where(row == 1, turned(joined, -5, 0), down)
    left = jnp.where(row == 2, down, up)
    return jnp.where(starts, right, left)


def join_third(near, third):
    row = iota(near.shape, 0)
    return jnp.where(
        row == 3, turned(third, 3, 0), jnp.where(row == 4, turned(third, -3, 0), near)
    )


def third_halo(joined):
    return jnp.where(iota(joined.shape, 0) < REACH, turned(joined, -3, 0), turned(joined, 3, 0))


def parts(both_ref):
    layers = both_ref.shape[0] // 2
    return both_ref.at[:layers], both_ref.at[layers:]


def prep_kernel(both_ref, pooled_ref, *refs):
    *out_refs, sum_ref = refs
    log_ref, source_ref = parts(both_ref)
    layers, rows, lanes = log_ref.shape
    starts = lax.axis_index("gy") == 0

    def put(slot, left, right):
        if len(out_refs) == 1:
            out_refs[0][slot] = jnp.where(starts, right, left)
        else:
            out_refs[0][slot], out_refs[1][slot] = left, right

    half = lanes // 2
    upper = iota((SUBLANES, lanes), 0) < REACH
    pieces = []
    for x in range(2):
        for ref in (log_ref, source_ref):
            both = ref[2 * x] + ref[2 * x + 1]
            pieces.append(row_pairs(both[:SUBLANES], both[SUBLANES:], sum_ref))
    log0, source0, log1, source1 = lane_pairs(pieces)
    log0, log1 = log0 * 0.125, log1 * 0.125
    pooled_ref[0] = jnp.concatenate([log0, source0], axis=1)
    pooled_ref[1] = jnp.concatenate([log1, source1], axis=1)
    for layer in range(layers):
        put(
            layer,
            jnp.where(upper, log_ref[layer, :SUBLANES], turned(source_ref[layer, :SUBLANES], REACH, 0)),
            jnp.where(upper, turned(source_ref[layer, SUBLANES:], REACH, 0), log_ref[layer, SUBLANES:]),
        )
    pair = iota((SUBLANES, half), 0) // 2

    def four(*tiles):
        merged = jnp.where(
            pair == 0, tiles[0], jnp.where(pair == 1, tiles[1], jnp.where(pair == 2, tiles[2], tiles[3]))
        )
        return jnp.concatenate([merged, merged], axis=1)

    put(
        layers,
        four(turned(log1, -2, 0), log0, turned(source1, 2, 0), turned(source0, 4, 0)),
        four(turned(log0, -4, 0), turned(log1, -2, 0), source0, turned(source1, 2, 0)),
    )


def prep(both, ny):
    layers, rows, lanes = both.shape[0] // 2, *both.shape[1:]
    outs = 1 if ny == 2 else 2

    def tiles(count):
        return jax.ShapeDtypeStruct((count, SUBLANES, lanes), jnp.float32)

    return pl.pallas_call(
        prep_kernel,
        out_shape=(tiles(2),) + (tiles(layers + 1),) * outs,
        in_specs=[VMEM],
        out_specs=(VMEM,) * (1 + outs),
        scratch_shapes=[pltpu.VMEM((lanes // LANES, 2 * SUBLANES, LANES), jnp.float32)],
        compiler_params=pltpu.CompilerParams(vmem_limit_bytes=8 << 20),
        cost_estimate=pl.CostEstimate(flops=5_000_000, bytes_accessed=700_000, transcendentals=0),
        name="prep",
    )(both)


def raw_kernel(to_right_if_odd, both_ref, after_ref, out_ref):
    log_ref, source_ref = parts(both_ref)
    layers = log_ref.shape[0]
    odd = lax.axis_index("gx") % 2
    skip = odd if to_right_if_odd else 1 - odd
    for layer in range(layers):
        out_ref[layer] = log_ref[layer]
    for layer in range(layers - 1):
        out_ref[layers + layer] = source_ref[layer + skip]


def raw_block(both, after, to_right_if_odd):
    layers, rows, lanes = both.shape[0] // 2, *both.shape[1:]
    return pl.pallas_call(
        functools.partial(raw_kernel, to_right_if_odd),
        out_shape=jax.ShapeDtypeStruct((2 * layers - 1, rows, lanes), jnp.float32),
        in_specs=[VMEM, ANY],
        out_specs=VMEM,
        compiler_params=pltpu.CompilerParams(vmem_limit_bytes=8 << 20),
        cost_estimate=pl.CostEstimate(flops=1_000_000, bytes_accessed=500_000, transcendentals=0),
        name="raw_block",
    )(both, after)


def halos_kernel(wide, both_ref, pooled_ref, *refs):
    *got_refs, halo_ref, sent_ref, sum_ref = refs
    layers, lanes = got_refs[0].shape[0] - 1, got_refs[0].shape[2]
    iy = lax.axis_index("gy")
    even, starts = iy % 2 == 0, iy == 0
    half = lanes // 2
    upper = iota((SUBLANES, lanes), 0) < REACH
    row = iota((SUBLANES, half), 0)

    def got(slot):
        tiles = tuple(ref[slot] for ref in got_refs)
        return from_right(even, tiles), from_left(even, tiles)

    strips = [got(layer) for layer in range(layers)]
    extra = [tile[:, :half] for tile in got(layers)]
    pieces = []
    for side in range(2 if wide else 1):
        both = [strips[2 * x][side] + strips[2 * x + 1][side] for x in range(2)]
        pieces.append(row_pairs(*both, sum_ref))
    fine_rows = lane_pairs(pieces)

    def right_halos(rows, extra):
        rows = jnp.where(row % 4 < 2, rows * 0.125, rows)
        return [
            jnp.where(row < 2, near, jnp.where((row == 4) | (row == 5), far, more))
            for near, far, more in (
                (rows, turned(rows, 2, 0), extra),
                (turned(rows, 4, 0), turned(rows, -2, 0), turned(extra, 2, 0)),
            )
        ]

    def left_halos(rows, extra):
        rows = jnp.where(row % 4 >= 2, rows * 0.125, rows)
        return [
            jnp.where((row == 2) | (row == 3), near, jnp.where(row >= 6, far, more))
            for near, far, more in (
                (rows, turned(rows, -2, 0), extra),
                (turned(rows, 4, 0), turned(rows, 2, 0), turned(extra, -2, 0)),
            )
        ]

    right, left = right_halos(fine_rows[0], extra[0]), left_halos(fine_rows[-1], extra[1])
    if wide:
        top = row < REACH
        halos = [jnp.where(top, right[x], turned(left[x], REACH, 0)) for x in range(2)]
        halos += [jnp.where(top, turned(right[x], REACH, 0), left[x]) for x in range(2)]
    else:
        halos = [jnp.where(starts, right[x], left[x]) for x in range(2)]

    def pair(left, right):
        return jnp.concatenate([left, right], axis=1)

    for i in range(len(halos) // 2):
        halo_ref[i] = pair(halos[2 * i], halos[2 * i + 1])
    pairs = {}
    rows = both_ref.shape[1]
    for a, ref in enumerate(parts(both_ref)):
        for layer in range(layers):
            for i in range(rows // SUBLANES):
                pairs["own", a, layer, i] = edges(ref[layer, i * SUBLANES : (i + 1) * SUBLANES])
    for x in range(2):
        for a in range(2):
            pairs["pooled", x, a] = edges(pooled_ref[x, :, a * half : (a + 1) * half])
    for i, halo in enumerate(halos):
        pairs["halo", i // 2, i % 2] = edges(halo)
    for g, ref in enumerate(got_refs):
        for layer in range(layers):
            pairs["got", g, layer] = edges(ref[layer])
    slots, _ = lane_slots(layers, rows // SUBLANES, len(got_refs))
    sent_ref[...] = write_lanes([pairs[key] for key in slots])


def pooled_halos(both, pooled, got):
    slots, rows, lanes = got[0].shape
    return pl.pallas_call(
        functools.partial(halos_kernel, len(got) == 2),
        out_shape=(
            jax.ShapeDtypeStruct((len(got), SUBLANES, lanes), jnp.float32),
            jax.ShapeDtypeStruct((SUBLANES, LANES), jnp.float32),
        ),
        in_specs=[VMEM] * (2 + len(got)),
        out_specs=(VMEM,) * 2,
        scratch_shapes=[pltpu.VMEM((lanes // LANES, 2 * SUBLANES, LANES), jnp.float32)],
        compiler_params=pltpu.CompilerParams(vmem_limit_bytes=8 << 20),
        cost_estimate=AHEAD,
        name="halos",
    )(both, pooled, *got)


def pack_far_kernel(wide, pooled_ref, halo_ref, lanes_ref, *far_refs):
    half = pooled_ref.shape[2] // 2
    low = lax.axis_index("gx") % 4 < 2

    def tiles(inner):
        return (
            pooled_ref[inner, :, :half],
            pooled_ref[1 - inner, :, :half],
            pooled_ref[inner, :, half:],
            halo_ref[0, :, inner * half : (inner + 1) * half],
        )

    for group, ref in enumerate(far_refs):
        for i, (right, left) in enumerate(zip(tiles(1), tiles(0))):
            put(ref, i * (half // LANES), jnp.where(low, *((right, left) if group == 0 else (left, right))))
        put(ref, 4 * (half // LANES), lanes_ref[...])
        for spare in range(4 * (half // LANES) + 1, ref.shape[0] // SUBLANES):
            put(ref, spare, jnp.zeros((SUBLANES, LANES), jnp.float32))


def pack_far(pooled, halos, early, n_far, wide):
    _, rows, lanes = pooled.shape
    far_rows = max(2 * lanes // LANES + 1, 0 if wide else near_layout(lanes, wide)[1]) * SUBLANES
    return pl.pallas_call(
        functools.partial(pack_far_kernel, wide),
        out_shape=(jax.ShapeDtypeStruct((far_rows, LANES), jnp.float32),) * n_far,
        in_specs=[VMEM] * 3,
        out_specs=(VMEM,) * n_far,
        compiler_params=pltpu.CompilerParams(vmem_limit_bytes=8 << 20),
        cost_estimate=pl.CostEstimate(flops=1_000_000, bytes_accessed=500_000, transcendentals=0),
        name="pack_far",
    )(pooled, halos, early)


def pack_near_kernel(wide, pooled_ref, halo_ref, early_ref, after_ref, *refs):
    *got_refs, first_ref, second_ref = refs
    layers, lanes = got_refs[0].shape[0] - 1, got_refs[0].shape[2]
    ix, iy = lax.axis_index("gx"), lax.axis_index("gy")
    even, starts = iy % 2 == 0, iy == 0
    half = lanes // 2
    upper = iota((SUBLANES, lanes), 0) < REACH

    def got(slot):
        tiles = tuple(ref[slot] for ref in got_refs)
        return from_right(even, tiles), from_left(even, tiles)

    strips = [got(layer) for layer in range(layers)]
    halos = [halo_ref[i // 2, :, (i % 2) * half : (i % 2 + 1) * half] for i in range(4 if wide else 2)]
    sources = [pooled_ref[x, :, half:] for x in range(2)]

    slots, shared = lane_slots(layers, 2, len(got_refs))

    def strip_lanes(layer):
        tiles = tuple(read_lanes(early_ref[...], slots["got", g, layer]) for g in range(len(got_refs)))
        return from_right(even, tiles), from_left(even, tiles)

    def halo_lanes(i):
        return read_lanes(early_ref[...], slots["halo", i // 2, i % 2])

    def near_tiles(order, strips, halos):
        near, beyond = order[0] // 2, order[-1] // 2
        width = strips[0][0].shape[1]
        upper = iota((SUBLANES, width), 0) < REACH
        if wide:
            log_rows = [jnp.where(upper, *strips[layer]) for layer in range(layers)]
            source_rows = [turned(jnp.where(upper, *strips[layer][::-1]), REACH, 0) for layer in range(layers)]
            return {
                "log1": join_third(log_rows[order[0]], log_rows[order[2]]),
                "source1": source_rows[order[0]],
                "log2": log_rows[order[1]],
                "source2": source_rows[order[1]],
                "halo0": halos[near],
                "halo1": halos[beyond],
                "halo2": halos[2 + near],
                "halo3": halos[2 + beyond],
            }
        first, second, third = (strips[layer][0] for layer in order[:3])
        place = iota((SUBLANES, width), 0)
        right = jnp.where(place == 3, turned(third, 3, 0), jnp.where(place >= 6, turned(second, -2, 0), first))
        left = jnp.where(place == 4, turned(third, -3, 0), jnp.where(place < 2, turned(second, 2, 0), first))
        line = jnp.where(starts, second[4:5], second[3:4])
        if width == LANES:
            lines = jnp.broadcast_to(line, (SUBLANES, LANES))
        else:
            lines = jnp.zeros((SUBLANES, LANES), jnp.float32)
            for j in range(width // LANES):
                lines = jnp.where(iota(lines.shape, 0) == j, line[:, j * LANES : (j + 1) * LANES], lines)
        return {
            "strip": jnp.where(starts, right, left),
            "halo": join_halo(halos[near], halos[beyond], starts),
            "row": lines,
        }

    def side(order):
        tiles = near_tiles(order, strips, halos)
        tiles["source"] = sources[order[-1] // 2]
        lanes_tile = early_ref[...]
        n_halos = 4 if wide else 2
        beside = near_tiles(
            order, [strip_lanes(layer) for layer in range(layers)], [halo_lanes(i) for i in range(n_halos)]
        )
        for name, slot in near_lane_slots(lanes, wide, shared).items():
            lanes_tile = add_lanes(lanes_tile, slot, beside[name])
        tiles["lanes"] = lanes_tile
        return tiles

    forward = list(range(layers))
    layout, _ = near_layout(lanes, wide)
    right, left = side(forward[::-1]), side(forward)
    for name, (start, _) in layout.items():
        put(first_ref, start, jnp.where(ix % 2 == 0, right[name], left[name]))
        put(second_ref, start, jnp.where(ix % 2 == 0, left[name], right[name]))


def pack_near(pooled, halos, early, after, got):
    slots, rows, lanes = got[0].shape
    wide = len(got) == 2
    out = jax.ShapeDtypeStruct((near_layout(lanes, wide)[1] * SUBLANES, LANES), jnp.float32)
    return pl.pallas_call(
        functools.partial(pack_near_kernel, wide),
        out_shape=(out, out),
        in_specs=[VMEM] * 3 + [ANY] + [VMEM] * len(got),
        out_specs=(VMEM,) * 2,
        compiler_params=pltpu.CompilerParams(vmem_limit_bytes=8 << 20),
        cost_estimate=pl.CostEstimate(flops=1_000_000, bytes_accessed=500_000, transcendentals=0),
        name="pack_near",
    )(pooled, halos, early, after, *got)


def pool_kernel(after_ref, first_ref, second_ref, out_ref, sum_ref):
    layers = REACH
    even = lax.axis_index("gx") % 2 == 0
    pieces = []
    for side, pick in enumerate((from_left, from_right)):

        def block(slot):
            return pick(even, (first_ref[slot], second_ref[slot]))

        for top in (0, 2, layers + 1 if side == 0 else layers):
            both = block(top) + block(top + 1)
            pieces.append(row_pairs(both[:SUBLANES], both[SUBLANES:], sum_ref))
    for i, tile in enumerate(lane_pairs(pieces)):
        put(out_ref, i * (tile.shape[1] // LANES), tile * (0.125 if i % 3 < 2 else 1.0))


def pool(after, raw):
    _, rows, lanes = raw[0].shape
    return pl.pallas_call(
        pool_kernel,
        out_shape=jax.ShapeDtypeStruct((6 * (lanes // 2 // LANES) * SUBLANES, LANES), jnp.float32),
        in_specs=[ANY] + [VMEM] * 2,
        out_specs=VMEM,
        scratch_shapes=[pltpu.VMEM((lanes // LANES, 2 * SUBLANES, LANES), jnp.float32)],
        compiler_params=pltpu.CompilerParams(vmem_limit_bytes=16 << 20),
        cost_estimate=pl.CostEstimate(flops=1_000_000, bytes_accessed=1_000_000, transcendentals=0),
        name="pool",
    )(after, *raw)


def near_part(refs, even, lanes, wide, side, name):
    start, count = near_layout(lanes, wide)[0][name]
    pick = from_left if side == 0 else from_right
    got = pick(even, tuple(take(ref, start, count) for ref in refs))
    return rows_to_lanes(got, lanes // LANES) if name == "row" else got


def far_part(refs, low, lanes, side, i):
    count = lanes // 2 // LANES
    pick = from_left if side == 0 else from_right
    return pick(low, tuple(take(ref, i * count, count) for ref in refs))


def coarse_kernel(peers, n_far, own_ref, halo_ref, pool_ref, first_ref, second_ref, *refs):
    near_refs, far_refs = (first_ref, second_ref), refs[:n_far]
    early_ref, coef_ref, out_ref, wide_ref, *scratch = refs[n_far:]
    ix, iy, iz = (lax.axis_index(axis) for axis in AXES)
    nx, ny, nz = peers
    wide = ny > 2
    fine_lanes = own_ref.shape[2]
    lanes, rows = fine_lanes // 2, SUBLANES
    even, low, starts = ix % 2 == 0, ix % 4 < 2, iy == 0
    top = iota((rows, lanes + LANES), 0) < REACH
    slots, shared = lane_slots(REACH, 2, 2 if wide else 1)
    near_slots = near_lane_slots(fine_lanes, wide, shared)
    own_lanes = early_ref[...]
    near_lanes = [near_part(near_refs, even, fine_lanes, wide, side, "lanes") for side in range(2)]
    far_lanes = [
        pick(low, tuple(take(ref, 4 * (lanes // LANES), 1) for ref in far_refs))
        for pick in (from_left, from_right)
    ]

    def columns(half):
        return slice(half * lanes, (half + 1) * lanes)

    def join(core, tile, slot):
        return jnp.concatenate([core, read_lanes(tile, slot)], axis=1)

    def near(side, name):
        core = near_part(near_refs, even, fine_lanes, wide, side, name)
        return join(core, near_lanes[side], near_slots[name])

    def far(side, i):
        core = far_part(far_refs, low, fine_lanes, side, i)
        return join(core, far_lanes[side], slots["pooled", 1 - side, 0])

    def split(tile, a):
        other = turned(tile, REACH, 0)
        return jnp.where(top, tile, other) if a == 0 else jnp.where(top, other, tile)

    def window(a, k):
        block, layer = k // 2 - 2, k % 2
        nearest = layer == (1 if block < 0 else 0)
        side = 0 if block < 0 else 1
        if abs(block) == 2:
            if a == 1:
                core = far(side, 2)
                return jnp.concatenate([core, jnp.zeros_like(core)], axis=0)
            halo = far(side, 3)
            halo = halo if wide else split(halo, 0)
            return jnp.concatenate([far(side, 0 if nearest else 1), halo], axis=0)
        if block == 0:
            core = join(own_ref[layer, :, columns(a)], own_lanes, slots["pooled", layer, a])
            if wide:
                halo = join(halo_ref[a, :, columns(layer)], own_lanes, slots["halo", a, layer])
            else:
                halo = split(join(halo_ref[0, :, columns(layer)], own_lanes, slots["halo", 0, layer]), a)
            return jnp.concatenate([core, halo], axis=0)
        if a == 0 or nearest:
            i = layer if a == 0 else 2
            core = take(pool_ref, (3 * side + i) * (lanes // LANES), lanes // LANES)
        else:
            core = near_part(near_refs, even, fine_lanes, wide, side, "source")
        core = join(core, near_lanes[side], slots["pooled", layer, a])
        if wide:
            halo = near(side, f"halo{2 * a + (0 if nearest else 1)}")
        else:
            joined = near(side, "halo")
            halo = split(joined if nearest else beyond_halo(joined, starts), a)
        return jnp.concatenate([core, halo], axis=0)

    def open_face(inside):
        return jnp.where(inside, 4.0, 0.0)

    faces = [4.0] * 9
    faces[1], faces[3] = open_face(ix > 1), open_face(ix > 0)
    faces[5], faces[7] = open_face(ix < nx - 1), open_face(ix < nx - 2)
    *scratch, p_ref = scratch

    def emit(layer, tile, value):
        p_ref[layer * rows : (layer + 1) * rows, tile * LANES : (tile + 1) * LANES] = value

    iterate(
        2 + 2 * REACH,
        rows,
        2 * rows,
        lanes // LANES + 1,
        functools.partial(window, 0),
        functools.partial(window, 1),
        faces,
        row_numerators(2 * rows, rows, iy, ny, 2.0),
        lane_numerators(2 * rows, iz, nz, 2.0) + [4.0],
        coef_ref,
        8.0 * storage_rate,
        emit,
        scratch,
    )
    widen = (iota((lanes, 2 * lanes), 0) == iota((lanes, 2 * lanes), 1) // 2).astype(jnp.bfloat16)
    spread = exact_dot(p_ref[...], widen)
    for x in range(2):
        for tile in range(2 * lanes // LANES):
            part = slice(tile * LANES, (tile + 1) * LANES)
            for half in range(2):
                wide_ref[tile, pl.ds(half, rows, stride=2), :] = spread[x * rows : (x + 1) * rows, part]
            for twin in range(2):
                out_ref[2 * x + twin, :, part] = wide_ref[tile]


def coarse_level(own, halos, pooled, near, far, early, coefficients, peers):
    lanes = own.shape[2] // 2
    window = (2 + 2 * REACH, SUBLANES, 2 * SUBLANES, lanes // LANES + 1)
    return pl.pallas_call(
        functools.partial(coarse_kernel, peers, len(far)),
        out_shape=jax.ShapeDtypeStruct((REACH, 2 * SUBLANES, 2 * lanes), jnp.float32),
        in_specs=[VMEM] * (7 + len(far)),
        out_specs=VMEM,
        scratch_shapes=[pltpu.VMEM((2 * lanes // LANES, 2 * SUBLANES, LANES), jnp.float32)]
        + window_scratch(*window)
        + [pltpu.VMEM((2 * SUBLANES, lanes), jnp.float32)],
        compiler_params=pltpu.CompilerParams(vmem_limit_bytes=24 << 20),
        cost_estimate=pl.CostEstimate(flops=20_000_000, bytes_accessed=4_000_000, transcendentals=0),
        name="coarse_level",
    )(own, halos, pooled, *near, *far, early, coefficients)


def fine_kernel(peers, n_far, both_ref, *refs):
    log_ref, source_ref = parts(both_ref)
    layers, rows, lanes = log_ref.shape
    ix, iy, iz = (lax.axis_index(axis) for axis in AXES)
    nx, ny, nz = peers
    wide = ny > 2
    n_got = 2 if wide else 1
    got_refs, refs = refs[:n_got], refs[n_got:]
    second_ref, first_ref = refs[:2]
    second_near_ref, first_near_ref, early_ref, spread_ref = refs[2 + n_far : 6 + n_far]
    near_refs = first_near_ref, second_near_ref
    coef_ref, fine_ref, diff_ref, *scratch = refs[6 + n_far :]
    even, starts = ix % 2 == 0, iy == 0
    count = 3 * layers
    upper = iota((SUBLANES, lanes + LANES), 0) < REACH
    slots, shared = lane_slots(layers, rows // SUBLANES, n_got)
    near_slots = near_lane_slots(lanes, wide, shared)
    own_lanes = early_ref[...]
    near_lanes = [near_part(near_refs, even, lanes, wide, side, "lanes") for side in range(2)]

    def join(core, tile, *keys):
        beside = jnp.concatenate([read_lanes(tile, key) for key in keys], axis=0)
        return jnp.concatenate([core, beside], axis=1)

    def near(side, name):
        return join(near_part(near_refs, even, lanes, wide, side, name), near_lanes[side], near_slots[name])

    def near_halo(a, side, distance):
        if wide:
            tile = near(side, ("log" if a == 0 else "source") + ("2" if distance == 2 else "1"))
        elif a == 1:
            return near(side, "row") if distance == 2 else turned(near(side, "strip"), REACH, 0)
        else:
            tile = near(side, "strip")
            if distance == 2:
                return jnp.where(starts, turned(tile, 2, 0), turned(tile, -2, 0))
        return third_halo(tile) if a == 0 and distance > 2 else tile

    def window(a, k):
        block, layer = k // layers - 1, k % layers
        if block == 0:
            core = (log_ref, source_ref)[a][layer]
            core = join(core, own_lanes, *(slots["own", a, layer, i] for i in range(rows // SUBLANES)))
            tiles = tuple(
                join(ref[layer], own_lanes, slots["got", g, layer]) for g, ref in enumerate(got_refs)
            )
            halo = tiles[0]
            if wide:
                sides = from_right(iy % 2 == 0, tiles), from_left(iy % 2 == 0, tiles)
                halo = jnp.where(upper, *(sides if a == 0 else sides[::-1]))
            if a == 1:
                halo = turned(halo, REACH, 0)
            return jnp.concatenate([core, halo], axis=0)
        side, pick = (0, from_left) if block < 0 else (1, from_right)
        slot = layer if a == 0 else layers + layer - (1 if block < 0 else 0)
        core = pick(even, (first_ref[slot], second_ref[slot]))
        core = join(core, near_lanes[side], *(slots["own", a, layer, i] for i in range(rows // SUBLANES)))
        halo = near_halo(a, side, layers - layer if block < 0 else layer + 1)
        return jnp.concatenate([core, halo], axis=0)

    faces = [2.0] * (count - 1)
    faces[layers - 1] = jnp.where(ix > 0, 2.0, 0.0)
    faces[2 * layers - 1] = jnp.where(ix < nx - 1, 2.0, 0.0)

    def emit(layer, tile, value):
        part = slice(tile * LANES, (tile + 1) * LANES)
        fine_ref[layer, :, part] = value
        diff_ref[layer, :, part] = value - spread_ref[layer, :, part]

    iterate(
        count,
        rows,
        rows + 2 * REACH,
        lanes // LANES + 1,
        functools.partial(window, 0),
        functools.partial(window, 1),
        faces,
        row_numerators(rows + 2 * REACH, rows, iy, ny, 1.0),
        lane_numerators(rows + 2 * REACH, iz, nz, 1.0) + [2.0],
        coef_ref,
        storage_rate,
        emit,
        scratch,
    )


def fine_level(both, got, raw, far, near, early, spread, coefficients, peers):
    layers, rows, lanes = spread.shape
    window = (layers + 2 * REACH, rows, rows + 2 * REACH, lanes // LANES + 1)
    out = jax.ShapeDtypeStruct(spread.shape, jnp.float32)
    return pl.pallas_call(
        functools.partial(fine_kernel, peers, len(far)),
        out_shape=(out, out),
        in_specs=[VMEM] * (3 + len(got)) + [ANY] * len(far) + [VMEM] * 5,
        out_specs=(VMEM, VMEM),
        scratch_shapes=window_scratch(*window),
        compiler_params=pltpu.CompilerParams(vmem_limit_bytes=24 << 20),
        cost_estimate=pl.CostEstimate(flops=20_000_000, bytes_accessed=10_000_000, transcendentals=0),
        name="fine_level",
    )(both, *got, *raw[::-1], *far, *near[::-1], early, spread, coefficients)


def shards(peers, log_perm, source, low_bound, high_bound):
    nx, ny, nz = peers
    layers, rows, lanes = log_perm.shape
    assert layers == REACH and rows == 2 * SUBLANES and nx > 2 and nz == 2
    both = jnp.concatenate([log_perm, source])
    own, *rows_sent = prep(both, ny)
    if ny == 2:
        got = (permute(rows_sent[0], "gy", ny, [(0, 1)]),)
    else:
        got = swap("gy", ny, rows_sent[1], rows_sent[0])
    for_second = raw_block(both, rows_sent[0], True)
    second = permute(for_second, "gx", nx, neighbour_pairs(nx, 1))
    for_first = raw_block(both, for_second, False)
    raw = (permute(for_first, "gx", nx, neighbour_pairs(nx, 0)), second)
    far_groups = far_pairs(nx)
    halos, lanes_sent = pooled_halos(both, own, got)
    early = lax.ppermute(lanes_sent, "gz", [(0, 1), (1, 0)])
    for_far = pack_far(own, halos, early, len(far_groups), ny > 2)
    far = [permute(tiles, "gx", nx, group) for tiles, group in zip(for_far, far_groups)]
    for_first, for_second = pack_near(own, halos, early, for_far[0], got)
    second = permute(for_second, "gx", nx, neighbour_pairs(nx, 1))
    near = (permute(for_first, "gx", nx, neighbour_pairs(nx, 0)), second)
    coefficients = chebyshev_coefficients(low_bound, high_bound, for_first)
    pooled = pool(coefficients, raw)
    spread = coarse_level(own, halos, pooled, near, far, early, coefficients, peers)
    return fine_level(both, got, raw, far, near, early, spread, coefficients, peers)


def solution(mesh):
    peers = tuple(mesh.shape[axis] for axis in AXES)
    split = P(("groups", "gx"), "gy", "gz")
    return jax.shard_map(
        functools.partial(shards, peers),
        mesh=mesh,
        in_specs=(split, split, P(), P()),
        out_specs=(split, split),
        check_vma=False,
    )
```

```python
import functools

import jax
import jax.numpy as jnp
from jax import lax
from jax.experimental import pallas as pl
from jax.experimental.pallas import tpu as pltpu
from jax.sharding import PartitionSpec as P

DEGREE = 3
REACH = DEGREE + 1
LANES = 128
SUBLANES = 8
storage_rate = 0.1
AXES = ("gx", "gy", "gz")
VMEM = pl.BlockSpec(memory_space=pltpu.VMEM)
ANY = pl.BlockSpec(memory_space=pl.ANY)


AHEAD = pl.CostEstimate(flops=50_000_000_000, bytes_accessed=1_000_000, transcendentals=0)


def iota(shape, dim):
    return lax.broadcasted_iota(jnp.int32, shape, dim)


def turned(value, shift, axis):
    size = value.shape[axis]
    return pltpu.roll(value, shift % size, axis)


def permute(value, axis, peers, pairs):
    cores = lax.axis_size("gz")
    if axis == "gz" or cores % 2:
        return lax.ppermute(value, axis, [pair for i, j in pairs for pair in ((i, j), (j, i))])
    partner = {}
    for i, j in pairs:
        partner[i], partner[j] = j, i
    moves = [
        (i * cores + core, partner[i] * cores + core if i in partner else i * cores + (core ^ 1))
        for i in range(peers)
        for core in range(cores)
    ]
    return lax.ppermute(value, (axis, "gz"), moves)


def neighbour_pairs(peers, start):
    return [(i, i + 1) for i in range(start, peers - 1, 2)]


def first_swap(axis, peers, right, left):
    even = lax.axis_index(axis) % 2 == 0
    return permute(jnp.where(even, right, left), axis, peers, neighbour_pairs(peers, 0))


def second_swap(axis, peers, right, left):
    even = lax.axis_index(axis) % 2 == 0
    return permute(jnp.where(even, left, right), axis, peers, neighbour_pairs(peers, 1))


def swap(axis, peers, right, left):
    got = (first_swap(axis, peers, right, left),)
    return got if peers == 2 else got + (second_swap(axis, peers, right, left),)


def far_pairs(peers):
    pairs = [(i, i + 2) for i in range(peers - 2)]
    groups = [[pair for pair in pairs if pair[0] % 4 < 2], [pair for pair in pairs if pair[0] % 4 >= 2]]
    return [group for group in groups if group]


def from_right(is_first, got):
    return got[0] if len(got) == 1 else jnp.where(is_first, got[0], got[1])


def from_left(is_first, got):
    return got[0] if len(got) == 1 else jnp.where(is_first, got[1], got[0])


def inverse(value):
    guess = pl.reciprocal(value, approx=True)
    return guess * (2.0 - value * guess)


def row_numerators(rows, own, index, peers, face_scale):
    place = iota((rows, LANES), 0)
    right = jnp.where(index < peers - 1, 2.0 * face_scale, 0.0)
    left = jnp.where(index > 0, 2.0 * face_scale, 0.0)
    return jnp.where(place == own - 1, right, jnp.where(place == rows - 1, left, 2.0 * face_scale))


def lane_numerators(rows, index, peers, face_scale):
    place = iota((rows, LANES), 1)
    right = jnp.where(index < peers - 1, 2.0 * face_scale, 0.0)
    left = jnp.where(index > 0, 2.0 * face_scale, 0.0)
    return [jnp.where(place == LANES - 1, side, 2.0 * face_scale) for side in (right, left)]


def lane_tiles(value):
    return [value[:, i : i + LANES] for i in range(0, value.shape[1], LANES)]


def beside(tiles, shift):
    moved = [turned(tile, shift, 1) for tile in tiles]
    lane = iota(tiles[0].shape, 1)
    seam = LANES - 1 if shift < 0 else 0
    return [
        jnp.where(lane == seam, moved[(j - shift) % len(tiles)], moved[j]) for j in range(len(tiles))
    ]


def store_rows(ref, k, j, value):
    rows = value.shape[0]
    ref[k, j, SUBLANES : SUBLANES + rows] = value
    ref[k, j, SUBLANES - 1 : SUBLANES] = value[rows - 1 :]
    ref[k, j, SUBLANES + rows : SUBLANES + rows + 1] = value[:1]


def iterate(count, own_rows, rows, tiles, log_at, source_at, x_faces, y_top, z_top, coef_ref, storage, emit, refs):
    k_ref, tx_ref, ty_ref, tzr_ref, tzl_ref, diag_ref, w_ref, d_ref, r_ref, p_ref = refs
    own_tiles = tiles - 1

    def away(k):
        return max(0, REACH - k, k - (count - 1 - REACH))

    def extent(k, step):
        left = DEGREE - step - away(k)
        return None if left < 0 else (own_rows, own_tiles) if left == 0 else (rows, tiles)

    def coefficient(i, size):
        return jnp.concatenate([coef_ref[i]] * (size // SUBLANES), axis=0)

    z_tops = [z_top[0] if j == own_tiles - 1 else z_top[1] if j == own_tiles else None for j in range(tiles)]

    def resistance(k):
        return [jnp.exp(-tile) for tile in lane_tiles(log_at(k))]

    after = resistance(0)
    tx_before = None
    for k in range(count):
        here = after
        if k + 1 < count:
            after = resistance(k + 1)
            outer = max(away(k), away(k + 1))
            size, number = (rows, tiles) if outer < REACH else (own_rows, own_tiles)
            tx = [x_faces[k] * inverse(here[j][:size] + after[j][:size]) for j in range(number)]
            for j in range(number):
                tx_ref[k, j, :size] = tx[j]
        if away(k) <= DEGREE:
            size, number = extent(k, 0)
            right = beside(here, -1)
            tz = []
            for j in range(tiles):
                scale = z_tops[j][:size] if z_tops[j] is not None else z_top[2]
                tz.append(scale * inverse(here[j][:size] + right[j][:size]))
            tz_left = beside(tz, 1)
            source = lane_tiles(source_at(k))
            for j in range(number):
                store_rows(k_ref, k, j, here[j])
                ty = y_top * inverse(here[j] + k_ref[k, j, SUBLANES + 1 : SUBLANES + 1 + rows])
                store_rows(ty_ref, k, j, ty)
                ty_before = ty_ref[k, j, SUBLANES - 1 : SUBLANES - 1 + size]
                diagonal = storage + (tx_before[j][:size] + tx[j][:size])
                diagonal = diagonal + (ty[:size] + ty_before) + (tz[j] + tz_left[j])
                w = inverse(diagonal)
                direction = source[j][:size] * (coefficient(0, size) * w)
                if (size, number) == (rows, tiles):
                    store_rows(d_ref.at[0], k, j, direction)
                else:
                    d_ref[0, k, j, SUBLANES : SUBLANES + size] = direction
                if extent(k, 1) is not None:
                    tzr_ref[k, j, :size] = tz[j]
                    tzl_ref[k, j, :size] = tz_left[j]
                    diag_ref[k, j, :size] = diagonal
                    w_ref[k, j, :size] = w
                    r_ref[k, j, :size] = source[j][:size]
        tx_before = tx
    for step in range(1, DEGREE + 1):
        old, new = d_ref.at[(step - 1) % 2], d_ref.at[step % 2]
        for k in range(count):
            if extent(k, step) is None:
                continue
            size, number = extent(k, step)
            middle = slice(SUBLANES, SUBLANES + size)
            keep, gain = coefficient(2 * step - 1, size), coefficient(2 * step, size)
            here = [old[k, j, middle] for j in range(tiles)]
            right, left = beside(here, -1), beside(here, 1)
            for j in range(number):
                applied = tx_ref[k, j, :size] * old[k + 1, j, middle] + tx_ref[k - 1, j, :size] * old[k - 1, j, middle]
                applied += (
                    ty_ref[k, j, middle] * old[k, j, SUBLANES + 1 : SUBLANES + 1 + size]
                    + ty_ref[k, j, SUBLANES - 1 : SUBLANES - 1 + size] * old[k, j, SUBLANES - 1 : SUBLANES - 1 + size]
                )
                applied += tzr_ref[k, j, :size] * right[j] + tzl_ref[k, j, :size] * left[j]
                residual = r_ref[k, j, :size] - (diag_ref[k, j, :size] * here[j] - applied)
                fresh = keep * here[j] + gain * (residual * w_ref[k, j, :size])
                if away(k) == 0 and j < own_tiles:
                    so_far = here[j][:own_rows] if step == 1 else p_ref[k, j]
                    total = so_far + fresh[:own_rows]
                    if step == DEGREE:
                        emit(k - REACH, j, total)
                    else:
                        p_ref[k, j] = total
                if step < DEGREE:
                    r_ref[k, j, :size] = residual
                    if (size, number) == (rows, tiles):
                        store_rows(new, k, j, fresh)
                    else:
                        new[k, j, middle] = fresh


def coefficients_kernel(low_ref, high_ref, after_ref, coef_ref):
    low, high = (jnp.full((SUBLANES, LANES), ref[0]) for ref in (low_ref, high_ref))
    theta, delta = (high + low) * 0.5, (high - low) * 0.5
    sigma = theta / delta
    rho = 1.0 / sigma
    coef_ref[0] = 1.0 / theta
    for step in range(DEGREE):
        rho_next = 1.0 / (2.0 * sigma - rho)
        coef_ref[1 + 2 * step] = rho_next * rho
        coef_ref[2 + 2 * step] = 2.0 * rho_next / delta
        rho = rho_next


def chebyshev_coefficients(low_bound, high_bound, after):
    return pl.pallas_call(
        coefficients_kernel,
        out_shape=jax.ShapeDtypeStruct((1 + 2 * DEGREE, SUBLANES, LANES), jnp.float32),
        in_specs=[pl.BlockSpec(memory_space=pltpu.SMEM)] * 2 + [ANY],
        out_specs=VMEM,
        compiler_params=pltpu.CompilerParams(vmem_limit_bytes=4 << 20),
        cost_estimate=pl.CostEstimate(flops=1_000_000, bytes_accessed=100_000, transcendentals=0),
        name="coefficients",
    )(low_bound, high_bound, after)


def put(ref, tile, value):
    for i in range(value.shape[1] // LANES):
        ref[(tile + i) * SUBLANES : (tile + i + 1) * SUBLANES, :] = value[:, i * LANES : (i + 1) * LANES]


def take(ref, tile, count):
    tiles = [ref[(tile + i) * SUBLANES : (tile + i + 1) * SUBLANES, :] for i in range(count)]
    return tiles[0] if count == 1 else jnp.concatenate(tiles, axis=1)


def edges(value):
    lanes = value.shape[-1]
    value = value if isinstance(value, jax.Array) else value.at
    return value[:, lanes - LANES :], value[:, :LANES]


def write_lanes(pairs):
    starts = lax.axis_index("gz") == 0
    each = LANES // REACH
    group = iota((SUBLANES, LANES), 1) // REACH
    merged = None
    for j, (last, first) in enumerate(pairs):
        moved = turned(jnp.where(starts, last, first), REACH * j, 1)
        place = jnp.where(starts, (j - 1) % each, j)
        merged = moved if merged is None else jnp.where(group == place, moved, merged)
    return merged


def read_lanes(tile, slot):
    return turned(tile, -REACH * slot, 1)


def add_lanes(tile, slot, value):
    starts = lax.axis_index("gz") == 0
    group = iota((SUBLANES, LANES), 1) // REACH
    place = jnp.where(starts, slot, (slot - 1) % (LANES // REACH))
    return jnp.where(group == place, turned(value, REACH * slot, 1), tile)


def lane_slots(layers, row_tiles, n_got):
    keys = [("own", a, layer, i) for a in range(2) for layer in range(layers) for i in range(row_tiles)]
    keys += [("pooled", x, a) for x in range(2) for a in range(2)]
    shared = len(keys)
    keys += [("halo", i, half) for i in range(n_got) for half in range(2)]
    keys += [("got", g, layer) for g in range(n_got) for layer in range(layers)]
    return {key: i for i, key in enumerate(keys)}, shared


def near_layout(lanes, wide):
    whole, half = lanes // LANES, lanes // LANES // 2
    if wide:
        parts = [("log1", whole), ("source1", whole), ("log2", whole), ("source2", whole)]
        parts += [(name, half) for name in ("halo0", "halo1", "halo2", "halo3", "source")]
    else:
        parts = [("strip", whole), ("halo", half), ("source", half), ("row", 1)]
    layout, start = {}, 0
    for name, count in parts + [("lanes", 1)]:
        layout[name] = (start, count)
        start += count
    return layout, start


def near_lane_slots(lanes, wide, shared):
    names = [name for name in near_layout(lanes, wide)[0] if name not in ("source", "lanes")]
    return {name: shared + i for i, name in enumerate(names)}


def rows_to_lanes(row_tile, count):
    return jnp.concatenate(
        [jnp.broadcast_to(row_tile[j : j + 1], (SUBLANES, LANES)) for j in range(count)], axis=1
    )


def window_scratch(count, own_rows, rows, tiles):
    plain = pltpu.VMEM((count, tiles, rows, LANES), jnp.float32)
    margins = pltpu.VMEM((count, tiles, rows + 2 * SUBLANES, LANES), jnp.float32)
    pair = pltpu.VMEM((2, count, tiles, rows + 2 * SUBLANES, LANES), jnp.float32)
    total = pltpu.VMEM((count, tiles, own_rows, LANES), jnp.float32)
    return [margins, plain, margins, plain, plain, plain, plain, pair, plain, total]


def exact_dot(value, zero_one):
    parts = []
    for _ in range(3):
        part = value.astype(jnp.bfloat16)
        parts.append(part)
        value = value - part.astype(jnp.float32)
    rows = value.shape[0]
    out = jnp.dot(jnp.concatenate(parts, axis=0), zero_one, preferred_element_type=jnp.float32)
    return (out[2 * rows :] + out[rows : 2 * rows]) + out[:rows]


def row_pairs(top, bottom, sum_ref):
    tiles = top.shape[1] // LANES
    for tile in range(tiles):
        columns = slice(tile * LANES, (tile + 1) * LANES)
        sum_ref[tile, :SUBLANES] = top[:, columns]
        sum_ref[tile, SUBLANES:] = bottom[:, columns]
    return jnp.concatenate(
        [
            sum_ref[tile, pl.ds(0, SUBLANES, stride=2), :] + sum_ref[tile, pl.ds(1, SUBLANES, stride=2), :]
            for tile in range(tiles)
        ],
        axis=1,
    )


def lane_pairs(pieces):
    lanes = pieces[0].shape[1]
    pick = (iota((lanes, lanes // 2), 0) // 2 == iota((lanes, lanes // 2), 1)).astype(jnp.bfloat16)
    pooled = exact_dot(jnp.concatenate(pieces, axis=0), pick)
    return [pooled[SUBLANES * i : SUBLANES * (i + 1)] for i in range(len(pieces))]


def join_halo(near, beyond, starts):
    row = iota(near.shape, 0)
    up, down = turned(beyond, 3, 0), turned(beyond, -3, 0)
    right = jnp.where((row == 3) | (row == 7), up, jnp.where(row == 6, turned(beyond, 5, 0), near))
    left = jnp.where((row == 0) | (row == 4), down, jnp.where(row == 5, up, near))
    return jnp.where(starts, right, left)


def beyond_halo(joined, starts):
    row = iota(joined.shape, 0)
    up, down = turned(joined, 3, 0), turned(joined, -3, 0)
    right = jnp.where(row == 1, turned(joined, -5, 0), down)
    left = jnp.where(row == 2, down, up)
    return jnp.where(starts, right, left)


def join_third(near, third):
    row = iota(near.shape, 0)
    return jnp.where(
        row == 3, turned(third, 3, 0), jnp.where(row == 4, turned(third, -3, 0), near)
    )


def third_halo(joined):
    return jnp.where(iota(joined.shape, 0) < REACH, turned(joined, -3, 0), turned(joined, 3, 0))


def parts(both_ref):
    layers = both_ref.shape[0] // 2
    return both_ref.at[:layers], both_ref.at[layers:]


def prep_kernel(both_ref, pooled_ref, *refs):
    *out_refs, sum_ref = refs
    log_ref, source_ref = parts(both_ref)
    layers, rows, lanes = log_ref.shape
    starts = lax.axis_index("gy") == 0

    def put(slot, left, right):
        if len(out_refs) == 1:
            out_refs[0][slot] = jnp.where(starts, right, left)
        else:
            out_refs[0][slot], out_refs[1][slot] = left, right

    half = lanes // 2
    upper = iota((SUBLANES, lanes), 0) < REACH
    pieces = []
    for x in range(2):
        for ref in (log_ref, source_ref):
            both = ref[2 * x] + ref[2 * x + 1]
            pieces.append(row_pairs(both[:SUBLANES], both[SUBLANES:], sum_ref))
    log0, source0, log1, source1 = lane_pairs(pieces)
    log0, log1 = log0 * 0.125, log1 * 0.125
    pooled_ref[0] = jnp.concatenate([log0, source0], axis=1)
    pooled_ref[1] = jnp.concatenate([log1, source1], axis=1)
    for layer in range(layers):
        put(
            layer,
            jnp.where(upper, log_ref[layer, :SUBLANES], turned(source_ref[layer, :SUBLANES], REACH, 0)),
            jnp.where(upper, turned(source_ref[layer, SUBLANES:], REACH, 0), log_ref[layer, SUBLANES:]),
        )
    pair = iota((SUBLANES, half), 0) // 2

    def four(*tiles):
        merged = jnp.where(
            pair == 0, tiles[0], jnp.where(pair == 1, tiles[1], jnp.where(pair == 2, tiles[2], tiles[3]))
        )
        return jnp.concatenate([merged, merged], axis=1)

    put(
        layers,
        four(turned(log1, -2, 0), log0, turned(source1, 2, 0), turned(source0, 4, 0)),
        four(turned(log0, -4, 0), turned(log1, -2, 0), source0, turned(source1, 2, 0)),
    )


def prep(both, ny):
    layers, rows, lanes = both.shape[0] // 2, *both.shape[1:]
    outs = 1 if ny == 2 else 2

    def tiles(count):
        return jax.ShapeDtypeStruct((count, SUBLANES, lanes), jnp.float32)

    return pl.pallas_call(
        prep_kernel,
        out_shape=(tiles(2),) + (tiles(layers + 1),) * outs,
        in_specs=[VMEM],
        out_specs=(VMEM,) * (1 + outs),
        scratch_shapes=[pltpu.VMEM((lanes // LANES, 2 * SUBLANES, LANES), jnp.float32)],
        compiler_params=pltpu.CompilerParams(vmem_limit_bytes=8 << 20),
        cost_estimate=pl.CostEstimate(flops=5_000_000, bytes_accessed=700_000, transcendentals=0),
        name="prep",
    )(both)


def raw_kernel(to_right_if_odd, both_ref, after_ref, out_ref):
    log_ref, source_ref = parts(both_ref)
    layers = log_ref.shape[0]
    odd = lax.axis_index("gx") % 2
    skip = odd if to_right_if_odd else 1 - odd
    for layer in range(layers):
        out_ref[layer] = log_ref[layer]
    for layer in range(layers - 1):
        out_ref[layers + layer] = source_ref[layer + skip]


def raw_block(both, after, to_right_if_odd):
    layers, rows, lanes = both.shape[0] // 2, *both.shape[1:]
    return pl.pallas_call(
        functools.partial(raw_kernel, to_right_if_odd),
        out_shape=jax.ShapeDtypeStruct((2 * layers - 1, rows, lanes), jnp.float32),
        in_specs=[VMEM, ANY],
        out_specs=VMEM,
        compiler_params=pltpu.CompilerParams(vmem_limit_bytes=8 << 20),
        cost_estimate=pl.CostEstimate(flops=1_000_000, bytes_accessed=500_000, transcendentals=0),
        name="raw_block",
    )(both, after)


def halos_kernel(wide, both_ref, pooled_ref, *refs):
    *got_refs, halo_ref, sent_ref, sum_ref = refs
    layers, lanes = got_refs[0].shape[0] - 1, got_refs[0].shape[2]
    iy = lax.axis_index("gy")
    even, starts = iy % 2 == 0, iy == 0
    half = lanes // 2
    upper = iota((SUBLANES, lanes), 0) < REACH
    row = iota((SUBLANES, half), 0)

    def got(slot):
        tiles = tuple(ref[slot] for ref in got_refs)
        return from_right(even, tiles), from_left(even, tiles)

    strips = [got(layer) for layer in range(layers)]
    extra = [tile[:, :half] for tile in got(layers)]
    pieces = []
    for side in range(2 if wide else 1):
        both = [strips[2 * x][side] + strips[2 * x + 1][side] for x in range(2)]
        pieces.append(row_pairs(*both, sum_ref))
    fine_rows = lane_pairs(pieces)

    def right_halos(rows, extra):
        rows = jnp.where(row % 4 < 2, rows * 0.125, rows)
        return [
            jnp.where(row < 2, near, jnp.where((row == 4) | (row == 5), far, more))
            for near, far, more in (
                (rows, turned(rows, 2, 0), extra),
                (turned(rows, 4, 0), turned(rows, -2, 0), turned(extra, 2, 0)),
            )
        ]

    def left_halos(rows, extra):
        rows = jnp.where(row % 4 >= 2, rows * 0.125, rows)
        return [
            jnp.where((row == 2) | (row == 3), near, jnp.where(row >= 6, far, more))
            for near, far, more in (
                (rows, turned(rows, -2, 0), extra),
                (turned(rows, 4, 0), turned(rows, 2, 0), turned(extra, -2, 0)),
            )
        ]

    right, left = right_halos(fine_rows[0], extra[0]), left_halos(fine_rows[-1], extra[1])
    if wide:
        top = row < REACH
        halos = [jnp.where(top, right[x], turned(left[x], REACH, 0)) for x in range(2)]
        halos += [jnp.where(top, turned(right[x], REACH, 0), left[x]) for x in range(2)]
    else:
        halos = [jnp.where(starts, right[x], left[x]) for x in range(2)]

    def pair(left, right):
        return jnp.concatenate([left, right], axis=1)

    for i in range(len(halos) // 2):
        halo_ref[i] = pair(halos[2 * i], halos[2 * i + 1])
    pairs = {}
    rows = both_ref.shape[1]
    for a, ref in enumerate(parts(both_ref)):
        for layer in range(layers):
            for i in range(rows // SUBLANES):
                pairs["own", a, layer, i] = edges(ref[layer, i * SUBLANES : (i + 1) * SUBLANES])
    for x in range(2):
        for a in range(2):
            pairs["pooled", x, a] = edges(pooled_ref[x, :, a * half : (a + 1) * half])
    for i, halo in enumerate(halos):
        pairs["halo", i // 2, i % 2] = edges(halo)
    for g, ref in enumerate(got_refs):
        for layer in range(layers):
            pairs["got", g, layer] = edges(ref[layer])
    slots, _ = lane_slots(layers, rows // SUBLANES, len(got_refs))
    sent_ref[...] = write_lanes([pairs[key] for key in slots])


def pooled_halos(both, pooled, got):
    slots, rows, lanes = got[0].shape
    return pl.pallas_call(
        functools.partial(halos_kernel, len(got) == 2),
        out_shape=(
            jax.ShapeDtypeStruct((len(got), SUBLANES, lanes), jnp.float32),
            jax.ShapeDtypeStruct((SUBLANES, LANES), jnp.float32),
        ),
        in_specs=[VMEM] * (2 + len(got)),
        out_specs=(VMEM,) * 2,
        scratch_shapes=[pltpu.VMEM((lanes // LANES, 2 * SUBLANES, LANES), jnp.float32)],
        compiler_params=pltpu.CompilerParams(vmem_limit_bytes=8 << 20),
        cost_estimate=AHEAD,
        name="halos",
    )(both, pooled, *got)


def pack_far_kernel(wide, pooled_ref, halo_ref, lanes_ref, *far_refs):
    half = pooled_ref.shape[2] // 2
    low = lax.axis_index("gx") % 4 < 2

    def tiles(inner):
        return (
            pooled_ref[inner, :, :half],
            pooled_ref[1 - inner, :, :half],
            pooled_ref[inner, :, half:],
            halo_ref[0, :, inner * half : (inner + 1) * half],
        )

    for group, ref in enumerate(far_refs):
        for i, (right, left) in enumerate(zip(tiles(1), tiles(0))):
            put(ref, i * (half // LANES), jnp.where(low, *((right, left) if group == 0 else (left, right))))
        put(ref, 4 * (half // LANES), lanes_ref[...])


def pack_far(pooled, halos, early, n_far, wide):
    _, rows, lanes = pooled.shape
    far_rows = (2 * lanes // LANES + 1) * SUBLANES
    return pl.pallas_call(
        functools.partial(pack_far_kernel, wide),
        out_shape=(jax.ShapeDtypeStruct((far_rows, LANES), jnp.float32),) * n_far,
        in_specs=[VMEM] * 3,
        out_specs=(VMEM,) * n_far,
        compiler_params=pltpu.CompilerParams(vmem_limit_bytes=8 << 20),
        cost_estimate=pl.CostEstimate(flops=1_000_000, bytes_accessed=500_000, transcendentals=0),
        name="pack_far",
    )(pooled, halos, early)


def pack_near_kernel(wide, pooled_ref, halo_ref, early_ref, after_ref, *refs):
    *got_refs, first_ref, second_ref = refs
    layers, lanes = got_refs[0].shape[0] - 1, got_refs[0].shape[2]
    ix, iy = lax.axis_index("gx"), lax.axis_index("gy")
    even, starts = iy % 2 == 0, iy == 0
    half = lanes // 2
    upper = iota((SUBLANES, lanes), 0) < REACH

    def got(slot):
        tiles = tuple(ref[slot] for ref in got_refs)
        return from_right(even, tiles), from_left(even, tiles)

    strips = [got(layer) for layer in range(layers)]
    halos = [halo_ref[i // 2, :, (i % 2) * half : (i % 2 + 1) * half] for i in range(4 if wide else 2)]
    sources = [pooled_ref[x, :, half:] for x in range(2)]

    slots, shared = lane_slots(layers, 2, len(got_refs))

    def strip_lanes(layer):
        tiles = tuple(read_lanes(early_ref[...], slots["got", g, layer]) for g in range(len(got_refs)))
        return from_right(even, tiles), from_left(even, tiles)

    def halo_lanes(i):
        return read_lanes(early_ref[...], slots["halo", i // 2, i % 2])

    def near_tiles(order, strips, halos):
        near, beyond = order[0] // 2, order[-1] // 2
        width = strips[0][0].shape[1]
        upper = iota((SUBLANES, width), 0) < REACH
        if wide:
            log_rows = [jnp.where(upper, *strips[layer]) for layer in range(layers)]
            source_rows = [turned(jnp.where(upper, *strips[layer][::-1]), REACH, 0) for layer in range(layers)]
            return {
                "log1": join_third(log_rows[order[0]], log_rows[order[2]]),
                "source1": source_rows[order[0]],
                "log2": log_rows[order[1]],
                "source2": source_rows[order[1]],
                "halo0": halos[near],
                "halo1": halos[beyond],
                "halo2": halos[2 + near],
                "halo3": halos[2 + beyond],
            }
        first, second, third = (strips[layer][0] for layer in order[:3])
        place = iota((SUBLANES, width), 0)
        right = jnp.where(place == 3, turned(third, 3, 0), jnp.where(place >= 6, turned(second, -2, 0), first))
        left = jnp.where(place == 4, turned(third, -3, 0), jnp.where(place < 2, turned(second, 2, 0), first))
        line = jnp.where(starts, second[4:5], second[3:4])
        if width == LANES:
            lines = jnp.broadcast_to(line, (SUBLANES, LANES))
        else:
            lines = jnp.zeros((SUBLANES, LANES), jnp.float32)
            for j in range(width // LANES):
                lines = jnp.where(iota(lines.shape, 0) == j, line[:, j * LANES : (j + 1) * LANES], lines)
        return {
            "strip": jnp.where(starts, right, left),
            "halo": join_halo(halos[near], halos[beyond], starts),
            "row": lines,
        }

    def side(order):
        tiles = near_tiles(order, strips, halos)
        tiles["source"] = sources[order[-1] // 2]
        lanes_tile = early_ref[...]
        n_halos = 4 if wide else 2
        beside = near_tiles(
            order, [strip_lanes(layer) for layer in range(layers)], [halo_lanes(i) for i in range(n_halos)]
        )
        for name, slot in near_lane_slots(lanes, wide, shared).items():
            lanes_tile = add_lanes(lanes_tile, slot, beside[name])
        tiles["lanes"] = lanes_tile
        return tiles

    forward = list(range(layers))
    layout, _ = near_layout(lanes, wide)
    right, left = side(forward[::-1]), side(forward)
    for name, (start, _) in layout.items():
        put(first_ref, start, jnp.where(ix % 2 == 0, right[name], left[name]))
        put(second_ref, start, jnp.where(ix % 2 == 0, left[name], right[name]))


def pack_near(pooled, halos, early, after, got):
    slots, rows, lanes = got[0].shape
    wide = len(got) == 2
    out = jax.ShapeDtypeStruct((near_layout(lanes, wide)[1] * SUBLANES, LANES), jnp.float32)
    return pl.pallas_call(
        functools.partial(pack_near_kernel, wide),
        out_shape=(out, out),
        in_specs=[VMEM] * 3 + [ANY] + [VMEM] * len(got),
        out_specs=(VMEM,) * 2,
        compiler_params=pltpu.CompilerParams(vmem_limit_bytes=8 << 20),
        cost_estimate=pl.CostEstimate(flops=1_000_000, bytes_accessed=500_000, transcendentals=0),
        name="pack_near",
    )(pooled, halos, early, after, *got)


def pool_kernel(after_ref, first_ref, second_ref, out_ref, sum_ref):
    layers = REACH
    even = lax.axis_index("gx") % 2 == 0
    pieces = []
    for side, pick in enumerate((from_left, from_right)):

        def block(slot):
            return pick(even, (first_ref[slot], second_ref[slot]))

        for top in (0, 2, layers + 1 if side == 0 else layers):
            both = block(top) + block(top + 1)
            pieces.append(row_pairs(both[:SUBLANES], both[SUBLANES:], sum_ref))
    for i, tile in enumerate(lane_pairs(pieces)):
        put(out_ref, i * (tile.shape[1] // LANES), tile * (0.125 if i % 3 < 2 else 1.0))


def pool(after, raw):
    _, rows, lanes = raw[0].shape
    return pl.pallas_call(
        pool_kernel,
        out_shape=jax.ShapeDtypeStruct((6 * (lanes // 2 // LANES) * SUBLANES, LANES), jnp.float32),
        in_specs=[ANY] + [VMEM] * 2,
        out_specs=VMEM,
        scratch_shapes=[pltpu.VMEM((lanes // LANES, 2 * SUBLANES, LANES), jnp.float32)],
        compiler_params=pltpu.CompilerParams(vmem_limit_bytes=16 << 20),
        cost_estimate=pl.CostEstimate(flops=1_000_000, bytes_accessed=1_000_000, transcendentals=0),
        name="pool",
    )(after, *raw)


def near_part(refs, even, lanes, wide, side, name):
    start, count = near_layout(lanes, wide)[0][name]
    pick = from_left if side == 0 else from_right
    got = pick(even, tuple(take(ref, start, count) for ref in refs))
    return rows_to_lanes(got, lanes // LANES) if name == "row" else got


def far_part(refs, low, lanes, side, i):
    count = lanes // 2 // LANES
    pick = from_left if side == 0 else from_right
    return pick(low, tuple(take(ref, i * count, count) for ref in refs))


def coarse_kernel(peers, n_far, own_ref, halo_ref, pool_ref, first_ref, second_ref, *refs):
    near_refs, far_refs = (first_ref, second_ref), refs[:n_far]
    early_ref, coef_ref, out_ref, wide_ref, *scratch = refs[n_far:]
    ix, iy, iz = (lax.axis_index(axis) for axis in AXES)
    nx, ny, nz = peers
    wide = ny > 2
    fine_lanes = own_ref.shape[2]
    lanes, rows = fine_lanes // 2, SUBLANES
    even, low, starts = ix % 2 == 0, ix % 4 < 2, iy == 0
    top = iota((rows, lanes + LANES), 0) < REACH
    slots, shared = lane_slots(REACH, 2, 2 if wide else 1)
    near_slots = near_lane_slots(fine_lanes, wide, shared)
    own_lanes = early_ref[...]
    near_lanes = [near_part(near_refs, even, fine_lanes, wide, side, "lanes") for side in range(2)]
    far_lanes = [
        pick(low, tuple(take(ref, 4 * (lanes // LANES), 1) for ref in far_refs))
        for pick in (from_left, from_right)
    ]

    def columns(half):
        return slice(half * lanes, (half + 1) * lanes)

    def join(core, tile, slot):
        return jnp.concatenate([core, read_lanes(tile, slot)], axis=1)

    def near(side, name):
        core = near_part(near_refs, even, fine_lanes, wide, side, name)
        return join(core, near_lanes[side], near_slots[name])

    def far(side, i):
        core = far_part(far_refs, low, fine_lanes, side, i)
        return join(core, far_lanes[side], slots["pooled", 1 - side, 0])

    def split(tile, a):
        other = turned(tile, REACH, 0)
        return jnp.where(top, tile, other) if a == 0 else jnp.where(top, other, tile)

    def window(a, k):
        block, layer = k // 2 - 2, k % 2
        nearest = layer == (1 if block < 0 else 0)
        side = 0 if block < 0 else 1
        if abs(block) == 2:
            if a == 1:
                core = far(side, 2)
                return jnp.concatenate([core, jnp.zeros_like(core)], axis=0)
            halo = far(side, 3)
            halo = halo if wide else split(halo, 0)
            return jnp.concatenate([far(side, 0 if nearest else 1), halo], axis=0)
        if block == 0:
            core = join(own_ref[layer, :, columns(a)], own_lanes, slots["pooled", layer, a])
            if wide:
                halo = join(halo_ref[a, :, columns(layer)], own_lanes, slots["halo", a, layer])
            else:
                halo = split(join(halo_ref[0, :, columns(layer)], own_lanes, slots["halo", 0, layer]), a)
            return jnp.concatenate([core, halo], axis=0)
        if a == 0 or nearest:
            i = layer if a == 0 else 2
            core = take(pool_ref, (3 * side + i) * (lanes // LANES), lanes // LANES)
        else:
            core = near_part(near_refs, even, fine_lanes, wide, side, "source")
        core = join(core, near_lanes[side], slots["pooled", layer, a])
        if wide:
            halo = near(side, f"halo{2 * a + (0 if nearest else 1)}")
        else:
            joined = near(side, "halo")
            halo = split(joined if nearest else beyond_halo(joined, starts), a)
        return jnp.concatenate([core, halo], axis=0)

    def open_face(inside):
        return jnp.where(inside, 4.0, 0.0)

    faces = [4.0] * 9
    faces[1], faces[3] = open_face(ix > 1), open_face(ix > 0)
    faces[5], faces[7] = open_face(ix < nx - 1), open_face(ix < nx - 2)
    *scratch, p_ref = scratch

    def emit(layer, tile, value):
        p_ref[layer * rows : (layer + 1) * rows, tile * LANES : (tile + 1) * LANES] = value

    iterate(
        2 + 2 * REACH,
        rows,
        2 * rows,
        lanes // LANES + 1,
        functools.partial(window, 0),
        functools.partial(window, 1),
        faces,
        row_numerators(2 * rows, rows, iy, ny, 2.0),
        lane_numerators(2 * rows, iz, nz, 2.0) + [4.0],
        coef_ref,
        8.0 * storage_rate,
        emit,
        scratch,
    )
    widen = (iota((lanes, 2 * lanes), 0) == iota((lanes, 2 * lanes), 1) // 2).astype(jnp.bfloat16)
    spread = exact_dot(p_ref[...], widen)
    for x in range(2):
        for tile in range(2 * lanes // LANES):
            part = slice(tile * LANES, (tile + 1) * LANES)
            for half in range(2):
                wide_ref[tile, pl.ds(half, rows, stride=2), :] = spread[x * rows : (x + 1) * rows, part]
            for twin in range(2):
                out_ref[2 * x + twin, :, part] = wide_ref[tile]


def coarse_level(own, halos, pooled, near, far, early, coefficients, peers):
    lanes = own.shape[2] // 2
    window = (2 + 2 * REACH, SUBLANES, 2 * SUBLANES, lanes // LANES + 1)
    return pl.pallas_call(
        functools.partial(coarse_kernel, peers, len(far)),
        out_shape=jax.ShapeDtypeStruct((REACH, 2 * SUBLANES, 2 * lanes), jnp.float32),
        in_specs=[VMEM] * (7 + len(far)),
        out_specs=VMEM,
        scratch_shapes=[pltpu.VMEM((2 * lanes // LANES, 2 * SUBLANES, LANES), jnp.float32)]
        + window_scratch(*window)
        + [pltpu.VMEM((2 * SUBLANES, lanes), jnp.float32)],
        compiler_params=pltpu.CompilerParams(vmem_limit_bytes=24 << 20),
        cost_estimate=pl.CostEstimate(flops=20_000_000, bytes_accessed=4_000_000, transcendentals=0),
        name="coarse_level",
    )(own, halos, pooled, *near, *far, early, coefficients)


def fine_kernel(peers, n_far, both_ref, *refs):
    log_ref, source_ref = parts(both_ref)
    layers, rows, lanes = log_ref.shape
    ix, iy, iz = (lax.axis_index(axis) for axis in AXES)
    nx, ny, nz = peers
    wide = ny > 2
    n_got = 2 if wide else 1
    got_refs, refs = refs[:n_got], refs[n_got:]
    second_ref, first_ref = refs[:2]
    second_near_ref, first_near_ref, early_ref, spread_ref = refs[2 + n_far : 6 + n_far]
    near_refs = first_near_ref, second_near_ref
    coef_ref, fine_ref, diff_ref, *scratch = refs[6 + n_far :]
    even, starts = ix % 2 == 0, iy == 0
    count = 3 * layers
    upper = iota((SUBLANES, lanes + LANES), 0) < REACH
    slots, shared = lane_slots(layers, rows // SUBLANES, n_got)
    near_slots = near_lane_slots(lanes, wide, shared)
    own_lanes = early_ref[...]
    near_lanes = [near_part(near_refs, even, lanes, wide, side, "lanes") for side in range(2)]

    def join(core, tile, *keys):
        beside = jnp.concatenate([read_lanes(tile, key) for key in keys], axis=0)
        return jnp.concatenate([core, beside], axis=1)

    def near(side, name):
        return join(near_part(near_refs, even, lanes, wide, side, name), near_lanes[side], near_slots[name])

    def near_halo(a, side, distance):
        if wide:
            tile = near(side, ("log" if a == 0 else "source") + ("2" if distance == 2 else "1"))
        elif a == 1:
            return near(side, "row") if distance == 2 else turned(near(side, "strip"), REACH, 0)
        else:
            tile = near(side, "strip")
            if distance == 2:
                return jnp.where(starts, turned(tile, 2, 0), turned(tile, -2, 0))
        return third_halo(tile) if a == 0 and distance > 2 else tile

    def window(a, k):
        block, layer = k // layers - 1, k % layers
        if block == 0:
            core = (log_ref, source_ref)[a][layer]
            core = join(core, own_lanes, *(slots["own", a, layer, i] for i in range(rows // SUBLANES)))
            tiles = tuple(
                join(ref[layer], own_lanes, slots["got", g, layer]) for g, ref in enumerate(got_refs)
            )
            halo = tiles[0]
            if wide:
                sides = from_right(iy % 2 == 0, tiles), from_left(iy % 2 == 0, tiles)
                halo = jnp.where(upper, *(sides if a == 0 else sides[::-1]))
            if a == 1:
                halo = turned(halo, REACH, 0)
            return jnp.concatenate([core, halo], axis=0)
        side, pick = (0, from_left) if block < 0 else (1, from_right)
        slot = layer if a == 0 else layers + layer - (1 if block < 0 else 0)
        core = pick(even, (first_ref[slot], second_ref[slot]))
        core = join(core, near_lanes[side], *(slots["own", a, layer, i] for i in range(rows // SUBLANES)))
        halo = near_halo(a, side, layers - layer if block < 0 else layer + 1)
        return jnp.concatenate([core, halo], axis=0)

    faces = [2.0] * (count - 1)
    faces[layers - 1] = jnp.where(ix > 0, 2.0, 0.0)
    faces[2 * layers - 1] = jnp.where(ix < nx - 1, 2.0, 0.0)

    def emit(layer, tile, value):
        part = slice(tile * LANES, (tile + 1) * LANES)
        fine_ref[layer, :, part] = value
        diff_ref[layer, :, part] = value - spread_ref[layer, :, part]

    iterate(
        count,
        rows,
        rows + 2 * REACH,
        lanes // LANES + 1,
        functools.partial(window, 0),
        functools.partial(window, 1),
        faces,
        row_numerators(rows + 2 * REACH, rows, iy, ny, 1.0),
        lane_numerators(rows + 2 * REACH, iz, nz, 1.0) + [2.0],
        coef_ref,
        storage_rate,
        emit,
        scratch,
    )


def fine_level(both, got, raw, far, near, early, spread, coefficients, peers):
    layers, rows, lanes = spread.shape
    window = (layers + 2 * REACH, rows, rows + 2 * REACH, lanes // LANES + 1)
    out = jax.ShapeDtypeStruct(spread.shape, jnp.float32)
    return pl.pallas_call(
        functools.partial(fine_kernel, peers, len(far)),
        out_shape=(out, out),
        in_specs=[VMEM] * (3 + len(got)) + [ANY] * len(far) + [VMEM] * 5,
        out_specs=(VMEM, VMEM),
        scratch_shapes=window_scratch(*window),
        compiler_params=pltpu.CompilerParams(vmem_limit_bytes=24 << 20),
        cost_estimate=pl.CostEstimate(flops=20_000_000, bytes_accessed=10_000_000, transcendentals=0),
        name="fine_level",
    )(both, *got, *raw[::-1], *far, *near[::-1], early, spread, coefficients)


def shards(peers, log_perm, source, low_bound, high_bound):
    nx, ny, nz = peers
    layers, rows, lanes = log_perm.shape
    assert layers == REACH and rows == 2 * SUBLANES and nx > 2 and nz == 2
    both = jnp.concatenate([log_perm, source])
    own, *rows_sent = prep(both, ny)
    if ny == 2:
        got = (permute(rows_sent[0], "gy", ny, [(0, 1)]),)
    else:
        got = swap("gy", ny, rows_sent[1], rows_sent[0])
    for_second = raw_block(both, rows_sent[0], True)
    second = permute(for_second, "gx", nx, neighbour_pairs(nx, 1))
    for_first = raw_block(both, for_second, False)
    raw = (permute(for_first, "gx", nx, neighbour_pairs(nx, 0)), second)
    far_groups = far_pairs(nx)
    halos, lanes_sent = pooled_halos(both, own, got)
    early = lax.ppermute(lanes_sent, "gz", [(0, 1), (1, 0)])
    for_far = pack_far(own, halos, early, len(far_groups), ny > 2)
    far = [permute(tiles, "gx", nx, group) for tiles, group in zip(for_far, far_groups)]
    for_first, for_second = pack_near(own, halos, early, for_far[0], got)
    second = permute(for_second, "gx", nx, neighbour_pairs(nx, 1))
    near = (permute(for_first, "gx", nx, neighbour_pairs(nx, 0)), second)
    coefficients = chebyshev_coefficients(low_bound, high_bound, for_first)
    pooled = pool(coefficients, raw)
    spread = coarse_level(own, halos, pooled, near, far, early, coefficients, peers)
    return fine_level(both, got, raw, far, near, early, spread, coefficients, peers)


def solution(mesh):
    peers = tuple(mesh.shape[axis] for axis in AXES)
    split = P(("groups", "gx"), "gy", "gz")
    return jax.shard_map(
        functools.partial(shards, peers),
        mesh=mesh,
        in_specs=(split, split, P(), P()),
        out_specs=(split, split),
        check_vma=False,
    )
```

```python
import functools

import jax
import jax.numpy as jnp
from jax import lax
from jax.experimental import pallas as pl
from jax.experimental.pallas import tpu as pltpu
from jax.sharding import PartitionSpec as P

DEGREE = 3
REACH = DEGREE + 1
LANES = 128
SUBLANES = 8
storage_rate = 0.1
AXES = ("gx", "gy", "gz")
VMEM = pl.BlockSpec(memory_space=pltpu.VMEM)
ANY = pl.BlockSpec(memory_space=pl.ANY)


AHEAD = pl.CostEstimate(flops=50_000_000_000, bytes_accessed=1_000_000, transcendentals=0)


def iota(shape, dim):
    return lax.broadcasted_iota(jnp.int32, shape, dim)


def turned(value, shift, axis):
    size = value.shape[axis]
    return pltpu.roll(value, shift % size, axis)


def permute(value, axis, peers, pairs):
    cores = lax.axis_size("gz")
    if axis == "gz" or cores % 2:
        return lax.ppermute(value, axis, [pair for i, j in pairs for pair in ((i, j), (j, i))])
    partner = {}
    for i, j in pairs:
        partner[i], partner[j] = j, i
    moves = [
        (i * cores + core, partner[i] * cores + core if i in partner else i * cores + (core ^ 1))
        for i in range(peers)
        for core in range(cores)
    ]
    return lax.ppermute(value, (axis, "gz"), moves)


def neighbour_pairs(peers, start):
    return [(i, i + 1) for i in range(start, peers - 1, 2)]


def first_swap(axis, peers, right, left):
    even = lax.axis_index(axis) % 2 == 0
    return permute(jnp.where(even, right, left), axis, peers, neighbour_pairs(peers, 0))


def second_swap(axis, peers, right, left):
    even = lax.axis_index(axis) % 2 == 0
    return permute(jnp.where(even, left, right), axis, peers, neighbour_pairs(peers, 1))


def swap(axis, peers, right, left):
    got = (first_swap(axis, peers, right, left),)
    return got if peers == 2 else got + (second_swap(axis, peers, right, left),)


def far_pairs(peers):
    pairs = [(i, i + 2) for i in range(peers - 2)]
    groups = [[pair for pair in pairs if pair[0] % 4 < 2], [pair for pair in pairs if pair[0] % 4 >= 2]]
    return [group for group in groups if group]


def from_right(is_first, got):
    return got[0] if len(got) == 1 else jnp.where(is_first, got[0], got[1])


def from_left(is_first, got):
    return got[0] if len(got) == 1 else jnp.where(is_first, got[1], got[0])


def inverse(value):
    guess = pl.reciprocal(value, approx=True)
    return guess * (2.0 - value * guess)


def row_numerators(rows, own, index, peers, face_scale):
    place = iota((rows, LANES), 0)
    right = jnp.where(index < peers - 1, 2.0 * face_scale, 0.0)
    left = jnp.where(index > 0, 2.0 * face_scale, 0.0)
    return jnp.where(place == own - 1, right, jnp.where(place == rows - 1, left, 2.0 * face_scale))


def lane_numerators(rows, index, peers, face_scale):
    place = iota((rows, LANES), 1)
    right = jnp.where(index < peers - 1, 2.0 * face_scale, 0.0)
    left = jnp.where(index > 0, 2.0 * face_scale, 0.0)
    return [jnp.where(place == LANES - 1, side, 2.0 * face_scale) for side in (right, left)]


def lane_tiles(value):
    return [value[:, i : i + LANES] for i in range(0, value.shape[1], LANES)]


def beside(tiles, shift):
    moved = [turned(tile, shift, 1) for tile in tiles]
    lane = iota(tiles[0].shape, 1)
    seam = LANES - 1 if shift < 0 else 0
    return [
        jnp.where(lane == seam, moved[(j - shift) % len(tiles)], moved[j]) for j in range(len(tiles))
    ]


def store_rows(ref, k, j, value):
    rows = value.shape[0]
    ref[k, j, SUBLANES : SUBLANES + rows] = value
    ref[k, j, SUBLANES - 1 : SUBLANES] = value[rows - 1 :]
    ref[k, j, SUBLANES + rows : SUBLANES + rows + 1] = value[:1]


def iterate(count, own_rows, rows, tiles, log_at, source_at, x_faces, y_top, z_top, coef_ref, storage, emit, refs):
    k_ref, tx_ref, ty_ref, tzr_ref, tzl_ref, diag_ref, w_ref, d_ref, r_ref, p_ref = refs
    own_tiles = tiles - 1

    def away(k):
        return max(0, REACH - k, k - (count - 1 - REACH))

    def extent(k, step):
        left = DEGREE - step - away(k)
        return None if left < 0 else (own_rows, own_tiles) if left == 0 else (rows, tiles)

    def coefficient(i, size):
        return jnp.concatenate([coef_ref[i]] * (size // SUBLANES), axis=0)

    z_tops = [z_top[0] if j == own_tiles - 1 else z_top[1] if j == own_tiles else None for j in range(tiles)]

    def resistance(k):
        return [jnp.exp(-tile) for tile in lane_tiles(log_at(k))]

    after = resistance(0)
    tx_before = None
    for k in range(count):
        here = after
        if k + 1 < count:
            after = resistance(k + 1)
            outer = max(away(k), away(k + 1))
            size, number = (rows, tiles) if outer < REACH else (own_rows, own_tiles)
            tx = [x_faces[k] * inverse(here[j][:size] + after[j][:size]) for j in range(number)]
            for j in range(number):
                tx_ref[k, j, :size] = tx[j]
        if away(k) <= DEGREE:
            size, number = extent(k, 0)
            right = beside(here, -1)
            tz = []
            for j in range(tiles):
                scale = z_tops[j][:size] if z_tops[j] is not None else z_top[2]
                tz.append(scale * inverse(here[j][:size] + right[j][:size]))
            tz_left = beside(tz, 1)
            source = lane_tiles(source_at(k))
            for j in range(number):
                store_rows(k_ref, k, j, here[j])
                ty = y_top * inverse(here[j] + k_ref[k, j, SUBLANES + 1 : SUBLANES + 1 + rows])
                store_rows(ty_ref, k, j, ty)
                ty_before = ty_ref[k, j, SUBLANES - 1 : SUBLANES - 1 + size]
                diagonal = storage + (tx_before[j][:size] + tx[j][:size])
                diagonal = diagonal + (ty[:size] + ty_before) + (tz[j] + tz_left[j])
                w = inverse(diagonal)
                direction = source[j][:size] * (coefficient(0, size) * w)
                if (size, number) == (rows, tiles):
                    store_rows(d_ref.at[0], k, j, direction)
                else:
                    d_ref[0, k, j, SUBLANES : SUBLANES + size] = direction
                if extent(k, 1) is not None:
                    tzr_ref[k, j, :size] = tz[j]
                    tzl_ref[k, j, :size] = tz_left[j]
                    diag_ref[k, j, :size] = diagonal
                    w_ref[k, j, :size] = w
                    r_ref[k, j, :size] = source[j][:size]
        tx_before = tx
    for step in range(1, DEGREE + 1):
        old, new = d_ref.at[(step - 1) % 2], d_ref.at[step % 2]
        for k in range(count):
            if extent(k, step) is None:
                continue
            size, number = extent(k, step)
            middle = slice(SUBLANES, SUBLANES + size)
            keep, gain = coefficient(2 * step - 1, size), coefficient(2 * step, size)
            here = [old[k, j, middle] for j in range(tiles)]
            right, left = beside(here, -1), beside(here, 1)
            for j in range(number):
                applied = tx_ref[k, j, :size] * old[k + 1, j, middle] + tx_ref[k - 1, j, :size] * old[k - 1, j, middle]
                applied += (
                    ty_ref[k, j, middle] * old[k, j, SUBLANES + 1 : SUBLANES + 1 + size]
                    + ty_ref[k, j, SUBLANES - 1 : SUBLANES - 1 + size] * old[k, j, SUBLANES - 1 : SUBLANES - 1 + size]
                )
                applied += tzr_ref[k, j, :size] * right[j] + tzl_ref[k, j, :size] * left[j]
                residual = r_ref[k, j, :size] - (diag_ref[k, j, :size] * here[j] - applied)
                fresh = keep * here[j] + gain * (residual * w_ref[k, j, :size])
                if away(k) == 0 and j < own_tiles:
                    so_far = here[j][:own_rows] if step == 1 else p_ref[k, j]
                    total = so_far + fresh[:own_rows]
                    if step == DEGREE:
                        emit(k - REACH, j, total)
                    else:
                        p_ref[k, j] = total
                if step < DEGREE:
                    r_ref[k, j, :size] = residual
                    if (size, number) == (rows, tiles):
                        store_rows(new, k, j, fresh)
                    else:
                        new[k, j, middle] = fresh


def coefficients_kernel(low_ref, high_ref, after_ref, coef_ref):
    low, high = (jnp.full((SUBLANES, LANES), ref[0]) for ref in (low_ref, high_ref))
    theta, delta = (high + low) * 0.5, (high - low) * 0.5
    sigma = theta / delta
    rho = 1.0 / sigma
    coef_ref[0] = 1.0 / theta
    for step in range(DEGREE):
        rho_next = 1.0 / (2.0 * sigma - rho)
        coef_ref[1 + 2 * step] = rho_next * rho
        coef_ref[2 + 2 * step] = 2.0 * rho_next / delta
        rho = rho_next


def chebyshev_coefficients(low_bound, high_bound, after):
    return pl.pallas_call(
        coefficients_kernel,
        out_shape=jax.ShapeDtypeStruct((1 + 2 * DEGREE, SUBLANES, LANES), jnp.float32),
        in_specs=[pl.BlockSpec(memory_space=pltpu.SMEM)] * 2 + [ANY],
        out_specs=VMEM,
        compiler_params=pltpu.CompilerParams(vmem_limit_bytes=4 << 20),
        cost_estimate=pl.CostEstimate(flops=1_000_000, bytes_accessed=100_000, transcendentals=0),
        name="coefficients",
    )(low_bound, high_bound, after)


def put(ref, tile, value):
    for i in range(value.shape[1] // LANES):
        ref[(tile + i) * SUBLANES : (tile + i + 1) * SUBLANES, :] = value[:, i * LANES : (i + 1) * LANES]


def take(ref, tile, count):
    tiles = [ref[(tile + i) * SUBLANES : (tile + i + 1) * SUBLANES, :] for i in range(count)]
    return tiles[0] if count == 1 else jnp.concatenate(tiles, axis=1)


def edges(value):
    lanes = value.shape[-1]
    value = value if isinstance(value, jax.Array) else value.at
    return value[:, lanes - LANES :], value[:, :LANES]


def write_lanes(pairs):
    starts = lax.axis_index("gz") == 0
    each = LANES // REACH
    group = iota((SUBLANES, LANES), 1) // REACH
    merged = None
    for j, (last, first) in enumerate(pairs):
        moved = turned(jnp.where(starts, last, first), REACH * j, 1)
        place = jnp.where(starts, (j - 1) % each, j)
        merged = moved if merged is None else jnp.where(group == place, moved, merged)
    return merged


def read_lanes(tile, slot):
    return turned(tile, -REACH * slot, 1)


def add_lanes(tile, slot, value):
    starts = lax.axis_index("gz") == 0
    group = iota((SUBLANES, LANES), 1) // REACH
    place = jnp.where(starts, slot, (slot - 1) % (LANES // REACH))
    return jnp.where(group == place, turned(value, REACH * slot, 1), tile)


def lane_slots(layers, row_tiles, n_got):
    keys = [("own", a, layer, i) for a in range(2) for layer in range(layers) for i in range(row_tiles)]
    keys += [("pooled", x, a) for x in range(2) for a in range(2)]
    shared = len(keys)
    keys += [("halo", i, half) for i in range(n_got) for half in range(2)]
    keys += [("got", g, layer) for g in range(n_got) for layer in range(layers)]
    return {key: i for i, key in enumerate(keys)}, shared


def near_layout(lanes, wide):
    whole, half = lanes // LANES, lanes // LANES // 2
    if wide:
        parts = [("log1", whole), ("source1", whole), ("log2", whole), ("source2", whole)]
        parts += [(name, half) for name in ("halo0", "halo1", "halo2", "halo3", "source")]
    else:
        parts = [("strip", whole), ("halo", half), ("source", half), ("row", 1)]
    layout, start = {}, 0
    for name, count in parts + [("lanes", 1)]:
        layout[name] = (start, count)
        start += count
    return layout, start


def near_lane_slots(lanes, wide, shared):
    names = [name for name in near_layout(lanes, wide)[0] if name not in ("source", "lanes")]
    return {name: shared + i for i, name in enumerate(names)}


def rows_to_lanes(row_tile, count):
    return jnp.concatenate(
        [jnp.broadcast_to(row_tile[j : j + 1], (SUBLANES, LANES)) for j in range(count)], axis=1
    )


def window_scratch(count, own_rows, rows, tiles):
    plain = pltpu.VMEM((count, tiles, rows, LANES), jnp.float32)
    margins = pltpu.VMEM((count, tiles, rows + 2 * SUBLANES, LANES), jnp.float32)
    pair = pltpu.VMEM((2, count, tiles, rows + 2 * SUBLANES, LANES), jnp.float32)
    total = pltpu.VMEM((count, tiles, own_rows, LANES), jnp.float32)
    return [margins, plain, margins, plain, plain, plain, plain, pair, plain, total]


def exact_dot(value, zero_one):
    parts = []
    for _ in range(3):
        part = value.astype(jnp.bfloat16)
        parts.append(part)
        value = value - part.astype(jnp.float32)
    rows = value.shape[0]
    out = jnp.dot(jnp.concatenate(parts, axis=0), zero_one, preferred_element_type=jnp.float32)
    return (out[2 * rows :] + out[rows : 2 * rows]) + out[:rows]


def row_pairs(top, bottom, sum_ref):
    tiles = top.shape[1] // LANES
    for tile in range(tiles):
        columns = slice(tile * LANES, (tile + 1) * LANES)
        sum_ref[tile, :SUBLANES] = top[:, columns]
        sum_ref[tile, SUBLANES:] = bottom[:, columns]
    return jnp.concatenate(
        [
            sum_ref[tile, pl.ds(0, SUBLANES, stride=2), :] + sum_ref[tile, pl.ds(1, SUBLANES, stride=2), :]
            for tile in range(tiles)
        ],
        axis=1,
    )


def lane_pairs(pieces):
    lanes = pieces[0].shape[1]
    pick = (iota((lanes, lanes // 2), 0) // 2 == iota((lanes, lanes // 2), 1)).astype(jnp.bfloat16)
    pooled = exact_dot(jnp.concatenate(pieces, axis=0), pick)
    return [pooled[SUBLANES * i : SUBLANES * (i + 1)] for i in range(len(pieces))]


def join_halo(near, beyond, starts):
    row = iota(near.shape, 0)
    up, down = turned(beyond, 3, 0), turned(beyond, -3, 0)
    right = jnp.where((row == 3) | (row == 7), up, jnp.where(row == 6, turned(beyond, 5, 0), near))
    left = jnp.where((row == 0) | (row == 4), down, jnp.where(row == 5, up, near))
    return jnp.where(starts, right, left)


def beyond_halo(joined, starts):
    row = iota(joined.shape, 0)
    up, down = turned(joined, 3, 0), turned(joined, -3, 0)
    right = jnp.where(row == 1, turned(joined, -5, 0), down)
    left = jnp.where(row == 2, down, up)
    return jnp.where(starts, right, left)


def join_third(near, third):
    row = iota(near.shape, 0)
    return jnp.where(
        row == 3, turned(third, 3, 0), jnp.where(row == 4, turned(third, -3, 0), near)
    )


def third_halo(joined):
    return jnp.where(iota(joined.shape, 0) < REACH, turned(joined, -3, 0), turned(joined, 3, 0))


def parts(both_ref):
    layers = both_ref.shape[0] // 2
    return both_ref.at[:layers], both_ref.at[layers:]


def prep_kernel(both_ref, pooled_ref, *refs):
    *out_refs, sum_ref = refs
    log_ref, source_ref = parts(both_ref)
    layers, rows, lanes = log_ref.shape
    starts = lax.axis_index("gy") == 0

    def put(slot, left, right):
        if len(out_refs) == 1:
            out_refs[0][slot] = jnp.where(starts, right, left)
        else:
            out_refs[0][slot], out_refs[1][slot] = left, right

    half = lanes // 2
    upper = iota((SUBLANES, lanes), 0) < REACH
    pieces = []
    for x in range(2):
        for ref in (log_ref, source_ref):
            both = ref[2 * x] + ref[2 * x + 1]
            pieces.append(row_pairs(both[:SUBLANES], both[SUBLANES:], sum_ref))
    log0, source0, log1, source1 = lane_pairs(pieces)
    log0, log1 = log0 * 0.125, log1 * 0.125
    pooled_ref[0] = jnp.concatenate([log0, source0], axis=1)
    pooled_ref[1] = jnp.concatenate([log1, source1], axis=1)
    for layer in range(layers):
        put(
            layer,
            jnp.where(upper, log_ref[layer, :SUBLANES], turned(source_ref[layer, :SUBLANES], REACH, 0)),
            jnp.where(upper, turned(source_ref[layer, SUBLANES:], REACH, 0), log_ref[layer, SUBLANES:]),
        )
    pair = iota((SUBLANES, half), 0) // 2

    def four(*tiles):
        merged = jnp.where(
            pair == 0, tiles[0], jnp.where(pair == 1, tiles[1], jnp.where(pair == 2, tiles[2], tiles[3]))
        )
        return jnp.concatenate([merged, merged], axis=1)

    put(
        layers,
        four(turned(log1, -2, 0), log0, turned(source1, 2, 0), turned(source0, 4, 0)),
        four(turned(log0, -4, 0), turned(log1, -2, 0), source0, turned(source1, 2, 0)),
    )


def prep(both, ny):
    layers, rows, lanes = both.shape[0] // 2, *both.shape[1:]
    outs = 1 if ny == 2 else 2

    def tiles(count):
        return jax.ShapeDtypeStruct((count, SUBLANES, lanes), jnp.float32)

    return pl.pallas_call(
        prep_kernel,
        out_shape=(tiles(2),) + (tiles(layers + 1),) * outs,
        in_specs=[VMEM],
        out_specs=(VMEM,) * (1 + outs),
        scratch_shapes=[pltpu.VMEM((lanes // LANES, 2 * SUBLANES, LANES), jnp.float32)],
        compiler_params=pltpu.CompilerParams(vmem_limit_bytes=8 << 20),
        cost_estimate=pl.CostEstimate(flops=5_000_000, bytes_accessed=700_000, transcendentals=0),
        name="prep",
    )(both)


def raw_kernel(to_right_if_odd, both_ref, after_ref, out_ref):
    log_ref, source_ref = parts(both_ref)
    layers = log_ref.shape[0]
    odd = lax.axis_index("gx") % 2
    skip = odd if to_right_if_odd else 1 - odd
    for layer in range(layers):
        out_ref[layer] = log_ref[layer]
    for layer in range(layers - 1):
        out_ref[layers + layer] = source_ref[layer + skip]


def raw_block(both, after, to_right_if_odd):
    layers, rows, lanes = both.shape[0] // 2, *both.shape[1:]
    return pl.pallas_call(
        functools.partial(raw_kernel, to_right_if_odd),
        out_shape=jax.ShapeDtypeStruct((2 * layers - 1, rows, lanes), jnp.float32),
        in_specs=[VMEM, ANY],
        out_specs=VMEM,
        compiler_params=pltpu.CompilerParams(vmem_limit_bytes=8 << 20),
        cost_estimate=pl.CostEstimate(flops=1_000_000, bytes_accessed=500_000, transcendentals=0),
        name="raw_block",
    )(both, after)


def halos_kernel(wide, both_ref, pooled_ref, *refs):
    *got_refs, halo_ref, sent_ref, sum_ref = refs
    layers, lanes = got_refs[0].shape[0] - 1, got_refs[0].shape[2]
    iy = lax.axis_index("gy")
    even, starts = iy % 2 == 0, iy == 0
    half = lanes // 2
    upper = iota((SUBLANES, lanes), 0) < REACH
    row = iota((SUBLANES, half), 0)

    def got(slot):
        tiles = tuple(ref[slot] for ref in got_refs)
        return from_right(even, tiles), from_left(even, tiles)

    strips = [got(layer) for layer in range(layers)]
    extra = [tile[:, :half] for tile in got(layers)]
    pieces = []
    for side in range(2 if wide else 1):
        both = [strips[2 * x][side] + strips[2 * x + 1][side] for x in range(2)]
        pieces.append(row_pairs(*both, sum_ref))
    fine_rows = lane_pairs(pieces)

    def right_halos(rows, extra):
        rows = jnp.where(row % 4 < 2, rows * 0.125, rows)
        return [
            jnp.where(row < 2, near, jnp.where((row == 4) | (row == 5), far, more))
            for near, far, more in (
                (rows, turned(rows, 2, 0), extra),
                (turned(rows, 4, 0), turned(rows, -2, 0), turned(extra, 2, 0)),
            )
        ]

    def left_halos(rows, extra):
        rows = jnp.where(row % 4 >= 2, rows * 0.125, rows)
        return [
            jnp.where((row == 2) | (row == 3), near, jnp.where(row >= 6, far, more))
            for near, far, more in (
                (rows, turned(rows, -2, 0), extra),
                (turned(rows, 4, 0), turned(rows, 2, 0), turned(extra, -2, 0)),
            )
        ]

    right, left = right_halos(fine_rows[0], extra[0]), left_halos(fine_rows[-1], extra[1])
    if wide:
        top = row < REACH
        halos = [jnp.where(top, right[x], turned(left[x], REACH, 0)) for x in range(2)]
        halos += [jnp.where(top, turned(right[x], REACH, 0), left[x]) for x in range(2)]
    else:
        halos = [jnp.where(starts, right[x], left[x]) for x in range(2)]

    def pair(left, right):
        return jnp.concatenate([left, right], axis=1)

    for i in range(len(halos) // 2):
        halo_ref[i] = pair(halos[2 * i], halos[2 * i + 1])
    pairs = {}
    rows = both_ref.shape[1]
    for a, ref in enumerate(parts(both_ref)):
        for layer in range(layers):
            for i in range(rows // SUBLANES):
                pairs["own", a, layer, i] = edges(ref[layer, i * SUBLANES : (i + 1) * SUBLANES])
    for x in range(2):
        for a in range(2):
            pairs["pooled", x, a] = edges(pooled_ref[x, :, a * half : (a + 1) * half])
    for i, halo in enumerate(halos):
        pairs["halo", i // 2, i % 2] = edges(halo)
    for g, ref in enumerate(got_refs):
        for layer in range(layers):
            pairs["got", g, layer] = edges(ref[layer])
    slots, _ = lane_slots(layers, rows // SUBLANES, len(got_refs))
    sent_ref[...] = write_lanes([pairs[key] for key in slots])


def pooled_halos(both, pooled, got):
    slots, rows, lanes = got[0].shape
    return pl.pallas_call(
        functools.partial(halos_kernel, len(got) == 2),
        out_shape=(
            jax.ShapeDtypeStruct((len(got), SUBLANES, lanes), jnp.float32),
            jax.ShapeDtypeStruct((SUBLANES, LANES), jnp.float32),
        ),
        in_specs=[VMEM] * (2 + len(got)),
        out_specs=(VMEM,) * 2,
        scratch_shapes=[pltpu.VMEM((lanes // LANES, 2 * SUBLANES, LANES), jnp.float32)],
        compiler_params=pltpu.CompilerParams(vmem_limit_bytes=8 << 20),
        cost_estimate=AHEAD,
        name="halos",
    )(both, pooled, *got)


def pack_far_kernel(wide, pooled_ref, halo_ref, lanes_ref, *far_refs):
    half = pooled_ref.shape[2] // 2
    low = lax.axis_index("gx") % 4 < 2

    def tiles(inner):
        return (
            pooled_ref[inner, :, :half],
            pooled_ref[1 - inner, :, :half],
            pooled_ref[inner, :, half:],
            halo_ref[0, :, inner * half : (inner + 1) * half],
        )

    for group, ref in enumerate(far_refs):
        for i, (right, left) in enumerate(zip(tiles(1), tiles(0))):
            put(ref, i * (half // LANES), jnp.where(low, *((right, left) if group == 0 else (left, right))))
        put(ref, 4 * (half // LANES), lanes_ref[...])
        for spare in range(4 * (half // LANES) + 1, ref.shape[0] // SUBLANES):
            put(ref, spare, jnp.zeros((SUBLANES, LANES), jnp.float32))


def pack_far(pooled, halos, early, n_far, wide):
    _, rows, lanes = pooled.shape
    far_rows = max(2 * lanes // LANES + 1, 0 if wide else near_layout(lanes, wide)[1]) * SUBLANES
    return pl.pallas_call(
        functools.partial(pack_far_kernel, wide),
        out_shape=(jax.ShapeDtypeStruct((far_rows, LANES), jnp.float32),) * n_far,
        in_specs=[VMEM] * 3,
        out_specs=(VMEM,) * n_far,
        compiler_params=pltpu.CompilerParams(vmem_limit_bytes=8 << 20),
        cost_estimate=pl.CostEstimate(flops=1_000_000, bytes_accessed=500_000, transcendentals=0),
        name="pack_far",
    )(pooled, halos, early)


def pack_near_kernel(wide, pooled_ref, halo_ref, early_ref, after_ref, *refs):
    *got_refs, first_ref, second_ref = refs
    layers, lanes = got_refs[0].shape[0] - 1, got_refs[0].shape[2]
    ix, iy = lax.axis_index("gx"), lax.axis_index("gy")
    even, starts = iy % 2 == 0, iy == 0
    half = lanes // 2
    upper = iota((SUBLANES, lanes), 0) < REACH

    def got(slot):
        tiles = tuple(ref[slot] for ref in got_refs)
        return from_right(even, tiles), from_left(even, tiles)

    strips = [got(layer) for layer in range(layers)]
    halos = [halo_ref[i // 2, :, (i % 2) * half : (i % 2 + 1) * half] for i in range(4 if wide else 2)]
    sources = [pooled_ref[x, :, half:] for x in range(2)]

    slots, shared = lane_slots(layers, 2, len(got_refs))

    def strip_lanes(layer):
        tiles = tuple(read_lanes(early_ref[...], slots["got", g, layer]) for g in range(len(got_refs)))
        return from_right(even, tiles), from_left(even, tiles)

    def halo_lanes(i):
        return read_lanes(early_ref[...], slots["halo", i // 2, i % 2])

    def near_tiles(order, strips, halos):
        near, beyond = order[0] // 2, order[-1] // 2
        width = strips[0][0].shape[1]
        upper = iota((SUBLANES, width), 0) < REACH
        if wide:
            log_rows = [jnp.where(upper, *strips[layer]) for layer in range(layers)]
            source_rows = [turned(jnp.where(upper, *strips[layer][::-1]), REACH, 0) for layer in range(layers)]
            return {
                "log1": join_third(log_rows[order[0]], log_rows[order[2]]),
                "source1": source_rows[order[0]],
                "log2": log_rows[order[1]],
                "source2": source_rows[order[1]],
                "halo0": halos[near],
                "halo1": halos[beyond],
                "halo2": halos[2 + near],
                "halo3": halos[2 + beyond],
            }
        first, second, third = (strips[layer][0] for layer in order[:3])
        place = iota((SUBLANES, width), 0)
        right = jnp.where(place == 3, turned(third, 3, 0), jnp.where(place >= 6, turned(second, -2, 0), first))
        left = jnp.where(place == 4, turned(third, -3, 0), jnp.where(place < 2, turned(second, 2, 0), first))
        line = jnp.where(starts, second[4:5], second[3:4])
        if width == LANES:
            lines = jnp.broadcast_to(line, (SUBLANES, LANES))
        else:
            lines = jnp.zeros((SUBLANES, LANES), jnp.float32)
            for j in range(width // LANES):
                lines = jnp.where(iota(lines.shape, 0) == j, line[:, j * LANES : (j + 1) * LANES], lines)
        return {
            "strip": jnp.where(starts, right, left),
            "halo": join_halo(halos[near], halos[beyond], starts),
            "row": lines,
        }

    def side(order):
        tiles = near_tiles(order, strips, halos)
        tiles["source"] = sources[order[-1] // 2]
        lanes_tile = early_ref[...]
        n_halos = 4 if wide else 2
        beside = near_tiles(
            order, [strip_lanes(layer) for layer in range(layers)], [halo_lanes(i) for i in range(n_halos)]
        )
        for name, slot in near_lane_slots(lanes, wide, shared).items():
            lanes_tile = add_lanes(lanes_tile, slot, beside[name])
        tiles["lanes"] = lanes_tile
        return tiles

    forward = list(range(layers))
    layout, _ = near_layout(lanes, wide)
    right, left = side(forward[::-1]), side(forward)
    for name, (start, _) in layout.items():
        put(first_ref, start, jnp.where(ix % 2 == 0, right[name], left[name]))
        put(second_ref, start, jnp.where(ix % 2 == 0, left[name], right[name]))


def pack_near(pooled, halos, early, after, got):
    slots, rows, lanes = got[0].shape
    wide = len(got) == 2
    out = jax.ShapeDtypeStruct((near_layout(lanes, wide)[1] * SUBLANES, LANES), jnp.float32)
    return pl.pallas_call(
        functools.partial(pack_near_kernel, wide),
        out_shape=(out, out),
        in_specs=[VMEM] * 3 + [ANY] + [VMEM] * len(got),
        out_specs=(VMEM,) * 2,
        compiler_params=pltpu.CompilerParams(vmem_limit_bytes=8 << 20),
        cost_estimate=pl.CostEstimate(flops=1_000_000, bytes_accessed=500_000, transcendentals=0),
        name="pack_near",
    )(pooled, halos, early, after, *got)


def pool_kernel(after_ref, first_ref, second_ref, out_ref, sum_ref):
    layers = REACH
    even = lax.axis_index("gx") % 2 == 0
    pieces = []
    for side, pick in enumerate((from_left, from_right)):

        def block(slot):
            return pick(even, (first_ref[slot], second_ref[slot]))

        for top in (0, 2, layers + 1 if side == 0 else layers):
            both = block(top) + block(top + 1)
            pieces.append(row_pairs(both[:SUBLANES], both[SUBLANES:], sum_ref))
    for i, tile in enumerate(lane_pairs(pieces)):
        put(out_ref, i * (tile.shape[1] // LANES), tile * (0.125 if i % 3 < 2 else 1.0))


def pool(after, raw):
    _, rows, lanes = raw[0].shape
    return pl.pallas_call(
        pool_kernel,
        out_shape=jax.ShapeDtypeStruct((6 * (lanes // 2 // LANES) * SUBLANES, LANES), jnp.float32),
        in_specs=[ANY] + [VMEM] * 2,
        out_specs=VMEM,
        scratch_shapes=[pltpu.VMEM((lanes // LANES, 2 * SUBLANES, LANES), jnp.float32)],
        compiler_params=pltpu.CompilerParams(vmem_limit_bytes=16 << 20),
        cost_estimate=pl.CostEstimate(flops=1_000_000, bytes_accessed=1_000_000, transcendentals=0),
        name="pool",
    )(after, *raw)


def near_part(refs, even, lanes, wide, side, name):
    start, count = near_layout(lanes, wide)[0][name]
    pick = from_left if side == 0 else from_right
    got = pick(even, tuple(take(ref, start, count) for ref in refs))
    return rows_to_lanes(got, lanes // LANES) if name == "row" else got


def far_part(refs, low, lanes, side, i):
    count = lanes // 2 // LANES
    pick = from_left if side == 0 else from_right
    return pick(low, tuple(take(ref, i * count, count) for ref in refs))


def coarse_part(peers, n_far, own_ref, halo_ref, pool_ref, first_ref, second_ref, *refs):
    near_refs, far_refs = (first_ref, second_ref), refs[:n_far]
    early_ref, coef_ref, out_ref, wide_ref, *scratch = refs[n_far:]
    ix, iy, iz = (lax.axis_index(axis) for axis in AXES)
    nx, ny, nz = peers
    wide = ny > 2
    fine_lanes = own_ref.shape[2]
    lanes, rows = fine_lanes // 2, SUBLANES
    even, low, starts = ix % 2 == 0, ix % 4 < 2, iy == 0
    top = iota((rows, lanes + LANES), 0) < REACH
    slots, shared = lane_slots(REACH, 2, 2 if wide else 1)
    near_slots = near_lane_slots(fine_lanes, wide, shared)
    own_lanes = early_ref[...]
    near_lanes = [near_part(near_refs, even, fine_lanes, wide, side, "lanes") for side in range(2)]
    far_lanes = [
        pick(low, tuple(take(ref, 4 * (lanes // LANES), 1) for ref in far_refs))
        for pick in (from_left, from_right)
    ]

    def columns(half):
        return slice(half * lanes, (half + 1) * lanes)

    def join(core, tile, slot):
        return jnp.concatenate([core, read_lanes(tile, slot)], axis=1)

    def near(side, name):
        core = near_part(near_refs, even, fine_lanes, wide, side, name)
        return join(core, near_lanes[side], near_slots[name])

    def far(side, i):
        core = far_part(far_refs, low, fine_lanes, side, i)
        return join(core, far_lanes[side], slots["pooled", 1 - side, 0])

    def split(tile, a):
        other = turned(tile, REACH, 0)
        return jnp.where(top, tile, other) if a == 0 else jnp.where(top, other, tile)

    def window(a, k):
        block, layer = k // 2 - 2, k % 2
        nearest = layer == (1 if block < 0 else 0)
        side = 0 if block < 0 else 1
        if abs(block) == 2:
            if a == 1:
                core = far(side, 2)
                return jnp.concatenate([core, jnp.zeros_like(core)], axis=0)
            halo = far(side, 3)
            halo = halo if wide else split(halo, 0)
            return jnp.concatenate([far(side, 0 if nearest else 1), halo], axis=0)
        if block == 0:
            core = join(own_ref[layer, :, columns(a)], own_lanes, slots["pooled", layer, a])
            if wide:
                halo = join(halo_ref[a, :, columns(layer)], own_lanes, slots["halo", a, layer])
            else:
                halo = split(join(halo_ref[0, :, columns(layer)], own_lanes, slots["halo", 0, layer]), a)
            return jnp.concatenate([core, halo], axis=0)
        if a == 0 or nearest:
            i = layer if a == 0 else 2
            core = take(pool_ref, (3 * side + i) * (lanes // LANES), lanes // LANES)
        else:
            core = near_part(near_refs, even, fine_lanes, wide, side, "source")
        core = join(core, near_lanes[side], slots["pooled", layer, a])
        if wide:
            halo = near(side, f"halo{2 * a + (0 if nearest else 1)}")
        else:
            joined = near(side, "halo")
            halo = split(joined if nearest else beyond_halo(joined, starts), a)
        return jnp.concatenate([core, halo], axis=0)

    def open_face(inside):
        return jnp.where(inside, 4.0, 0.0)

    faces = [4.0] * 9
    faces[1], faces[3] = open_face(ix > 1), open_face(ix > 0)
    faces[5], faces[7] = open_face(ix < nx - 1), open_face(ix < nx - 2)
    *scratch, p_ref = scratch

    def emit(layer, tile, value):
        p_ref[layer * rows : (layer + 1) * rows, tile * LANES : (tile + 1) * LANES] = value

    iterate(
        2 + 2 * REACH,
        rows,
        2 * rows,
        lanes // LANES + 1,
        functools.partial(window, 0),
        functools.partial(window, 1),
        faces,
        row_numerators(2 * rows, rows, iy, ny, 2.0),
        lane_numerators(2 * rows, iz, nz, 2.0) + [4.0],
        coef_ref,
        8.0 * storage_rate,
        emit,
        scratch,
    )
    widen = (iota((lanes, 2 * lanes), 0) == iota((lanes, 2 * lanes), 1) // 2).astype(jnp.bfloat16)
    spread = exact_dot(p_ref[...], widen)
    for x in range(2):
        for tile in range(2 * lanes // LANES):
            part = slice(tile * LANES, (tile + 1) * LANES)
            for half in range(2):
                wide_ref[tile, pl.ds(half, rows, stride=2), :] = spread[x * rows : (x + 1) * rows, part]
            for twin in range(2):
                out_ref[2 * x + twin, :, part] = wide_ref[tile]


def levels_kernel(peers, n_far, both_ref, *refs):
    log_ref, source_ref = parts(both_ref)
    layers, rows, lanes = log_ref.shape
    ix, iy, iz = (lax.axis_index(axis) for axis in AXES)
    nx, ny, nz = peers
    wide = ny > 2
    n_got = 2 if wide else 1
    got_refs, refs = refs[:n_got], refs[n_got:]
    second_ref, first_ref = refs[:2]
    far_refs = refs[2 : 2 + n_far]
    second_near_ref, first_near_ref, early_ref, coef_ref = refs[2 + n_far : 6 + n_far]
    near_refs = first_near_ref, second_near_ref
    own_ref, halo_ref, pool_ref, fine_ref, diff_ref, *scratch = refs[6 + n_far :]
    scratch, (spread_ref, *coarse_scratch) = scratch[:10], scratch[10:]
    coarse_part(
        peers,
        n_far,
        own_ref,
        halo_ref,
        pool_ref,
        *near_refs,
        *far_refs,
        early_ref,
        coef_ref,
        spread_ref,
        *coarse_scratch,
    )
    even, starts = ix % 2 == 0, iy == 0
    count = 3 * layers
    upper = iota((SUBLANES, lanes + LANES), 0) < REACH
    slots, shared = lane_slots(layers, rows // SUBLANES, n_got)
    near_slots = near_lane_slots(lanes, wide, shared)
    own_lanes = early_ref[...]
    near_lanes = [near_part(near_refs, even, lanes, wide, side, "lanes") for side in range(2)]

    def join(core, tile, *keys):
        beside = jnp.concatenate([read_lanes(tile, key) for key in keys], axis=0)
        return jnp.concatenate([core, beside], axis=1)

    def near(side, name):
        return join(near_part(near_refs, even, lanes, wide, side, name), near_lanes[side], near_slots[name])

    def near_halo(a, side, distance):
        if wide:
            tile = near(side, ("log" if a == 0 else "source") + ("2" if distance == 2 else "1"))
        elif a == 1:
            return near(side, "row") if distance == 2 else turned(near(side, "strip"), REACH, 0)
        else:
            tile = near(side, "strip")
            if distance == 2:
                return jnp.where(starts, turned(tile, 2, 0), turned(tile, -2, 0))
        return third_halo(tile) if a == 0 and distance > 2 else tile

    def window(a, k):
        block, layer = k // layers - 1, k % layers
        if block == 0:
            core = (log_ref, source_ref)[a][layer]
            core = join(core, own_lanes, *(slots["own", a, layer, i] for i in range(rows // SUBLANES)))
            tiles = tuple(
                join(ref[layer], own_lanes, slots["got", g, layer]) for g, ref in enumerate(got_refs)
            )
            halo = tiles[0]
            if wide:
                sides = from_right(iy % 2 == 0, tiles), from_left(iy % 2 == 0, tiles)
                halo = jnp.where(upper, *(sides if a == 0 else sides[::-1]))
            if a == 1:
                halo = turned(halo, REACH, 0)
            return jnp.concatenate([core, halo], axis=0)
        side, pick = (0, from_left) if block < 0 else (1, from_right)
        slot = layer if a == 0 else layers + layer - (1 if block < 0 else 0)
        core = pick(even, (first_ref[slot], second_ref[slot]))
        core = join(core, near_lanes[side], *(slots["own", a, layer, i] for i in range(rows // SUBLANES)))
        halo = near_halo(a, side, layers - layer if block < 0 else layer + 1)
        return jnp.concatenate([core, halo], axis=0)

    faces = [2.0] * (count - 1)
    faces[layers - 1] = jnp.where(ix > 0, 2.0, 0.0)
    faces[2 * layers - 1] = jnp.where(ix < nx - 1, 2.0, 0.0)

    def emit(layer, tile, value):
        part = slice(tile * LANES, (tile + 1) * LANES)
        fine_ref[layer, :, part] = value
        diff_ref[layer, :, part] = value - spread_ref[layer, :, part]

    iterate(
        count,
        rows,
        rows + 2 * REACH,
        lanes // LANES + 1,
        functools.partial(window, 0),
        functools.partial(window, 1),
        faces,
        row_numerators(rows + 2 * REACH, rows, iy, ny, 1.0),
        lane_numerators(rows + 2 * REACH, iz, nz, 1.0) + [2.0],
        coef_ref,
        storage_rate,
        emit,
        scratch,
    )


def levels(both, got, raw, far, near, early, coefficients, own, halos, pooled, peers):
    layers, rows, lanes = both.shape[0] // 2, *both.shape[1:]
    half = lanes // 2
    out = jax.ShapeDtypeStruct((layers, rows, lanes), jnp.float32)
    return pl.pallas_call(
        functools.partial(levels_kernel, peers, len(far)),
        out_shape=(out, out),
        in_specs=[VMEM] * (10 + len(got) + len(far)),
        out_specs=(VMEM, VMEM),
        scratch_shapes=window_scratch(3 * layers, rows, rows + 2 * REACH, lanes // LANES + 1)
        + [
            pltpu.VMEM((layers, rows, lanes), jnp.float32),
            pltpu.VMEM((lanes // LANES, rows, LANES), jnp.float32),
        ]
        + window_scratch(2 + 2 * REACH, SUBLANES, 2 * SUBLANES, half // LANES + 1)
        + [pltpu.VMEM((2 * SUBLANES, half), jnp.float32)],
        compiler_params=pltpu.CompilerParams(vmem_limit_bytes=32 << 20),
        cost_estimate=pl.CostEstimate(flops=20_000_000, bytes_accessed=10_000_000, transcendentals=0),
        name="levels",
    )(both, *got, *raw[::-1], *far, *near[::-1], early, coefficients, own, halos, pooled)


def shards(peers, log_perm, source, low_bound, high_bound):
    nx, ny, nz = peers
    layers, rows, lanes = log_perm.shape
    assert layers == REACH and rows == 2 * SUBLANES and nx > 2 and nz == 2
    both = jnp.concatenate([log_perm, source])
    own, *rows_sent = prep(both, ny)
    if ny == 2:
        got = (permute(rows_sent[0], "gy", ny, [(0, 1)]),)
    else:
        got = swap("gy", ny, rows_sent[1], rows_sent[0])
    for_second = raw_block(both, rows_sent[0], True)
    second = permute(for_second, "gx", nx, neighbour_pairs(nx, 1))
    for_first = raw_block(both, for_second, False)
    raw = (permute(for_first, "gx", nx, neighbour_pairs(nx, 0)), second)
    far_groups = far_pairs(nx)
    halos, lanes_sent = pooled_halos(both, own, got)
    early = lax.ppermute(lanes_sent, "gz", [(0, 1), (1, 0)])
    for_far = pack_far(own, halos, early, len(far_groups), ny > 2)
    far = [permute(tiles, "gx", nx, group) for tiles, group in zip(for_far, far_groups)]
    for_first, for_second = pack_near(own, halos, early, for_far[0], got)
    second = permute(for_second, "gx", nx, neighbour_pairs(nx, 1))
    near = (permute(for_first, "gx", nx, neighbour_pairs(nx, 0)), second)
    coefficients = chebyshev_coefficients(low_bound, high_bound, for_first)
    pooled = pool(coefficients, raw)
    return levels(both, got, raw, far, near, early, coefficients, own, halos, pooled, peers)


def solution(mesh):
    peers = tuple(mesh.shape[axis] for axis in AXES)
    split = P(("groups", "gx"), "gy", "gz")
    return jax.shard_map(
        functools.partial(shards, peers),
        mesh=mesh,
        in_specs=(split, split, P(), P()),
        out_specs=(split, split),
        check_vma=False,
    )
```

```python
import functools

import jax
import jax.numpy as jnp
from jax import lax
from jax.experimental import pallas as pl
from jax.experimental.pallas import tpu as pltpu
from jax.sharding import PartitionSpec as P

DEGREE = 3
REACH = DEGREE + 1
LANES = 128
SUBLANES = 8
storage_rate = 0.1
AXES = ("gx", "gy", "gz")
VMEM = pl.BlockSpec(memory_space=pltpu.VMEM)
ANY = pl.BlockSpec(memory_space=pl.ANY)


AHEAD = pl.CostEstimate(flops=50_000_000_000, bytes_accessed=1_000_000, transcendentals=0)


def iota(shape, dim):
    return lax.broadcasted_iota(jnp.int32, shape, dim)


def turned(value, shift, axis):
    size = value.shape[axis]
    return pltpu.roll(value, shift % size, axis)


def permute(value, axis, peers, pairs):
    cores = lax.axis_size("gz")
    if axis == "gz" or cores % 2:
        return lax.ppermute(value, axis, [pair for i, j in pairs for pair in ((i, j), (j, i))])
    partner = {}
    for i, j in pairs:
        partner[i], partner[j] = j, i
    moves = [
        (i * cores + core, partner[i] * cores + core if i in partner else i * cores + (core ^ 1))
        for i in range(peers)
        for core in range(cores)
    ]
    return lax.ppermute(value, (axis, "gz"), moves)


def neighbour_pairs(peers, start):
    return [(i, i + 1) for i in range(start, peers - 1, 2)]


def first_swap(axis, peers, right, left):
    even = lax.axis_index(axis) % 2 == 0
    return permute(jnp.where(even, right, left), axis, peers, neighbour_pairs(peers, 0))


def second_swap(axis, peers, right, left):
    even = lax.axis_index(axis) % 2 == 0
    return permute(jnp.where(even, left, right), axis, peers, neighbour_pairs(peers, 1))


def swap(axis, peers, right, left):
    got = (first_swap(axis, peers, right, left),)
    return got if peers == 2 else got + (second_swap(axis, peers, right, left),)


def far_pairs(peers):
    pairs = [(i, i + 2) for i in range(peers - 2)]
    groups = [[pair for pair in pairs if pair[0] % 4 < 2], [pair for pair in pairs if pair[0] % 4 >= 2]]
    return [group for group in groups if group]


def from_right(is_first, got):
    return got[0] if len(got) == 1 else jnp.where(is_first, got[0], got[1])


def from_left(is_first, got):
    return got[0] if len(got) == 1 else jnp.where(is_first, got[1], got[0])


def inverse(value):
    guess = pl.reciprocal(value, approx=True)
    return guess * (2.0 - value * guess)


def row_numerators(rows, own, index, peers, face_scale):
    place = iota((rows, LANES), 0)
    right = jnp.where(index < peers - 1, 2.0 * face_scale, 0.0)
    left = jnp.where(index > 0, 2.0 * face_scale, 0.0)
    return jnp.where(place == own - 1, right, jnp.where(place == rows - 1, left, 2.0 * face_scale))


def lane_numerators(rows, index, peers, face_scale):
    place = iota((rows, LANES), 1)
    right = jnp.where(index < peers - 1, 2.0 * face_scale, 0.0)
    left = jnp.where(index > 0, 2.0 * face_scale, 0.0)
    return [jnp.where(place == LANES - 1, side, 2.0 * face_scale) for side in (right, left)]


def lane_tiles(value):
    return [value[:, i : i + LANES] for i in range(0, value.shape[1], LANES)]


def beside(tiles, shift):
    moved = [turned(tile, shift, 1) for tile in tiles]
    lane = iota(tiles[0].shape, 1)
    seam = LANES - 1 if shift < 0 else 0
    return [
        jnp.where(lane == seam, moved[(j - shift) % len(tiles)], moved[j]) for j in range(len(tiles))
    ]


def store_rows(ref, k, j, value):
    rows = value.shape[0]
    ref[k, j, SUBLANES : SUBLANES + rows] = value
    ref[k, j, SUBLANES - 1 : SUBLANES] = value[rows - 1 :]
    ref[k, j, SUBLANES + rows : SUBLANES + rows + 1] = value[:1]


def iterate(count, own_rows, rows, tiles, log_at, source_at, x_faces, y_top, z_top, coef_ref, storage, emit, refs, ready=None):
    k_ref, tx_ref, ty_ref, tzr_ref, tzl_ref, diag_ref, w_ref, d_ref, r_ref, p_ref = refs
    own_tiles = tiles - 1

    def away(k):
        return max(0, REACH - k, k - (count - 1 - REACH))

    def extent(k, step):
        left = DEGREE - step - away(k)
        return None if left < 0 else (own_rows, own_tiles) if left == 0 else (rows, tiles)

    def coefficient(i, size):
        return jnp.concatenate([coef_ref[i]] * (size // SUBLANES), axis=0)

    z_tops = [z_top[0] if j == own_tiles - 1 else z_top[1] if j == own_tiles else None for j in range(tiles)]

    def resistance(k):
        logs = lane_tiles(log_at(k))
        if ready is None:
            return [jnp.exp(-tile) for tile in logs]
        return [
            jnp.concatenate([ready[0][k, j], jnp.exp(-logs[j][own_rows:])], axis=0) for j in range(own_tiles)
        ] + [jnp.exp(-logs[own_tiles])]

    def along_x(k, j, size):
        if ready is None or j == own_tiles:
            return tx_ref[k, j, :size]
        if size == own_rows:
            return ready[1][k, j]
        return jnp.concatenate([ready[1][k, j], tx_ref[k, j, own_rows:size]], axis=0)

    after = resistance(0)
    tx_before = None
    for k in range(count):
        here = after
        if k + 1 < count:
            after = resistance(k + 1)
            outer = max(away(k), away(k + 1))
            size, number = (rows, tiles) if outer < REACH else (own_rows, own_tiles)
            tx = []
            for j in range(number):
                begin = 0 if ready is None or j == own_tiles else own_rows
                if begin < size:
                    tx_ref[k, j, begin:size] = x_faces[k] * inverse(here[j][begin:size] + after[j][begin:size])
                tx.append(along_x(k, j, size))
        if away(k) <= DEGREE:
            size, number = extent(k, 0)
            right = beside(here, -1)
            tz = []
            for j in range(tiles):
                scale = z_tops[j][:size] if z_tops[j] is not None else z_top[2]
                tz.append(scale * inverse(here[j][:size] + right[j][:size]))
            tz_left = beside(tz, 1)
            source = lane_tiles(source_at(k))
            for j in range(number):
                store_rows(k_ref, k, j, here[j])
                ty = y_top * inverse(here[j] + k_ref[k, j, SUBLANES + 1 : SUBLANES + 1 + rows])
                store_rows(ty_ref, k, j, ty)
                ty_before = ty_ref[k, j, SUBLANES - 1 : SUBLANES - 1 + size]
                diagonal = storage + (tx_before[j][:size] + tx[j][:size])
                diagonal = diagonal + (ty[:size] + ty_before) + (tz[j] + tz_left[j])
                w = inverse(diagonal)
                direction = source[j][:size] * (coefficient(0, size) * w)
                if (size, number) == (rows, tiles):
                    store_rows(d_ref.at[0], k, j, direction)
                else:
                    d_ref[0, k, j, SUBLANES : SUBLANES + size] = direction
                if extent(k, 1) is not None:
                    tzr_ref[k, j, :size] = tz[j]
                    tzl_ref[k, j, :size] = tz_left[j]
                    diag_ref[k, j, :size] = diagonal
                    w_ref[k, j, :size] = w
                    r_ref[k, j, :size] = source[j][:size]
        tx_before = tx
    for step in range(1, DEGREE + 1):
        old, new = d_ref.at[(step - 1) % 2], d_ref.at[step % 2]
        for k in range(count):
            if extent(k, step) is None:
                continue
            size, number = extent(k, step)
            middle = slice(SUBLANES, SUBLANES + size)
            keep, gain = coefficient(2 * step - 1, size), coefficient(2 * step, size)
            here = [old[k, j, middle] for j in range(tiles)]
            right, left = beside(here, -1), beside(here, 1)
            for j in range(number):
                applied = along_x(k, j, size) * old[k + 1, j, middle] + along_x(k - 1, j, size) * old[k - 1, j, middle]
                applied += (
                    ty_ref[k, j, middle] * old[k, j, SUBLANES + 1 : SUBLANES + 1 + size]
                    + ty_ref[k, j, SUBLANES - 1 : SUBLANES - 1 + size] * old[k, j, SUBLANES - 1 : SUBLANES - 1 + size]
                )
                applied += tzr_ref[k, j, :size] * right[j] + tzl_ref[k, j, :size] * left[j]
                residual = r_ref[k, j, :size] - (diag_ref[k, j, :size] * here[j] - applied)
                fresh = keep * here[j] + gain * (residual * w_ref[k, j, :size])
                if away(k) == 0 and j < own_tiles:
                    so_far = here[j][:own_rows] if step == 1 else p_ref[k, j]
                    total = so_far + fresh[:own_rows]
                    if step == DEGREE:
                        emit(k - REACH, j, total)
                    else:
                        p_ref[k, j] = total
                if step < DEGREE:
                    r_ref[k, j, :size] = residual
                    if (size, number) == (rows, tiles):
                        store_rows(new, k, j, fresh)
                    else:
                        new[k, j, middle] = fresh


def coefficients_kernel(low_ref, high_ref, after_ref, coef_ref):
    low, high = (jnp.full((SUBLANES, LANES), ref[0]) for ref in (low_ref, high_ref))
    theta, delta = (high + low) * 0.5, (high - low) * 0.5
    sigma = theta / delta
    rho = 1.0 / sigma
    coef_ref[0] = 1.0 / theta
    for step in range(DEGREE):
        rho_next = 1.0 / (2.0 * sigma - rho)
        coef_ref[1 + 2 * step] = rho_next * rho
        coef_ref[2 + 2 * step] = 2.0 * rho_next / delta
        rho = rho_next


def chebyshev_coefficients(low_bound, high_bound, after):
    return pl.pallas_call(
        coefficients_kernel,
        out_shape=jax.ShapeDtypeStruct((1 + 2 * DEGREE, SUBLANES, LANES), jnp.float32),
        in_specs=[pl.BlockSpec(memory_space=pltpu.SMEM)] * 2 + [ANY],
        out_specs=VMEM,
        compiler_params=pltpu.CompilerParams(vmem_limit_bytes=4 << 20),
        cost_estimate=pl.CostEstimate(flops=1_000_000, bytes_accessed=100_000, transcendentals=0),
        name="coefficients",
    )(low_bound, high_bound, after)


def put(ref, tile, value):
    for i in range(value.shape[1] // LANES):
        ref[(tile + i) * SUBLANES : (tile + i + 1) * SUBLANES, :] = value[:, i * LANES : (i + 1) * LANES]


def take(ref, tile, count):
    tiles = [ref[(tile + i) * SUBLANES : (tile + i + 1) * SUBLANES, :] for i in range(count)]
    return tiles[0] if count == 1 else jnp.concatenate(tiles, axis=1)


def edges(value):
    lanes = value.shape[-1]
    value = value if isinstance(value, jax.Array) else value.at
    return value[:, lanes - LANES :], value[:, :LANES]


def write_lanes(pairs):
    starts = lax.axis_index("gz") == 0
    each = LANES // REACH
    group = iota((SUBLANES, LANES), 1) // REACH
    merged = None
    for j, (last, first) in enumerate(pairs):
        moved = turned(jnp.where(starts, last, first), REACH * j, 1)
        place = jnp.where(starts, (j - 1) % each, j)
        merged = moved if merged is None else jnp.where(group == place, moved, merged)
    return merged


def read_lanes(tile, slot):
    return turned(tile, -REACH * slot, 1)


def add_lanes(tile, slot, value):
    starts = lax.axis_index("gz") == 0
    group = iota((SUBLANES, LANES), 1) // REACH
    place = jnp.where(starts, slot, (slot - 1) % (LANES // REACH))
    return jnp.where(group == place, turned(value, REACH * slot, 1), tile)


def lane_slots(layers, row_tiles, n_got):
    keys = [("own", a, layer, i) for a in range(2) for layer in range(layers) for i in range(row_tiles)]
    keys += [("pooled", x, a) for x in range(2) for a in range(2)]
    shared = len(keys)
    keys += [("halo", i, half) for i in range(n_got) for half in range(2)]
    keys += [("got", g, layer) for g in range(n_got) for layer in range(layers)]
    return {key: i for i, key in enumerate(keys)}, shared


def near_layout(lanes, wide):
    whole, half = lanes // LANES, lanes // LANES // 2
    if wide:
        parts = [("log1", whole), ("source1", whole), ("log2", whole), ("source2", whole)]
        parts += [(name, half) for name in ("halo0", "halo1", "halo2", "halo3", "source")]
    else:
        parts = [("strip", whole), ("halo", half), ("source", half), ("row", 1)]
    layout, start = {}, 0
    for name, count in parts + [("lanes", 1)]:
        layout[name] = (start, count)
        start += count
    return layout, start


def near_lane_slots(lanes, wide, shared):
    names = [name for name in near_layout(lanes, wide)[0] if name not in ("source", "lanes")]
    return {name: shared + i for i, name in enumerate(names)}


def rows_to_lanes(row_tile, count):
    return jnp.concatenate(
        [jnp.broadcast_to(row_tile[j : j + 1], (SUBLANES, LANES)) for j in range(count)], axis=1
    )


def window_scratch(count, own_rows, rows, tiles):
    plain = pltpu.VMEM((count, tiles, rows, LANES), jnp.float32)
    margins = pltpu.VMEM((count, tiles, rows + 2 * SUBLANES, LANES), jnp.float32)
    pair = pltpu.VMEM((2, count, tiles, rows + 2 * SUBLANES, LANES), jnp.float32)
    total = pltpu.VMEM((count, tiles, own_rows, LANES), jnp.float32)
    return [margins, plain, margins, plain, plain, plain, plain, pair, plain, total]


def exact_dot(value, zero_one):
    parts = []
    for _ in range(3):
        part = value.astype(jnp.bfloat16)
        parts.append(part)
        value = value - part.astype(jnp.float32)
    rows = value.shape[0]
    out = jnp.dot(jnp.concatenate(parts, axis=0), zero_one, preferred_element_type=jnp.float32)
    return (out[2 * rows :] + out[rows : 2 * rows]) + out[:rows]


def row_pairs(top, bottom, sum_ref):
    tiles = top.shape[1] // LANES
    for tile in range(tiles):
        columns = slice(tile * LANES, (tile + 1) * LANES)
        sum_ref[tile, :SUBLANES] = top[:, columns]
        sum_ref[tile, SUBLANES:] = bottom[:, columns]
    return jnp.concatenate(
        [
            sum_ref[tile, pl.ds(0, SUBLANES, stride=2), :] + sum_ref[tile, pl.ds(1, SUBLANES, stride=2), :]
            for tile in range(tiles)
        ],
        axis=1,
    )


def lane_pairs(pieces):
    lanes = pieces[0].shape[1]
    pick = (iota((lanes, lanes // 2), 0) // 2 == iota((lanes, lanes // 2), 1)).astype(jnp.bfloat16)
    pooled = exact_dot(jnp.concatenate(pieces, axis=0), pick)
    return [pooled[SUBLANES * i : SUBLANES * (i + 1)] for i in range(len(pieces))]


def join_halo(near, beyond, starts):
    row = iota(near.shape, 0)
    up, down = turned(beyond, 3, 0), turned(beyond, -3, 0)
    right = jnp.where((row == 3) | (row == 7), up, jnp.where(row == 6, turned(beyond, 5, 0), near))
    left = jnp.where((row == 0) | (row == 4), down, jnp.where(row == 5, up, near))
    return jnp.where(starts, right, left)


def beyond_halo(joined, starts):
    row = iota(joined.shape, 0)
    up, down = turned(joined, 3, 0), turned(joined, -3, 0)
    right = jnp.where(row == 1, turned(joined, -5, 0), down)
    left = jnp.where(row == 2, down, up)
    return jnp.where(starts, right, left)


def join_third(near, third):
    row = iota(near.shape, 0)
    return jnp.where(
        row == 3, turned(third, 3, 0), jnp.where(row == 4, turned(third, -3, 0), near)
    )


def third_halo(joined):
    return jnp.where(iota(joined.shape, 0) < REACH, turned(joined, -3, 0), turned(joined, 3, 0))


def parts(both_ref):
    layers = both_ref.shape[0] // 2
    return both_ref.at[:layers], both_ref.at[layers:]


def prep_kernel(both_ref, pooled_ref, *refs):
    *out_refs, sum_ref = refs
    log_ref, source_ref = parts(both_ref)
    layers, rows, lanes = log_ref.shape
    starts = lax.axis_index("gy") == 0

    def put(slot, left, right):
        if len(out_refs) == 1:
            out_refs[0][slot] = jnp.where(starts, right, left)
        else:
            out_refs[0][slot], out_refs[1][slot] = left, right

    half = lanes // 2
    upper = iota((SUBLANES, lanes), 0) < REACH
    pieces = []
    for x in range(2):
        for ref in (log_ref, source_ref):
            both = ref[2 * x] + ref[2 * x + 1]
            pieces.append(row_pairs(both[:SUBLANES], both[SUBLANES:], sum_ref))
    log0, source0, log1, source1 = lane_pairs(pieces)
    log0, log1 = log0 * 0.125, log1 * 0.125
    pooled_ref[0] = jnp.concatenate([log0, source0], axis=1)
    pooled_ref[1] = jnp.concatenate([log1, source1], axis=1)
    for layer in range(layers):
        put(
            layer,
            jnp.where(upper, log_ref[layer, :SUBLANES], turned(source_ref[layer, :SUBLANES], REACH, 0)),
            jnp.where(upper, turned(source_ref[layer, SUBLANES:], REACH, 0), log_ref[layer, SUBLANES:]),
        )
    pair = iota((SUBLANES, half), 0) // 2

    def four(*tiles):
        merged = jnp.where(
            pair == 0, tiles[0], jnp.where(pair == 1, tiles[1], jnp.where(pair == 2, tiles[2], tiles[3]))
        )
        return jnp.concatenate([merged, merged], axis=1)

    put(
        layers,
        four(turned(log1, -2, 0), log0, turned(source1, 2, 0), turned(source0, 4, 0)),
        four(turned(log0, -4, 0), turned(log1, -2, 0), source0, turned(source1, 2, 0)),
    )


def prep(both, ny):
    layers, rows, lanes = both.shape[0] // 2, *both.shape[1:]
    outs = 1 if ny == 2 else 2

    def tiles(count):
        return jax.ShapeDtypeStruct((count, SUBLANES, lanes), jnp.float32)

    return pl.pallas_call(
        prep_kernel,
        out_shape=(tiles(2),) + (tiles(layers + 1),) * outs,
        in_specs=[VMEM],
        out_specs=(VMEM,) * (1 + outs),
        scratch_shapes=[pltpu.VMEM((lanes // LANES, 2 * SUBLANES, LANES), jnp.float32)],
        compiler_params=pltpu.CompilerParams(vmem_limit_bytes=8 << 20),
        cost_estimate=pl.CostEstimate(flops=5_000_000, bytes_accessed=700_000, transcendentals=0),
        name="prep",
    )(both)


def raw_kernel(to_right_if_odd, both_ref, after_ref, out_ref):
    log_ref, source_ref = parts(both_ref)
    layers = log_ref.shape[0]
    odd = lax.axis_index("gx") % 2
    skip = odd if to_right_if_odd else 1 - odd
    for layer in range(layers):
        out_ref[layer] = log_ref[layer]
    for layer in range(layers - 1):
        out_ref[layers + layer] = source_ref[layer + skip]


def raw_block(both, after, to_right_if_odd):
    layers, rows, lanes = both.shape[0] // 2, *both.shape[1:]
    return pl.pallas_call(
        functools.partial(raw_kernel, to_right_if_odd),
        out_shape=jax.ShapeDtypeStruct((2 * layers - 1, rows, lanes), jnp.float32),
        in_specs=[VMEM, ANY],
        out_specs=VMEM,
        compiler_params=pltpu.CompilerParams(vmem_limit_bytes=8 << 20),
        cost_estimate=pl.CostEstimate(flops=1_000_000, bytes_accessed=500_000, transcendentals=0),
        name="raw_block",
    )(both, after)


def halos_kernel(wide, both_ref, pooled_ref, *refs):
    *got_refs, halo_ref, sent_ref, sum_ref = refs
    layers, lanes = got_refs[0].shape[0] - 1, got_refs[0].shape[2]
    iy = lax.axis_index("gy")
    even, starts = iy % 2 == 0, iy == 0
    half = lanes // 2
    upper = iota((SUBLANES, lanes), 0) < REACH
    row = iota((SUBLANES, half), 0)

    def got(slot):
        tiles = tuple(ref[slot] for ref in got_refs)
        return from_right(even, tiles), from_left(even, tiles)

    strips = [got(layer) for layer in range(layers)]
    extra = [tile[:, :half] for tile in got(layers)]
    pieces = []
    for side in range(2 if wide else 1):
        both = [strips[2 * x][side] + strips[2 * x + 1][side] for x in range(2)]
        pieces.append(row_pairs(*both, sum_ref))
    fine_rows = lane_pairs(pieces)

    def right_halos(rows, extra):
        rows = jnp.where(row % 4 < 2, rows * 0.125, rows)
        return [
            jnp.where(row < 2, near, jnp.where((row == 4) | (row == 5), far, more))
            for near, far, more in (
                (rows, turned(rows, 2, 0), extra),
                (turned(rows, 4, 0), turned(rows, -2, 0), turned(extra, 2, 0)),
            )
        ]

    def left_halos(rows, extra):
        rows = jnp.where(row % 4 >= 2, rows * 0.125, rows)
        return [
            jnp.where((row == 2) | (row == 3), near, jnp.where(row >= 6, far, more))
            for near, far, more in (
                (rows, turned(rows, -2, 0), extra),
                (turned(rows, 4, 0), turned(rows, 2, 0), turned(extra, -2, 0)),
            )
        ]

    right, left = right_halos(fine_rows[0], extra[0]), left_halos(fine_rows[-1], extra[1])
    if wide:
        top = row < REACH
        halos = [jnp.where(top, right[x], turned(left[x], REACH, 0)) for x in range(2)]
        halos += [jnp.where(top, turned(right[x], REACH, 0), left[x]) for x in range(2)]
    else:
        halos = [jnp.where(starts, right[x], left[x]) for x in range(2)]

    def pair(left, right):
        return jnp.concatenate([left, right], axis=1)

    for i in range(len(halos) // 2):
        halo_ref[i] = pair(halos[2 * i], halos[2 * i + 1])
    pairs = {}
    rows = both_ref.shape[1]
    for a, ref in enumerate(parts(both_ref)):
        for layer in range(layers):
            for i in range(rows // SUBLANES):
                pairs["own", a, layer, i] = edges(ref[layer, i * SUBLANES : (i + 1) * SUBLANES])
    for x in range(2):
        for a in range(2):
            pairs["pooled", x, a] = edges(pooled_ref[x, :, a * half : (a + 1) * half])
    for i, halo in enumerate(halos):
        pairs["halo", i // 2, i % 2] = edges(halo)
    for g, ref in enumerate(got_refs):
        for layer in range(layers):
            pairs["got", g, layer] = edges(ref[layer])
    slots, _ = lane_slots(layers, rows // SUBLANES, len(got_refs))
    sent_ref[...] = write_lanes([pairs[key] for key in slots])


def pooled_halos(both, pooled, got):
    slots, rows, lanes = got[0].shape
    return pl.pallas_call(
        functools.partial(halos_kernel, len(got) == 2),
        out_shape=(
            jax.ShapeDtypeStruct((len(got), SUBLANES, lanes), jnp.float32),
            jax.ShapeDtypeStruct((SUBLANES, LANES), jnp.float32),
        ),
        in_specs=[VMEM] * (2 + len(got)),
        out_specs=(VMEM,) * 2,
        scratch_shapes=[pltpu.VMEM((lanes // LANES, 2 * SUBLANES, LANES), jnp.float32)],
        compiler_params=pltpu.CompilerParams(vmem_limit_bytes=8 << 20),
        cost_estimate=AHEAD,
        name="halos",
    )(both, pooled, *got)


def pack_far_kernel(wide, pooled_ref, halo_ref, lanes_ref, *far_refs):
    half = pooled_ref.shape[2] // 2
    low = lax.axis_index("gx") % 4 < 2

    def tiles(inner):
        return (
            pooled_ref[inner, :, :half],
            pooled_ref[1 - inner, :, :half],
            pooled_ref[inner, :, half:],
            halo_ref[0, :, inner * half : (inner + 1) * half],
        )

    for group, ref in enumerate(far_refs):
        for i, (right, left) in enumerate(zip(tiles(1), tiles(0))):
            put(ref, i * (half // LANES), jnp.where(low, *((right, left) if group == 0 else (left, right))))
        put(ref, 4 * (half // LANES), lanes_ref[...])
        for spare in range(4 * (half // LANES) + 1, ref.shape[0] // SUBLANES):
            put(ref, spare, jnp.zeros((SUBLANES, LANES), jnp.float32))


def pack_far(pooled, halos, early, n_far, wide):
    _, rows, lanes = pooled.shape
    far_rows = max(2 * lanes // LANES + 1, 0 if wide else near_layout(lanes, wide)[1]) * SUBLANES
    return pl.pallas_call(
        functools.partial(pack_far_kernel, wide),
        out_shape=(jax.ShapeDtypeStruct((far_rows, LANES), jnp.float32),) * n_far,
        in_specs=[VMEM] * 3,
        out_specs=(VMEM,) * n_far,
        compiler_params=pltpu.CompilerParams(vmem_limit_bytes=8 << 20),
        cost_estimate=pl.CostEstimate(flops=1_000_000, bytes_accessed=500_000, transcendentals=0),
        name="pack_far",
    )(pooled, halos, early)


def pack_near_kernel(wide, pooled_ref, halo_ref, early_ref, after_ref, *refs):
    *got_refs, first_ref, second_ref = refs
    layers, lanes = got_refs[0].shape[0] - 1, got_refs[0].shape[2]
    ix, iy = lax.axis_index("gx"), lax.axis_index("gy")
    even, starts = iy % 2 == 0, iy == 0
    half = lanes // 2
    upper = iota((SUBLANES, lanes), 0) < REACH

    def got(slot):
        tiles = tuple(ref[slot] for ref in got_refs)
        return from_right(even, tiles), from_left(even, tiles)

    strips = [got(layer) for layer in range(layers)]
    halos = [halo_ref[i // 2, :, (i % 2) * half : (i % 2 + 1) * half] for i in range(4 if wide else 2)]
    sources = [pooled_ref[x, :, half:] for x in range(2)]

    slots, shared = lane_slots(layers, 2, len(got_refs))

    def strip_lanes(layer):
        tiles = tuple(read_lanes(early_ref[...], slots["got", g, layer]) for g in range(len(got_refs)))
        return from_right(even, tiles), from_left(even, tiles)

    def halo_lanes(i):
        return read_lanes(early_ref[...], slots["halo", i // 2, i % 2])

    def near_tiles(order, strips, halos):
        near, beyond = order[0] // 2, order[-1] // 2
        width = strips[0][0].shape[1]
        upper = iota((SUBLANES, width), 0) < REACH
        if wide:
            log_rows = [jnp.where(upper, *strips[layer]) for layer in range(layers)]
            source_rows = [turned(jnp.where(upper, *strips[layer][::-1]), REACH, 0) for layer in range(layers)]
            return {
                "log1": join_third(log_rows[order[0]], log_rows[order[2]]),
                "source1": source_rows[order[0]],
                "log2": log_rows[order[1]],
                "source2": source_rows[order[1]],
                "halo0": halos[near],
                "halo1": halos[beyond],
                "halo2": halos[2 + near],
                "halo3": halos[2 + beyond],
            }
        first, second, third = (strips[layer][0] for layer in order[:3])
        place = iota((SUBLANES, width), 0)
        right = jnp.where(place == 3, turned(third, 3, 0), jnp.where(place >= 6, turned(second, -2, 0), first))
        left = jnp.where(place == 4, turned(third, -3, 0), jnp.where(place < 2, turned(second, 2, 0), first))
        line = jnp.where(starts, second[4:5], second[3:4])
        if width == LANES:
            lines = jnp.broadcast_to(line, (SUBLANES, LANES))
        else:
            lines = jnp.zeros((SUBLANES, LANES), jnp.float32)
            for j in range(width // LANES):
                lines = jnp.where(iota(lines.shape, 0) == j, line[:, j * LANES : (j + 1) * LANES], lines)
        return {
            "strip": jnp.where(starts, right, left),
            "halo": join_halo(halos[near], halos[beyond], starts),
            "row": lines,
        }

    def side(order):
        tiles = near_tiles(order, strips, halos)
        tiles["source"] = sources[order[-1] // 2]
        lanes_tile = early_ref[...]
        n_halos = 4 if wide else 2
        beside = near_tiles(
            order, [strip_lanes(layer) for layer in range(layers)], [halo_lanes(i) for i in range(n_halos)]
        )
        for name, slot in near_lane_slots(lanes, wide, shared).items():
            lanes_tile = add_lanes(lanes_tile, slot, beside[name])
        tiles["lanes"] = lanes_tile
        return tiles

    forward = list(range(layers))
    layout, _ = near_layout(lanes, wide)
    right, left = side(forward[::-1]), side(forward)
    for name, (start, _) in layout.items():
        put(first_ref, start, jnp.where(ix % 2 == 0, right[name], left[name]))
        put(second_ref, start, jnp.where(ix % 2 == 0, left[name], right[name]))


def pack_near(pooled, halos, early, after, got):
    slots, rows, lanes = got[0].shape
    wide = len(got) == 2
    out = jax.ShapeDtypeStruct((near_layout(lanes, wide)[1] * SUBLANES, LANES), jnp.float32)
    return pl.pallas_call(
        functools.partial(pack_near_kernel, wide),
        out_shape=(out, out),
        in_specs=[VMEM] * 3 + [ANY] + [VMEM] * len(got),
        out_specs=(VMEM,) * 2,
        compiler_params=pltpu.CompilerParams(vmem_limit_bytes=8 << 20),
        cost_estimate=pl.CostEstimate(flops=1_000_000, bytes_accessed=500_000, transcendentals=0),
        name="pack_near",
    )(pooled, halos, early, after, *got)


def pool_kernel(after_ref, first_ref, second_ref, out_ref, sum_ref):
    layers = REACH
    even = lax.axis_index("gx") % 2 == 0
    pieces = []
    for side, pick in enumerate((from_left, from_right)):

        def block(slot):
            return pick(even, (first_ref[slot], second_ref[slot]))

        for top in (0, 2, layers + 1 if side == 0 else layers):
            both = block(top) + block(top + 1)
            pieces.append(row_pairs(both[:SUBLANES], both[SUBLANES:], sum_ref))
    for i, tile in enumerate(lane_pairs(pieces)):
        put(out_ref, i * (tile.shape[1] // LANES), tile * (0.125 if i % 3 < 2 else 1.0))


def pool(after, raw):
    _, rows, lanes = raw[0].shape
    return pl.pallas_call(
        pool_kernel,
        out_shape=jax.ShapeDtypeStruct((6 * (lanes // 2 // LANES) * SUBLANES, LANES), jnp.float32),
        in_specs=[ANY] + [VMEM] * 2,
        out_specs=VMEM,
        scratch_shapes=[pltpu.VMEM((lanes // LANES, 2 * SUBLANES, LANES), jnp.float32)],
        compiler_params=pltpu.CompilerParams(vmem_limit_bytes=16 << 20),
        cost_estimate=pl.CostEstimate(flops=1_000_000, bytes_accessed=1_000_000, transcendentals=0),
        name="pool",
    )(after, *raw)


def x_faces_of(layers, ix, nx):
    faces = [2.0] * (3 * layers - 1)
    faces[layers - 1] = jnp.where(ix > 0, 2.0, 0.0)
    faces[2 * layers - 1] = jnp.where(ix < nx - 1, 2.0, 0.0)
    return faces


def ahead_kernel(nx, after_ref, both_ref, first_ref, second_ref, inverse_ref, tx_ref):
    log_ref, _ = parts(both_ref)
    layers, rows, lanes = log_ref.shape
    ix = lax.axis_index("gx")
    faces = x_faces_of(layers, ix, nx)
    before = None
    for k in range(3 * layers):
        side, layer = k // layers - 1, k % layers
        if side == 0:
            log = log_ref[layer]
        else:
            log = (from_left if side < 0 else from_right)(ix % 2 == 0, (first_ref[layer], second_ref[layer]))
        here = [jnp.exp(-tile) for tile in lane_tiles(log)]
        for j, tile in enumerate(here):
            inverse_ref[k, j] = tile
            if k > 0:
                tx_ref[k - 1, j] = faces[k - 1] * inverse(before[j] + tile)
        before = here


def ahead(after, both, raw, nx):
    layers, rows, lanes = both.shape[0] // 2, *both.shape[1:]

    def tiles(count):
        return jax.ShapeDtypeStruct((count, lanes // LANES, rows, LANES), jnp.float32)

    return pl.pallas_call(
        functools.partial(ahead_kernel, nx),
        out_shape=(tiles(3 * layers), tiles(3 * layers - 1)),
        in_specs=[ANY] + [VMEM] * 3,
        out_specs=(VMEM,) * 2,
        compiler_params=pltpu.CompilerParams(vmem_limit_bytes=16 << 20),
        cost_estimate=pl.CostEstimate(flops=1_000_000, bytes_accessed=1_000_000, transcendentals=0),
        name="ahead",
    )(after, both, *raw)


def near_part(refs, even, lanes, wide, side, name):
    start, count = near_layout(lanes, wide)[0][name]
    pick = from_left if side == 0 else from_right
    got = pick(even, tuple(take(ref, start, count) for ref in refs))
    return rows_to_lanes(got, lanes // LANES) if name == "row" else got


def far_part(refs, low, lanes, side, i):
    count = lanes // 2 // LANES
    pick = from_left if side == 0 else from_right
    return pick(low, tuple(take(ref, i * count, count) for ref in refs))


def coarse_part(peers, n_far, own_ref, halo_ref, pool_ref, first_ref, second_ref, *refs):
    near_refs, far_refs = (first_ref, second_ref), refs[:n_far]
    early_ref, coef_ref, out_ref, wide_ref, *scratch = refs[n_far:]
    ix, iy, iz = (lax.axis_index(axis) for axis in AXES)
    nx, ny, nz = peers
    wide = ny > 2
    fine_lanes = own_ref.shape[2]
    lanes, rows = fine_lanes // 2, SUBLANES
    even, low, starts = ix % 2 == 0, ix % 4 < 2, iy == 0
    top = iota((rows, lanes + LANES), 0) < REACH
    slots, shared = lane_slots(REACH, 2, 2 if wide else 1)
    near_slots = near_lane_slots(fine_lanes, wide, shared)
    own_lanes = early_ref[...]
    near_lanes = [near_part(near_refs, even, fine_lanes, wide, side, "lanes") for side in range(2)]
    far_lanes = [
        pick(low, tuple(take(ref, 4 * (lanes // LANES), 1) for ref in far_refs))
        for pick in (from_left, from_right)
    ]

    def columns(half):
        return slice(half * lanes, (half + 1) * lanes)

    def join(core, tile, slot):
        return jnp.concatenate([core, read_lanes(tile, slot)], axis=1)

    def near(side, name):
        core = near_part(near_refs, even, fine_lanes, wide, side, name)
        return join(core, near_lanes[side], near_slots[name])

    def far(side, i):
        core = far_part(far_refs, low, fine_lanes, side, i)
        return join(core, far_lanes[side], slots["pooled", 1 - side, 0])

    def split(tile, a):
        other = turned(tile, REACH, 0)
        return jnp.where(top, tile, other) if a == 0 else jnp.where(top, other, tile)

    def window(a, k):
        block, layer = k // 2 - 2, k % 2
        nearest = layer == (1 if block < 0 else 0)
        side = 0 if block < 0 else 1
        if abs(block) == 2:
            if a == 1:
                core = far(side, 2)
                return jnp.concatenate([core, jnp.zeros_like(core)], axis=0)
            halo = far(side, 3)
            halo = halo if wide else split(halo, 0)
            return jnp.concatenate([far(side, 0 if nearest else 1), halo], axis=0)
        if block == 0:
            core = join(own_ref[layer, :, columns(a)], own_lanes, slots["pooled", layer, a])
            if wide:
                halo = join(halo_ref[a, :, columns(layer)], own_lanes, slots["halo", a, layer])
            else:
                halo = split(join(halo_ref[0, :, columns(layer)], own_lanes, slots["halo", 0, layer]), a)
            return jnp.concatenate([core, halo], axis=0)
        if a == 0 or nearest:
            i = layer if a == 0 else 2
            core = take(pool_ref, (3 * side + i) * (lanes // LANES), lanes // LANES)
        else:
            core = near_part(near_refs, even, fine_lanes, wide, side, "source")
        core = join(core, near_lanes[side], slots["pooled", layer, a])
        if wide:
            halo = near(side, f"halo{2 * a + (0 if nearest else 1)}")
        else:
            joined = near(side, "halo")
            halo = split(joined if nearest else beyond_halo(joined, starts), a)
        return jnp.concatenate([core, halo], axis=0)

    def open_face(inside):
        return jnp.where(inside, 4.0, 0.0)

    faces = [4.0] * 9
    faces[1], faces[3] = open_face(ix > 1), open_face(ix > 0)
    faces[5], faces[7] = open_face(ix < nx - 1), open_face(ix < nx - 2)
    *scratch, p_ref = scratch

    def emit(layer, tile, value):
        p_ref[layer * rows : (layer + 1) * rows, tile * LANES : (tile + 1) * LANES] = value

    iterate(
        2 + 2 * REACH,
        rows,
        2 * rows,
        lanes // LANES + 1,
        functools.partial(window, 0),
        functools.partial(window, 1),
        faces,
        row_numerators(2 * rows, rows, iy, ny, 2.0),
        lane_numerators(2 * rows, iz, nz, 2.0) + [4.0],
        coef_ref,
        8.0 * storage_rate,
        emit,
        scratch,
    )
    widen = (iota((lanes, 2 * lanes), 0) == iota((lanes, 2 * lanes), 1) // 2).astype(jnp.bfloat16)
    spread = exact_dot(p_ref[...], widen)
    for x in range(2):
        for tile in range(2 * lanes // LANES):
            part = slice(tile * LANES, (tile + 1) * LANES)
            for half in range(2):
                wide_ref[tile, pl.ds(half, rows, stride=2), :] = spread[x * rows : (x + 1) * rows, part]
            for twin in range(2):
                out_ref[2 * x + twin, :, part] = wide_ref[tile]


def levels_kernel(peers, n_far, both_ref, *refs):
    log_ref, source_ref = parts(both_ref)
    layers, rows, lanes = log_ref.shape
    ix, iy, iz = (lax.axis_index(axis) for axis in AXES)
    nx, ny, nz = peers
    wide = ny > 2
    n_got = 2 if wide else 1
    got_refs, refs = refs[:n_got], refs[n_got:]
    second_ref, first_ref = refs[:2]
    far_refs = refs[2 : 2 + n_far]
    second_near_ref, first_near_ref, early_ref, coef_ref = refs[2 + n_far : 6 + n_far]
    near_refs = first_near_ref, second_near_ref
    own_ref, halo_ref, pool_ref, inverse_ref, tx_ref, fine_ref, diff_ref, *scratch = refs[6 + n_far :]
    scratch, (spread_ref, *coarse_scratch) = scratch[:10], scratch[10:]
    coarse_part(
        peers,
        n_far,
        own_ref,
        halo_ref,
        pool_ref,
        *near_refs,
        *far_refs,
        early_ref,
        coef_ref,
        spread_ref,
        *coarse_scratch,
    )
    even, starts = ix % 2 == 0, iy == 0
    count = 3 * layers
    upper = iota((SUBLANES, lanes + LANES), 0) < REACH
    slots, shared = lane_slots(layers, rows // SUBLANES, n_got)
    near_slots = near_lane_slots(lanes, wide, shared)
    own_lanes = early_ref[...]
    near_lanes = [near_part(near_refs, even, lanes, wide, side, "lanes") for side in range(2)]

    def join(core, tile, *keys):
        beside = jnp.concatenate([read_lanes(tile, key) for key in keys], axis=0)
        return jnp.concatenate([core, beside], axis=1)

    def near(side, name):
        return join(near_part(near_refs, even, lanes, wide, side, name), near_lanes[side], near_slots[name])

    def near_halo(a, side, distance):
        if wide:
            tile = near(side, ("log" if a == 0 else "source") + ("2" if distance == 2 else "1"))
        elif a == 1:
            return near(side, "row") if distance == 2 else turned(near(side, "strip"), REACH, 0)
        else:
            tile = near(side, "strip")
            if distance == 2:
                return jnp.where(starts, turned(tile, 2, 0), turned(tile, -2, 0))
        return third_halo(tile) if a == 0 and distance > 2 else tile

    def window(a, k):
        block, layer = k // layers - 1, k % layers
        if block == 0:
            core = (log_ref, source_ref)[a][layer]
            core = join(core, own_lanes, *(slots["own", a, layer, i] for i in range(rows // SUBLANES)))
            tiles = tuple(
                join(ref[layer], own_lanes, slots["got", g, layer]) for g, ref in enumerate(got_refs)
            )
            halo = tiles[0]
            if wide:
                sides = from_right(iy % 2 == 0, tiles), from_left(iy % 2 == 0, tiles)
                halo = jnp.where(upper, *(sides if a == 0 else sides[::-1]))
            if a == 1:
                halo = turned(halo, REACH, 0)
            return jnp.concatenate([core, halo], axis=0)
        side, pick = (0, from_left) if block < 0 else (1, from_right)
        slot = layer if a == 0 else layers + layer - (1 if block < 0 else 0)
        core = pick(even, (first_ref[slot], second_ref[slot]))
        core = join(core, near_lanes[side], *(slots["own", a, layer, i] for i in range(rows // SUBLANES)))
        halo = near_halo(a, side, layers - layer if block < 0 else layer + 1)
        return jnp.concatenate([core, halo], axis=0)

    faces = x_faces_of(layers, ix, nx)

    def emit(layer, tile, value):
        part = slice(tile * LANES, (tile + 1) * LANES)
        fine_ref[layer, :, part] = value
        diff_ref[layer, :, part] = value - spread_ref[layer, :, part]

    iterate(
        count,
        rows,
        rows + 2 * REACH,
        lanes // LANES + 1,
        functools.partial(window, 0),
        functools.partial(window, 1),
        faces,
        row_numerators(rows + 2 * REACH, rows, iy, ny, 1.0),
        lane_numerators(rows + 2 * REACH, iz, nz, 1.0) + [2.0],
        coef_ref,
        storage_rate,
        emit,
        scratch,
        (inverse_ref, tx_ref),
    )


def levels(both, got, raw, far, near, early, coefficients, own, halos, pooled, ready, peers):
    layers, rows, lanes = both.shape[0] // 2, *both.shape[1:]
    half = lanes // 2
    out = jax.ShapeDtypeStruct((layers, rows, lanes), jnp.float32)
    return pl.pallas_call(
        functools.partial(levels_kernel, peers, len(far)),
        out_shape=(out, out),
        in_specs=[VMEM] * (12 + len(got) + len(far)),
        out_specs=(VMEM, VMEM),
        scratch_shapes=window_scratch(3 * layers, rows, rows + 2 * REACH, lanes // LANES + 1)
        + [
            pltpu.VMEM((layers, rows, lanes), jnp.float32),
            pltpu.VMEM((lanes // LANES, rows, LANES), jnp.float32),
        ]
        + window_scratch(2 + 2 * REACH, SUBLANES, 2 * SUBLANES, half // LANES + 1)
        + [pltpu.VMEM((2 * SUBLANES, half), jnp.float32)],
        compiler_params=pltpu.CompilerParams(vmem_limit_bytes=32 << 20),
        cost_estimate=pl.CostEstimate(flops=20_000_000, bytes_accessed=10_000_000, transcendentals=0),
        name="levels",
    )(both, *got, *raw[::-1], *far, *near[::-1], early, coefficients, own, halos, pooled, *ready)


def shards(peers, log_perm, source, low_bound, high_bound):
    nx, ny, nz = peers
    layers, rows, lanes = log_perm.shape
    assert layers == REACH and rows == 2 * SUBLANES and nx > 2 and nz == 2
    both = jnp.concatenate([log_perm, source])
    own, *rows_sent = prep(both, ny)
    if ny == 2:
        got = (permute(rows_sent[0], "gy", ny, [(0, 1)]),)
    else:
        got = swap("gy", ny, rows_sent[1], rows_sent[0])
    for_second = raw_block(both, rows_sent[0], True)
    second = permute(for_second, "gx", nx, neighbour_pairs(nx, 1))
    for_first = raw_block(both, for_second, False)
    raw = (permute(for_first, "gx", nx, neighbour_pairs(nx, 0)), second)
    far_groups = far_pairs(nx)
    halos, lanes_sent = pooled_halos(both, own, got)
    early = lax.ppermute(lanes_sent, "gz", [(0, 1), (1, 0)])
    for_far = pack_far(own, halos, early, len(far_groups), ny > 2)
    far = [permute(tiles, "gx", nx, group) for tiles, group in zip(for_far, far_groups)]
    for_first, for_second = pack_near(own, halos, early, for_far[0], got)
    second = permute(for_second, "gx", nx, neighbour_pairs(nx, 1))
    near = (permute(for_first, "gx", nx, neighbour_pairs(nx, 0)), second)
    coefficients = chebyshev_coefficients(low_bound, high_bound, for_first)
    pooled = pool(coefficients, raw)
    ready = ahead(pooled, both, raw, nx)
    return levels(both, got, raw, far, near, early, coefficients, own, halos, pooled, ready, peers)


def solution(mesh):
    peers = tuple(mesh.shape[axis] for axis in AXES)
    split = P(("groups", "gx"), "gy", "gz")
    return jax.shard_map(
        functools.partial(shards, peers),
        mesh=mesh,
        in_specs=(split, split, P(), P()),
        out_specs=(split, split),
        check_vma=False,
    )
```

```python
import functools

import jax
import jax.numpy as jnp
from jax import lax
from jax.experimental import pallas as pl
from jax.experimental.pallas import tpu as pltpu
from jax.sharding import PartitionSpec as P

DEGREE = 3
REACH = DEGREE + 1
LANES = 128
SUBLANES = 8
storage_rate = 0.1
AXES = ("gx", "gy", "gz")
VMEM = pl.BlockSpec(memory_space=pltpu.VMEM)
ANY = pl.BlockSpec(memory_space=pl.ANY)


AHEAD = pl.CostEstimate(flops=50_000_000_000, bytes_accessed=1_000_000, transcendentals=0)


def iota(shape, dim):
    return lax.broadcasted_iota(jnp.int32, shape, dim)


def turned(value, shift, axis):
    size = value.shape[axis]
    return pltpu.roll(value, shift % size, axis)


def permute(value, axis, peers, pairs):
    cores = lax.axis_size("gz")
    if axis == "gz" or cores % 2:
        return lax.ppermute(value, axis, [pair for i, j in pairs for pair in ((i, j), (j, i))])
    partner = {}
    for i, j in pairs:
        partner[i], partner[j] = j, i
    moves = [
        (i * cores + core, partner[i] * cores + core if i in partner else i * cores + (core ^ 1))
        for i in range(peers)
        for core in range(cores)
    ]
    return lax.ppermute(value, (axis, "gz"), moves)


def neighbour_pairs(peers, start):
    return [(i, i + 1) for i in range(start, peers - 1, 2)]


def first_swap(axis, peers, right, left):
    even = lax.axis_index(axis) % 2 == 0
    return permute(jnp.where(even, right, left), axis, peers, neighbour_pairs(peers, 0))


def second_swap(axis, peers, right, left):
    even = lax.axis_index(axis) % 2 == 0
    return permute(jnp.where(even, left, right), axis, peers, neighbour_pairs(peers, 1))


def swap(axis, peers, right, left):
    got = (first_swap(axis, peers, right, left),)
    return got if peers == 2 else got + (second_swap(axis, peers, right, left),)


def far_pairs(peers):
    pairs = [(i, i + 2) for i in range(peers - 2)]
    groups = [[pair for pair in pairs if pair[0] % 4 < 2], [pair for pair in pairs if pair[0] % 4 >= 2]]
    return [group for group in groups if group]


def from_right(is_first, got):
    return got[0] if len(got) == 1 else jnp.where(is_first, got[0], got[1])


def from_left(is_first, got):
    return got[0] if len(got) == 1 else jnp.where(is_first, got[1], got[0])


def inverse(value):
    guess = pl.reciprocal(value, approx=True)
    return guess * (2.0 - value * guess)


def row_numerators(rows, own, index, peers, face_scale):
    place = iota((rows, LANES), 0)
    right = jnp.where(index < peers - 1, 2.0 * face_scale, 0.0)
    left = jnp.where(index > 0, 2.0 * face_scale, 0.0)
    return jnp.where(place == own - 1, right, jnp.where(place == rows - 1, left, 2.0 * face_scale))


def lane_numerators(rows, index, peers, face_scale):
    place = iota((rows, LANES), 1)
    right = jnp.where(index < peers - 1, 2.0 * face_scale, 0.0)
    left = jnp.where(index > 0, 2.0 * face_scale, 0.0)
    return [jnp.where(place == LANES - 1, side, 2.0 * face_scale) for side in (right, left)]


def lane_tiles(value):
    return [value[:, i : i + LANES] for i in range(0, value.shape[1], LANES)]


def beside(tiles, shift):
    moved = [turned(tile, shift, 1) for tile in tiles]
    lane = iota(tiles[0].shape, 1)
    seam = LANES - 1 if shift < 0 else 0
    return [
        jnp.where(lane == seam, moved[(j - shift) % len(tiles)], moved[j]) for j in range(len(tiles))
    ]


def store_rows(ref, k, j, value):
    rows = value.shape[0]
    ref[k, j, SUBLANES : SUBLANES + rows] = value
    ref[k, j, SUBLANES - 1 : SUBLANES] = value[rows - 1 :]
    ref[k, j, SUBLANES + rows : SUBLANES + rows + 1] = value[:1]


def iterate(count, own_rows, rows, tiles, log_at, source_at, x_faces, y_top, z_top, coef_ref, storage, emit, refs, ready=None):
    k_ref, tx_ref, ty_ref, tzr_ref, tzl_ref, diag_ref, w_ref, d_ref, r_ref, p_ref = refs
    own_tiles = tiles - 1

    def away(k):
        return max(0, REACH - k, k - (count - 1 - REACH))

    def extent(k, step):
        left = DEGREE - step - away(k)
        return None if left < 0 else (own_rows, own_tiles) if left == 0 else (rows, tiles)

    def coefficient(i, size):
        return jnp.concatenate([coef_ref[i]] * (size // SUBLANES), axis=0)

    z_tops = [z_top[0] if j == own_tiles - 1 else z_top[1] if j == own_tiles else None for j in range(tiles)]

    def resistance(k):
        logs = lane_tiles(log_at(k))
        if ready is None:
            return [jnp.exp(-tile) for tile in logs]
        return [
            jnp.concatenate([ready[0][k, j], jnp.exp(-logs[j][own_rows:])], axis=0) for j in range(own_tiles)
        ] + [jnp.exp(-logs[own_tiles])]

    def along_x(k, j, size):
        if ready is None or j == own_tiles:
            return tx_ref[k, j, :size]
        if size == own_rows:
            return ready[1][k, j]
        return jnp.concatenate([ready[1][k, j], tx_ref[k, j, own_rows:size]], axis=0)

    after = resistance(0)
    tx_before = None
    for k in range(count):
        here = after
        if k + 1 < count:
            after = resistance(k + 1)
            outer = max(away(k), away(k + 1))
            size, number = (rows, tiles) if outer < REACH else (own_rows, own_tiles)
            tx = []
            for j in range(number):
                begin = 0 if ready is None or j == own_tiles else own_rows
                if begin < size:
                    tx_ref[k, j, begin:size] = x_faces[k] * inverse(here[j][begin:size] + after[j][begin:size])
                tx.append(along_x(k, j, size))
        if away(k) <= DEGREE:
            size, number = extent(k, 0)
            right = beside(here, -1)
            tz = []
            for j in range(tiles):
                scale = z_tops[j][:size] if z_tops[j] is not None else z_top[2]
                tz.append(scale * inverse(here[j][:size] + right[j][:size]))
            tz_left = beside(tz, 1)
            source = lane_tiles(source_at(k))
            for j in range(number):
                store_rows(k_ref, k, j, here[j])
                ty = y_top * inverse(here[j] + k_ref[k, j, SUBLANES + 1 : SUBLANES + 1 + rows])
                store_rows(ty_ref, k, j, ty)
                ty_before = ty_ref[k, j, SUBLANES - 1 : SUBLANES - 1 + size]
                diagonal = storage + (tx_before[j][:size] + tx[j][:size])
                diagonal = diagonal + (ty[:size] + ty_before) + (tz[j] + tz_left[j])
                w = inverse(diagonal)
                direction = source[j][:size] * (coefficient(0, size) * w)
                if (size, number) == (rows, tiles):
                    store_rows(d_ref.at[0], k, j, direction)
                else:
                    d_ref[0, k, j, SUBLANES : SUBLANES + size] = direction
                if extent(k, 1) is not None:
                    tzr_ref[k, j, :size] = tz[j]
                    tzl_ref[k, j, :size] = tz_left[j]
                    diag_ref[k, j, :size] = diagonal
                    w_ref[k, j, :size] = w
                    r_ref[k, j, :size] = source[j][:size]
        tx_before = tx
    for step in range(1, DEGREE + 1):
        old, new = d_ref.at[(step - 1) % 2], d_ref.at[step % 2]
        for k in range(count):
            if extent(k, step) is None:
                continue
            size, number = extent(k, step)
            middle = slice(SUBLANES, SUBLANES + size)
            keep, gain = coefficient(2 * step - 1, size), coefficient(2 * step, size)
            here = [old[k, j, middle] for j in range(tiles)]
            right, left = beside(here, -1), beside(here, 1)
            for j in range(number):
                applied = along_x(k, j, size) * old[k + 1, j, middle] + along_x(k - 1, j, size) * old[k - 1, j, middle]
                applied += (
                    ty_ref[k, j, middle] * old[k, j, SUBLANES + 1 : SUBLANES + 1 + size]
                    + ty_ref[k, j, SUBLANES - 1 : SUBLANES - 1 + size] * old[k, j, SUBLANES - 1 : SUBLANES - 1 + size]
                )
                applied += tzr_ref[k, j, :size] * right[j] + tzl_ref[k, j, :size] * left[j]
                residual = r_ref[k, j, :size] - (diag_ref[k, j, :size] * here[j] - applied)
                fresh = keep * here[j] + gain * (residual * w_ref[k, j, :size])
                if away(k) == 0 and j < own_tiles:
                    so_far = here[j][:own_rows] if step == 1 else p_ref[k, j]
                    total = so_far + fresh[:own_rows]
                    if step == DEGREE:
                        emit(k - REACH, j, total)
                    else:
                        p_ref[k, j] = total
                if step < DEGREE:
                    r_ref[k, j, :size] = residual
                    if (size, number) == (rows, tiles):
                        store_rows(new, k, j, fresh)
                    else:
                        new[k, j, middle] = fresh


def coefficients_kernel(low_ref, high_ref, after_ref, coef_ref):
    low, high = (jnp.full((SUBLANES, LANES), ref[0]) for ref in (low_ref, high_ref))
    theta, delta = (high + low) * 0.5, (high - low) * 0.5
    sigma = theta / delta
    rho = 1.0 / sigma
    coef_ref[0] = 1.0 / theta
    for step in range(DEGREE):
        rho_next = 1.0 / (2.0 * sigma - rho)
        coef_ref[1 + 2 * step] = rho_next * rho
        coef_ref[2 + 2 * step] = 2.0 * rho_next / delta
        rho = rho_next


def chebyshev_coefficients(low_bound, high_bound, after):
    return pl.pallas_call(
        coefficients_kernel,
        out_shape=jax.ShapeDtypeStruct((1 + 2 * DEGREE, SUBLANES, LANES), jnp.float32),
        in_specs=[pl.BlockSpec(memory_space=pltpu.SMEM)] * 2 + [ANY],
        out_specs=VMEM,
        compiler_params=pltpu.CompilerParams(vmem_limit_bytes=4 << 20),
        cost_estimate=pl.CostEstimate(flops=1_000_000, bytes_accessed=100_000, transcendentals=0),
        name="coefficients",
    )(low_bound, high_bound, after)


def put(ref, tile, value):
    for i in range(value.shape[1] // LANES):
        ref[(tile + i) * SUBLANES : (tile + i + 1) * SUBLANES, :] = value[:, i * LANES : (i + 1) * LANES]


def take(ref, tile, count):
    tiles = [ref[(tile + i) * SUBLANES : (tile + i + 1) * SUBLANES, :] for i in range(count)]
    return tiles[0] if count == 1 else jnp.concatenate(tiles, axis=1)


def edges(value):
    lanes = value.shape[-1]
    value = value if isinstance(value, jax.Array) else value.at
    return value[:, lanes - LANES :], value[:, :LANES]


def write_lanes(pairs):
    starts = lax.axis_index("gz") == 0
    each = LANES // REACH
    group = iota((SUBLANES, LANES), 1) // REACH
    merged = None
    for j, (last, first) in enumerate(pairs):
        moved = turned(jnp.where(starts, last, first), REACH * j, 1)
        place = jnp.where(starts, (j - 1) % each, j)
        merged = moved if merged is None else jnp.where(group == place, moved, merged)
    return merged


def read_lanes(tile, slot):
    return turned(tile, -REACH * slot, 1)


def add_lanes(tile, slot, value):
    starts = lax.axis_index("gz") == 0
    group = iota((SUBLANES, LANES), 1) // REACH
    place = jnp.where(starts, slot, (slot - 1) % (LANES // REACH))
    return jnp.where(group == place, turned(value, REACH * slot, 1), tile)


def lane_slots(layers, row_tiles, n_got):
    keys = [("own", a, layer, i) for a in range(2) for layer in range(layers) for i in range(row_tiles)]
    keys += [("pooled", x, a) for x in range(2) for a in range(2)]
    shared = len(keys)
    keys += [("halo", i, half) for i in range(n_got) for half in range(2)]
    keys += [("got", g, layer) for g in range(n_got) for layer in range(layers)]
    return {key: i for i, key in enumerate(keys)}, shared


def near_layout(lanes, wide):
    whole, half = lanes // LANES, lanes // LANES // 2
    if wide:
        parts = [("log1", whole), ("source1", whole), ("log2", whole), ("source2", whole)]
        parts += [(name, half) for name in ("halo0", "halo1", "halo2", "halo3", "source")]
    else:
        parts = [("strip", whole), ("halo", half), ("source", half), ("row", 1)]
    layout, start = {}, 0
    for name, count in parts + [("lanes", 1)]:
        layout[name] = (start, count)
        start += count
    return layout, start


def near_lane_slots(lanes, wide, shared):
    names = [name for name in near_layout(lanes, wide)[0] if name not in ("source", "lanes")]
    return {name: shared + i for i, name in enumerate(names)}


def rows_to_lanes(row_tile, count):
    return jnp.concatenate(
        [jnp.broadcast_to(row_tile[j : j + 1], (SUBLANES, LANES)) for j in range(count)], axis=1
    )


def window_scratch(count, own_rows, rows, tiles):
    plain = pltpu.VMEM((count, tiles, rows, LANES), jnp.float32)
    margins = pltpu.VMEM((count, tiles, rows + 2 * SUBLANES, LANES), jnp.float32)
    pair = pltpu.VMEM((2, count, tiles, rows + 2 * SUBLANES, LANES), jnp.float32)
    total = pltpu.VMEM((count, tiles, own_rows, LANES), jnp.float32)
    return [margins, plain, margins, plain, plain, plain, plain, pair, plain, total]


def exact_dot(value, zero_one):
    parts = []
    for _ in range(3):
        part = value.astype(jnp.bfloat16)
        parts.append(part)
        value = value - part.astype(jnp.float32)
    rows = value.shape[0]
    out = jnp.dot(jnp.concatenate(parts, axis=0), zero_one, preferred_element_type=jnp.float32)
    return (out[2 * rows :] + out[rows : 2 * rows]) + out[:rows]


def row_pairs(top, bottom, sum_ref):
    tiles = top.shape[1] // LANES
    for tile in range(tiles):
        columns = slice(tile * LANES, (tile + 1) * LANES)
        sum_ref[tile, :SUBLANES] = top[:, columns]
        sum_ref[tile, SUBLANES:] = bottom[:, columns]
    return jnp.concatenate(
        [
            sum_ref[tile, pl.ds(0, SUBLANES, stride=2), :] + sum_ref[tile, pl.ds(1, SUBLANES, stride=2), :]
            for tile in range(tiles)
        ],
        axis=1,
    )


def lane_pairs(pieces):
    lanes = pieces[0].shape[1]
    pick = (iota((lanes, lanes // 2), 0) // 2 == iota((lanes, lanes // 2), 1)).astype(jnp.bfloat16)
    pooled = exact_dot(jnp.concatenate(pieces, axis=0), pick)
    return [pooled[SUBLANES * i : SUBLANES * (i + 1)] for i in range(len(pieces))]


def join_halo(near, beyond, starts):
    row = iota(near.shape, 0)
    up, down = turned(beyond, 3, 0), turned(beyond, -3, 0)
    right = jnp.where((row == 3) | (row == 7), up, jnp.where(row == 6, turned(beyond, 5, 0), near))
    left = jnp.where((row == 0) | (row == 4), down, jnp.where(row == 5, up, near))
    return jnp.where(starts, right, left)


def beyond_halo(joined, starts):
    row = iota(joined.shape, 0)
    up, down = turned(joined, 3, 0), turned(joined, -3, 0)
    right = jnp.where(row == 1, turned(joined, -5, 0), down)
    left = jnp.where(row == 2, down, up)
    return jnp.where(starts, right, left)


def join_third(near, third):
    row = iota(near.shape, 0)
    return jnp.where(
        row == 3, turned(third, 3, 0), jnp.where(row == 4, turned(third, -3, 0), near)
    )


def third_halo(joined):
    return jnp.where(iota(joined.shape, 0) < REACH, turned(joined, -3, 0), turned(joined, 3, 0))


def parts(both_ref):
    layers = both_ref.shape[0] // 2
    return both_ref.at[:layers], both_ref.at[layers:]


def prep_kernel(both_ref, pooled_ref, *refs):
    *out_refs, sum_ref = refs
    log_ref, source_ref = parts(both_ref)
    layers, rows, lanes = log_ref.shape
    starts = lax.axis_index("gy") == 0

    def put(slot, left, right):
        if len(out_refs) == 1:
            out_refs[0][slot] = jnp.where(starts, right, left)
        else:
            out_refs[0][slot], out_refs[1][slot] = left, right

    half = lanes // 2
    upper = iota((SUBLANES, lanes), 0) < REACH
    pieces = []
    for x in range(2):
        for ref in (log_ref, source_ref):
            both = ref[2 * x] + ref[2 * x + 1]
            pieces.append(row_pairs(both[:SUBLANES], both[SUBLANES:], sum_ref))
    log0, source0, log1, source1 = lane_pairs(pieces)
    log0, log1 = log0 * 0.125, log1 * 0.125
    pooled_ref[0] = jnp.concatenate([log0, source0], axis=1)
    pooled_ref[1] = jnp.concatenate([log1, source1], axis=1)
    for layer in range(layers):
        put(
            layer,
            jnp.where(upper, log_ref[layer, :SUBLANES], turned(source_ref[layer, :SUBLANES], REACH, 0)),
            jnp.where(upper, turned(source_ref[layer, SUBLANES:], REACH, 0), log_ref[layer, SUBLANES:]),
        )
    pair = iota((SUBLANES, half), 0) // 2

    def four(*tiles):
        merged = jnp.where(
            pair == 0, tiles[0], jnp.where(pair == 1, tiles[1], jnp.where(pair == 2, tiles[2], tiles[3]))
        )
        return jnp.concatenate([merged, merged], axis=1)

    put(
        layers,
        four(turned(log1, -2, 0), log0, turned(source1, 2, 0), turned(source0, 4, 0)),
        four(turned(log0, -4, 0), turned(log1, -2, 0), source0, turned(source1, 2, 0)),
    )


def prep(both, ny):
    layers, rows, lanes = both.shape[0] // 2, *both.shape[1:]
    outs = 1 if ny == 2 else 2

    def tiles(count):
        return jax.ShapeDtypeStruct((count, SUBLANES, lanes), jnp.float32)

    return pl.pallas_call(
        prep_kernel,
        out_shape=(tiles(2),) + (tiles(layers + 1),) * outs,
        in_specs=[VMEM],
        out_specs=(VMEM,) * (1 + outs),
        scratch_shapes=[pltpu.VMEM((lanes // LANES, 2 * SUBLANES, LANES), jnp.float32)],
        compiler_params=pltpu.CompilerParams(vmem_limit_bytes=8 << 20),
        cost_estimate=pl.CostEstimate(flops=5_000_000, bytes_accessed=700_000, transcendentals=0),
        name="prep",
    )(both)


def raw_kernel(to_right_if_odd, both_ref, after_ref, out_ref):
    log_ref, source_ref = parts(both_ref)
    layers = log_ref.shape[0]
    odd = lax.axis_index("gx") % 2
    skip = odd if to_right_if_odd else 1 - odd
    for layer in range(layers):
        out_ref[layer] = log_ref[layer]
    for layer in range(layers - 1):
        out_ref[layers + layer] = source_ref[layer + skip]


def raw_block(both, after, to_right_if_odd):
    layers, rows, lanes = both.shape[0] // 2, *both.shape[1:]
    return pl.pallas_call(
        functools.partial(raw_kernel, to_right_if_odd),
        out_shape=jax.ShapeDtypeStruct((2 * layers - 1, rows, lanes), jnp.float32),
        in_specs=[VMEM, ANY],
        out_specs=VMEM,
        compiler_params=pltpu.CompilerParams(vmem_limit_bytes=8 << 20),
        cost_estimate=pl.CostEstimate(flops=1_000_000, bytes_accessed=500_000, transcendentals=0),
        name="raw_block",
    )(both, after)


def halos_kernel(wide, both_ref, pooled_ref, *refs):
    *got_refs, halo_ref, sent_ref, sum_ref = refs
    layers, lanes = got_refs[0].shape[0] - 1, got_refs[0].shape[2]
    iy = lax.axis_index("gy")
    even, starts = iy % 2 == 0, iy == 0
    half = lanes // 2
    upper = iota((SUBLANES, lanes), 0) < REACH
    row = iota((SUBLANES, half), 0)

    def got(slot):
        tiles = tuple(ref[slot] for ref in got_refs)
        return from_right(even, tiles), from_left(even, tiles)

    strips = [got(layer) for layer in range(layers)]
    extra = [tile[:, :half] for tile in got(layers)]
    pieces = []
    for side in range(2 if wide else 1):
        both = [strips[2 * x][side] + strips[2 * x + 1][side] for x in range(2)]
        pieces.append(row_pairs(*both, sum_ref))
    fine_rows = lane_pairs(pieces)

    def right_halos(rows, extra):
        rows = jnp.where(row % 4 < 2, rows * 0.125, rows)
        return [
            jnp.where(row < 2, near, jnp.where((row == 4) | (row == 5), far, more))
            for near, far, more in (
                (rows, turned(rows, 2, 0), extra),
                (turned(rows, 4, 0), turned(rows, -2, 0), turned(extra, 2, 0)),
            )
        ]

    def left_halos(rows, extra):
        rows = jnp.where(row % 4 >= 2, rows * 0.125, rows)
        return [
            jnp.where((row == 2) | (row == 3), near, jnp.where(row >= 6, far, more))
            for near, far, more in (
                (rows, turned(rows, -2, 0), extra),
                (turned(rows, 4, 0), turned(rows, 2, 0), turned(extra, -2, 0)),
            )
        ]

    right, left = right_halos(fine_rows[0], extra[0]), left_halos(fine_rows[-1], extra[1])
    if wide:
        top = row < REACH
        halos = [jnp.where(top, right[x], turned(left[x], REACH, 0)) for x in range(2)]
        halos += [jnp.where(top, turned(right[x], REACH, 0), left[x]) for x in range(2)]
    else:
        halos = [jnp.where(starts, right[x], left[x]) for x in range(2)]

    def pair(left, right):
        return jnp.concatenate([left, right], axis=1)

    for i in range(len(halos) // 2):
        halo_ref[i] = pair(halos[2 * i], halos[2 * i + 1])
    pairs = {}
    rows = both_ref.shape[1]
    for a, ref in enumerate(parts(both_ref)):
        for layer in range(layers):
            for i in range(rows // SUBLANES):
                pairs["own", a, layer, i] = edges(ref[layer, i * SUBLANES : (i + 1) * SUBLANES])
    for x in range(2):
        for a in range(2):
            pairs["pooled", x, a] = edges(pooled_ref[x, :, a * half : (a + 1) * half])
    for i, halo in enumerate(halos):
        pairs["halo", i // 2, i % 2] = edges(halo)
    for g, ref in enumerate(got_refs):
        for layer in range(layers):
            pairs["got", g, layer] = edges(ref[layer])
    slots, _ = lane_slots(layers, rows // SUBLANES, len(got_refs))
    sent_ref[...] = jnp.zeros(sent_ref.shape, jnp.float32)
    sent_ref[:SUBLANES] = write_lanes([pairs[key] for key in slots])


def pooled_halos(both, pooled, got):
    slots, rows, lanes = got[0].shape
    return pl.pallas_call(
        functools.partial(halos_kernel, len(got) == 2),
        out_shape=(
            jax.ShapeDtypeStruct((len(got), SUBLANES, lanes), jnp.float32),
            jax.ShapeDtypeStruct((LANES, LANES), jnp.float32),
        ),
        in_specs=[VMEM] * (2 + len(got)),
        out_specs=(VMEM,) * 2,
        scratch_shapes=[pltpu.VMEM((lanes // LANES, 2 * SUBLANES, LANES), jnp.float32)],
        compiler_params=pltpu.CompilerParams(vmem_limit_bytes=8 << 20),
        cost_estimate=AHEAD,
        name="halos",
    )(both, pooled, *got)


def pack_far_kernel(wide, pooled_ref, halo_ref, *far_refs):
    half = pooled_ref.shape[2] // 2
    low = lax.axis_index("gx") % 4 < 2

    def tiles(inner):
        return (
            pooled_ref[inner, :, :half],
            pooled_ref[1 - inner, :, :half],
            pooled_ref[inner, :, half:],
            halo_ref[0, :, inner * half : (inner + 1) * half],
        )

    for group, ref in enumerate(far_refs):
        for i, (right, left) in enumerate(zip(tiles(1), tiles(0))):
            put(ref, i * (half // LANES), jnp.where(low, *((right, left) if group == 0 else (left, right))))
        for spare in range(4 * (half // LANES), ref.shape[0] // SUBLANES):
            put(ref, spare, jnp.zeros((SUBLANES, LANES), jnp.float32))


def pack_far(pooled, halos, n_far, wide):
    _, rows, lanes = pooled.shape
    far_rows = max(2 * lanes // LANES + 1, 0 if wide else near_layout(lanes, wide)[1]) * SUBLANES
    return pl.pallas_call(
        functools.partial(pack_far_kernel, wide),
        out_shape=(jax.ShapeDtypeStruct((far_rows, LANES), jnp.float32),) * n_far,
        in_specs=[VMEM] * 2,
        out_specs=(VMEM,) * n_far,
        compiler_params=pltpu.CompilerParams(vmem_limit_bytes=8 << 20),
        cost_estimate=pl.CostEstimate(flops=1_000_000, bytes_accessed=500_000, transcendentals=0),
        name="pack_far",
    )(pooled, halos)


def pack_near_kernel(wide, pooled_ref, halo_ref, early_ref, after_ref, *refs):
    *got_refs, first_ref, second_ref = refs
    layers, lanes = got_refs[0].shape[0] - 1, got_refs[0].shape[2]
    ix, iy = lax.axis_index("gx"), lax.axis_index("gy")
    even, starts = iy % 2 == 0, iy == 0
    half = lanes // 2
    upper = iota((SUBLANES, lanes), 0) < REACH

    def got(slot):
        tiles = tuple(ref[slot] for ref in got_refs)
        return from_right(even, tiles), from_left(even, tiles)

    strips = [got(layer) for layer in range(layers)]
    halos = [halo_ref[i // 2, :, (i % 2) * half : (i % 2 + 1) * half] for i in range(4 if wide else 2)]
    sources = [pooled_ref[x, :, half:] for x in range(2)]

    slots, shared = lane_slots(layers, 2, len(got_refs))

    def strip_lanes(layer):
        tiles = tuple(read_lanes(early_ref[:SUBLANES], slots["got", g, layer]) for g in range(len(got_refs)))
        return from_right(even, tiles), from_left(even, tiles)

    def halo_lanes(i):
        return read_lanes(early_ref[:SUBLANES], slots["halo", i // 2, i % 2])

    def near_tiles(order, strips, halos):
        near, beyond = order[0] // 2, order[-1] // 2
        width = strips[0][0].shape[1]
        upper = iota((SUBLANES, width), 0) < REACH
        if wide:
            log_rows = [jnp.where(upper, *strips[layer]) for layer in range(layers)]
            source_rows = [turned(jnp.where(upper, *strips[layer][::-1]), REACH, 0) for layer in range(layers)]
            return {
                "log1": join_third(log_rows[order[0]], log_rows[order[2]]),
                "source1": source_rows[order[0]],
                "log2": log_rows[order[1]],
                "source2": source_rows[order[1]],
                "halo0": halos[near],
                "halo1": halos[beyond],
                "halo2": halos[2 + near],
                "halo3": halos[2 + beyond],
            }
        first, second, third = (strips[layer][0] for layer in order[:3])
        place = iota((SUBLANES, width), 0)
        right = jnp.where(place == 3, turned(third, 3, 0), jnp.where(place >= 6, turned(second, -2, 0), first))
        left = jnp.where(place == 4, turned(third, -3, 0), jnp.where(place < 2, turned(second, 2, 0), first))
        line = jnp.where(starts, second[4:5], second[3:4])
        if width == LANES:
            lines = jnp.broadcast_to(line, (SUBLANES, LANES))
        else:
            lines = jnp.zeros((SUBLANES, LANES), jnp.float32)
            for j in range(width // LANES):
                lines = jnp.where(iota(lines.shape, 0) == j, line[:, j * LANES : (j + 1) * LANES], lines)
        return {
            "strip": jnp.where(starts, right, left),
            "halo": join_halo(halos[near], halos[beyond], starts),
            "row": lines,
        }

    def side(order):
        tiles = near_tiles(order, strips, halos)
        tiles["source"] = sources[order[-1] // 2]
        lanes_tile = early_ref[:SUBLANES]
        n_halos = 4 if wide else 2
        beside = near_tiles(
            order, [strip_lanes(layer) for layer in range(layers)], [halo_lanes(i) for i in range(n_halos)]
        )
        for name, slot in near_lane_slots(lanes, wide, shared).items():
            lanes_tile = add_lanes(lanes_tile, slot, beside[name])
        tiles["lanes"] = lanes_tile
        return tiles

    forward = list(range(layers))
    layout, _ = near_layout(lanes, wide)
    right, left = side(forward[::-1]), side(forward)
    for name, (start, _) in layout.items():
        put(first_ref, start, jnp.where(ix % 2 == 0, right[name], left[name]))
        put(second_ref, start, jnp.where(ix % 2 == 0, left[name], right[name]))


def pack_near(pooled, halos, early, after, got):
    slots, rows, lanes = got[0].shape
    wide = len(got) == 2
    out = jax.ShapeDtypeStruct((near_layout(lanes, wide)[1] * SUBLANES, LANES), jnp.float32)
    return pl.pallas_call(
        functools.partial(pack_near_kernel, wide),
        out_shape=(out, out),
        in_specs=[VMEM] * 3 + [ANY] + [VMEM] * len(got),
        out_specs=(VMEM,) * 2,
        compiler_params=pltpu.CompilerParams(vmem_limit_bytes=8 << 20),
        cost_estimate=pl.CostEstimate(flops=1_000_000, bytes_accessed=500_000, transcendentals=0),
        name="pack_near",
    )(pooled, halos, early, after, *got)


def pool_kernel(after_ref, first_ref, second_ref, out_ref, sum_ref):
    layers = REACH
    even = lax.axis_index("gx") % 2 == 0
    pieces = []
    for side, pick in enumerate((from_left, from_right)):

        def block(slot):
            return pick(even, (first_ref[slot], second_ref[slot]))

        for top in (0, 2, layers + 1 if side == 0 else layers):
            both = block(top) + block(top + 1)
            pieces.append(row_pairs(both[:SUBLANES], both[SUBLANES:], sum_ref))
    for i, tile in enumerate(lane_pairs(pieces)):
        put(out_ref, i * (tile.shape[1] // LANES), tile * (0.125 if i % 3 < 2 else 1.0))


def pool(after, raw):
    _, rows, lanes = raw[0].shape
    return pl.pallas_call(
        pool_kernel,
        out_shape=jax.ShapeDtypeStruct((6 * (lanes // 2 // LANES) * SUBLANES, LANES), jnp.float32),
        in_specs=[ANY] + [VMEM] * 2,
        out_specs=VMEM,
        scratch_shapes=[pltpu.VMEM((lanes // LANES, 2 * SUBLANES, LANES), jnp.float32)],
        compiler_params=pltpu.CompilerParams(vmem_limit_bytes=16 << 20),
        cost_estimate=pl.CostEstimate(flops=1_000_000, bytes_accessed=1_000_000, transcendentals=0),
        name="pool",
    )(after, *raw)


def x_faces_of(layers, ix, nx):
    faces = [2.0] * (3 * layers - 1)
    faces[layers - 1] = jnp.where(ix > 0, 2.0, 0.0)
    faces[2 * layers - 1] = jnp.where(ix < nx - 1, 2.0, 0.0)
    return faces


def ahead_kernel(nx, after_ref, both_ref, first_ref, second_ref, inverse_ref, tx_ref):
    log_ref, _ = parts(both_ref)
    layers, rows, lanes = log_ref.shape
    ix = lax.axis_index("gx")
    faces = x_faces_of(layers, ix, nx)
    before = None
    for k in range(3 * layers):
        side, layer = k // layers - 1, k % layers
        if side == 0:
            log = log_ref[layer]
        else:
            log = (from_left if side < 0 else from_right)(ix % 2 == 0, (first_ref[layer], second_ref[layer]))
        here = [jnp.exp(-tile) for tile in lane_tiles(log)]
        for j, tile in enumerate(here):
            inverse_ref[k, j] = tile
            if k > 0:
                tx_ref[k - 1, j] = faces[k - 1] * inverse(before[j] + tile)
        before = here


def ahead(after, both, raw, nx):
    layers, rows, lanes = both.shape[0] // 2, *both.shape[1:]

    def tiles(count):
        return jax.ShapeDtypeStruct((count, lanes // LANES, rows, LANES), jnp.float32)

    return pl.pallas_call(
        functools.partial(ahead_kernel, nx),
        out_shape=(tiles(3 * layers), tiles(3 * layers - 1)),
        in_specs=[ANY] + [VMEM] * 3,
        out_specs=(VMEM,) * 2,
        compiler_params=pltpu.CompilerParams(vmem_limit_bytes=16 << 20),
        cost_estimate=pl.CostEstimate(flops=1_000_000, bytes_accessed=1_000_000, transcendentals=0),
        name="ahead",
    )(after, both, *raw)


def near_part(refs, even, lanes, wide, side, name):
    start, count = near_layout(lanes, wide)[0][name]
    pick = from_left if side == 0 else from_right
    got = pick(even, tuple(take(ref, start, count) for ref in refs))
    return rows_to_lanes(got, lanes // LANES) if name == "row" else got


def far_part(refs, low, lanes, side, i):
    count = lanes // 2 // LANES
    pick = from_left if side == 0 else from_right
    return pick(low, tuple(take(ref, i * count, count) for ref in refs))


def far_lanes_kernel(lanes, after_ref, *refs):
    *far_refs, sent_ref = refs
    low = lax.axis_index("gx") % 4 < 2
    sent_ref[...] = write_lanes([edges(far_part(far_refs, low, lanes, side, 0)) for side in range(2)])


def far_lanes(after, far, lanes):
    return pl.pallas_call(
        functools.partial(far_lanes_kernel, lanes),
        out_shape=jax.ShapeDtypeStruct((SUBLANES, LANES), jnp.float32),
        in_specs=[ANY] + [VMEM] * len(far),
        out_specs=VMEM,
        compiler_params=pltpu.CompilerParams(vmem_limit_bytes=4 << 20),
        cost_estimate=pl.CostEstimate(flops=1_000_000, bytes_accessed=100_000, transcendentals=0),
        name="far_lanes",
    )(after, *far)


def coarse_part(peers, n_far, own_ref, halo_ref, pool_ref, first_ref, second_ref, *refs):
    near_refs, far_refs = (first_ref, second_ref), refs[:n_far]
    early_ref, beyond_ref, coef_ref, out_ref, wide_ref, *scratch = refs[n_far:]
    ix, iy, iz = (lax.axis_index(axis) for axis in AXES)
    nx, ny, nz = peers
    wide = ny > 2
    fine_lanes = own_ref.shape[2]
    lanes, rows = fine_lanes // 2, SUBLANES
    even, low, starts = ix % 2 == 0, ix % 4 < 2, iy == 0
    top = iota((rows, lanes + LANES), 0) < REACH
    slots, shared = lane_slots(REACH, 2, 2 if wide else 1)
    near_slots = near_lane_slots(fine_lanes, wide, shared)
    own_lanes = early_ref[:SUBLANES]
    near_lanes = [near_part(near_refs, even, fine_lanes, wide, side, "lanes") for side in range(2)]

    def columns(half):
        return slice(half * lanes, (half + 1) * lanes)

    def join(core, tile, slot):
        return jnp.concatenate([core, read_lanes(tile, slot)], axis=1)

    def near(side, name):
        core = near_part(near_refs, even, fine_lanes, wide, side, name)
        return join(core, near_lanes[side], near_slots[name])

    def far(side, i):
        core = far_part(far_refs, low, fine_lanes, side, i)
        return join(core, beyond_ref[...], side)

    def split(tile, a):
        other = turned(tile, REACH, 0)
        return jnp.where(top, tile, other) if a == 0 else jnp.where(top, other, tile)

    def window(a, k):
        block, layer = k // 2 - 2, k % 2
        nearest = layer == (1 if block < 0 else 0)
        side = 0 if block < 0 else 1
        if abs(block) == 2:
            if a == 1:
                core = far(side, 2)
                return jnp.concatenate([core, jnp.zeros_like(core)], axis=0)
            halo = far(side, 3)
            halo = halo if wide else split(halo, 0)
            return jnp.concatenate([far(side, 0 if nearest else 1), halo], axis=0)
        if block == 0:
            core = join(own_ref[layer, :, columns(a)], own_lanes, slots["pooled", layer, a])
            if wide:
                halo = join(halo_ref[a, :, columns(layer)], own_lanes, slots["halo", a, layer])
            else:
                halo = split(join(halo_ref[0, :, columns(layer)], own_lanes, slots["halo", 0, layer]), a)
            return jnp.concatenate([core, halo], axis=0)
        if a == 0 or nearest:
            i = layer if a == 0 else 2
            core = take(pool_ref, (3 * side + i) * (lanes // LANES), lanes // LANES)
        else:
            core = near_part(near_refs, even, fine_lanes, wide, side, "source")
        core = join(core, near_lanes[side], slots["pooled", layer, a])
        if wide:
            halo = near(side, f"halo{2 * a + (0 if nearest else 1)}")
        else:
            joined = near(side, "halo")
            halo = split(joined if nearest else beyond_halo(joined, starts), a)
        return jnp.concatenate([core, halo], axis=0)

    def open_face(inside):
        return jnp.where(inside, 4.0, 0.0)

    faces = [4.0] * 9
    faces[1], faces[3] = open_face(ix > 1), open_face(ix > 0)
    faces[5], faces[7] = open_face(ix < nx - 1), open_face(ix < nx - 2)
    *scratch, p_ref = scratch

    def emit(layer, tile, value):
        p_ref[layer * rows : (layer + 1) * rows, tile * LANES : (tile + 1) * LANES] = value

    iterate(
        2 + 2 * REACH,
        rows,
        2 * rows,
        lanes // LANES + 1,
        functools.partial(window, 0),
        functools.partial(window, 1),
        faces,
        row_numerators(2 * rows, rows, iy, ny, 2.0),
        lane_numerators(2 * rows, iz, nz, 2.0) + [4.0],
        coef_ref,
        8.0 * storage_rate,
        emit,
        scratch,
    )
    widen = (iota((lanes, 2 * lanes), 0) == iota((lanes, 2 * lanes), 1) // 2).astype(jnp.bfloat16)
    spread = exact_dot(p_ref[...], widen)
    for x in range(2):
        for tile in range(2 * lanes // LANES):
            part = slice(tile * LANES, (tile + 1) * LANES)
            for half in range(2):
                wide_ref[tile, pl.ds(half, rows, stride=2), :] = spread[x * rows : (x + 1) * rows, part]
            for twin in range(2):
                out_ref[2 * x + twin, :, part] = wide_ref[tile]


def levels_kernel(peers, n_far, both_ref, *refs):
    log_ref, source_ref = parts(both_ref)
    layers, rows, lanes = log_ref.shape
    ix, iy, iz = (lax.axis_index(axis) for axis in AXES)
    nx, ny, nz = peers
    wide = ny > 2
    n_got = 2 if wide else 1
    got_refs, refs = refs[:n_got], refs[n_got:]
    second_ref, first_ref = refs[:2]
    far_refs = refs[2 : 2 + n_far]
    second_near_ref, first_near_ref, early_ref, coef_ref = refs[2 + n_far : 6 + n_far]
    near_refs = first_near_ref, second_near_ref
    own_ref, halo_ref, pool_ref, beyond_ref, inverse_ref, tx_ref, fine_ref, diff_ref, *scratch = refs[6 + n_far :]
    scratch, (spread_ref, *coarse_scratch) = scratch[:10], scratch[10:]
    coarse_part(
        peers,
        n_far,
        own_ref,
        halo_ref,
        pool_ref,
        *near_refs,
        *far_refs,
        early_ref,
        beyond_ref,
        coef_ref,
        spread_ref,
        *coarse_scratch,
    )
    even, starts = ix % 2 == 0, iy == 0
    count = 3 * layers
    upper = iota((SUBLANES, lanes + LANES), 0) < REACH
    slots, shared = lane_slots(layers, rows // SUBLANES, n_got)
    near_slots = near_lane_slots(lanes, wide, shared)
    own_lanes = early_ref[:SUBLANES]
    near_lanes = [near_part(near_refs, even, lanes, wide, side, "lanes") for side in range(2)]

    def join(core, tile, *keys):
        beside = jnp.concatenate([read_lanes(tile, key) for key in keys], axis=0)
        return jnp.concatenate([core, beside], axis=1)

    def near(side, name):
        return join(near_part(near_refs, even, lanes, wide, side, name), near_lanes[side], near_slots[name])

    def near_halo(a, side, distance):
        if wide:
            tile = near(side, ("log" if a == 0 else "source") + ("2" if distance == 2 else "1"))
        elif a == 1:
            return near(side, "row") if distance == 2 else turned(near(side, "strip"), REACH, 0)
        else:
            tile = near(side, "strip")
            if distance == 2:
                return jnp.where(starts, turned(tile, 2, 0), turned(tile, -2, 0))
        return third_halo(tile) if a == 0 and distance > 2 else tile

    def window(a, k):
        block, layer = k // layers - 1, k % layers
        if block == 0:
            core = (log_ref, source_ref)[a][layer]
            core = join(core, own_lanes, *(slots["own", a, layer, i] for i in range(rows // SUBLANES)))
            tiles = tuple(
                join(ref[layer], own_lanes, slots["got", g, layer]) for g, ref in enumerate(got_refs)
            )
            halo = tiles[0]
            if wide:
                sides = from_right(iy % 2 == 0, tiles), from_left(iy % 2 == 0, tiles)
                halo = jnp.where(upper, *(sides if a == 0 else sides[::-1]))
            if a == 1:
                halo = turned(halo, REACH, 0)
            return jnp.concatenate([core, halo], axis=0)
        side, pick = (0, from_left) if block < 0 else (1, from_right)
        slot = layer if a == 0 else layers + layer - (1 if block < 0 else 0)
        core = pick(even, (first_ref[slot], second_ref[slot]))
        core = join(core, near_lanes[side], *(slots["own", a, layer, i] for i in range(rows // SUBLANES)))
        halo = near_halo(a, side, layers - layer if block < 0 else layer + 1)
        return jnp.concatenate([core, halo], axis=0)

    faces = x_faces_of(layers, ix, nx)

    def emit(layer, tile, value):
        part = slice(tile * LANES, (tile + 1) * LANES)
        fine_ref[layer, :, part] = value
        diff_ref[layer, :, part] = value - spread_ref[layer, :, part]

    iterate(
        count,
        rows,
        rows + 2 * REACH,
        lanes // LANES + 1,
        functools.partial(window, 0),
        functools.partial(window, 1),
        faces,
        row_numerators(rows + 2 * REACH, rows, iy, ny, 1.0),
        lane_numerators(rows + 2 * REACH, iz, nz, 1.0) + [2.0],
        coef_ref,
        storage_rate,
        emit,
        scratch,
        (inverse_ref, tx_ref),
    )


def levels(both, got, raw, far, near, early, coefficients, own, halos, pooled, beyond, ready, peers):
    layers, rows, lanes = both.shape[0] // 2, *both.shape[1:]
    half = lanes // 2
    out = jax.ShapeDtypeStruct((layers, rows, lanes), jnp.float32)
    return pl.pallas_call(
        functools.partial(levels_kernel, peers, len(far)),
        out_shape=(out, out),
        in_specs=[VMEM] * (13 + len(got) + len(far)),
        out_specs=(VMEM, VMEM),
        scratch_shapes=window_scratch(3 * layers, rows, rows + 2 * REACH, lanes // LANES + 1)
        + [
            pltpu.VMEM((layers, rows, lanes), jnp.float32),
            pltpu.VMEM((lanes // LANES, rows, LANES), jnp.float32),
        ]
        + window_scratch(2 + 2 * REACH, SUBLANES, 2 * SUBLANES, half // LANES + 1)
        + [pltpu.VMEM((2 * SUBLANES, half), jnp.float32)],
        compiler_params=pltpu.CompilerParams(vmem_limit_bytes=32 << 20),
        cost_estimate=pl.CostEstimate(flops=20_000_000, bytes_accessed=10_000_000, transcendentals=0),
        name="levels",
    )(both, *got, *raw[::-1], *far, *near[::-1], early, coefficients, own, halos, pooled, beyond, *ready)


def shards(peers, log_perm, source, low_bound, high_bound):
    nx, ny, nz = peers
    layers, rows, lanes = log_perm.shape
    assert layers == REACH and rows == 2 * SUBLANES and nx > 2 and nz == 2
    both = jnp.concatenate([log_perm, source])
    own, *rows_sent = prep(both, ny)
    if ny == 2:
        got = (permute(rows_sent[0], "gy", ny, [(0, 1)]),)
    else:
        got = swap("gy", ny, rows_sent[1], rows_sent[0])
    for_second = raw_block(both, rows_sent[0], True)
    second = permute(for_second, "gx", nx, neighbour_pairs(nx, 1))
    for_first = raw_block(both, for_second, False)
    raw = (permute(for_first, "gx", nx, neighbour_pairs(nx, 0)), second)
    far_groups = far_pairs(nx)
    halos, lanes_sent = pooled_halos(both, own, got)
    early = lax.ppermute(lanes_sent, "gz", [(0, 1), (1, 0)])
    for_far = pack_far(own, halos, len(far_groups), ny > 2)
    far = [permute(tiles, "gx", nx, group) for tiles, group in zip(for_far, far_groups)]
    for_first, for_second = pack_near(own, halos, early, for_far[0], got)
    second = permute(for_second, "gx", nx, neighbour_pairs(nx, 1))
    near = (permute(for_first, "gx", nx, neighbour_pairs(nx, 0)), second)
    coefficients = chebyshev_coefficients(low_bound, high_bound, for_first)
    pooled = pool(coefficients, raw)
    ready = ahead(pooled, both, raw, nx)
    beyond = lax.ppermute(far_lanes(coefficients, far, lanes), "gz", [(0, 1), (1, 0)])
    return levels(both, got, raw, far, near, early, coefficients, own, halos, pooled, beyond, ready, peers)


def solution(mesh):
    peers = tuple(mesh.shape[axis] for axis in AXES)
    split = P(("groups", "gx"), "gy", "gz")
    return jax.shard_map(
        functools.partial(shards, peers),
        mesh=mesh,
        in_specs=(split, split, P(), P()),
        out_specs=(split, split),
        check_vma=False,
    )
```
